32 devices in a mesh: dp: 8 (over y, x, core), owner: 4 (over z).
Axes of the slice: x: 2, y: 2, z: 4, core: 2. Of those that a mesh axis runs over, the one named last changes fastest.
Arguments:
- gradients: bfloat16 [32, 704, 1024], P(None, 'dp', 'owner')
- momentum: float32 [32, 704, 1024], P(None, 'dp', 'owner'), may hold values from -6 to 6
- owner_table: int32 [32], replicated, may hold values from 0 to 31, as said below
Outputs:
- new_momentum: float32 [32, 704, 1024], P(None, 'dp', 'owner')
- update: bfloat16 [32, 704, 1024], P(None, 'dp', 'owner')
- owned: bfloat16 [64, 704, 1024], P(('dp', 'owner'))
The draws below stay inside these ranges and needn't reach their ends.
Inputs may be any that keep to these rules, and one draw needn't show every extreme that they name: owner_table[i] numbers a device as 4 times its dp index plus its owner index; exactly half of the devices own 2 matrices each and the others own none; the first and the last device are always among the owners.
All inputs are finite; a program needn't handle non-finite values.
Results may differ from the reference program's by a relative error of at most 0.0083.
Values may be sent and summed in bfloat16 or wider, within the bound.
No kernel may reach another device: no remote copies, remote signals or barrier semaphores. Data moves between devices by JAX's collectives and lax.ppermute only.
A program may use at most 128 MiB of HBM per device.

```python
import math
import jax
import jax.numpy as jnp
from jax import lax

D = 1024
FF = 704
ITERS = 2
CAP = 2
MATS = 32
DEVICES = 32


def draw_gradients(key, part):
    key = jax.random.fold_in(key, 11)
    key_base, key_rows, key_cols = jax.random.split(key, 3)
    row_scale = jnp.exp(jax.random.uniform(key_rows, (MATS, FF, 1), jnp.float32, math.log(0.3), math.log(3.0)))
    col_scale = jnp.exp(jax.random.uniform(key_cols, (MATS, 1, D), jnp.float32, math.log(0.3), math.log(3.0)))
    values = jax.random.normal(key_base, (MATS, FF, D), jnp.float32) * row_scale * col_scale
    return values.astype(jnp.bfloat16)


def draw_owner_table(key, part):
    key = jax.random.fold_in(key, 5)
    key_pick, key_order = jax.random.split(key, 2)
    half_count = DEVICES // CAP
    middle = (jax.random.permutation(key_pick, DEVICES - 2) + 1).astype(jnp.int32)
    ends = jnp.array([0, DEVICES - 1], dtype=jnp.int32)
    busy_devices = jnp.concatenate([ends, middle[:half_count - 2]]).astype(jnp.int32)
    busy_devices = busy_devices[jax.random.permutation(key_order, half_count)]
    picks = jnp.arange(MATS, dtype=jnp.int32) % half_count
    return busy_devices[picks].astype(jnp.int32)


def block_levels(rng, shape, cuts, smallest, largest):
    gain, own = 1.0, jax.random.fold_in(rng, 6)
    for dim, blocks in cuts:
        heights = jnp.exp(jax.random.uniform(jax.random.fold_in(own, dim), (blocks,), jnp.float32, smallest / len(cuts), largest / len(cuts)))
        gain = gain * jnp.repeat(heights, shape[dim] // blocks).reshape([-1 if axis == dim else 1 for axis in range(len(shape))])
    return gain


def scatter_about(rng, extent, deviation, most, cuts=(), kind=jnp.bfloat16):
    factor_of = block_levels(rng, extent, cuts, -0.22, 0.18) if cuts else 1.0
    values = jax.random.normal(rng, extent, jnp.float32) * deviation * factor_of
    return jnp.minimum(jnp.maximum(values, -most), most).astype(kind)


def setup_inputs(seed: int = 0) -> dict:
    keys = jax.random.split(jax.random.key(seed), 4)
    return {
        "gradients": draw_gradients(jax.random.fold_in(keys[3], 71), 0),
        "momentum": scatter_about(keys[1], (MATS, FF, D), 1.0, 6.0, ((1, 8), (2, 4)), jnp.float32),
        "owner_table": draw_owner_table(jax.random.fold_in(keys[3], 71), 0),
    }


coef_a = 3.4445
coef_b = -4.775
coef_c = 2.0315
momentum_beta = 0.95
epsilon = 1e-07

def orthogonalize(matrix):
    widened = matrix.astype(jnp.float32)
    magnitude = jnp.sqrt(jnp.sum(widened * widened))
    current = (widened / (magnitude + epsilon)).astype(jnp.bfloat16)
    update_scale = 0.2 * math.sqrt(max(FF, D))
    result = current
    for iteration in range(ITERS):
        current_wide = current.astype(jnp.float32)
        gram_matrix = jnp.dot(current_wide, current_wide.T, preferred_element_type=jnp.float32).astype(jnp.bfloat16)
        gram_wide = gram_matrix.astype(jnp.float32)
        square = jnp.dot(gram_wide, gram_wide, preferred_element_type=jnp.float32)
        mixing = (coef_b * gram_wide + coef_c * square).astype(jnp.bfloat16)
        combined = coef_a * current_wide + jnp.dot(mixing.astype(jnp.float32), current_wide, preferred_element_type=jnp.float32)
        if iteration + 1 < ITERS:
            current = combined.astype(jnp.bfloat16)
        else:
            result = (update_scale * combined).astype(jnp.bfloat16)
    return result

def reference(gradients, momentum, owner_table):
    new_momentum = momentum_beta * momentum + gradients.astype(jnp.float32)
    nesterov = (gradients.astype(jnp.float32) + momentum_beta * new_momentum).astype(jnp.bfloat16)
    update = lax.map(orthogonalize, nesterov)
    positions = jnp.arange(MATS, dtype=jnp.int32)
    same_owner = (owner_table[None, :] == owner_table[:, None]) & (positions[None, :] < positions[:, None])
    slot_rank = lax.optimization_barrier(jnp.sum(same_owner.astype(jnp.int32), axis=1)).astype(jnp.int32)
    slot_index = (owner_table * CAP + slot_rank).astype(jnp.int32)
    owned = jnp.zeros((DEVICES * CAP, FF, D), jnp.bfloat16).at[slot_index].set(update)
    return (new_momentum, update, owned)
```

```python
import functools
import math

import jax
import jax.numpy as jnp
from jax import lax
from jax.experimental import pallas as pl
from jax.experimental.pallas import tpu as pltpu
from jax.sharding import PartitionSpec as P

ITERS = 2
CAP = 2

coef_a = 3.4445
coef_b = -4.775
coef_c = 2.0315
momentum_beta = 0.95
epsilon = 1e-07

AXES = ("dp", "owner")
VMEM_BYTES = 56 * 1024 * 1024


def round_up(value, multiple):
    return -(-value // multiple) * multiple


def pack_kernel(chunk, owner_ref, g_ref, m_ref, nm_ref, first_ref, second_ref, count_ref):
    step = pl.program_id(0)
    devices = first_ref.shape[0]

    @pl.when(step == 0)
    def _():
        first_ref[...] = jnp.zeros_like(first_ref)
        second_ref[...] = jnp.zeros_like(second_ref)

        @pl.loop(0, devices)
        def _(d):
            count_ref[d] = 0

    for j in range(chunk):
        owner = owner_ref[step * chunk + j]
        rank = count_ref[owner]
        count_ref[owner] = rank + 1
        grad = g_ref[j].astype(jnp.float32)
        new = momentum_beta * m_ref[j] + grad
        nm_ref[j] = new
        nesterov = (grad + momentum_beta * new).astype(jnp.bfloat16)

        @pl.when(rank == 0)
        def _():
            first_ref[owner] = nesterov

        @pl.when(rank == 1)
        def _():
            second_ref[owner] = nesterov


def pack(gradients, momentum, owner_table, devices):
    mats, rows, cols = gradients.shape
    chunk = 8
    block = pl.BlockSpec((chunk, rows, cols), lambda i, table: (i, 0, 0))
    slots = pl.BlockSpec((devices, rows, cols), lambda i, table: (0, 0, 0))
    slot_shape = jax.ShapeDtypeStruct((devices, rows, cols), jnp.bfloat16)
    return pl.pallas_call(
        functools.partial(pack_kernel, chunk),
        grid_spec=pltpu.PrefetchScalarGridSpec(
            num_scalar_prefetch=1,
            grid=(mats // chunk,),
            in_specs=[block, block],
            out_specs=[block, slots, slots],
            scratch_shapes=[pltpu.SMEM((devices,), jnp.int32)],
        ),
        out_shape=[jax.ShapeDtypeStruct(momentum.shape, jnp.float32), slot_shape, slot_shape],
        compiler_params=pltpu.CompilerParams(vmem_limit_bytes=VMEM_BYTES),
        cost_estimate=pl.CostEstimate(
            flops=4 * mats * rows * cols, bytes_accessed=14 * mats * rows * cols, transcendentals=0
        ),
        name="pack",
    )(owner_table, gradients, momentum)


def matmul(lhs, rhs, rhs_dim):
    return lax.dot_general(
        lhs, rhs, (((1,), (rhs_dim,)), ((), ())), preferred_element_type=jnp.float32
    )


def ortho_kernel(row_size, col_size, tile_blocks, *refs):
    x_ref, owned_ref, back_ref, x_s, y_s, gram_s, mix_s = refs[0], *refs[-6:]
    _, rows, cols = x_ref.shape
    padded = round_up(rows, 16)
    tile = padded * tile_blocks
    tiles = row_size // tile_blocks

    total = jnp.zeros((1, cols), jnp.float32)
    for r in range(row_size):
        if padded > rows:
            x_s[r * padded + rows : (r + 1) * padded, :] = jnp.zeros(
                (padded - rows, x_s.shape[1]), x_s.dtype
            )
        for c in range(col_size):
            block = x_ref[r * col_size + c]
            x_s[r * padded : r * padded + rows, c * cols : (c + 1) * cols] = block
            wide = block.astype(jnp.float32)
            total += jnp.sum(wide * wide, axis=0, keepdims=True)
    magnitude = jnp.sqrt(jnp.sum(total, axis=1, keepdims=True))
    inverse = 1.0 / (magnitude + epsilon)
    update_scale = 0.2 * math.sqrt(max(rows * row_size, cols * col_size))

    for iteration in range(ITERS):
        src = x_s if iteration == 0 else y_s
        for t in range(tiles):
            span = slice(t * tile, (t + 1) * tile)
            gram = matmul(src[span, :], src[...], 1)
            if iteration == 0:
                gram = gram * (inverse * inverse)
            gram_s[span, :] = gram.astype(jnp.bfloat16)
        for t in range(tiles):
            span = slice(t * tile, (t + 1) * tile)
            square = matmul(gram_s[span, :], gram_s[...], 0)
            mix_s[span, :] = (
                coef_b * gram_s[span, :].astype(jnp.float32) + coef_c * square
            ).astype(jnp.bfloat16)
        for t in range(tiles):
            span = slice(t * tile, (t + 1) * tile)
            combined = coef_a * src[span, :].astype(jnp.float32) + matmul(
                mix_s[span, :], src[...], 0
            )
            if iteration == 0:
                combined = combined * inverse
            if iteration + 1 < ITERS:
                y_s[span, :] = combined.astype(jnp.bfloat16)
            else:
                result = (update_scale * combined).astype(jnp.bfloat16)
                for j in range(tile_blocks):
                    r = t * tile_blocks + j
                    block = result[j * padded : j * padded + rows, :]
                    owned_ref[0, r * rows : (r + 1) * rows, :] = block
                    for c in range(col_size):
                        back_ref[r * col_size + c] = block[:, c * cols : (c + 1) * cols]


def orthogonalize(arrived, slot, row_size, col_size, owned):
    devices, rows, cols = arrived.shape
    height, width = rows * row_size, cols * col_size
    padded = round_up(rows, 16) * row_size
    tile_blocks = max(row_size // 2, 1)
    whole = pl.BlockSpec((devices, rows, cols), lambda i: (0, 0, 0))
    in_specs, operands, aliases = [whole], [arrived], {}
    if owned is not None:
        in_specs.append(pl.BlockSpec(memory_space=pl.ANY))
        operands.append(owned)
        aliases = {1: 0}
    return pl.pallas_call(
        functools.partial(ortho_kernel, row_size, col_size, tile_blocks),
        grid=(1,),
        in_specs=in_specs,
        out_specs=[pl.BlockSpec((1, height, width), lambda i: (slot, 0, 0)), whole],
        out_shape=[
            jax.ShapeDtypeStruct((CAP, height, width), jnp.bfloat16),
            jax.ShapeDtypeStruct((devices, rows, cols), jnp.bfloat16),
        ],
        scratch_shapes=[
            pltpu.VMEM((padded, width), jnp.bfloat16),
            pltpu.VMEM((padded, width), jnp.bfloat16),
            pltpu.VMEM((padded, padded), jnp.bfloat16),
            pltpu.VMEM((padded, padded), jnp.bfloat16),
        ],
        input_output_aliases=aliases,
        compiler_params=pltpu.CompilerParams(vmem_limit_bytes=VMEM_BYTES),
        cost_estimate=pl.CostEstimate(
            flops=2 * ITERS * padded * padded * (2 * width + padded),
            bytes_accessed=6 * height * width,
            transcendentals=0,
        ),
        name="orthogonalize",
    )(*operands)


def unpack_kernel(owner_ref, first_ref, second_ref, update_ref, count_ref):
    mats = update_ref.shape[0]
    devices = first_ref.shape[0]

    @pl.loop(0, devices)
    def _(d):
        count_ref[d] = 0

    for i in range(mats):
        owner = owner_ref[i]
        rank = count_ref[owner]
        count_ref[owner] = rank + 1

        @pl.when(rank == 0)
        def _():
            update_ref[i] = first_ref[owner]

        @pl.when(rank == 1)
        def _():
            update_ref[i] = second_ref[owner]


def unpack(first, second, owner_table):
    devices, rows, cols = first.shape
    mats = owner_table.shape[0]
    slots = pl.BlockSpec((devices, rows, cols), lambda i, table: (0, 0, 0))
    return pl.pallas_call(
        unpack_kernel,
        grid_spec=pltpu.PrefetchScalarGridSpec(
            num_scalar_prefetch=1,
            grid=(1,),
            in_specs=[slots, slots],
            out_specs=pl.BlockSpec((mats, rows, cols), lambda i, table: (0, 0, 0)),
            scratch_shapes=[pltpu.SMEM((devices,), jnp.int32)],
        ),
        out_shape=jax.ShapeDtypeStruct((mats, rows, cols), jnp.bfloat16),
        compiler_params=pltpu.CompilerParams(vmem_limit_bytes=VMEM_BYTES),
        cost_estimate=pl.CostEstimate(
            flops=0, bytes_accessed=6 * devices * rows * cols, transcendentals=0
        ),
        name="unpack",
    )(owner_table, first, second)


def exchange(blocks):
    return lax.all_to_all(blocks, AXES, split_axis=0, concat_axis=0, tiled=True)


def on_device(gradients, momentum, owner_table):
    row_size = lax.axis_size("dp")
    col_size = lax.axis_size("owner")
    devices = row_size * col_size
    new_momentum, first, second = pack(gradients, momentum, owner_table, devices)
    owned, back_first = orthogonalize(exchange(first), 0, row_size, col_size, None)
    owned, back_second = orthogonalize(exchange(second), 1, row_size, col_size, owned)
    update = unpack(exchange(back_first), exchange(back_second), owner_table)
    return (new_momentum, update, owned)


def solution(mesh):
    return jax.shard_map(
        on_device,
        mesh=mesh,
        in_specs=(P(None, "dp", "owner"), P(None, "dp", "owner"), P()),
        out_specs=(P(None, "dp", "owner"), P(None, "dp", "owner"), P(("dp", "owner"), None, None)),
        check_vma=False,
    )
```

```python
import functools
import math

import jax
import jax.numpy as jnp
from jax import lax
from jax.experimental import pallas as pl
from jax.experimental.pallas import tpu as pltpu
from jax.sharding import PartitionSpec as P

ITERS = 2
CAP = 2

coef_a = 3.4445
coef_b = -4.775
coef_c = 2.0315
momentum_beta = 0.95
epsilon = 1e-07

AXES = ("dp", "owner")
VMEM_BYTES = 56 * 1024 * 1024


def round_up(value, multiple):
    return -(-value // multiple) * multiple


def pack_kernel(
    chunk, owner_ref, g_ref, m_ref, nm_ref, first_ref, second_ref, host_ref, count_ref, helper_ref
):
    step = pl.program_id(0)
    devices = first_ref.shape[0]
    mats = host_ref.shape[0]

    @pl.when(step == 0)
    def _():
        second_ref[...] = jnp.zeros_like(second_ref)

        @pl.loop(0, devices)
        def _(d):
            count_ref[d] = 0

        @pl.loop(0, mats)
        def _(i):
            count_ref[owner_ref[i]] = 1

        def list_idle(d, found):
            helper_ref[found] = d
            return found + 1 - count_ref[d]

        lax.fori_loop(0, devices, list_idle, 0)

        def list_owners(d, found):
            owns = count_ref[d]
            count_ref[d] = found
            return found + owns

        lax.fori_loop(0, devices, list_owners, 0)

        @pl.loop(0, mats)
        def _(i):
            host_ref[i] = -1

        def place(i, _):
            owner = owner_ref[i]
            found = count_ref[owner]
            again = found < 0
            host_ref[i] = jnp.where(again, helper_ref[jnp.where(again, -1 - found, 0)], owner)
            count_ref[owner] = jnp.where(again, found, -1 - found)
            return 0

        lax.fori_loop(0, mats, place, 0)

    for j in range(chunk):
        owner = owner_ref[step * chunk + j]
        host = host_ref[step * chunk + j]
        grad = g_ref[j].astype(jnp.float32)
        new = momentum_beta * m_ref[j] + grad
        nm_ref[j] = new
        nesterov = (grad + momentum_beta * new).astype(jnp.bfloat16)
        first_ref[host] = nesterov

        @pl.when(host != owner)
        def _():
            second_ref[owner] = nesterov


def pack(gradients, momentum, owner_table, devices):
    mats, rows, cols = gradients.shape
    chunk = 8
    block = pl.BlockSpec((chunk, rows, cols), lambda i, table: (i, 0, 0))
    slots = pl.BlockSpec((devices, rows, cols), lambda i, table: (0, 0, 0))
    slot_shape = jax.ShapeDtypeStruct((devices, rows, cols), jnp.bfloat16)
    return pl.pallas_call(
        functools.partial(pack_kernel, chunk),
        grid_spec=pltpu.PrefetchScalarGridSpec(
            num_scalar_prefetch=1,
            grid=(mats // chunk,),
            in_specs=[block, block],
            out_specs=[block, slots, slots, pl.BlockSpec(memory_space=pltpu.SMEM)],
            scratch_shapes=[
                pltpu.SMEM((devices,), jnp.int32),
                pltpu.SMEM((devices + 1,), jnp.int32),
            ],
        ),
        out_shape=[
            jax.ShapeDtypeStruct(momentum.shape, jnp.float32),
            slot_shape,
            slot_shape,
            jax.ShapeDtypeStruct((mats,), jnp.int32),
        ],
        compiler_params=pltpu.CompilerParams(vmem_limit_bytes=VMEM_BYTES),
        cost_estimate=pl.CostEstimate(
            flops=4 * mats * rows * cols, bytes_accessed=14 * mats * rows * cols, transcendentals=0
        ),
        name="pack",
    )(owner_table, gradients, momentum)


def matmul(lhs, rhs, rhs_dim):
    return lax.dot_general(
        lhs, rhs, (((1,), (rhs_dim,)), ((), ())), preferred_element_type=jnp.float32
    )


def ortho_kernel(row_size, col_size, tile_blocks, slot, *refs):
    owns_ref, x_ref = refs[:2]
    x_s, y_s, gram_s, mix_s = refs[-4:]
    if slot == 0:
        owned_ref, back_ref = refs[2:4]
    else:
        owned_ref, back_ref = refs[3], None
    owns = owns_ref[0] != 0
    _, rows, cols = x_ref.shape
    padded = round_up(rows, 16)
    tile = padded * tile_blocks
    tiles = row_size // tile_blocks

    total = jnp.zeros((1, cols), jnp.float32)
    for r in range(row_size):
        if padded > rows:
            x_s[r * padded + rows : (r + 1) * padded, :] = jnp.zeros(
                (padded - rows, x_s.shape[1]), x_s.dtype
            )
        for c in range(col_size):
            block = x_ref[r * col_size + c]
            x_s[r * padded : r * padded + rows, c * cols : (c + 1) * cols] = block
            wide = block.astype(jnp.float32)
            total += jnp.sum(wide * wide, axis=0, keepdims=True)
    magnitude = jnp.sqrt(jnp.sum(total, axis=1, keepdims=True))
    inverse = 1.0 / (magnitude + epsilon)
    update_scale = 0.2 * math.sqrt(max(rows * row_size, cols * col_size))

    for iteration in range(ITERS):
        src = x_s if iteration == 0 else y_s
        for t in range(tiles):
            span = slice(t * tile, (t + 1) * tile)
            gram = matmul(src[span, :], src[...], 1)
            if iteration == 0:
                gram = gram * (inverse * inverse)
            gram_s[span, :] = gram.astype(jnp.bfloat16)
        for t in range(tiles):
            span = slice(t * tile, (t + 1) * tile)
            square = matmul(gram_s[span, :], gram_s[...], 0)
            mix_s[span, :] = (
                coef_b * gram_s[span, :].astype(jnp.float32) + coef_c * square
            ).astype(jnp.bfloat16)
        for t in range(tiles):
            span = slice(t * tile, (t + 1) * tile)
            combined = coef_a * src[span, :].astype(jnp.float32) + matmul(
                mix_s[span, :], src[...], 0
            )
            if iteration == 0:
                combined = combined * inverse
            if iteration + 1 < ITERS:
                y_s[span, :] = combined.astype(jnp.bfloat16)
            else:
                result = (update_scale * combined).astype(jnp.bfloat16)
                for j in range(tile_blocks):
                    r = t * tile_blocks + j
                    block = result[j * padded : j * padded + rows, :]
                    owned_ref[0, r * rows : (r + 1) * rows, :] = jnp.where(
                        owns, block, jnp.zeros_like(block)
                    )
                    if back_ref is not None:
                        for c in range(col_size):
                            back_ref[r * col_size + c] = block[:, c * cols : (c + 1) * cols]


def orthogonalize(owns, arrived, slot, row_size, col_size, owned=None):
    devices, rows, cols = arrived.shape
    height, width = rows * row_size, cols * col_size
    padded = round_up(rows, 16) * row_size
    tile_blocks = max(row_size // 2, 1)
    whole = pl.BlockSpec((devices, rows, cols), lambda i: (0, 0, 0))
    in_specs, operands, aliases = [pl.BlockSpec(memory_space=pltpu.SMEM), whole], [owns, arrived], {}
    out_specs = [pl.BlockSpec((1, height, width), lambda i: (slot, 0, 0))]
    out_shape = [jax.ShapeDtypeStruct((CAP, height, width), jnp.bfloat16)]
    if slot == 0:
        out_specs.append(whole)
        out_shape.append(jax.ShapeDtypeStruct((devices, rows, cols), jnp.bfloat16))
    else:
        in_specs.append(pl.BlockSpec(memory_space=pl.ANY))
        operands.append(owned)
        aliases = {2: 0}
    return pl.pallas_call(
        functools.partial(ortho_kernel, row_size, col_size, tile_blocks, slot),
        grid=(1,),
        in_specs=in_specs,
        out_specs=out_specs,
        out_shape=out_shape,
        scratch_shapes=[
            pltpu.VMEM((padded, width), jnp.bfloat16),
            pltpu.VMEM((padded, width), jnp.bfloat16),
            pltpu.VMEM((padded, padded), jnp.bfloat16),
            pltpu.VMEM((padded, padded), jnp.bfloat16),
        ],
        input_output_aliases=aliases,
        compiler_params=pltpu.CompilerParams(vmem_limit_bytes=VMEM_BYTES),
        cost_estimate=pl.CostEstimate(
            flops=2 * ITERS * padded * padded * (2 * width + padded),
            bytes_accessed=6 * height * width,
            transcendentals=0,
        ),
        name="orthogonalize",
    )(*operands)


def unpack_kernel(host_ref, back_ref, update_ref):
    for i in range(update_ref.shape[0]):
        update_ref[i] = back_ref[host_ref[i]]


def unpack(back, host):
    devices, rows, cols = back.shape
    mats = host.shape[0]
    return pl.pallas_call(
        unpack_kernel,
        grid_spec=pltpu.PrefetchScalarGridSpec(
            num_scalar_prefetch=1,
            grid=(1,),
            in_specs=[pl.BlockSpec((devices, rows, cols), lambda i, table: (0, 0, 0))],
            out_specs=pl.BlockSpec((mats, rows, cols), lambda i, table: (0, 0, 0)),
        ),
        out_shape=jax.ShapeDtypeStruct((mats, rows, cols), jnp.bfloat16),
        compiler_params=pltpu.CompilerParams(vmem_limit_bytes=VMEM_BYTES),
        cost_estimate=pl.CostEstimate(
            flops=0, bytes_accessed=4 * devices * rows * cols, transcendentals=0
        ),
        name="unpack",
    )(host, back)


def exchange(blocks):
    return lax.all_to_all(blocks, AXES, split_axis=0, concat_axis=0, tiled=True)


def on_device(gradients, momentum, owner_table):
    row_size = lax.axis_size("dp")
    col_size = lax.axis_size("owner")
    devices = row_size * col_size
    me = lax.axis_index("dp") * col_size + lax.axis_index("owner")
    owns = jnp.any(owner_table == me).astype(jnp.int32).reshape(1)
    new_momentum, first, second, host = pack(gradients, momentum, owner_table, devices)
    owned, back = orthogonalize(owns, exchange(first), 0, row_size, col_size)
    (owned,) = orthogonalize(owns, exchange(second), 1, row_size, col_size, owned)
    update = unpack(exchange(back), host)
    return (new_momentum, update, owned)


def solution(mesh):
    return jax.shard_map(
        on_device,
        mesh=mesh,
        in_specs=(P(None, "dp", "owner"), P(None, "dp", "owner"), P()),
        out_specs=(P(None, "dp", "owner"), P(None, "dp", "owner"), P(("dp", "owner"), None, None)),
        check_vma=False,
    )
```

```python
import functools
import math

import jax
import jax.numpy as jnp
from jax import lax
from jax.experimental import pallas as pl
from jax.experimental.pallas import tpu as pltpu
from jax.sharding import PartitionSpec as P

ITERS = 2
CAP = 2

coef_a = 3.4445
coef_b = -4.775
coef_c = 2.0315
momentum_beta = 0.95
epsilon = 1e-07

AXES = ("dp", "owner")
VMEM_BYTES = 56 * 1024 * 1024
PARAMS = pltpu.CompilerParams(vmem_limit_bytes=VMEM_BYTES)
SMEM = pl.BlockSpec(memory_space=pltpu.SMEM)

NOTHING, SINGLE, PAIRED = 0, 1, 2


def round_up(value, multiple):
    return -(-value // multiple) * multiple


def whole(shape):
    return pl.BlockSpec(shape, lambda *_: (0,) * len(shape))


def nesterov_of(grad_ref, momentum_ref, j):
    grad = grad_ref[j].astype(jnp.float32)
    new = momentum_beta * momentum_ref[j] + grad
    return new, (grad + momentum_beta * new).astype(jnp.bfloat16)


def pack_kernel(
    chunk, col_size, owner_ref, g_ref, m_ref, first_ref, host_ref, kind_ref, most_ref,
    idle_ref, helper_ref, layer_ref,
):
    step = pl.program_id(0)
    devices = first_ref.shape[0]
    mats = host_ref.shape[0]

    @pl.when(step == 0)
    def _():
        @pl.loop(0, devices)
        def _(d):
            kind_ref[d] = 0

        @pl.loop(0, col_size)
        def _(z):
            layer_ref[z] = 0

        @pl.loop(0, mats)
        def _(i):
            kind_ref[owner_ref[i]] = 1

        def list_idle(d, found):
            idle_ref[found] = d
            taken = kind_ref[d] + kind_ref[d ^ col_size]
            return found + jnp.where(taken == 0, 1, 0)

        lax.fori_loop(0, devices, list_idle, 0)

        def plan_chip(k, carry):
            found, most = carry
            low = (k // col_size) * 2 * col_size + k % col_size
            high = low + col_size
            owns_low, owns_high = kind_ref[low], kind_ref[high]
            paired = owns_low + owns_high == 2
            z = k % col_size
            place = layer_ref[z]
            layer_ref[z] = jnp.where(paired, place + 2, place)
            kind_ref[low] = jnp.where(paired, PAIRED + place, owns_low)
            kind_ref[high] = jnp.where(paired, PAIRED + place + 1, owns_high)
            helper_ref[low] = jnp.where(paired, idle_ref[found], high)
            helper_ref[high] = jnp.where(paired, idle_ref[found + 1], low)
            return jnp.where(paired, found + 2, found), jnp.maximum(most, layer_ref[z])

        _, most = lax.fori_loop(0, devices // 2, plan_chip, (0, 0))
        most_ref[0] = most

        def place_matrix(i, _):
            owner = owner_ref[i]
            helper = helper_ref[owner]
            again = helper < 0
            host_ref[i] = jnp.where(again, -1 - helper, owner)
            helper_ref[owner] = -1 - helper
            return 0

        lax.fori_loop(0, mats, place_matrix, 0)

    for j in range(chunk):
        _, nesterov = nesterov_of(g_ref, m_ref, j)
        first_ref[host_ref[step * chunk + j]] = nesterov


def pack(gradients, momentum, owner_table, devices, col_size):
    mats, rows, cols = gradients.shape
    chunk = 8
    block = pl.BlockSpec((chunk, rows, cols), lambda i, *_: (i, 0, 0))
    return pl.pallas_call(
        functools.partial(pack_kernel, chunk, col_size),
        grid_spec=pltpu.PrefetchScalarGridSpec(
            num_scalar_prefetch=1,
            grid=(mats // chunk,),
            in_specs=[block, block],
            out_specs=[whole((devices, rows, cols)), SMEM, SMEM, SMEM],
            scratch_shapes=[
                pltpu.SMEM((devices + 1,), jnp.int32),
                pltpu.SMEM((devices,), jnp.int32),
                pltpu.SMEM((col_size,), jnp.int32),
            ],
        ),
        out_shape=[
            jax.ShapeDtypeStruct((devices, rows, cols), jnp.bfloat16),
            jax.ShapeDtypeStruct((mats,), jnp.int32),
            jax.ShapeDtypeStruct((devices,), jnp.int32),
            jax.ShapeDtypeStruct((1,), jnp.int32),
        ],
        compiler_params=PARAMS,
        cost_estimate=pl.CostEstimate(
            flops=4 * mats * rows * cols, bytes_accessed=8 * mats * rows * cols, transcendentals=0
        ),
        name="pack",
    )(owner_table, gradients, momentum)


def momentum_kernel(
    chunk, col_size, room, owner_ref, host_ref, kind_ref, g_ref, m_ref, nm_ref, *refs
):
    near_refs, far_ref, held = refs[:col_size], refs[col_size], refs[col_size + 1]
    step = pl.program_id(0)
    here = lax.axis_index("owner")
    for j in range(chunk):
        new, nesterov = nesterov_of(g_ref, m_ref, j)
        nm_ref[j] = new
        owner = owner_ref[step * chunk + j]
        place = kind_ref[owner] - PAIRED
        second = (host_ref[step * chunk + j] != owner) & (place >= 0)
        layer = owner % col_size

        @pl.when(second & (place < room))
        def _():
            held[(layer ^ here) * room + place] = nesterov

        @pl.when(second & (place >= room))
        def _():
            far_ref[layer * room + place - room] = nesterov

    @pl.when(step == pl.num_programs(0) - 1)
    def _():
        for offset in range(col_size):
            near_refs[offset][...] = held[offset * room : (offset + 1) * room]


def update_momentum(gradients, momentum, owner_table, host, kind, col_size, room):
    mats, rows, cols = gradients.shape
    chunk = 8
    block = pl.BlockSpec((chunk, rows, cols), lambda i, *_: (i, 0, 0))
    near = jax.ShapeDtypeStruct((room, rows, cols), jnp.bfloat16)
    far = jax.ShapeDtypeStruct((col_size * room, rows, cols), jnp.bfloat16)
    new_momentum, *near, far = pl.pallas_call(
        functools.partial(momentum_kernel, chunk, col_size, room),
        grid_spec=pltpu.PrefetchScalarGridSpec(
            num_scalar_prefetch=3,
            grid=(mats // chunk,),
            in_specs=[block, block],
            out_specs=[block] + [whole(near.shape)] * col_size + [whole(far.shape)],
            scratch_shapes=[pltpu.VMEM(far.shape, jnp.bfloat16)],
        ),
        out_shape=[jax.ShapeDtypeStruct(momentum.shape, jnp.float32)] + [near] * col_size + [far],
        compiler_params=PARAMS,
        cost_estimate=pl.CostEstimate(
            flops=4 * mats * rows * cols, bytes_accessed=12 * mats * rows * cols, transcendentals=0
        ),
        name="update_momentum",
    )(owner_table, host, kind, gradients, momentum)
    return new_momentum, near, far


def forward_kernel(col_size, row_size, room, kind_ref, *refs):
    near_refs, far_ref, out_refs = refs[:col_size], refs[col_size], refs[col_size + 1 :]
    row, col = lax.axis_index("dp"), lax.axis_index("owner")
    for offset in range(row_size):
        place = jnp.maximum(kind_ref[(row ^ offset) * col_size + col] - PAIRED, 0)

        @pl.when(place < room)
        def _():
            for z in range(col_size):
                out_refs[offset][col ^ z] = near_refs[z][place]

        @pl.when(place >= room)
        def _():
            for z in range(col_size):
                out_refs[offset][z] = far_ref[z * room + place - room]


def forward(kind, near, far, row_size, col_size, room):
    _, rows, cols = far.shape
    out = jax.ShapeDtypeStruct((col_size, rows, cols), jnp.bfloat16)
    return pl.pallas_call(
        functools.partial(forward_kernel, col_size, row_size, room),
        grid=(1,),
        in_specs=[SMEM] + [whole(near[0].shape)] * col_size + [whole(far.shape)],
        out_specs=[whole(out.shape)] * row_size,
        out_shape=[out] * row_size,
        compiler_params=PARAMS,
        cost_estimate=pl.CostEstimate(
            flops=0, bytes_accessed=8 * col_size * room * rows * cols, transcendentals=0
        ),
        name="forward",
    )(kind, *near, far)


def matmul(lhs, rhs, rhs_dim):
    return lax.dot_general(
        lhs, rhs, (((1,), (rhs_dim,)), ((), ())), preferred_element_type=jnp.float32
    )


def newton_schulz(rows, cols, row_size, col_size, x_s, y_s, gram_s, mix_s, write):
    padded = round_up(rows, 16)
    tile_blocks = max(row_size // 2, 1)
    tile = padded * tile_blocks
    tiles = row_size // tile_blocks

    total = jnp.zeros((1, cols), jnp.float32)
    for r in range(row_size):
        for c in range(col_size):
            wide = x_s[r * padded : (r + 1) * padded, c * cols : (c + 1) * cols]
            wide = wide.astype(jnp.float32)
            total += jnp.sum(wide * wide, axis=0, keepdims=True)
    magnitude = jnp.sqrt(jnp.sum(total, axis=1, keepdims=True))
    inverse = 1.0 / (magnitude + epsilon)
    update_scale = 0.2 * math.sqrt(max(rows * row_size, cols * col_size))

    for iteration in range(ITERS):
        src = x_s if iteration == 0 else y_s
        for t in range(tiles):
            span = slice(t * tile, (t + 1) * tile)
            gram = matmul(src[span, :], src[...], 1)
            if iteration == 0:
                gram = gram * (inverse * inverse)
            gram_s[span, :] = gram.astype(jnp.bfloat16)
        for t in range(tiles):
            span = slice(t * tile, (t + 1) * tile)
            square = matmul(gram_s[span, :], gram_s[...], 0)
            mix_s[span, :] = (
                coef_b * gram_s[span, :].astype(jnp.float32) + coef_c * square
            ).astype(jnp.bfloat16)
        for t in range(tiles):
            span = slice(t * tile, (t + 1) * tile)
            combined = coef_a * src[span, :].astype(jnp.float32) + matmul(
                mix_s[span, :], src[...], 0
            )
            if iteration == 0:
                combined = combined * inverse
            if iteration + 1 < ITERS:
                y_s[span, :] = combined.astype(jnp.bfloat16)
            else:
                result = (update_scale * combined).astype(jnp.bfloat16)
                for j in range(tile_blocks):
                    write(t * tile_blocks + j, result[j * padded : j * padded + rows, :])


def clear_padding(x_s, rows, row_size):
    padded = round_up(rows, 16)
    if padded > rows:
        for r in range(row_size):
            x_s[r * padded + rows : (r + 1) * padded, :] = jnp.zeros(
                (padded - rows, x_s.shape[1]), x_s.dtype
            )


def gather_blocks(x_ref, x_s, row_size, col_size):
    _, rows, cols = x_ref.shape
    padded = round_up(rows, 16)
    for r in range(row_size):
        for c in range(col_size):
            x_s[r * padded : r * padded + rows, c * cols : (c + 1) * cols] = x_ref[
                r * col_size + c
            ]


def hosted_kernel(row_size, col_size, kind_ref, x_ref, owned_ref, back_ref, *scratch):
    _, rows, cols = x_ref.shape
    me = lax.axis_index("dp") * col_size + lax.axis_index("owner")
    owns = kind_ref[me] != NOTHING
    clear_padding(scratch[0], rows, row_size)
    gather_blocks(x_ref, scratch[0], row_size, col_size)

    def write(r, block):
        owned_ref[0, r * rows : (r + 1) * rows, :] = jnp.where(owns, block, jnp.zeros_like(block))
        for c in range(col_size):
            back_ref[r * col_size + c] = block[:, c * cols : (c + 1) * cols]

    newton_schulz(rows, cols, row_size, col_size, *scratch, write)


def second_kernel(row_size, col_size, kind_ref, shared_ref, *refs):
    row_refs, owned_ref, scratch = refs[:row_size], refs[row_size + 1], refs[row_size + 2 :]
    x_s = scratch[0]
    _, rows, cols = shared_ref.shape
    padded = round_up(rows, 16)
    row = lax.axis_index("dp")
    kind = kind_ref[row * col_size + lax.axis_index("owner")]
    clear_padding(x_s, rows, row_size)

    @pl.when(kind < PAIRED)
    def _():
        gather_blocks(shared_ref, x_s, row_size, col_size)

    @pl.when(kind >= PAIRED)
    def _():
        for offset in range(row_size):
            start = pl.multiple_of((row ^ offset) * padded, 16)
            for c in range(col_size):
                x_s[pl.ds(start, rows), c * cols : (c + 1) * cols] = row_refs[offset][c]

    def write(r, block):
        owned_ref[0, r * rows : (r + 1) * rows, :] = jnp.where(
            kind != NOTHING, block, jnp.zeros_like(block)
        )

    newton_schulz(rows, cols, row_size, col_size, *scratch, write)


def ortho_scratch(rows, cols, row_size, col_size):
    padded, width = round_up(rows, 16) * row_size, cols * col_size
    return [
        pltpu.VMEM((padded, width), jnp.bfloat16),
        pltpu.VMEM((padded, width), jnp.bfloat16),
        pltpu.VMEM((padded, padded), jnp.bfloat16),
        pltpu.VMEM((padded, padded), jnp.bfloat16),
    ]


def ortho_cost(rows, cols, row_size, col_size):
    padded, width = round_up(rows, 16) * row_size, cols * col_size
    return pl.CostEstimate(
        flops=2 * ITERS * padded * padded * (2 * width + padded),
        bytes_accessed=6 * padded * width,
        transcendentals=0,
    )


def orthogonalize_hosted(kind, arrived, row_size, col_size):
    devices, rows, cols = arrived.shape
    height, width = rows * row_size, cols * col_size
    return pl.pallas_call(
        functools.partial(hosted_kernel, row_size, col_size),
        grid=(1,),
        in_specs=[SMEM, whole(arrived.shape)],
        out_specs=[whole((1, height, width)), whole(arrived.shape)],
        out_shape=[
            jax.ShapeDtypeStruct((CAP, height, width), jnp.bfloat16),
            jax.ShapeDtypeStruct(arrived.shape, jnp.bfloat16),
        ],
        scratch_shapes=ortho_scratch(rows, cols, row_size, col_size),
        compiler_params=PARAMS,
        cost_estimate=ortho_cost(rows, cols, row_size, col_size),
        name="orthogonalize_hosted",
    )(kind, arrived)


def orthogonalize_second(kind, shared, by_row, owned, row_size, col_size):
    devices, rows, cols = shared.shape
    height, width = rows * row_size, cols * col_size
    return pl.pallas_call(
        functools.partial(second_kernel, row_size, col_size),
        grid=(1,),
        in_specs=[SMEM, whole(shared.shape)]
        + [whole(by_row[0].shape)] * row_size
        + [pl.BlockSpec(memory_space=pl.ANY)],
        out_specs=pl.BlockSpec((1, height, width), lambda i: (1, 0, 0)),
        out_shape=jax.ShapeDtypeStruct((CAP, height, width), jnp.bfloat16),
        scratch_shapes=ortho_scratch(rows, cols, row_size, col_size),
        input_output_aliases={2 + row_size: 0},
        compiler_params=PARAMS,
        cost_estimate=ortho_cost(rows, cols, row_size, col_size),
        name="orthogonalize_second",
    )(kind, shared, *by_row, owned)


def unpack_kernel(host_ref, back_ref, update_ref, sems):
    mats = update_ref.shape[0]

    def copy(i):
        return pltpu.make_async_copy(back_ref.at[host_ref[i]], update_ref.at[i], sems.at[i])

    @pl.loop(0, mats)
    def _(i):
        copy(i).start()

    @pl.loop(0, mats)
    def _(i):
        copy(i).wait()


def unpack(back, host):
    devices, rows, cols = back.shape
    mats = host.shape[0]
    return pl.pallas_call(
        unpack_kernel,
        grid_spec=pltpu.PrefetchScalarGridSpec(
            num_scalar_prefetch=1,
            grid=(1,),
            in_specs=[pl.BlockSpec(memory_space=pl.ANY)],
            out_specs=pl.BlockSpec(memory_space=pl.ANY),
            scratch_shapes=[pltpu.SemaphoreType.DMA((mats,))],
        ),
        out_shape=jax.ShapeDtypeStruct((mats, rows, cols), jnp.bfloat16),
        compiler_params=PARAMS,
        cost_estimate=pl.CostEstimate(
            flops=0, bytes_accessed=4 * mats * rows * cols, transcendentals=0
        ),
        name="unpack",
    )(host, back)


def exchange(blocks):
    return lax.all_to_all(blocks, AXES, split_axis=0, concat_axis=0, tiled=True)


def swap(block, axis, offset):
    size = lax.axis_size(axis)
    return lax.ppermute(block, axis, [(i, i ^ offset) for i in range(size)])


def on_device(gradients, momentum, owner_table):
    row_size = lax.axis_size("dp")
    col_size = lax.axis_size("owner")
    devices = row_size * col_size
    room = max(row_size // 2, 1)

    first, host, kind, most = pack(gradients, momentum, owner_table, devices, col_size)
    arrived = exchange(first)
    new_momentum, near, far = update_momentum(
        gradients, momentum, owner_table, host, kind, col_size, room
    )
    far = lax.cond(
        most[0] > room,
        lambda blocks: lax.all_to_all(blocks, "owner", split_axis=0, concat_axis=0, tiled=True),
        lambda blocks: blocks,
        far,
    )

    arrived, near = lax.optimization_barrier((arrived, near))
    near = [near[0]] + [swap(near[z], "owner", z) for z in range(1, col_size)]
    shared = swap(arrived, "dp", 1)
    owned, back = orthogonalize_hosted(kind, arrived, row_size, col_size)
    returned = exchange(back)
    by_row = forward(kind, near, far, row_size, col_size, room)
    by_row = [by_row[0]] + [swap(by_row[r], "dp", r) for r in range(1, row_size)]
    owned = orthogonalize_second(kind, shared, by_row, owned, row_size, col_size)
    update = unpack(returned, host)
    return (new_momentum, update, owned)


def solution(mesh):
    return jax.shard_map(
        on_device,
        mesh=mesh,
        in_specs=(P(None, "dp", "owner"), P(None, "dp", "owner"), P()),
        out_specs=(P(None, "dp", "owner"), P(None, "dp", "owner"), P(("dp", "owner"), None, None)),
        check_vma=False,
    )
```

```python
import functools
import math

import jax
import jax.numpy as jnp
from jax import lax
from jax.experimental import pallas as pl
from jax.experimental.pallas import tpu as pltpu
from jax.sharding import PartitionSpec as P

ITERS = 2
CAP = 2

coef_a = 3.4445
coef_b = -4.775
coef_c = 2.0315
momentum_beta = 0.95
epsilon = 1e-07

AXES = ("dp", "owner")
VMEM_BYTES = 60 * 1024 * 1024
PARAMS = pltpu.CompilerParams(vmem_limit_bytes=VMEM_BYTES)
SMEM = pl.BlockSpec(memory_space=pltpu.SMEM)

NOTHING, SINGLE, PAIRED = 0, 1, 2


def round_up(value, multiple):
    return -(-value // multiple) * multiple


def whole(shape):
    return pl.BlockSpec(shape, lambda *_: (0,) * len(shape))


def nesterov_of(grad_ref, momentum_ref, j):
    grad = grad_ref[j].astype(jnp.float32)
    new = momentum_beta * momentum_ref[j] + grad
    return new, (grad + momentum_beta * new).astype(jnp.bfloat16)


def pack_kernel(
    chunk, col_size, owner_ref, g_ref, m_ref, first_ref, host_ref, kind_ref, most_ref,
    idle_ref, helper_ref, layer_ref,
):
    step = pl.program_id(0)
    devices = first_ref.shape[0]
    mats = host_ref.shape[0]

    @pl.when(step == 0)
    def _():
        @pl.loop(0, devices)
        def _(d):
            kind_ref[d] = 0

        @pl.loop(0, col_size)
        def _(z):
            layer_ref[z] = 0

        @pl.loop(0, mats)
        def _(i):
            kind_ref[owner_ref[i]] = 1

        def list_idle(d, found):
            idle_ref[found] = d
            taken = kind_ref[d] + kind_ref[d ^ col_size]
            return found + jnp.where(taken == 0, 1, 0)

        lax.fori_loop(0, devices, list_idle, 0)

        def plan_chip(k, carry):
            found, most = carry
            low = (k // col_size) * 2 * col_size + k % col_size
            high = low + col_size
            owns_low, owns_high = kind_ref[low], kind_ref[high]
            paired = owns_low + owns_high == 2
            z = k % col_size
            place = layer_ref[z]
            layer_ref[z] = jnp.where(paired, place + 2, place)
            kind_ref[low] = jnp.where(paired, PAIRED + place, owns_low)
            kind_ref[high] = jnp.where(paired, PAIRED + place + 1, owns_high)
            helper_ref[low] = jnp.where(paired, idle_ref[found], high)
            helper_ref[high] = jnp.where(paired, idle_ref[found + 1], low)
            return jnp.where(paired, found + 2, found), jnp.maximum(most, layer_ref[z])

        _, most = lax.fori_loop(0, devices // 2, plan_chip, (0, 0))
        most_ref[0] = most

        def place_matrix(i, _):
            owner = owner_ref[i]
            helper = helper_ref[owner]
            again = helper < 0
            host_ref[i] = jnp.where(again, -1 - helper, owner)
            helper_ref[owner] = -1 - helper
            return 0

        lax.fori_loop(0, mats, place_matrix, 0)

    for j in range(chunk):
        _, nesterov = nesterov_of(g_ref, m_ref, j)
        first_ref[host_ref[step * chunk + j]] = nesterov


def pack(gradients, momentum, owner_table, devices, col_size):
    mats, rows, cols = gradients.shape
    chunk = 8
    block = pl.BlockSpec((chunk, rows, cols), lambda i, *_: (i, 0, 0))
    return pl.pallas_call(
        functools.partial(pack_kernel, chunk, col_size),
        grid_spec=pltpu.PrefetchScalarGridSpec(
            num_scalar_prefetch=1,
            grid=(mats // chunk,),
            in_specs=[block, block],
            out_specs=[whole((devices, rows, cols)), SMEM, SMEM, SMEM],
            scratch_shapes=[
                pltpu.SMEM((devices + 1,), jnp.int32),
                pltpu.SMEM((devices,), jnp.int32),
                pltpu.SMEM((col_size,), jnp.int32),
            ],
        ),
        out_shape=[
            jax.ShapeDtypeStruct((devices, rows, cols), jnp.bfloat16),
            jax.ShapeDtypeStruct((mats,), jnp.int32),
            jax.ShapeDtypeStruct((devices,), jnp.int32),
            jax.ShapeDtypeStruct((1,), jnp.int32),
        ],
        compiler_params=PARAMS,
        cost_estimate=pl.CostEstimate(
            flops=4 * mats * rows * cols, bytes_accessed=8 * mats * rows * cols, transcendentals=0
        ),
        name="pack",
    )(owner_table, gradients, momentum)


def momentum_kernel(
    chunk, col_size, room, owner_ref, host_ref, kind_ref, g_ref, m_ref, nm_ref, near_ref, far_ref
):
    step = pl.program_id(0)
    for j in range(chunk):
        new, nesterov = nesterov_of(g_ref, m_ref, j)
        nm_ref[j] = new
        owner = owner_ref[step * chunk + j]
        place = kind_ref[owner] - PAIRED
        second = (host_ref[step * chunk + j] != owner) & (place >= 0)
        layer = owner % col_size

        @pl.when(second & (place < room))
        def _():
            near_ref[layer * room + place] = nesterov

        @pl.when(second & (place >= room))
        def _():
            far_ref[layer * room + place - room] = nesterov


def update_momentum(gradients, momentum, owner_table, host, kind, col_size, room):
    mats, rows, cols = gradients.shape
    chunk = 8
    block = pl.BlockSpec((chunk, rows, cols), lambda i, *_: (i, 0, 0))
    part = jax.ShapeDtypeStruct((col_size * room, rows, cols), jnp.bfloat16)
    return pl.pallas_call(
        functools.partial(momentum_kernel, chunk, col_size, room),
        grid_spec=pltpu.PrefetchScalarGridSpec(
            num_scalar_prefetch=3,
            grid=(mats // chunk,),
            in_specs=[block, block],
            out_specs=[block, whole(part.shape), whole(part.shape)],
        ),
        out_shape=[jax.ShapeDtypeStruct(momentum.shape, jnp.float32), part, part],
        compiler_params=PARAMS,
        cost_estimate=pl.CostEstimate(
            flops=4 * mats * rows * cols, bytes_accessed=12 * mats * rows * cols, transcendentals=0
        ),
        name="update_momentum",
    )(owner_table, host, kind, gradients, momentum)


def forward_kernel(col_size, row_size, room, kind_ref, near_ref, far_ref, *out_refs):
    row, col = lax.axis_index("dp"), lax.axis_index("owner")
    for offset in range(row_size):
        place = jnp.maximum(kind_ref[(row ^ offset) * col_size + col] - PAIRED, 0)

        @pl.when(place < room)
        def _():
            for z in range(col_size):
                out_refs[offset][z] = near_ref[z * room + place]

        @pl.when(place >= room)
        def _():
            for z in range(col_size):
                out_refs[offset][z] = far_ref[z * room + place - room]


def forward(kind, near, far, row_size, col_size, room):
    _, rows, cols = far.shape
    out = jax.ShapeDtypeStruct((col_size, rows, cols), jnp.bfloat16)
    return pl.pallas_call(
        functools.partial(forward_kernel, col_size, row_size, room),
        grid=(1,),
        in_specs=[SMEM, whole(near.shape), whole(far.shape)],
        out_specs=[whole(out.shape)] * row_size,
        out_shape=[out] * row_size,
        compiler_params=PARAMS,
        cost_estimate=pl.CostEstimate(
            flops=0, bytes_accessed=8 * col_size * room * rows * cols, transcendentals=0
        ),
        name="forward",
    )(kind, near, far)


def matmul(lhs, rhs, rhs_dim):
    return lax.dot_general(
        lhs, rhs, (((1,), (rhs_dim,)), ((), ())), preferred_element_type=jnp.float32
    )


def newton_schulz(rows, cols, row_size, col_size, x_s, y_s, gram_s, mix_s, write):
    padded = round_up(rows, 16)
    tile_blocks = max(row_size // 2, 1)
    tile = padded * tile_blocks
    tiles = row_size // tile_blocks

    total = jnp.zeros((1, cols), jnp.float32)
    for r in range(row_size):
        for c in range(col_size):
            wide = x_s[r * padded : (r + 1) * padded, c * cols : (c + 1) * cols]
            wide = wide.astype(jnp.float32)
            total += jnp.sum(wide * wide, axis=0, keepdims=True)
    magnitude = jnp.sqrt(jnp.sum(total, axis=1, keepdims=True))
    inverse = 1.0 / (magnitude + epsilon)
    update_scale = 0.2 * math.sqrt(max(rows * row_size, cols * col_size))

    for iteration in range(ITERS):
        src = x_s if iteration == 0 else y_s
        for t in range(tiles):
            span = slice(t * tile, (t + 1) * tile)
            gram = matmul(src[span, :], src[...], 1)
            if iteration == 0:
                gram = gram * (inverse * inverse)
            gram_s[span, :] = gram.astype(jnp.bfloat16)
        for t in range(tiles):
            span = slice(t * tile, (t + 1) * tile)
            square = matmul(gram_s[span, :], gram_s[...], 0)
            mix_s[span, :] = (
                coef_b * gram_s[span, :].astype(jnp.float32) + coef_c * square
            ).astype(jnp.bfloat16)
        for t in range(tiles):
            span = slice(t * tile, (t + 1) * tile)
            combined = coef_a * src[span, :].astype(jnp.float32) + matmul(
                mix_s[span, :], src[...], 0
            )
            if iteration == 0:
                combined = combined * inverse
            if iteration + 1 < ITERS:
                y_s[span, :] = combined.astype(jnp.bfloat16)
            else:
                result = (update_scale * combined).astype(jnp.bfloat16)
                for j in range(tile_blocks):
                    write(t * tile_blocks + j, result[j * padded : j * padded + rows, :])


def clear_padding(x_s, rows, row_size):
    padded = round_up(rows, 16)
    if padded > rows:
        for r in range(row_size):
            x_s[r * padded + rows : (r + 1) * padded, :] = jnp.zeros(
                (padded - rows, x_s.shape[1]), x_s.dtype
            )


def gather_blocks(x_ref, x_s, row_size, col_size):
    _, rows, cols = x_ref.shape
    padded = round_up(rows, 16)
    for r in range(row_size):
        for c in range(col_size):
            x_s[r * padded : r * padded + rows, c * cols : (c + 1) * cols] = x_ref[
                r * col_size + c
            ]


def hosted_kernel(row_size, col_size, kind_ref, x_ref, owned_ref, back_ref, *scratch):
    _, rows, cols = x_ref.shape
    me = lax.axis_index("dp") * col_size + lax.axis_index("owner")
    owns = kind_ref[me] != NOTHING
    clear_padding(scratch[0], rows, row_size)
    gather_blocks(x_ref, scratch[0], row_size, col_size)

    def write(r, block):
        owned_ref[0, r * rows : (r + 1) * rows, :] = jnp.where(owns, block, jnp.zeros_like(block))
        for c in range(col_size):
            back_ref[r * col_size + c] = block[:, c * cols : (c + 1) * cols]

    newton_schulz(rows, cols, row_size, col_size, *scratch, write)


def second_kernel(row_size, col_size, kind_ref, shared_ref, *refs):
    row_refs, owned_ref, scratch = refs[:row_size], refs[row_size + 1], refs[row_size + 2 :]
    x_s = scratch[0]
    _, rows, cols = shared_ref.shape
    padded = round_up(rows, 16)
    row = lax.axis_index("dp")
    kind = kind_ref[row * col_size + lax.axis_index("owner")]
    clear_padding(x_s, rows, row_size)

    @pl.when(kind < PAIRED)
    def _():
        gather_blocks(shared_ref, x_s, row_size, col_size)

    @pl.when(kind >= PAIRED)
    def _():
        for offset in range(row_size):
            start = pl.multiple_of((row ^ offset) * padded, 16)
            for c in range(col_size):
                x_s[pl.ds(start, rows), c * cols : (c + 1) * cols] = row_refs[offset][c]

    def write(r, block):
        owned_ref[0, r * rows : (r + 1) * rows, :] = jnp.where(
            kind != NOTHING, block, jnp.zeros_like(block)
        )

    newton_schulz(rows, cols, row_size, col_size, *scratch, write)


def ortho_scratch(rows, cols, row_size, col_size):
    padded, width = round_up(rows, 16) * row_size, cols * col_size
    return [
        pltpu.VMEM((padded, width), jnp.bfloat16),
        pltpu.VMEM((padded, width), jnp.bfloat16),
        pltpu.VMEM((padded, padded), jnp.bfloat16),
        pltpu.VMEM((padded, padded), jnp.bfloat16),
    ]


def ortho_cost(rows, cols, row_size, col_size):
    padded, width = round_up(rows, 16) * row_size, cols * col_size
    return pl.CostEstimate(
        flops=2 * ITERS * padded * padded * (2 * width + padded),
        bytes_accessed=6 * padded * width,
        transcendentals=0,
    )


def orthogonalize_hosted(kind, arrived, row_size, col_size):
    devices, rows, cols = arrived.shape
    height, width = rows * row_size, cols * col_size
    return pl.pallas_call(
        functools.partial(hosted_kernel, row_size, col_size),
        grid=(1,),
        in_specs=[SMEM, whole(arrived.shape)],
        out_specs=[whole((1, height, width)), whole(arrived.shape)],
        out_shape=[
            jax.ShapeDtypeStruct((CAP, height, width), jnp.bfloat16),
            jax.ShapeDtypeStruct(arrived.shape, jnp.bfloat16),
        ],
        scratch_shapes=ortho_scratch(rows, cols, row_size, col_size),
        compiler_params=PARAMS,
        cost_estimate=ortho_cost(rows, cols, row_size, col_size),
        name="orthogonalize_hosted",
    )(kind, arrived)


def orthogonalize_second(kind, shared, by_row, owned, row_size, col_size):
    devices, rows, cols = shared.shape
    height, width = rows * row_size, cols * col_size
    return pl.pallas_call(
        functools.partial(second_kernel, row_size, col_size),
        grid=(1,),
        in_specs=[SMEM, whole(shared.shape)]
        + [whole(by_row[0].shape)] * row_size
        + [pl.BlockSpec(memory_space=pl.ANY)],
        out_specs=pl.BlockSpec((1, height, width), lambda i: (1, 0, 0)),
        out_shape=jax.ShapeDtypeStruct((CAP, height, width), jnp.bfloat16),
        scratch_shapes=ortho_scratch(rows, cols, row_size, col_size),
        input_output_aliases={2 + row_size: 0},
        compiler_params=PARAMS,
        cost_estimate=ortho_cost(rows, cols, row_size, col_size),
        name="orthogonalize_second",
    )(kind, shared, *by_row, owned)


def unpack_kernel(chunk, host_ref, back_ref, update_ref):
    step = pl.program_id(0)
    for j in range(chunk):
        update_ref[j] = back_ref[host_ref[step * chunk + j]]


def unpack(back, host):
    devices, rows, cols = back.shape
    mats = host.shape[0]
    chunk = 8
    return pl.pallas_call(
        functools.partial(unpack_kernel, chunk),
        grid_spec=pltpu.PrefetchScalarGridSpec(
            num_scalar_prefetch=1,
            grid=(mats // chunk,),
            in_specs=[whole(back.shape)],
            out_specs=pl.BlockSpec((chunk, rows, cols), lambda i, *_: (i, 0, 0)),
        ),
        out_shape=jax.ShapeDtypeStruct((mats, rows, cols), jnp.bfloat16),
        compiler_params=PARAMS,
        cost_estimate=pl.CostEstimate(
            flops=0, bytes_accessed=4 * mats * rows * cols, transcendentals=0
        ),
        name="unpack",
    )(host, back)


def exchange(blocks, axes):
    return lax.all_to_all(blocks, axes, split_axis=0, concat_axis=0, tiled=True)


def swap(block, axis, offset):
    size = lax.axis_size(axis)
    return lax.ppermute(block, axis, [(i, i ^ offset) for i in range(size)])


def on_device(gradients, momentum, owner_table):
    row_size = lax.axis_size("dp")
    col_size = lax.axis_size("owner")
    devices = row_size * col_size
    room = max(row_size // 2, 1)

    first, host, kind, most = pack(gradients, momentum, owner_table, devices, col_size)
    arrived = exchange(first, AXES)
    new_momentum, near, far = update_momentum(
        gradients, momentum, owner_table, host, kind, col_size, room
    )
    arrived, near, far = lax.optimization_barrier((arrived, near, far))
    near = exchange(near, "owner")
    shared = swap(arrived, "dp", 1)
    owned, back = orthogonalize_hosted(kind, arrived, row_size, col_size)
    far = lax.cond(most[0] > room, lambda part: exchange(part, "owner"), lambda part: part, far)
    returned = exchange(back, AXES)
    by_row = forward(kind, near, far, row_size, col_size, room)
    by_row = [by_row[0]] + [swap(by_row[r], "dp", r) for r in range(1, row_size)]
    owned = orthogonalize_second(kind, shared, by_row, owned, row_size, col_size)
    update = unpack(returned, host)
    return (new_momentum, update, owned)


def solution(mesh):
    return jax.shard_map(
        on_device,
        mesh=mesh,
        in_specs=(P(None, "dp", "owner"), P(None, "dp", "owner"), P()),
        out_specs=(P(None, "dp", "owner"), P(None, "dp", "owner"), P(("dp", "owner"), None, None)),
        check_vma=False,
    )
```

```python
import functools
import math

import jax
import jax.numpy as jnp
from jax import lax
from jax.experimental import pallas as pl
from jax.experimental.pallas import tpu as pltpu
from jax.sharding import PartitionSpec as P

ITERS = 2
CAP = 2

coef_a = 3.4445
coef_b = -4.775
coef_c = 2.0315
momentum_beta = 0.95
epsilon = 1e-07

AXES = ("dp", "owner")
MIB = 1024 * 1024
PARAMS = pltpu.CompilerParams(vmem_limit_bytes=24 * MIB)
PACK_PARAMS = pltpu.CompilerParams(vmem_limit_bytes=60 * MIB)
SMEM = pl.BlockSpec(memory_space=pltpu.SMEM)

NOTHING, SINGLE, PAIRED = 0, 1, 2


def round_up(value, multiple):
    return -(-value // multiple) * multiple


def whole(shape):
    return pl.BlockSpec(shape, lambda *_: (0,) * len(shape))


def nesterov_of(grad_ref, momentum_ref, j):
    grad = grad_ref[j].astype(jnp.float32)
    new = momentum_beta * momentum_ref[j] + grad
    return new, (grad + momentum_beta * new).astype(jnp.bfloat16)


def pack_kernel(
    chunk, col_size, owner_ref, g_ref, m_ref, first_ref, host_ref, kind_ref, most_ref,
    idle_ref, helper_ref, layer_ref,
):
    step = pl.program_id(0)
    devices = first_ref.shape[0]
    mats = host_ref.shape[0]

    @pl.when(step == 0)
    def _():
        @pl.loop(0, devices)
        def _(d):
            kind_ref[d] = 0

        @pl.loop(0, col_size)
        def _(z):
            layer_ref[z] = 0

        @pl.loop(0, mats)
        def _(i):
            kind_ref[owner_ref[i]] = 1

        def list_idle(d, found):
            idle_ref[found] = d
            taken = kind_ref[d] + kind_ref[d ^ col_size]
            return found + jnp.where(taken == 0, 1, 0)

        lax.fori_loop(0, devices, list_idle, 0)

        def plan_chip(k, carry):
            found, most = carry
            low = (k // col_size) * 2 * col_size + k % col_size
            high = low + col_size
            owns_low, owns_high = kind_ref[low], kind_ref[high]
            paired = owns_low + owns_high == 2
            z = k % col_size
            place = layer_ref[z]
            layer_ref[z] = jnp.where(paired, place + 2, place)
            kind_ref[low] = jnp.where(paired, PAIRED + place, owns_low)
            kind_ref[high] = jnp.where(paired, PAIRED + place + 1, owns_high)
            helper_ref[low] = jnp.where(paired, idle_ref[found], high)
            helper_ref[high] = jnp.where(paired, idle_ref[found + 1], low)
            return jnp.where(paired, found + 2, found), jnp.maximum(most, layer_ref[z])

        _, most = lax.fori_loop(0, devices // 2, plan_chip, (0, 0))
        most_ref[0] = most

        def place_matrix(i, _):
            owner = owner_ref[i]
            helper = helper_ref[owner]
            again = helper < 0
            host_ref[i] = jnp.where(again, -1 - helper, owner)
            helper_ref[owner] = -1 - helper
            return 0

        lax.fori_loop(0, mats, place_matrix, 0)

    for j in range(chunk):
        _, nesterov = nesterov_of(g_ref, m_ref, j)
        first_ref[host_ref[step * chunk + j]] = nesterov


def pack(gradients, momentum, owner_table, devices, col_size):
    mats, rows, cols = gradients.shape
    chunk = 8
    block = pl.BlockSpec((chunk, rows, cols), lambda i, *_: (i, 0, 0))
    return pl.pallas_call(
        functools.partial(pack_kernel, chunk, col_size),
        grid_spec=pltpu.PrefetchScalarGridSpec(
            num_scalar_prefetch=1,
            grid=(mats // chunk,),
            in_specs=[block, block],
            out_specs=[whole((devices, rows, cols)), SMEM, SMEM, SMEM],
            scratch_shapes=[
                pltpu.SMEM((devices + 1,), jnp.int32),
                pltpu.SMEM((devices,), jnp.int32),
                pltpu.SMEM((col_size,), jnp.int32),
            ],
        ),
        out_shape=[
            jax.ShapeDtypeStruct((devices, rows, cols), jnp.bfloat16),
            jax.ShapeDtypeStruct((mats,), jnp.int32),
            jax.ShapeDtypeStruct((devices,), jnp.int32),
            jax.ShapeDtypeStruct((1,), jnp.int32),
        ],
        compiler_params=PACK_PARAMS,
        cost_estimate=pl.CostEstimate(
            flops=4 * mats * rows * cols, bytes_accessed=8 * mats * rows * cols, transcendentals=0
        ),
        name="pack",
    )(owner_table, gradients, momentum)


def momentum_kernel(
    chunk, col_size, room, owner_ref, host_ref, kind_ref, g_ref, m_ref, nm_ref, *refs
):
    near_refs, far_ref, held = refs[:col_size], refs[col_size], refs[col_size + 1]
    step = pl.program_id(0)
    here = lax.axis_index("owner")
    for j in range(chunk):
        new, nesterov = nesterov_of(g_ref, m_ref, j)
        nm_ref[j] = new
        owner = owner_ref[step * chunk + j]
        place = kind_ref[owner] - PAIRED
        second = (host_ref[step * chunk + j] != owner) & (place >= 0)
        layer = owner % col_size

        @pl.when(second & (place < room))
        def _():
            held[(layer ^ here) * room + place] = nesterov

        @pl.when(second & (place >= room))
        def _():
            far_ref[layer * room + place - room] = nesterov

    @pl.when(step == pl.num_programs(0) - 1)
    def _():
        for offset in range(col_size):
            near_refs[offset][...] = held[offset * room : (offset + 1) * room]


def update_momentum(gradients, momentum, owner_table, host, kind, col_size, room):
    mats, rows, cols = gradients.shape
    chunk = 8
    block = pl.BlockSpec((chunk, rows, cols), lambda i, *_: (i, 0, 0))
    near = jax.ShapeDtypeStruct((room, rows, cols), jnp.bfloat16)
    far = jax.ShapeDtypeStruct((col_size * room, rows, cols), jnp.bfloat16)
    new_momentum, *near, far = pl.pallas_call(
        functools.partial(momentum_kernel, chunk, col_size, room),
        grid_spec=pltpu.PrefetchScalarGridSpec(
            num_scalar_prefetch=3,
            grid=(mats // chunk,),
            in_specs=[block, block],
            out_specs=[block] + [whole(near.shape)] * col_size + [whole(far.shape)],
            scratch_shapes=[pltpu.VMEM(far.shape, jnp.bfloat16)],
        ),
        out_shape=[jax.ShapeDtypeStruct(momentum.shape, jnp.float32)] + [near] * col_size + [far],
        compiler_params=PARAMS,
        cost_estimate=pl.CostEstimate(
            flops=4 * mats * rows * cols, bytes_accessed=12 * mats * rows * cols, transcendentals=0
        ),
        name="update_momentum",
    )(owner_table, host, kind, gradients, momentum)
    return new_momentum, near, far


def forward_kernel(col_size, row_size, room, kind_ref, *refs):
    near_refs, far_ref, out_refs = refs[:col_size], refs[col_size], refs[col_size + 1 :]
    row, col = lax.axis_index("dp"), lax.axis_index("owner")
    for offset in range(row_size):
        place = jnp.maximum(kind_ref[(row ^ offset) * col_size + col] - PAIRED, 0)

        @pl.when(place < room)
        def _():
            for z in range(col_size):
                out_refs[offset][col ^ z] = near_refs[z][place]

        @pl.when(place >= room)
        def _():
            for z in range(col_size):
                out_refs[offset][z] = far_ref[z * room + place - room]


def forward(kind, near, far, row_size, col_size, room):
    _, rows, cols = far.shape
    out = jax.ShapeDtypeStruct((col_size, rows, cols), jnp.bfloat16)
    return pl.pallas_call(
        functools.partial(forward_kernel, col_size, row_size, room),
        grid=(1,),
        in_specs=[SMEM] + [whole(near[0].shape)] * col_size + [whole(far.shape)],
        out_specs=[whole(out.shape)] * row_size,
        out_shape=[out] * row_size,
        compiler_params=PARAMS,
        cost_estimate=pl.CostEstimate(
            flops=0, bytes_accessed=8 * col_size * room * rows * cols, transcendentals=0
        ),
        name="forward",
    )(kind, *near, far)


def matmul(lhs, rhs, rhs_dim):
    return lax.dot_general(
        lhs, rhs, (((1,), (rhs_dim,)), ((), ())), preferred_element_type=jnp.float32
    )


def newton_schulz(rows, cols, row_size, col_size, x_s, y_s, gram_s, mix_s, write):
    padded = round_up(rows, 16)
    tile_blocks = max(row_size // 2, 1)
    tile = padded * tile_blocks
    tiles = row_size // tile_blocks

    total = jnp.zeros((1, cols), jnp.float32)
    for r in range(row_size):
        for c in range(col_size):
            wide = x_s[r * padded : (r + 1) * padded, c * cols : (c + 1) * cols]
            wide = wide.astype(jnp.float32)
            total += jnp.sum(wide * wide, axis=0, keepdims=True)
    magnitude = jnp.sqrt(jnp.sum(total, axis=1, keepdims=True))
    inverse = 1.0 / (magnitude + epsilon)
    update_scale = 0.2 * math.sqrt(max(rows * row_size, cols * col_size))

    for iteration in range(ITERS):
        src = x_s if iteration == 0 else y_s
        for t in range(tiles):
            span = slice(t * tile, (t + 1) * tile)
            gram = matmul(src[span, :], src[...], 1)
            if iteration == 0:
                gram = gram * (inverse * inverse)
            gram_s[span, :] = gram.astype(jnp.bfloat16)
        for t in range(tiles):
            span = slice(t * tile, (t + 1) * tile)
            square = matmul(gram_s[span, :], gram_s[...], 0)
            mix_s[span, :] = (
                coef_b * gram_s[span, :].astype(jnp.float32) + coef_c * square
            ).astype(jnp.bfloat16)
        for t in range(tiles):
            span = slice(t * tile, (t + 1) * tile)
            combined = coef_a * src[span, :].astype(jnp.float32) + matmul(
                mix_s[span, :], src[...], 0
            )
            if iteration == 0:
                combined = combined * inverse
            if iteration + 1 < ITERS:
                y_s[span, :] = combined.astype(jnp.bfloat16)
            else:
                result = (update_scale * combined).astype(jnp.bfloat16)
                for j in range(tile_blocks):
                    write(t * tile_blocks + j, result[j * padded : j * padded + rows, :])


def clear_padding(x_s, rows, row_size):
    padded = round_up(rows, 16)
    if padded > rows:
        for r in range(row_size):
            x_s[r * padded + rows : (r + 1) * padded, :] = jnp.zeros(
                (padded - rows, x_s.shape[1]), x_s.dtype
            )


def gather_blocks(x_ref, x_s, row_size, col_size):
    _, rows, cols = x_ref.shape
    padded = round_up(rows, 16)
    for r in range(row_size):
        for c in range(col_size):
            x_s[r * padded : r * padded + rows, c * cols : (c + 1) * cols] = x_ref[
                r * col_size + c
            ]


def hosted_kernel(row_size, col_size, kind_ref, x_ref, owned_ref, back_ref, *scratch):
    _, rows, cols = x_ref.shape
    me = lax.axis_index("dp") * col_size + lax.axis_index("owner")
    owns = kind_ref[me] != NOTHING
    clear_padding(scratch[0], rows, row_size)
    gather_blocks(x_ref, scratch[0], row_size, col_size)

    def write(r, block):
        owned_ref[0, r * rows : (r + 1) * rows, :] = jnp.where(owns, block, jnp.zeros_like(block))
        for c in range(col_size):
            back_ref[r * col_size + c] = block[:, c * cols : (c + 1) * cols]

    newton_schulz(rows, cols, row_size, col_size, *scratch, write)


def second_kernel(row_size, col_size, kind_ref, shared_ref, *refs):
    row_refs, owned_ref, scratch = refs[:row_size], refs[row_size + 1], refs[row_size + 2 :]
    x_s = scratch[0]
    _, rows, cols = shared_ref.shape
    padded = round_up(rows, 16)
    row = lax.axis_index("dp")
    kind = kind_ref[row * col_size + lax.axis_index("owner")]
    clear_padding(x_s, rows, row_size)

    @pl.when(kind < PAIRED)
    def _():
        gather_blocks(shared_ref, x_s, row_size, col_size)

    @pl.when(kind >= PAIRED)
    def _():
        for offset in range(row_size):
            start = pl.multiple_of((row ^ offset) * padded, 16)
            for c in range(col_size):
                x_s[pl.ds(start, rows), c * cols : (c + 1) * cols] = row_refs[offset][c]

    def write(r, block):
        owned_ref[0, r * rows : (r + 1) * rows, :] = jnp.where(
            kind != NOTHING, block, jnp.zeros_like(block)
        )

    newton_schulz(rows, cols, row_size, col_size, *scratch, write)


def ortho_scratch(rows, cols, row_size, col_size):
    padded, width = round_up(rows, 16) * row_size, cols * col_size
    return [
        pltpu.VMEM((padded, width), jnp.bfloat16),
        pltpu.VMEM((padded, width), jnp.bfloat16),
        pltpu.VMEM((padded, padded), jnp.bfloat16),
        pltpu.VMEM((padded, padded), jnp.bfloat16),
    ]


def ortho_cost(rows, cols, row_size, col_size):
    padded, width = round_up(rows, 16) * row_size, cols * col_size
    return pl.CostEstimate(
        flops=2 * ITERS * padded * padded * (2 * width + padded),
        bytes_accessed=6 * padded * width,
        transcendentals=0,
    )


def orthogonalize_hosted(kind, arrived, row_size, col_size):
    devices, rows, cols = arrived.shape
    height, width = rows * row_size, cols * col_size
    return pl.pallas_call(
        functools.partial(hosted_kernel, row_size, col_size),
        grid=(1,),
        in_specs=[SMEM, whole(arrived.shape)],
        out_specs=[whole((1, height, width)), whole(arrived.shape)],
        out_shape=[
            jax.ShapeDtypeStruct((CAP, height, width), jnp.bfloat16),
            jax.ShapeDtypeStruct(arrived.shape, jnp.bfloat16),
        ],
        scratch_shapes=ortho_scratch(rows, cols, row_size, col_size),
        compiler_params=PARAMS,
        cost_estimate=ortho_cost(rows, cols, row_size, col_size),
        name="orthogonalize_hosted",
    )(kind, arrived)


def orthogonalize_second(kind, shared, by_row, owned, row_size, col_size):
    devices, rows, cols = shared.shape
    height, width = rows * row_size, cols * col_size
    return pl.pallas_call(
        functools.partial(second_kernel, row_size, col_size),
        grid=(1,),
        in_specs=[SMEM, whole(shared.shape)]
        + [whole(by_row[0].shape)] * row_size
        + [pl.BlockSpec(memory_space=pl.ANY)],
        out_specs=pl.BlockSpec((1, height, width), lambda i: (1, 0, 0)),
        out_shape=jax.ShapeDtypeStruct((CAP, height, width), jnp.bfloat16),
        scratch_shapes=ortho_scratch(rows, cols, row_size, col_size),
        input_output_aliases={2 + row_size: 0},
        compiler_params=PARAMS,
        cost_estimate=ortho_cost(rows, cols, row_size, col_size),
        name="orthogonalize_second",
    )(kind, shared, *by_row, owned)


def unpack_kernel(chunk, host_ref, back_ref, update_ref):
    step = pl.program_id(0)
    for j in range(chunk):
        update_ref[j] = back_ref[host_ref[step * chunk + j]]


def unpack(back, host):
    devices, rows, cols = back.shape
    mats = host.shape[0]
    chunk = 8
    return pl.pallas_call(
        functools.partial(unpack_kernel, chunk),
        grid_spec=pltpu.PrefetchScalarGridSpec(
            num_scalar_prefetch=1,
            grid=(mats // chunk,),
            in_specs=[whole(back.shape)],
            out_specs=pl.BlockSpec((chunk, rows, cols), lambda i, *_: (i, 0, 0)),
        ),
        out_shape=jax.ShapeDtypeStruct((mats, rows, cols), jnp.bfloat16),
        compiler_params=PARAMS,
        cost_estimate=pl.CostEstimate(
            flops=0, bytes_accessed=4 * mats * rows * cols, transcendentals=0
        ),
        name="unpack",
    )(host, back)


def exchange(blocks, axes):
    return lax.all_to_all(blocks, axes, split_axis=0, concat_axis=0, tiled=True)


def swap(block, axis, offset):
    size = lax.axis_size(axis)
    return lax.ppermute(block, axis, [(i, i ^ offset) for i in range(size)])


def on_device(gradients, momentum, owner_table):
    row_size = lax.axis_size("dp")
    col_size = lax.axis_size("owner")
    devices = row_size * col_size
    room = max(row_size // 2, 1)

    first, host, kind, most = pack(gradients, momentum, owner_table, devices, col_size)
    arrived = exchange(first, AXES)
    new_momentum, near, far = update_momentum(
        gradients, momentum, owner_table, host, kind, col_size, room
    )
    arrived, near, far = lax.optimization_barrier((arrived, near, far))
    near = [near[0]] + [swap(near[z], "owner", z) for z in range(1, col_size)]
    shared = swap(arrived, "dp", 1)
    owned, back = orthogonalize_hosted(kind, arrived, row_size, col_size)
    far = lax.cond(most[0] > room, lambda part: exchange(part, "owner"), lambda part: part, far)
    back, near, shared = lax.optimization_barrier((back, near, shared))
    returned = exchange(back, AXES)
    by_row = forward(kind, near, far, row_size, col_size, room)
    by_row = [by_row[0]] + [swap(by_row[r], "dp", r) for r in range(1, row_size)]
    owned = orthogonalize_second(kind, shared, by_row, owned, row_size, col_size)
    update = unpack(returned, host)
    return (new_momentum, update, owned)


def solution(mesh):
    return jax.shard_map(
        on_device,
        mesh=mesh,
        in_specs=(P(None, "dp", "owner"), P(None, "dp", "owner"), P()),
        out_specs=(P(None, "dp", "owner"), P(None, "dp", "owner"), P(("dp", "owner"), None, None)),
        check_vma=False,
    )
```

```python
import functools
import math

import jax
import jax.numpy as jnp
from jax import lax
from jax.experimental import pallas as pl
from jax.experimental.pallas import tpu as pltpu
from jax.sharding import PartitionSpec as P

ITERS = 2
CAP = 2
HALVES = 2

coef_a = 3.4445
coef_b = -4.775
coef_c = 2.0315
momentum_beta = 0.95
epsilon = 1e-07

AXES = ("dp", "owner")
MIB = 1024 * 1024
PARAMS = pltpu.CompilerParams(vmem_limit_bytes=24 * MIB)
PACK_PARAMS = pltpu.CompilerParams(vmem_limit_bytes=60 * MIB)
SMEM = pl.BlockSpec(memory_space=pltpu.SMEM)


def round_up(value, multiple):
    return -(-value // multiple) * multiple


def whole(shape):
    return pl.BlockSpec(shape, lambda *_: (0,) * len(shape))


def nesterov_of(grad_ref, momentum_ref, j):
    grad = grad_ref[j].astype(jnp.float32)
    new = momentum_beta * momentum_ref[j] + grad
    return new, (grad + momentum_beta * new).astype(jnp.bfloat16)


def store_slot(slot, plan, i, owner, nesterov, slot_ref):
    other_ref, rank_ref = plan

    @pl.when(rank_ref[i] == slot)
    def _():
        slot_ref[owner] = nesterov
        slot_ref[other_ref[owner]] = nesterov


def pack_kernel(
    chunk, col_size, owner_ref, g_ref, m_ref, first_ref, other_ref, rank_ref, count_ref, list_ref
):
    step = pl.program_id(0)
    devices = first_ref.shape[0]
    mats = rank_ref.shape[0]

    def half_of(d):
        return (d % col_size) // (col_size // HALVES)

    @pl.when(step == 0)
    def _():
        @pl.loop(0, devices)
        def _(d):
            count_ref[d] = 0

        def rank_matrix(i, _):
            owner = owner_ref[i]
            rank_ref[i] = count_ref[owner]
            count_ref[owner] = count_ref[owner] + 1
            return 0

        lax.fori_loop(0, mats, rank_matrix, 0)

        def list_device(d, found):
            owns = jnp.minimum(count_ref[d], 1)
            half = half_of(d)
            row = 2 * jnp.where(owns == 1, half, 1 - half) + owns
            place = found[0]
            for k in range(1, 2 * HALVES):
                place = jnp.where(row == k, found[k], place)
            list_ref[row * devices + place] = d
            return tuple(n + jnp.where(row == k, 1, 0) for k, n in enumerate(found))

        found = lax.fori_loop(0, devices, list_device, (0,) * (2 * HALVES))
        for half in range(HALVES):

            def pair(k, _):
                idle = list_ref[2 * half * devices + k]
                other_ref[list_ref[(2 * half + 1) * devices + k]] = idle
                other_ref[idle] = idle
                return 0

            lax.fori_loop(0, found[2 * half + 1], pair, 0)

    for j in range(chunk):
        i = step * chunk + j
        _, nesterov = nesterov_of(g_ref, m_ref, j)
        store_slot(0, (other_ref, rank_ref), i, owner_ref[i], nesterov, first_ref)


def pack(gradients, momentum, owner_table, devices, col_size):
    mats, rows, cols = gradients.shape
    chunk = 8
    block = pl.BlockSpec((chunk, rows, cols), lambda i, *_: (i, 0, 0))
    return pl.pallas_call(
        functools.partial(pack_kernel, chunk, col_size),
        grid_spec=pltpu.PrefetchScalarGridSpec(
            num_scalar_prefetch=1,
            grid=(mats // chunk,),
            in_specs=[block, block],
            out_specs=[whole((devices, rows, cols)), SMEM, SMEM],
            scratch_shapes=[
                pltpu.SMEM((devices,), jnp.int32),
                pltpu.SMEM((2 * HALVES * devices,), jnp.int32),
            ],
        ),
        out_shape=[
            jax.ShapeDtypeStruct((devices, rows, cols), jnp.bfloat16),
            jax.ShapeDtypeStruct((devices,), jnp.int32),
            jax.ShapeDtypeStruct((mats,), jnp.int32),
        ],
        compiler_params=PACK_PARAMS,
        cost_estimate=pl.CostEstimate(
            flops=4 * mats * rows * cols, bytes_accessed=8 * mats * rows * cols, transcendentals=0
        ),
        name="pack",
    )(owner_table, gradients, momentum)


def momentum_kernel(chunk, owner_ref, other_ref, rank_ref, g_ref, m_ref, nm_ref, second_ref):
    step = pl.program_id(0)
    for j in range(chunk):
        i = step * chunk + j
        new, nesterov = nesterov_of(g_ref, m_ref, j)
        nm_ref[j] = new
        store_slot(1, (other_ref, rank_ref), i, owner_ref[i], nesterov, second_ref)


def update_momentum(gradients, momentum, owner_table, other, rank):
    mats, rows, cols = gradients.shape
    devices = other.shape[0]
    chunk = 8
    block = pl.BlockSpec((chunk, rows, cols), lambda i, *_: (i, 0, 0))
    return pl.pallas_call(
        functools.partial(momentum_kernel, chunk),
        grid_spec=pltpu.PrefetchScalarGridSpec(
            num_scalar_prefetch=3,
            grid=(mats // chunk,),
            in_specs=[block, block],
            out_specs=[block, whole((devices, rows, cols))],
        ),
        out_shape=[
            jax.ShapeDtypeStruct(momentum.shape, jnp.float32),
            jax.ShapeDtypeStruct((devices, rows, cols), jnp.bfloat16),
        ],
        compiler_params=PARAMS,
        cost_estimate=pl.CostEstimate(
            flops=4 * mats * rows * cols, bytes_accessed=12 * mats * rows * cols, transcendentals=0
        ),
        name="update_momentum",
    )(owner_table, other, rank, gradients, momentum)


def matmul(lhs, rhs, rhs_dim):
    return lax.dot_general(
        lhs, rhs, (((1,), (rhs_dim,)), ((), ())), preferred_element_type=jnp.float32
    )


def newton_schulz(rows, cols, row_size, col_size, x_s, y_s, gram_s, mix_s, write):
    padded = round_up(rows, 16)
    tile_blocks = max(row_size // 2, 1)
    tile = padded * tile_blocks
    tiles = row_size // tile_blocks

    total = jnp.zeros((1, cols), jnp.float32)
    for r in range(row_size):
        for c in range(col_size):
            wide = x_s[r * padded : (r + 1) * padded, c * cols : (c + 1) * cols]
            wide = wide.astype(jnp.float32)
            total += jnp.sum(wide * wide, axis=0, keepdims=True)
    magnitude = jnp.sqrt(jnp.sum(total, axis=1, keepdims=True))
    inverse = 1.0 / (magnitude + epsilon)
    update_scale = 0.2 * math.sqrt(max(rows * row_size, cols * col_size))

    for iteration in range(ITERS):
        src = x_s if iteration == 0 else y_s
        for t in range(tiles):
            span = slice(t * tile, (t + 1) * tile)
            gram = matmul(src[span, :], src[...], 1)
            if iteration == 0:
                gram = gram * (inverse * inverse)
            gram_s[span, :] = gram.astype(jnp.bfloat16)
        for t in range(tiles):
            span = slice(t * tile, (t + 1) * tile)
            square = matmul(gram_s[span, :], gram_s[...], 0)
            mix_s[span, :] = (
                coef_b * gram_s[span, :].astype(jnp.float32) + coef_c * square
            ).astype(jnp.bfloat16)
        for t in range(tiles):
            span = slice(t * tile, (t + 1) * tile)
            combined = coef_a * src[span, :].astype(jnp.float32) + matmul(
                mix_s[span, :], src[...], 0
            )
            if iteration == 0:
                combined = combined * inverse
            if iteration + 1 < ITERS:
                y_s[span, :] = combined.astype(jnp.bfloat16)
            else:
                result = (update_scale * combined).astype(jnp.bfloat16)
                for j in range(tile_blocks):
                    write(t * tile_blocks + j, result[j * padded : j * padded + rows, :])


def clear_padding(x_s, rows, row_size):
    padded = round_up(rows, 16)
    if padded > rows:
        for r in range(row_size):
            x_s[r * padded + rows : (r + 1) * padded, :] = jnp.zeros(
                (padded - rows, x_s.shape[1]), x_s.dtype
            )


def gather_blocks(x_ref, x_s, row_size, col_size):
    _, rows, cols = x_ref.shape
    padded = round_up(rows, 16)
    for r in range(row_size):
        for c in range(col_size):
            x_s[r * padded : r * padded + rows, c * cols : (c + 1) * cols] = x_ref[
                r * col_size + c
            ]


def ortho_kernel(row_size, col_size, slot, other_ref, x_ref, *refs):
    owned_ref, back_ref = refs[slot : slot + 2]
    scratch = refs[slot + 2 :]
    _, rows, cols = x_ref.shape
    width = col_size // HALVES
    col = lax.axis_index("owner")
    me = lax.axis_index("dp") * col_size + col
    owns = other_ref[me] != me
    low = col < width
    clear_padding(scratch[0], rows, row_size)
    gather_blocks(x_ref, scratch[0], row_size, col_size)

    def write(r, block):
        owned_ref[0, r * rows : (r + 1) * rows, :] = jnp.where(owns, block, jnp.zeros_like(block))
        for c in range(width):
            back_ref[r * width + c] = jnp.where(
                low,
                block[:, c * cols : (c + 1) * cols],
                block[:, (c + width) * cols : (c + width + 1) * cols],
            )

    newton_schulz(rows, cols, row_size, col_size, *scratch, write)


def orthogonalize(slot, other, arrived, row_size, col_size, owned=None):
    devices, rows, cols = arrived.shape
    height, width = rows * row_size, cols * col_size
    padded = round_up(rows, 16) * row_size
    in_specs, operands = [SMEM, whole(arrived.shape)], [other, arrived]
    if slot:
        in_specs.append(pl.BlockSpec(memory_space=pl.ANY))
        operands.append(owned)
    back = (devices // HALVES, rows, cols)
    return pl.pallas_call(
        functools.partial(ortho_kernel, row_size, col_size, slot),
        grid=(1,),
        in_specs=in_specs,
        out_specs=[pl.BlockSpec((1, height, width), lambda i: (slot, 0, 0)), whole(back)],
        out_shape=[
            jax.ShapeDtypeStruct((CAP, height, width), jnp.bfloat16),
            jax.ShapeDtypeStruct(back, jnp.bfloat16),
        ],
        scratch_shapes=[
            pltpu.VMEM((padded, width), jnp.bfloat16),
            pltpu.VMEM((padded, width), jnp.bfloat16),
            pltpu.VMEM((padded, padded), jnp.bfloat16),
            pltpu.VMEM((padded, padded), jnp.bfloat16),
        ],
        input_output_aliases={2: 0} if slot else {},
        compiler_params=PARAMS,
        cost_estimate=pl.CostEstimate(
            flops=2 * ITERS * padded * padded * (2 * width + padded),
            bytes_accessed=6 * padded * width,
            transcendentals=0,
        ),
        name="orthogonalize",
    )(*operands)


def unpack_kernel(
    chunk, col_size, owner_ref, other_ref, rank_ref, first_ref, second_ref, update_ref
):
    step = pl.program_id(0)
    width = col_size // HALVES
    half = lax.axis_index("owner") // width
    for j in range(chunk):
        i = step * chunk + j
        owner = owner_ref[i]
        host = jnp.where((owner % col_size) // width == half, owner, other_ref[owner])
        place = (host // col_size) * width + host % width

        @pl.when(rank_ref[i] == 0)
        def _():
            update_ref[j] = first_ref[place]

        @pl.when(rank_ref[i] == 1)
        def _():
            update_ref[j] = second_ref[place]


def unpack(owner_table, other, rank, first, second, col_size):
    places, rows, cols = first.shape
    mats = owner_table.shape[0]
    chunk = 8
    return pl.pallas_call(
        functools.partial(unpack_kernel, chunk, col_size),
        grid_spec=pltpu.PrefetchScalarGridSpec(
            num_scalar_prefetch=3,
            grid=(mats // chunk,),
            in_specs=[whole(first.shape)] * 2,
            out_specs=pl.BlockSpec((chunk, rows, cols), lambda i, *_: (i, 0, 0)),
        ),
        out_shape=jax.ShapeDtypeStruct((mats, rows, cols), jnp.bfloat16),
        compiler_params=PARAMS,
        cost_estimate=pl.CostEstimate(
            flops=0, bytes_accessed=4 * mats * rows * cols, transcendentals=0
        ),
        name="unpack",
    )(owner_table, other, rank, first, second)


def exchange(blocks, groups=None):
    return lax.all_to_all(
        blocks, AXES, split_axis=0, concat_axis=0, tiled=True, axis_index_groups=groups
    )


def on_device(gradients, momentum, owner_table):
    row_size = lax.axis_size("dp")
    col_size = lax.axis_size("owner")
    devices = row_size * col_size
    width = col_size // HALVES
    halves = [
        [r * col_size + half * width + c for r in range(row_size) for c in range(width)]
        for half in range(HALVES)
    ]
    first, other, rank = pack(gradients, momentum, owner_table, devices, col_size)
    arrived_first = exchange(first)
    new_momentum, second = update_momentum(gradients, momentum, owner_table, other, rank)
    arrived_first, second = lax.optimization_barrier((arrived_first, second))
    arrived_second = exchange(second)
    owned, back_first = orthogonalize(0, other, arrived_first, row_size, col_size)
    back_first, arrived_second = lax.optimization_barrier((back_first, arrived_second))
    returned_first = exchange(back_first, halves)
    owned, back_second = orthogonalize(1, other, arrived_second, row_size, col_size, owned)
    returned_second = exchange(back_second, halves)
    update = unpack(owner_table, other, rank, returned_first, returned_second, col_size)
    return (new_momentum, update, owned)


def solution(mesh):
    return jax.shard_map(
        on_device,
        mesh=mesh,
        in_specs=(P(None, "dp", "owner"), P(None, "dp", "owner"), P()),
        out_specs=(P(None, "dp", "owner"), P(None, "dp", "owner"), P(("dp", "owner"), None, None)),
        check_vma=False,
    )
```

```python
import functools
import math

import jax
import jax.numpy as jnp
from jax import lax
from jax.experimental import pallas as pl
from jax.experimental.pallas import tpu as pltpu
from jax.sharding import PartitionSpec as P

ITERS = 2
CAP = 2
HALVES = 2

coef_a = 3.4445
coef_b = -4.775
coef_c = 2.0315
momentum_beta = 0.95
epsilon = 1e-07

AXES = ("dp", "owner")
MIB = 1024 * 1024
PARAMS = pltpu.CompilerParams(vmem_limit_bytes=24 * MIB)
PACK_PARAMS = pltpu.CompilerParams(vmem_limit_bytes=60 * MIB)
SMEM = pl.BlockSpec(memory_space=pltpu.SMEM)


def round_up(value, multiple):
    return -(-value // multiple) * multiple


def whole(shape):
    return pl.BlockSpec(shape, lambda *_: (0,) * len(shape))


def nesterov_of(grad_ref, momentum_ref, j):
    grad = grad_ref[j].astype(jnp.float32)
    new = momentum_beta * momentum_ref[j] + grad
    return new, (grad + momentum_beta * new).astype(jnp.bfloat16)


def store_slot(slot, plan, i, owner, nesterov, slot_ref):
    other_ref, rank_ref = plan

    @pl.when(rank_ref[i] == slot)
    def _():
        slot_ref[owner] = nesterov
        slot_ref[other_ref[owner]] = nesterov


def pack_kernel(
    chunk, col_size, owner_ref, g_ref, m_ref, first_ref, other_ref, rank_ref, count_ref, list_ref
):
    step = pl.program_id(0)
    devices = first_ref.shape[0]
    mats = rank_ref.shape[0]

    def half_of(d):
        return (d % col_size) // (col_size // HALVES)

    @pl.when(step == 0)
    def _():
        @pl.loop(0, devices)
        def _(d):
            count_ref[d] = 0

        def rank_matrix(i, _):
            owner = owner_ref[i]
            rank_ref[i] = count_ref[owner]
            count_ref[owner] = count_ref[owner] + 1
            return 0

        lax.fori_loop(0, mats, rank_matrix, 0)

        def list_device(d, found):
            owns = jnp.minimum(count_ref[d], 1)
            half = half_of(d)
            row = 2 * jnp.where(owns == 1, half, 1 - half) + owns
            place = found[0]
            for k in range(1, 2 * HALVES):
                place = jnp.where(row == k, found[k], place)
            list_ref[row * devices + place] = d
            return tuple(n + jnp.where(row == k, 1, 0) for k, n in enumerate(found))

        found = lax.fori_loop(0, devices, list_device, (0,) * (2 * HALVES))
        for half in range(HALVES):

            def pair(k, _):
                idle = list_ref[2 * half * devices + k]
                other_ref[list_ref[(2 * half + 1) * devices + k]] = idle
                other_ref[idle] = idle
                return 0

            lax.fori_loop(0, found[2 * half + 1], pair, 0)

    for j in range(chunk):
        i = step * chunk + j
        _, nesterov = nesterov_of(g_ref, m_ref, j)
        store_slot(0, (other_ref, rank_ref), i, owner_ref[i], nesterov, first_ref)


def pack(gradients, momentum, owner_table, devices, col_size):
    mats, rows, cols = gradients.shape
    chunk = 8
    block = pl.BlockSpec((chunk, rows, cols), lambda i, *_: (i, 0, 0))
    return pl.pallas_call(
        functools.partial(pack_kernel, chunk, col_size),
        grid_spec=pltpu.PrefetchScalarGridSpec(
            num_scalar_prefetch=1,
            grid=(mats // chunk,),
            in_specs=[block, block],
            out_specs=[whole((devices, rows, cols)), SMEM, SMEM],
            scratch_shapes=[
                pltpu.SMEM((devices,), jnp.int32),
                pltpu.SMEM((2 * HALVES * devices,), jnp.int32),
            ],
        ),
        out_shape=[
            jax.ShapeDtypeStruct((devices, rows, cols), jnp.bfloat16),
            jax.ShapeDtypeStruct((devices,), jnp.int32),
            jax.ShapeDtypeStruct((mats,), jnp.int32),
        ],
        compiler_params=PACK_PARAMS,
        cost_estimate=pl.CostEstimate(
            flops=4 * mats * rows * cols, bytes_accessed=8 * mats * rows * cols, transcendentals=0
        ),
        name="pack",
    )(owner_table, gradients, momentum)


def momentum_kernel(chunk, owner_ref, other_ref, rank_ref, g_ref, m_ref, nm_ref, second_ref):
    step = pl.program_id(0)
    for j in range(chunk):
        i = step * chunk + j
        new, nesterov = nesterov_of(g_ref, m_ref, j)
        nm_ref[j] = new
        store_slot(1, (other_ref, rank_ref), i, owner_ref[i], nesterov, second_ref)


def update_momentum(gradients, momentum, owner_table, other, rank):
    mats, rows, cols = gradients.shape
    devices = other.shape[0]
    chunk = 8
    block = pl.BlockSpec((chunk, rows, cols), lambda i, *_: (i, 0, 0))
    return pl.pallas_call(
        functools.partial(momentum_kernel, chunk),
        grid_spec=pltpu.PrefetchScalarGridSpec(
            num_scalar_prefetch=3,
            grid=(mats // chunk,),
            in_specs=[block, block],
            out_specs=[block, whole((devices, rows, cols))],
        ),
        out_shape=[
            jax.ShapeDtypeStruct(momentum.shape, jnp.float32),
            jax.ShapeDtypeStruct((devices, rows, cols), jnp.bfloat16),
        ],
        compiler_params=PARAMS,
        cost_estimate=pl.CostEstimate(
            flops=4 * mats * rows * cols, bytes_accessed=12 * mats * rows * cols, transcendentals=0
        ),
        name="update_momentum",
    )(owner_table, other, rank, gradients, momentum)


def matmul(lhs, rhs, rhs_dim):
    return lax.dot_general(
        lhs, rhs, (((1,), (rhs_dim,)), ((), ())), preferred_element_type=jnp.float32
    )


def newton_schulz(rows, cols, row_size, col_size, x_s, y_s, gram_s, mix_s, write):
    padded = round_up(rows, 16)
    tile_blocks = max(row_size // 2, 1)
    tile = padded * tile_blocks
    tiles = row_size // tile_blocks

    total = jnp.zeros((1, cols), jnp.float32)
    for r in range(row_size):
        for c in range(col_size):
            wide = x_s[r * padded : (r + 1) * padded, c * cols : (c + 1) * cols]
            wide = wide.astype(jnp.float32)
            total += jnp.sum(wide * wide, axis=0, keepdims=True)
    magnitude = jnp.sqrt(jnp.sum(total, axis=1, keepdims=True))
    inverse = 1.0 / (magnitude + epsilon)
    update_scale = 0.2 * math.sqrt(max(rows * row_size, cols * col_size))

    for iteration in range(ITERS):
        src = x_s if iteration == 0 else y_s
        for t in range(tiles):
            span = slice(t * tile, (t + 1) * tile)
            gram = matmul(src[span, :], src[...], 1)
            if iteration == 0:
                gram = gram * (inverse * inverse)
            gram_s[span, :] = gram.astype(jnp.bfloat16)
        for t in range(tiles):
            span = slice(t * tile, (t + 1) * tile)
            square = matmul(gram_s[span, :], gram_s[...], 0)
            mix_s[span, :] = (
                coef_b * gram_s[span, :].astype(jnp.float32) + coef_c * square
            ).astype(jnp.bfloat16)
        for t in range(tiles):
            span = slice(t * tile, (t + 1) * tile)
            combined = coef_a * src[span, :].astype(jnp.float32) + matmul(
                mix_s[span, :], src[...], 0
            )
            if iteration == 0:
                combined = combined * inverse
            if iteration + 1 < ITERS:
                y_s[span, :] = combined.astype(jnp.bfloat16)
            else:
                result = (update_scale * combined).astype(jnp.bfloat16)
                for j in range(tile_blocks):
                    write(t * tile_blocks + j, result[j * padded : j * padded + rows, :])


def clear_padding(x_s, rows, row_size):
    padded = round_up(rows, 16)
    if padded > rows:
        for r in range(row_size):
            x_s[r * padded + rows : (r + 1) * padded, :] = jnp.zeros(
                (padded - rows, x_s.shape[1]), x_s.dtype
            )


def gather_blocks(x_ref, x_s, row_size, col_size):
    _, rows, cols = x_ref.shape
    padded = round_up(rows, 16)
    for r in range(row_size):
        for c in range(col_size):
            x_s[r * padded : r * padded + rows, c * cols : (c + 1) * cols] = x_ref[
                r * col_size + c
            ]


def ortho_kernel(row_size, col_size, slot, other_ref, x_ref, *refs):
    _, rows, cols = x_ref.shape
    width = col_size // HALVES
    places = row_size * width
    if slot:
        owned_ref, back_ref = refs[1:3]
        scratch = refs[3:]
    else:
        owned_ref, offset_refs, back_ref = refs[0], refs[1 : 1 + places], refs[-1]
        scratch = refs[1 + places : -1]
    row, col = lax.axis_index("dp"), lax.axis_index("owner")
    me = row * col_size + col
    owns = other_ref[me] != me
    low = col < width
    clear_padding(scratch[0], rows, row_size)
    gather_blocks(x_ref, scratch[0], row_size, col_size)

    def write(r, block):
        owned_ref[0, r * rows : (r + 1) * rows, :] = jnp.where(owns, block, jnp.zeros_like(block))
        for c in range(width):
            place = r * width + c if slot else (r ^ row) * width + (c ^ (col % width))
            back_ref[place] = jnp.where(
                low,
                block[:, c * cols : (c + 1) * cols],
                block[:, (c + width) * cols : (c + width + 1) * cols],
            )

    newton_schulz(rows, cols, row_size, col_size, *scratch, write)
    if not slot:
        for offset in range(places):
            offset_refs[offset][...] = back_ref[offset]


def orthogonalize(slot, other, arrived, row_size, col_size, owned=None):
    devices, rows, cols = arrived.shape
    height, width = rows * row_size, cols * col_size
    padded = round_up(rows, 16) * row_size
    places = devices // HALVES
    in_specs, operands = [SMEM, whole(arrived.shape)], [other, arrived]
    scratch_shapes = [
        pltpu.VMEM((padded, width), jnp.bfloat16),
        pltpu.VMEM((padded, width), jnp.bfloat16),
        pltpu.VMEM((padded, padded), jnp.bfloat16),
        pltpu.VMEM((padded, padded), jnp.bfloat16),
    ]
    if slot:
        in_specs.append(pl.BlockSpec(memory_space=pl.ANY))
        operands.append(owned)
        back = [(places, rows, cols)]
    else:
        back = [(rows, cols)] * places
        scratch_shapes.append(pltpu.VMEM((places, rows, cols), jnp.bfloat16))
    owned, *back = pl.pallas_call(
        functools.partial(ortho_kernel, row_size, col_size, slot),
        grid=(1,),
        in_specs=in_specs,
        out_specs=[pl.BlockSpec((1, height, width), lambda i: (slot, 0, 0))]
        + [whole(shape) for shape in back],
        out_shape=[jax.ShapeDtypeStruct((CAP, height, width), jnp.bfloat16)]
        + [jax.ShapeDtypeStruct(shape, jnp.bfloat16) for shape in back],
        scratch_shapes=scratch_shapes,
        input_output_aliases={2: 0} if slot else {},
        compiler_params=PARAMS,
        cost_estimate=pl.CostEstimate(
            flops=2 * ITERS * padded * padded * (2 * width + padded),
            bytes_accessed=6 * padded * width,
            transcendentals=0,
        ),
        name="orthogonalize",
    )(*operands)
    return owned, back


def unpack_kernel(chunk, col_size, row_size, owner_ref, other_ref, rank_ref, *refs):
    width = col_size // HALVES
    places = row_size * width
    offset_refs, second_ref, update_ref, first_ref = refs[:places], *refs[places:]
    step = pl.program_id(0)
    row, col = lax.axis_index("dp"), lax.axis_index("owner")
    half = col // width

    @pl.when(step == 0)
    def _():
        for offset in range(places):
            first_ref[offset] = offset_refs[offset][...]

    for j in range(chunk):
        i = step * chunk + j
        owner = owner_ref[i]
        host = jnp.where((owner % col_size) // width == half, owner, other_ref[owner])
        host_row, host_col = host // col_size, host % width

        @pl.when(rank_ref[i] == 0)
        def _():
            update_ref[j] = first_ref[(host_row ^ row) * width + (host_col ^ (col % width))]

        @pl.when(rank_ref[i] == 1)
        def _():
            update_ref[j] = second_ref[host_row * width + host_col]


def unpack(owner_table, other, rank, first, second, row_size, col_size):
    places, rows, cols = second.shape
    mats = owner_table.shape[0]
    chunk = 8
    return pl.pallas_call(
        functools.partial(unpack_kernel, chunk, col_size, row_size),
        grid_spec=pltpu.PrefetchScalarGridSpec(
            num_scalar_prefetch=3,
            grid=(mats // chunk,),
            in_specs=[whole((rows, cols))] * places + [whole(second.shape)],
            out_specs=pl.BlockSpec((chunk, rows, cols), lambda i, *_: (i, 0, 0)),
            scratch_shapes=[pltpu.VMEM(second.shape, jnp.bfloat16)],
        ),
        out_shape=jax.ShapeDtypeStruct((mats, rows, cols), jnp.bfloat16),
        compiler_params=PARAMS,
        cost_estimate=pl.CostEstimate(
            flops=0, bytes_accessed=4 * mats * rows * cols, transcendentals=0
        ),
        name="unpack",
    )(owner_table, other, rank, *first, second)


def exchange(blocks, groups=None):
    return lax.all_to_all(
        blocks, AXES, split_axis=0, concat_axis=0, tiled=True, axis_index_groups=groups
    )


def swap(block, offset, devices):
    return lax.ppermute(block, AXES, [(d, d ^ offset) for d in range(devices)])


def on_device(gradients, momentum, owner_table):
    row_size = lax.axis_size("dp")
    col_size = lax.axis_size("owner")
    devices = row_size * col_size
    width = col_size // HALVES
    halves = [
        [r * col_size + half * width + c for r in range(row_size) for c in range(width)]
        for half in range(HALVES)
    ]
    first, other, rank = pack(gradients, momentum, owner_table, devices, col_size)
    arrived_first = exchange(first)
    new_momentum, second = update_momentum(gradients, momentum, owner_table, other, rank)
    arrived_first, second = lax.optimization_barrier((arrived_first, second))
    arrived_second = exchange(second)
    owned, back_first = orthogonalize(0, other, arrived_first, row_size, col_size)
    returned_first = [back_first[0]] + [
        swap(back_first[r * width + c], r * col_size + c, devices)
        for r in range(row_size)
        for c in range(width)
        if r or c
    ]
    returned_first, arrived_second = lax.optimization_barrier((returned_first, arrived_second))
    owned, back_second = orthogonalize(1, other, arrived_second, row_size, col_size, owned)
    returned_second = exchange(back_second[0], halves)
    update = unpack(
        owner_table, other, rank, returned_first, returned_second, row_size, col_size
    )
    return (new_momentum, update, owned)


def solution(mesh):
    return jax.shard_map(
        on_device,
        mesh=mesh,
        in_specs=(P(None, "dp", "owner"), P(None, "dp", "owner"), P()),
        out_specs=(P(None, "dp", "owner"), P(None, "dp", "owner"), P(("dp", "owner"), None, None)),
        check_vma=False,
    )
```

```python
import functools
import math

import jax
import jax.numpy as jnp
from jax import lax
from jax.experimental import pallas as pl
from jax.experimental.pallas import tpu as pltpu
from jax.sharding import PartitionSpec as P

ITERS = 2
CAP = 2
HALVES = 2
TILES = 2

coef_a = 3.4445
coef_b = -4.775
coef_c = 2.0315
momentum_beta = 0.95
epsilon = 1e-07

AXES = ("dp", "owner")
MIB = 1024 * 1024
PARAMS = pltpu.CompilerParams(vmem_limit_bytes=24 * MIB)
PACK_PARAMS = pltpu.CompilerParams(vmem_limit_bytes=60 * MIB)
SMEM = pl.BlockSpec(memory_space=pltpu.SMEM)


def round_up(value, multiple):
    return -(-value // multiple) * multiple


def whole(shape):
    return pl.BlockSpec(shape, lambda *_: (0,) * len(shape))


def nesterov_of(grad_ref, momentum_ref, j):
    grad = grad_ref[j].astype(jnp.float32)
    new = momentum_beta * momentum_ref[j] + grad
    return new, (grad + momentum_beta * new).astype(jnp.bfloat16)


def store_slot(slot, plan, i, owner, nesterov, slot_ref):
    other_ref, rank_ref = plan

    @pl.when(rank_ref[i] == slot)
    def _():
        slot_ref[owner] = nesterov
        slot_ref[other_ref[owner]] = nesterov


def pack_kernel(
    chunk, col_size, owner_ref, g_ref, m_ref, first_ref, other_ref, rank_ref, count_ref, list_ref
):
    step = pl.program_id(0)
    devices = first_ref.shape[0]
    mats = rank_ref.shape[0]

    def half_of(d):
        return (d % col_size) // (col_size // HALVES)

    @pl.when(step == 0)
    def _():
        @pl.loop(0, devices)
        def _(d):
            count_ref[d] = 0

        def rank_matrix(i, _):
            owner = owner_ref[i]
            rank_ref[i] = count_ref[owner]
            count_ref[owner] = count_ref[owner] + 1
            return 0

        lax.fori_loop(0, mats, rank_matrix, 0)

        def list_device(d, found):
            owns = jnp.minimum(count_ref[d], 1)
            half = half_of(d)
            row = 2 * jnp.where(owns == 1, half, 1 - half) + owns
            place = found[0]
            for k in range(1, 2 * HALVES):
                place = jnp.where(row == k, found[k], place)
            list_ref[row * devices + place] = d
            return tuple(n + jnp.where(row == k, 1, 0) for k, n in enumerate(found))

        found = lax.fori_loop(0, devices, list_device, (0,) * (2 * HALVES))
        for half in range(HALVES):

            def pair(k, _):
                idle = list_ref[2 * half * devices + k]
                other_ref[list_ref[(2 * half + 1) * devices + k]] = idle
                other_ref[idle] = idle
                return 0

            lax.fori_loop(0, found[2 * half + 1], pair, 0)

    for j in range(chunk):
        i = step * chunk + j
        _, nesterov = nesterov_of(g_ref, m_ref, j)
        store_slot(0, (other_ref, rank_ref), i, owner_ref[i], nesterov, first_ref)


def pack(gradients, momentum, owner_table, devices, col_size):
    mats, rows, cols = gradients.shape
    chunk = 8
    block = pl.BlockSpec((chunk, rows, cols), lambda i, *_: (i, 0, 0))
    return pl.pallas_call(
        functools.partial(pack_kernel, chunk, col_size),
        grid_spec=pltpu.PrefetchScalarGridSpec(
            num_scalar_prefetch=1,
            grid=(mats // chunk,),
            in_specs=[block, block],
            out_specs=[whole((devices, rows, cols)), SMEM, SMEM],
            scratch_shapes=[
                pltpu.SMEM((devices,), jnp.int32),
                pltpu.SMEM((2 * HALVES * devices,), jnp.int32),
            ],
        ),
        out_shape=[
            jax.ShapeDtypeStruct((devices, rows, cols), jnp.bfloat16),
            jax.ShapeDtypeStruct((devices,), jnp.int32),
            jax.ShapeDtypeStruct((mats,), jnp.int32),
        ],
        compiler_params=PACK_PARAMS,
        cost_estimate=pl.CostEstimate(
            flops=4 * mats * rows * cols, bytes_accessed=8 * mats * rows * cols, transcendentals=0
        ),
        name="pack",
    )(owner_table, gradients, momentum)


def momentum_kernel(chunk, owner_ref, other_ref, rank_ref, g_ref, m_ref, nm_ref, second_ref):
    step = pl.program_id(0)
    for j in range(chunk):
        i = step * chunk + j
        new, nesterov = nesterov_of(g_ref, m_ref, j)
        nm_ref[j] = new
        store_slot(1, (other_ref, rank_ref), i, owner_ref[i], nesterov, second_ref)


def update_momentum(gradients, momentum, owner_table, other, rank):
    mats, rows, cols = gradients.shape
    devices = other.shape[0]
    chunk = 8
    block = pl.BlockSpec((chunk, rows, cols), lambda i, *_: (i, 0, 0))
    return pl.pallas_call(
        functools.partial(momentum_kernel, chunk),
        grid_spec=pltpu.PrefetchScalarGridSpec(
            num_scalar_prefetch=3,
            grid=(mats // chunk,),
            in_specs=[block, block],
            out_specs=[block, whole((devices, rows, cols))],
        ),
        out_shape=[
            jax.ShapeDtypeStruct(momentum.shape, jnp.float32),
            jax.ShapeDtypeStruct((devices, rows, cols), jnp.bfloat16),
        ],
        compiler_params=PARAMS,
        cost_estimate=pl.CostEstimate(
            flops=4 * mats * rows * cols, bytes_accessed=12 * mats * rows * cols, transcendentals=0
        ),
        name="update_momentum",
    )(owner_table, other, rank, gradients, momentum)


def matmul(lhs, rhs, rhs_dim):
    return lax.dot_general(
        lhs, rhs, (((1,), (rhs_dim,)), ((), ())), preferred_element_type=jnp.float32
    )


def sum_rows(values):
    rows, cols = values.shape
    if rows % 8:
        return jnp.sum(values, axis=0, keepdims=True)
    return jnp.sum(values.reshape(rows // 8, 8, cols), axis=0)


def gather_blocks(x_ref, x_s, row_size, col_size):
    _, rows, cols = x_ref.shape
    height = rows * row_size
    total = 0.0
    for r in range(row_size):
        for c in range(col_size):
            block = x_ref[r * col_size + c]
            x_s[r * rows : (r + 1) * rows, c * cols : (c + 1) * cols] = block
            wide = block.astype(jnp.float32)
            total = total + sum_rows(wide * wide)
    x_s[height:, :] = jnp.zeros((x_s.shape[0] - height, x_s.shape[1]), x_s.dtype)
    return 1.0 / (jnp.sqrt(jnp.sum(total, keepdims=True)) + epsilon)


def newton_schulz(height, inverse, x_s, y_s, gram_s, write):
    padded, width = x_s.shape
    tile = height // TILES
    update_scale = 0.2 * math.sqrt(max(height, width))
    for ref in (y_s, gram_s):
        ref[height:, :] = jnp.zeros((padded - height, ref.shape[1]), ref.dtype)
    for iteration in range(ITERS):
        src = x_s if iteration == 0 else y_s
        for t in range(TILES):
            span = slice(t * tile, (t + 1) * tile)
            gram = matmul(src[span, :], src[...], 1)
            if iteration == 0:
                gram = gram * (inverse * inverse)
            gram_s[span, :] = gram.astype(jnp.bfloat16)
        for t in range(TILES):
            span = slice(t * tile, (t + 1) * tile)
            square = matmul(gram_s[span, :], gram_s[...], 0)
            mixing = coef_b * gram_s[span, :].astype(jnp.float32) + coef_c * square
            combined = coef_a * src[span, :].astype(jnp.float32) + matmul(
                mixing.astype(jnp.bfloat16), src[...], 0
            )
            if iteration == 0:
                combined = combined * inverse
            if iteration + 1 < ITERS:
                y_s[span, :] = combined.astype(jnp.bfloat16)
            else:
                write(t, (update_scale * combined).astype(jnp.bfloat16))


def ortho_kernel(row_size, col_size, slot, other_ref, x_ref, *refs):
    owned_ref, back_ref, x_s, y_s, gram_s, out_s, sems = refs[-7:]
    _, rows, cols = x_ref.shape
    width = col_size // HALVES
    height = rows * row_size
    tile = height // TILES
    col = lax.axis_index("owner")
    me = lax.axis_index("dp") * col_size + col
    owns = other_ref[me] != me
    low = col < width
    inverse = gather_blocks(x_ref, x_s, row_size, col_size)

    def copy_out(t):
        span = pl.ds(t * tile, tile)
        return pltpu.make_async_copy(out_s.at[span], owned_ref.at[slot, span], sems.at[t])

    def write(t, result):
        out_s[t * tile : (t + 1) * tile, :] = jnp.where(owns, result, jnp.zeros_like(result))
        copy_out(t).start()
        for j in range(row_size // TILES):
            block = result[j * rows : (j + 1) * rows, :]
            for c in range(width):
                back_ref[(t * (row_size // TILES) + j) * width + c, 0] = jnp.where(
                    low,
                    block[:, c * cols : (c + 1) * cols],
                    block[:, (c + width) * cols : (c + width + 1) * cols],
                )

    newton_schulz(height, inverse, x_s, y_s, gram_s, write)
    for t in range(TILES):
        copy_out(t).wait()


def orthogonalize(slot, other, arrived, row_size, col_size, made=()):
    devices, rows, cols = arrived.shape
    height, width = rows * row_size, cols * col_size
    padded = round_up(height, 256)
    places = devices // HALVES
    anywhere = pl.BlockSpec(memory_space=pl.ANY)
    return pl.pallas_call(
        functools.partial(ortho_kernel, row_size, col_size, slot),
        grid=(1,),
        in_specs=[SMEM, whole(arrived.shape)] + [anywhere] * len(made),
        out_specs=[anywhere, pl.BlockSpec((places, 1, rows, cols), lambda i: (0, slot, 0, 0))],
        out_shape=[
            jax.ShapeDtypeStruct((CAP, height, width), jnp.bfloat16),
            jax.ShapeDtypeStruct((places, CAP, rows, cols), jnp.bfloat16),
        ],
        scratch_shapes=[
            pltpu.VMEM((padded, width), jnp.bfloat16),
            pltpu.VMEM((padded, width), jnp.bfloat16),
            pltpu.VMEM((padded, padded), jnp.bfloat16),
            pltpu.VMEM((height, width), jnp.bfloat16),
            pltpu.SemaphoreType.DMA((TILES,)),
        ],
        input_output_aliases={2 + k: k for k in range(len(made))},
        compiler_params=PARAMS,
        cost_estimate=pl.CostEstimate(
            flops=2 * ITERS * padded * padded * (2 * width + padded),
            bytes_accessed=6 * padded * width,
            transcendentals=0,
        ),
        name="orthogonalize",
    )(other, arrived, *made)


def unpack_kernel(chunk, col_size, owner_ref, other_ref, rank_ref, back_ref, update_ref):
    step = pl.program_id(0)
    width = col_size // HALVES
    half = lax.axis_index("owner") // width
    for j in range(chunk):
        i = step * chunk + j
        owner = owner_ref[i]
        host = jnp.where((owner % col_size) // width == half, owner, other_ref[owner])
        update_ref[j] = back_ref[(host // col_size) * width + host % width, rank_ref[i]]


def unpack(owner_table, other, rank, back, col_size):
    _, _, rows, cols = back.shape
    mats = owner_table.shape[0]
    chunk = 8
    return pl.pallas_call(
        functools.partial(unpack_kernel, chunk, col_size),
        grid_spec=pltpu.PrefetchScalarGridSpec(
            num_scalar_prefetch=3,
            grid=(mats // chunk,),
            in_specs=[whole(back.shape)],
            out_specs=pl.BlockSpec((chunk, rows, cols), lambda i, *_: (i, 0, 0)),
        ),
        out_shape=jax.ShapeDtypeStruct((mats, rows, cols), jnp.bfloat16),
        compiler_params=PARAMS,
        cost_estimate=pl.CostEstimate(
            flops=0, bytes_accessed=4 * mats * rows * cols, transcendentals=0
        ),
        name="unpack",
    )(owner_table, other, rank, back)


def exchange(blocks, groups=None):
    return lax.all_to_all(
        blocks, AXES, split_axis=0, concat_axis=0, tiled=True, axis_index_groups=groups
    )


def on_device(gradients, momentum, owner_table):
    row_size = lax.axis_size("dp")
    col_size = lax.axis_size("owner")
    devices = row_size * col_size
    width = col_size // HALVES
    halves = [
        [r * col_size + half * width + c for r in range(row_size) for c in range(width)]
        for half in range(HALVES)
    ]
    first, other, rank = pack(gradients, momentum, owner_table, devices, col_size)
    arrived_first = exchange(first)
    new_momentum, second = update_momentum(gradients, momentum, owner_table, other, rank)
    arrived_first, second = lax.optimization_barrier((arrived_first, second))
    arrived_second = exchange(second)
    made = orthogonalize(0, other, arrived_first, row_size, col_size)
    owned, back = orthogonalize(1, other, arrived_second, row_size, col_size, made)
    update = unpack(owner_table, other, rank, exchange(back, halves), col_size)
    return (new_momentum, update, owned)


def solution(mesh):
    return jax.shard_map(
        on_device,
        mesh=mesh,
        in_specs=(P(None, "dp", "owner"), P(None, "dp", "owner"), P()),
        out_specs=(P(None, "dp", "owner"), P(None, "dp", "owner"), P(("dp", "owner"), None, None)),
        check_vma=False,
    )
```

```python
import functools
import math

import jax
import jax.numpy as jnp
from jax import lax
from jax.experimental import pallas as pl
from jax.experimental.pallas import tpu as pltpu
from jax.sharding import PartitionSpec as P

ITERS = 2
CAP = 2
HALVES = 2
TILES = 2

coef_a = 3.4445
coef_b = -4.775
coef_c = 2.0315
momentum_beta = 0.95
epsilon = 1e-07

AXES = ("dp", "owner")
MIB = 1024 * 1024
PARAMS = pltpu.CompilerParams(vmem_limit_bytes=24 * MIB)
PACK_PARAMS = pltpu.CompilerParams(vmem_limit_bytes=60 * MIB)
SMEM = pl.BlockSpec(memory_space=pltpu.SMEM)


def round_up(value, multiple):
    return -(-value // multiple) * multiple


def whole(shape):
    return pl.BlockSpec(shape, lambda *_: (0,) * len(shape))


def nesterov_of(grad_ref, momentum_ref, j):
    grad = grad_ref[j].astype(jnp.float32)
    new = momentum_beta * momentum_ref[j] + grad
    return new, (grad + momentum_beta * new).astype(jnp.bfloat16)


def store_slot(slot, plan, i, owner, nesterov, slot_ref):
    other_ref, rank_ref = plan

    @pl.when(rank_ref[i] == slot)
    def _():
        slot_ref[owner] = nesterov
        slot_ref[other_ref[owner]] = nesterov


def pack_kernel(
    chunk, col_size, owner_ref, g_ref, m_ref, first_ref, other_ref, rank_ref, count_ref, list_ref
):
    step = pl.program_id(0)
    devices = first_ref.shape[0]
    mats = rank_ref.shape[0]

    def half_of(d):
        return (d % col_size) // (col_size // HALVES)

    @pl.when(step == 0)
    def _():
        @pl.loop(0, devices)
        def _(d):
            count_ref[d] = 0

        def rank_matrix(i, _):
            owner = owner_ref[i]
            rank_ref[i] = count_ref[owner]
            count_ref[owner] = count_ref[owner] + 1
            return 0

        lax.fori_loop(0, mats, rank_matrix, 0)

        def list_device(d, found):
            owns = jnp.minimum(count_ref[d], 1)
            half = half_of(d)
            row = 2 * jnp.where(owns == 1, half, 1 - half) + owns
            place = found[0]
            for k in range(1, 2 * HALVES):
                place = jnp.where(row == k, found[k], place)
            list_ref[row * devices + place] = d
            return tuple(n + jnp.where(row == k, 1, 0) for k, n in enumerate(found))

        found = lax.fori_loop(0, devices, list_device, (0,) * (2 * HALVES))
        for half in range(HALVES):

            def pair(k, _):
                idle = list_ref[2 * half * devices + k]
                other_ref[list_ref[(2 * half + 1) * devices + k]] = idle
                other_ref[idle] = idle
                return 0

            lax.fori_loop(0, found[2 * half + 1], pair, 0)

    for j in range(chunk):
        i = step * chunk + j
        _, nesterov = nesterov_of(g_ref, m_ref, j)
        store_slot(0, (other_ref, rank_ref), i, owner_ref[i], nesterov, first_ref)


def pack(gradients, momentum, owner_table, devices, col_size):
    mats, rows, cols = gradients.shape
    chunk = 8
    block = pl.BlockSpec((chunk, rows, cols), lambda i, *_: (i, 0, 0))
    return pl.pallas_call(
        functools.partial(pack_kernel, chunk, col_size),
        grid_spec=pltpu.PrefetchScalarGridSpec(
            num_scalar_prefetch=1,
            grid=(mats // chunk,),
            in_specs=[block, block],
            out_specs=[whole((devices, rows, cols)), SMEM, SMEM],
            scratch_shapes=[
                pltpu.SMEM((devices,), jnp.int32),
                pltpu.SMEM((2 * HALVES * devices,), jnp.int32),
            ],
        ),
        out_shape=[
            jax.ShapeDtypeStruct((devices, rows, cols), jnp.bfloat16),
            jax.ShapeDtypeStruct((devices,), jnp.int32),
            jax.ShapeDtypeStruct((mats,), jnp.int32),
        ],
        compiler_params=PACK_PARAMS,
        cost_estimate=pl.CostEstimate(
            flops=4 * mats * rows * cols, bytes_accessed=8 * mats * rows * cols, transcendentals=0
        ),
        name="pack",
    )(owner_table, gradients, momentum)


def momentum_kernel(chunk, owner_ref, other_ref, rank_ref, g_ref, m_ref, nm_ref, second_ref):
    step = pl.program_id(0)
    for j in range(chunk):
        i = step * chunk + j
        new, nesterov = nesterov_of(g_ref, m_ref, j)
        nm_ref[j] = new
        store_slot(1, (other_ref, rank_ref), i, owner_ref[i], nesterov, second_ref)


def update_momentum(gradients, momentum, owner_table, other, rank):
    mats, rows, cols = gradients.shape
    devices = other.shape[0]
    chunk = 8
    block = pl.BlockSpec((chunk, rows, cols), lambda i, *_: (i, 0, 0))
    return pl.pallas_call(
        functools.partial(momentum_kernel, chunk),
        grid_spec=pltpu.PrefetchScalarGridSpec(
            num_scalar_prefetch=3,
            grid=(mats // chunk,),
            in_specs=[block, block],
            out_specs=[block, whole((devices, rows, cols))],
        ),
        out_shape=[
            jax.ShapeDtypeStruct(momentum.shape, jnp.float32),
            jax.ShapeDtypeStruct((devices, rows, cols), jnp.bfloat16),
        ],
        compiler_params=PARAMS,
        cost_estimate=pl.CostEstimate(
            flops=4 * mats * rows * cols, bytes_accessed=12 * mats * rows * cols, transcendentals=0
        ),
        name="update_momentum",
    )(owner_table, other, rank, gradients, momentum)


def matmul(lhs, rhs, rhs_dim):
    return lax.dot_general(
        lhs, rhs, (((1,), (rhs_dim,)), ((), ())), preferred_element_type=jnp.float32
    )


def sum_rows(values):
    rows, cols = values.shape
    if rows % 8:
        return jnp.sum(values, axis=0, keepdims=True)
    return jnp.sum(values.reshape(rows // 8, 8, cols), axis=0)


def gather_blocks(x_ref, x_s, row_size, col_size):
    _, rows, cols = x_ref.shape
    height = rows * row_size
    total = 0.0
    for r in range(row_size):
        for c in range(col_size):
            block = x_ref[r * col_size + c]
            x_s[r * rows : (r + 1) * rows, c * cols : (c + 1) * cols] = block
            wide = block.astype(jnp.float32)
            total = total + sum_rows(wide * wide)
    x_s[height:, :] = jnp.zeros((x_s.shape[0] - height, x_s.shape[1]), x_s.dtype)
    return 1.0 / (jnp.sqrt(jnp.sum(total, keepdims=True)) + epsilon)


def newton_schulz(height, inverse, x_s, y_s, gram_s, write):
    padded, width = x_s.shape
    tile = height // TILES
    update_scale = 0.2 * math.sqrt(max(height, width))
    for ref in (y_s, gram_s):
        ref[height:, :] = jnp.zeros((padded - height, ref.shape[1]), ref.dtype)
    for iteration in range(ITERS):
        src = x_s if iteration == 0 else y_s
        for t in range(TILES):
            span = slice(t * tile, (t + 1) * tile)
            gram = matmul(src[span, :], src[...], 1)
            if iteration == 0:
                gram = gram * (inverse * inverse)
            gram_s[span, :] = gram.astype(jnp.bfloat16)
        for t in range(TILES):
            span = slice(t * tile, (t + 1) * tile)
            square = matmul(gram_s[span, :], gram_s[...], 0)
            mixing = coef_b * gram_s[span, :].astype(jnp.float32) + coef_c * square
            combined = coef_a * src[span, :].astype(jnp.float32) + matmul(
                mixing.astype(jnp.bfloat16), src[...], 0
            )
            if iteration == 0:
                combined = combined * inverse
            if iteration + 1 < ITERS:
                y_s[span, :] = combined.astype(jnp.bfloat16)
            else:
                write(t, (update_scale * combined).astype(jnp.bfloat16))


def ortho_kernel(row_size, col_size, slot, other_ref, x_ref, *refs):
    _, rows, cols = x_ref.shape
    width = col_size // HALVES
    places = row_size * width
    height = rows * row_size
    tile = height // TILES
    if slot:
        owned_ref, back_ref, x_s, y_s, gram_s, out_s, sems = refs[1:]
    else:
        owned_ref, offset_refs = refs[0], refs[1 : 1 + places]
        x_s, y_s, gram_s, out_s, sems, back_ref = refs[1 + places :]
    row, col = lax.axis_index("dp"), lax.axis_index("owner")
    me = row * col_size + col
    owns = other_ref[me] != me
    low = col < width
    inverse = gather_blocks(x_ref, x_s, row_size, col_size)

    def copy_out(t):
        span = pl.ds(t * tile, tile)
        return pltpu.make_async_copy(out_s.at[span], owned_ref.at[slot, span], sems.at[t])

    def write(t, result):
        out_s[t * tile : (t + 1) * tile, :] = jnp.where(owns, result, jnp.zeros_like(result))
        copy_out(t).start()
        for j in range(row_size // TILES):
            block = result[j * rows : (j + 1) * rows, :]
            r = t * (row_size // TILES) + j
            for c in range(width):
                place = r * width + c if slot else (r ^ row) * width + (c ^ (col % width))
                back_ref[place] = jnp.where(
                    low,
                    block[:, c * cols : (c + 1) * cols],
                    block[:, (c + width) * cols : (c + width + 1) * cols],
                )

    newton_schulz(height, inverse, x_s, y_s, gram_s, write)
    if not slot:
        for offset in range(places):
            offset_refs[offset][...] = back_ref[offset]
    for t in range(TILES):
        copy_out(t).wait()


def orthogonalize(slot, other, arrived, row_size, col_size, owned=None):
    devices, rows, cols = arrived.shape
    height, width = rows * row_size, cols * col_size
    padded = round_up(height, 256)
    places = devices // HALVES
    anywhere = pl.BlockSpec(memory_space=pl.ANY)
    in_specs, operands = [SMEM, whole(arrived.shape)], [other, arrived]
    scratch_shapes = [
        pltpu.VMEM((padded, width), jnp.bfloat16),
        pltpu.VMEM((padded, width), jnp.bfloat16),
        pltpu.VMEM((padded, padded), jnp.bfloat16),
        pltpu.VMEM((height, width), jnp.bfloat16),
        pltpu.SemaphoreType.DMA((TILES,)),
    ]
    if slot:
        in_specs.append(anywhere)
        operands.append(owned)
        back = [(places, rows, cols)]
    else:
        back = [(rows, cols)] * places
        scratch_shapes.append(pltpu.VMEM((places, rows, cols), jnp.bfloat16))
    owned, *back = pl.pallas_call(
        functools.partial(ortho_kernel, row_size, col_size, slot),
        grid=(1,),
        in_specs=in_specs,
        out_specs=[anywhere] + [whole(shape) for shape in back],
        out_shape=[jax.ShapeDtypeStruct((CAP, height, width), jnp.bfloat16)]
        + [jax.ShapeDtypeStruct(shape, jnp.bfloat16) for shape in back],
        scratch_shapes=scratch_shapes,
        input_output_aliases={2: 0} if slot else {},
        compiler_params=PARAMS,
        cost_estimate=pl.CostEstimate(
            flops=2 * ITERS * padded * padded * (2 * width + padded),
            bytes_accessed=6 * padded * width,
            transcendentals=0,
        ),
        name="orthogonalize",
    )(*operands)
    return owned, back


def unpack_kernel(chunk, col_size, row_size, owner_ref, other_ref, rank_ref, *refs):
    width = col_size // HALVES
    places = row_size * width
    offset_refs, second_ref, update_ref, first_ref = refs[:places], *refs[places:]
    step = pl.program_id(0)
    row, col = lax.axis_index("dp"), lax.axis_index("owner")
    half = col // width

    @pl.when(step == 0)
    def _():
        for offset in range(places):
            first_ref[offset] = offset_refs[offset][...]

    for j in range(chunk):
        i = step * chunk + j
        owner = owner_ref[i]
        host = jnp.where((owner % col_size) // width == half, owner, other_ref[owner])
        host_row, host_col = host // col_size, host % width

        @pl.when(rank_ref[i] == 0)
        def _():
            update_ref[j] = first_ref[(host_row ^ row) * width + (host_col ^ (col % width))]

        @pl.when(rank_ref[i] == 1)
        def _():
            update_ref[j] = second_ref[host_row * width + host_col]


def unpack(owner_table, other, rank, first, second, row_size, col_size):
    places, rows, cols = second.shape
    mats = owner_table.shape[0]
    chunk = 8
    return pl.pallas_call(
        functools.partial(unpack_kernel, chunk, col_size, row_size),
        grid_spec=pltpu.PrefetchScalarGridSpec(
            num_scalar_prefetch=3,
            grid=(mats // chunk,),
            in_specs=[whole((rows, cols))] * places + [whole(second.shape)],
            out_specs=pl.BlockSpec((chunk, rows, cols), lambda i, *_: (i, 0, 0)),
            scratch_shapes=[pltpu.VMEM(second.shape, jnp.bfloat16)],
        ),
        out_shape=jax.ShapeDtypeStruct((mats, rows, cols), jnp.bfloat16),
        compiler_params=PARAMS,
        cost_estimate=pl.CostEstimate(
            flops=0, bytes_accessed=4 * mats * rows * cols, transcendentals=0
        ),
        name="unpack",
    )(owner_table, other, rank, *first, second)


def exchange(blocks, groups=None):
    return lax.all_to_all(
        blocks, AXES, split_axis=0, concat_axis=0, tiled=True, axis_index_groups=groups
    )


def swap(block, offset, devices):
    return lax.ppermute(block, AXES, [(d, d ^ offset) for d in range(devices)])


def on_device(gradients, momentum, owner_table):
    row_size = lax.axis_size("dp")
    col_size = lax.axis_size("owner")
    devices = row_size * col_size
    width = col_size // HALVES
    halves = [
        [r * col_size + half * width + c for r in range(row_size) for c in range(width)]
        for half in range(HALVES)
    ]
    first, other, rank = pack(gradients, momentum, owner_table, devices, col_size)
    arrived_first = exchange(first)
    new_momentum, second = update_momentum(gradients, momentum, owner_table, other, rank)
    arrived_first, second = lax.optimization_barrier((arrived_first, second))
    arrived_second = exchange(second)
    owned, back_first = orthogonalize(0, other, arrived_first, row_size, col_size)
    returned_first = [back_first[0]] + [
        swap(back_first[r * width + c], r * col_size + c, devices)
        for r in range(row_size)
        for c in range(width)
        if r or c
    ]
    owned, back_second = orthogonalize(1, other, arrived_second, row_size, col_size, owned)
    returned_first, back_second = lax.optimization_barrier((returned_first, back_second))
    returned_second = exchange(back_second[0], halves)
    update = unpack(
        owner_table, other, rank, returned_first, returned_second, row_size, col_size
    )
    return (new_momentum, update, owned)


def solution(mesh):
    return jax.shard_map(
        on_device,
        mesh=mesh,
        in_specs=(P(None, "dp", "owner"), P(None, "dp", "owner"), P()),
        out_specs=(P(None, "dp", "owner"), P(None, "dp", "owner"), P(("dp", "owner"), None, None)),
        check_vma=False,
    )
```

```python
import functools
import math

import jax
import jax.numpy as jnp
from jax import lax
from jax.experimental import pallas as pl
from jax.experimental.pallas import tpu as pltpu
from jax.sharding import PartitionSpec as P

ITERS = 2
CAP = 2
HALVES = 2
TILES = 2
LOW = 4

coef_a = 3.4445
coef_b = -4.775
coef_c = 2.0315
momentum_beta = 0.95
epsilon = 1e-07

AXES = ("dp", "owner")
MIB = 1024 * 1024
PARAMS = pltpu.CompilerParams(vmem_limit_bytes=24 * MIB)
PACK_PARAMS = pltpu.CompilerParams(vmem_limit_bytes=60 * MIB)
SMEM = pl.BlockSpec(memory_space=pltpu.SMEM)


def round_up(value, multiple):
    return -(-value // multiple) * multiple


def whole(shape):
    return pl.BlockSpec(shape, lambda *_: (0,) * len(shape))


def nesterov_of(grad_ref, momentum_ref, j):
    grad = grad_ref[j].astype(jnp.float32)
    new = momentum_beta * momentum_ref[j] + grad
    return new, (grad + momentum_beta * new).astype(jnp.bfloat16)


def store_slot(slot, plan, i, owner, nesterov, slot_ref):
    other_ref, rank_ref = plan

    @pl.when(rank_ref[i] == slot)
    def _():
        slot_ref[owner] = nesterov
        slot_ref[other_ref[owner]] = nesterov


def pack_kernel(
    chunk, col_size, owner_ref, g_ref, m_ref, first_ref, other_ref, rank_ref, count_ref, list_ref
):
    step = pl.program_id(0)
    devices = first_ref.shape[0]
    mats = rank_ref.shape[0]

    def half_of(d):
        return (d % col_size) // (col_size // HALVES)

    @pl.when(step == 0)
    def _():
        @pl.loop(0, devices)
        def _(d):
            count_ref[d] = 0

        def rank_matrix(i, _):
            owner = owner_ref[i]
            rank_ref[i] = count_ref[owner]
            count_ref[owner] = count_ref[owner] + 1
            return 0

        lax.fori_loop(0, mats, rank_matrix, 0)

        def list_device(d, found):
            owns = jnp.minimum(count_ref[d], 1)
            half = half_of(d)
            row = 2 * jnp.where(owns == 1, half, 1 - half) + owns
            place = found[0]
            for k in range(1, 2 * HALVES):
                place = jnp.where(row == k, found[k], place)
            list_ref[row * devices + place] = d
            return tuple(n + jnp.where(row == k, 1, 0) for k, n in enumerate(found))

        found = lax.fori_loop(0, devices, list_device, (0,) * (2 * HALVES))
        for half in range(HALVES):

            def pair(k, _):
                idle = list_ref[2 * half * devices + k]
                other_ref[list_ref[(2 * half + 1) * devices + k]] = idle
                other_ref[idle] = idle
                return 0

            lax.fori_loop(0, found[2 * half + 1], pair, 0)

    for j in range(chunk):
        i = step * chunk + j
        _, nesterov = nesterov_of(g_ref, m_ref, j)
        store_slot(0, (other_ref, rank_ref), i, owner_ref[i], nesterov, first_ref)


def pack(gradients, momentum, owner_table, devices, col_size):
    mats, rows, cols = gradients.shape
    chunk = 8
    block = pl.BlockSpec((chunk, rows, cols), lambda i, *_: (i, 0, 0))
    return pl.pallas_call(
        functools.partial(pack_kernel, chunk, col_size),
        grid_spec=pltpu.PrefetchScalarGridSpec(
            num_scalar_prefetch=1,
            grid=(mats // chunk,),
            in_specs=[block, block],
            out_specs=[whole((devices, rows, cols)), SMEM, SMEM],
            scratch_shapes=[
                pltpu.SMEM((devices,), jnp.int32),
                pltpu.SMEM((2 * HALVES * devices,), jnp.int32),
            ],
        ),
        out_shape=[
            jax.ShapeDtypeStruct((devices, rows, cols), jnp.bfloat16),
            jax.ShapeDtypeStruct((devices,), jnp.int32),
            jax.ShapeDtypeStruct((mats,), jnp.int32),
        ],
        compiler_params=PACK_PARAMS,
        cost_estimate=pl.CostEstimate(
            flops=4 * mats * rows * cols, bytes_accessed=8 * mats * rows * cols, transcendentals=0
        ),
        name="pack",
    )(owner_table, gradients, momentum)


def momentum_kernel(chunk, owner_ref, other_ref, rank_ref, g_ref, m_ref, nm_ref, second_ref):
    step = pl.program_id(0)
    for j in range(chunk):
        i = step * chunk + j
        new, nesterov = nesterov_of(g_ref, m_ref, j)
        nm_ref[j] = new
        store_slot(1, (other_ref, rank_ref), i, owner_ref[i], nesterov, second_ref)


def update_momentum(gradients, momentum, owner_table, other, rank):
    mats, rows, cols = gradients.shape
    devices = other.shape[0]
    chunk = 8
    block = pl.BlockSpec((chunk, rows, cols), lambda i, *_: (i, 0, 0))
    return pl.pallas_call(
        functools.partial(momentum_kernel, chunk),
        grid_spec=pltpu.PrefetchScalarGridSpec(
            num_scalar_prefetch=3,
            grid=(mats // chunk,),
            in_specs=[block, block],
            out_specs=[block, whole((devices, rows, cols))],
        ),
        out_shape=[
            jax.ShapeDtypeStruct(momentum.shape, jnp.float32),
            jax.ShapeDtypeStruct((devices, rows, cols), jnp.bfloat16),
        ],
        compiler_params=PARAMS,
        cost_estimate=pl.CostEstimate(
            flops=4 * mats * rows * cols, bytes_accessed=12 * mats * rows * cols, transcendentals=0
        ),
        name="update_momentum",
    )(owner_table, other, rank, gradients, momentum)


def matmul(lhs, rhs, rhs_dim):
    return lax.dot_general(
        lhs, rhs, (((1,), (rhs_dim,)), ((), ())), preferred_element_type=jnp.float32
    )


def sum_rows(values):
    rows, cols = values.shape
    if rows % 8:
        return jnp.sum(values, axis=0, keepdims=True)
    return jnp.sum(values.reshape(rows // 8, 8, cols), axis=0)


def gather_blocks(x_ref, x_s, row_size, col_size):
    _, rows, cols = x_ref.shape
    height = rows * row_size
    total = 0.0
    for r in range(row_size):
        for c in range(col_size):
            block = x_ref[r * col_size + c]
            x_s[r * rows : (r + 1) * rows, c * cols : (c + 1) * cols] = block
            wide = block.astype(jnp.float32)
            total = total + sum_rows(wide * wide)
    x_s[height:, :] = jnp.zeros((x_s.shape[0] - height, x_s.shape[1]), x_s.dtype)
    return 1.0 / (jnp.sqrt(jnp.sum(total, keepdims=True)) + epsilon)


def newton_schulz(height, inverse, x_s, y_s, gram_s, write):
    padded, width = x_s.shape
    tile = height // TILES
    update_scale = 0.2 * math.sqrt(max(height, width))
    for ref in (y_s, gram_s):
        ref[height:, :] = jnp.zeros((padded - height, ref.shape[1]), ref.dtype)
    for iteration in range(ITERS):
        src = x_s if iteration == 0 else y_s
        for t in range(TILES):
            span = slice(t * tile, (t + 1) * tile)
            gram = matmul(src[span, :], src[...], 1)
            if iteration == 0:
                gram = gram * (inverse * inverse)
            gram_s[span, :] = gram.astype(jnp.bfloat16)
        for t in range(TILES):
            span = slice(t * tile, (t + 1) * tile)
            square = matmul(gram_s[span, :], gram_s[...], 0)
            mixing = coef_b * gram_s[span, :].astype(jnp.float32) + coef_c * square
            combined = coef_a * src[span, :].astype(jnp.float32) + matmul(
                mixing.astype(jnp.bfloat16), src[...], 0
            )
            if iteration == 0:
                combined = combined * inverse
            if iteration + 1 < ITERS:
                y_s[span, :] = combined.astype(jnp.bfloat16)
            else:
                write(t, (update_scale * combined).astype(jnp.bfloat16))


def stage_place(row_offset, col_offset, row_size, width):
    high = row_offset // LOW * width + col_offset
    return row_offset % LOW * (row_size // LOW * width) + high


def ortho_kernel(row_size, col_size, slot, other_ref, x_ref, *refs):
    _, rows, cols = x_ref.shape
    width = col_size // HALVES
    places = row_size * width
    height = rows * row_size
    tile = height // TILES
    if slot:
        owned_ref, back_ref, x_s, y_s, gram_s, out_s, sems = refs[1:]
    else:
        owned_ref, low_refs = refs[0], refs[1 : 1 + LOW]
        x_s, y_s, gram_s, out_s, sems, back_ref = refs[1 + LOW :]
    row, col = lax.axis_index("dp"), lax.axis_index("owner")
    me = row * col_size + col
    owns = other_ref[me] != me
    low = col < width
    inverse = gather_blocks(x_ref, x_s, row_size, col_size)

    def copy_out(t):
        span = pl.ds(t * tile, tile)
        return pltpu.make_async_copy(out_s.at[span], owned_ref.at[slot, span], sems.at[t])

    def write(t, result):
        out_s[t * tile : (t + 1) * tile, :] = jnp.where(owns, result, jnp.zeros_like(result))
        copy_out(t).start()
        for j in range(row_size // TILES):
            block = result[j * rows : (j + 1) * rows, :]
            r = t * (row_size // TILES) + j
            for c in range(width):
                if slot:
                    place = r * width + c
                else:
                    place = stage_place(r ^ row, c ^ (col % width), row_size, width)
                back_ref[place] = jnp.where(
                    low,
                    block[:, c * cols : (c + 1) * cols],
                    block[:, (c + width) * cols : (c + width + 1) * cols],
                )

    newton_schulz(height, inverse, x_s, y_s, gram_s, write)
    if not slot:
        for k in range(LOW):
            low_refs[k][...] = back_ref[k * places // LOW : (k + 1) * places // LOW]
    for t in range(TILES):
        copy_out(t).wait()


def orthogonalize(slot, other, arrived, row_size, col_size, owned=None):
    devices, rows, cols = arrived.shape
    height, width = rows * row_size, cols * col_size
    padded = round_up(height, 256)
    places = devices // HALVES
    anywhere = pl.BlockSpec(memory_space=pl.ANY)
    in_specs, operands = [SMEM, whole(arrived.shape)], [other, arrived]
    scratch_shapes = [
        pltpu.VMEM((padded, width), jnp.bfloat16),
        pltpu.VMEM((padded, width), jnp.bfloat16),
        pltpu.VMEM((padded, padded), jnp.bfloat16),
        pltpu.VMEM((height, width), jnp.bfloat16),
        pltpu.SemaphoreType.DMA((TILES,)),
    ]
    if slot:
        in_specs.append(anywhere)
        operands.append(owned)
        back = [(places, rows, cols)]
    else:
        back = [(places // LOW, rows, cols)] * LOW
        scratch_shapes.append(pltpu.VMEM((places, rows, cols), jnp.bfloat16))
    owned, *back = pl.pallas_call(
        functools.partial(ortho_kernel, row_size, col_size, slot),
        grid=(1,),
        in_specs=in_specs,
        out_specs=[anywhere] + [whole(shape) for shape in back],
        out_shape=[jax.ShapeDtypeStruct((CAP, height, width), jnp.bfloat16)]
        + [jax.ShapeDtypeStruct(shape, jnp.bfloat16) for shape in back],
        scratch_shapes=scratch_shapes,
        input_output_aliases={2: 0} if slot else {},
        compiler_params=PARAMS,
        cost_estimate=pl.CostEstimate(
            flops=2 * ITERS * padded * padded * (2 * width + padded),
            bytes_accessed=6 * padded * width,
            transcendentals=0,
        ),
        name="orthogonalize",
    )(*operands)
    return owned, back


def restage_kernel(*refs):
    low_refs, high_refs = refs[:LOW], refs[LOW:]
    for h, high_ref in enumerate(high_refs):
        for k, low_ref in enumerate(low_refs):
            high_ref[k] = low_ref[h]


def restage(blocks):
    highs, rows, cols = blocks[0].shape
    out = jax.ShapeDtypeStruct((LOW, rows, cols), blocks[0].dtype)
    return pl.pallas_call(
        restage_kernel,
        grid=(1,),
        in_specs=[whole(blocks[0].shape)] * LOW,
        out_specs=[whole(out.shape)] * highs,
        out_shape=[out] * highs,
        compiler_params=PARAMS,
        cost_estimate=pl.CostEstimate(
            flops=0, bytes_accessed=4 * LOW * highs * rows * cols, transcendentals=0
        ),
        name="restage",
    )(*blocks)


def unpack_kernel(chunk, col_size, owner_ref, other_ref, rank_ref, *refs):
    width = col_size // HALVES
    high_refs, second_ref, update_ref, first_ref = refs[:-3], *refs[-3:]
    step = pl.program_id(0)
    row, col = lax.axis_index("dp"), lax.axis_index("owner")
    half = col // width

    @pl.when(step == 0)
    def _():
        for h, high_ref in enumerate(high_refs):
            first_ref[h * LOW : (h + 1) * LOW] = high_ref[...]

    for j in range(chunk):
        i = step * chunk + j
        owner = owner_ref[i]
        host = jnp.where((owner % col_size) // width == half, owner, other_ref[owner])
        host_row, host_col = host // col_size, host % width
        offset = host_row ^ row
        high = offset // LOW * width + (host_col ^ (col % width))

        @pl.when(rank_ref[i] == 0)
        def _():
            update_ref[j] = first_ref[high * LOW + offset % LOW]

        @pl.when(rank_ref[i] == 1)
        def _():
            update_ref[j] = second_ref[host_row * width + host_col]


def unpack(owner_table, other, rank, first, second, col_size):
    _, rows, cols = second.shape
    mats = owner_table.shape[0]
    chunk = 8
    return pl.pallas_call(
        functools.partial(unpack_kernel, chunk, col_size),
        grid_spec=pltpu.PrefetchScalarGridSpec(
            num_scalar_prefetch=3,
            grid=(mats // chunk,),
            in_specs=[whole(first[0].shape)] * len(first) + [whole(second.shape)],
            out_specs=pl.BlockSpec((chunk, rows, cols), lambda i, *_: (i, 0, 0)),
            scratch_shapes=[pltpu.VMEM(second.shape, jnp.bfloat16)],
        ),
        out_shape=jax.ShapeDtypeStruct((mats, rows, cols), jnp.bfloat16),
        compiler_params=PARAMS,
        cost_estimate=pl.CostEstimate(
            flops=0, bytes_accessed=4 * mats * rows * cols, transcendentals=0
        ),
        name="unpack",
    )(owner_table, other, rank, *first, second)


def exchange(blocks, groups=None):
    return lax.all_to_all(
        blocks, AXES, split_axis=0, concat_axis=0, tiled=True, axis_index_groups=groups
    )


def swap(block, offset, devices):
    return lax.ppermute(block, AXES, [(d, d ^ offset) for d in range(devices)])


def on_device(gradients, momentum, owner_table):
    row_size = lax.axis_size("dp")
    col_size = lax.axis_size("owner")
    devices = row_size * col_size
    width = col_size // HALVES
    halves = [
        [r * col_size + half * width + c for r in range(row_size) for c in range(width)]
        for half in range(HALVES)
    ]
    first, other, rank = pack(gradients, momentum, owner_table, devices, col_size)
    arrived_first = exchange(first)
    new_momentum, second = update_momentum(gradients, momentum, owner_table, other, rank)
    arrived_first, second = lax.optimization_barrier((arrived_first, second))
    arrived_second = exchange(second)
    owned, back_first = orthogonalize(0, other, arrived_first, row_size, col_size)
    low = [back_first[0]] + [
        swap(back_first[k], k * col_size, devices) for k in range(1, LOW)
    ]
    high = restage(low)
    high, arrived_second = lax.optimization_barrier((high, arrived_second))
    returned_first = [high[0]] + [
        swap(high[r * width + c], r * LOW * col_size + c, devices)
        for r in range(row_size // LOW)
        for c in range(width)
        if r or c
    ]
    owned, back_second = orthogonalize(1, other, arrived_second, row_size, col_size, owned)
    returned_first, back_second = lax.optimization_barrier((returned_first, back_second))
    returned_second = exchange(back_second[0], halves)
    update = unpack(owner_table, other, rank, returned_first, returned_second, col_size)
    return (new_momentum, update, owned)


def solution(mesh):
    return jax.shard_map(
        on_device,
        mesh=mesh,
        in_specs=(P(None, "dp", "owner"), P(None, "dp", "owner"), P()),
        out_specs=(P(None, "dp", "owner"), P(None, "dp", "owner"), P(("dp", "owner"), None, None)),
        check_vma=False,
    )
```

```python
import functools
import math

import jax
import jax.numpy as jnp
from jax import lax
from jax.experimental import pallas as pl
from jax.experimental.pallas import tpu as pltpu
from jax.sharding import PartitionSpec as P

ITERS = 2
CAP = 2
HALVES = 2
TILES = 2
LOW = 4

coef_a = 3.4445
coef_b = -4.775
coef_c = 2.0315
momentum_beta = 0.95
epsilon = 1e-07

AXES = ("dp", "owner")
MIB = 1024 * 1024
PARAMS = pltpu.CompilerParams(vmem_limit_bytes=24 * MIB)
PACK_PARAMS = pltpu.CompilerParams(vmem_limit_bytes=60 * MIB)
SMEM = pl.BlockSpec(memory_space=pltpu.SMEM)


def round_up(value, multiple):
    return -(-value // multiple) * multiple


def whole(shape):
    return pl.BlockSpec(shape, lambda *_: (0,) * len(shape))


def nesterov_of(grad_ref, momentum_ref, j):
    grad = grad_ref[j].astype(jnp.float32)
    new = momentum_beta * momentum_ref[j] + grad
    return new, (grad + momentum_beta * new).astype(jnp.bfloat16)


def store_slot(slot, plan, i, owner, nesterov, slot_ref):
    other_ref, rank_ref = plan

    @pl.when(rank_ref[i] == slot)
    def _():
        block = nesterov()
        slot_ref[owner] = block
        slot_ref[other_ref[owner]] = block


def make_plan(col_size, owner_ref, other_ref, rank_ref, count_ref, list_ref):
    devices, mats = other_ref.shape[0], rank_ref.shape[0]

    def clear(d, _):
        count_ref[d] = 0
        return 0

    lax.fori_loop(0, devices, clear, 0, unroll=8)

    def rank_matrix(i, _):
        owner = owner_ref[i]
        rank = count_ref[owner]
        rank_ref[i] = rank
        count_ref[owner] = rank + 1
        return 0

    lax.fori_loop(0, mats, rank_matrix, 0, unroll=8)

    def list_device(d, found):
        owns = jnp.minimum(count_ref[d], 1)
        half = (d % col_size) // (col_size // HALVES)
        row = 2 * jnp.where(owns == 1, half, 1 - half) + owns
        place = found[0]
        for k in range(1, 2 * HALVES):
            place = jnp.where(row == k, found[k], place)
        list_ref[row * devices + place] = d
        return tuple(n + jnp.where(row == k, 1, 0) for k, n in enumerate(found))

    found = lax.fori_loop(0, devices, list_device, (0,) * (2 * HALVES), unroll=8)
    for half in range(HALVES):

        def pair(k, _):
            idle = list_ref[2 * half * devices + k]
            other_ref[list_ref[(2 * half + 1) * devices + k]] = idle
            other_ref[idle] = idle
            return 0

        lax.fori_loop(0, found[2 * half + 1], pair, 0)


def pack_kernel(
    chunk, col_size, owner_ref, g_ref, m_ref, first_ref, other_ref, rank_ref,
    count_ref, list_ref, g_s, m_s, sems,
):
    mats = rank_ref.shape[0]

    def loads(k):
        span = pl.ds(k * chunk, chunk)
        return (
            pltpu.make_async_copy(g_ref.at[span], g_s.at[span], sems.at[0, k]),
            pltpu.make_async_copy(m_ref.at[span], m_s.at[span], sems.at[1, k]),
        )

    for k in range(mats // chunk):
        for load in loads(k):
            load.start()
    make_plan(col_size, owner_ref, other_ref, rank_ref, count_ref, list_ref)
    for k in range(mats // chunk):
        for load in loads(k):
            load.wait()
        for i in range(k * chunk, (k + 1) * chunk):
            store_slot(
                0, (other_ref, rank_ref), i, owner_ref[i],
                lambda: nesterov_of(g_s, m_s, i)[1], first_ref,
            )


def pack(gradients, momentum, owner_table, devices, col_size):
    mats, rows, cols = gradients.shape
    chunk = 8
    anywhere = pl.BlockSpec(memory_space=pl.ANY)
    return pl.pallas_call(
        functools.partial(pack_kernel, chunk, col_size),
        grid_spec=pltpu.PrefetchScalarGridSpec(
            num_scalar_prefetch=1,
            grid=(1,),
            in_specs=[anywhere, anywhere],
            out_specs=[whole((devices, rows, cols)), SMEM, SMEM],
            scratch_shapes=[
                pltpu.SMEM((devices,), jnp.int32),
                pltpu.SMEM((2 * HALVES * devices,), jnp.int32),
                pltpu.VMEM(gradients.shape, gradients.dtype),
                pltpu.VMEM(momentum.shape, momentum.dtype),
                pltpu.SemaphoreType.DMA((2, mats // chunk)),
            ],
        ),
        out_shape=[
            jax.ShapeDtypeStruct((devices, rows, cols), jnp.bfloat16),
            jax.ShapeDtypeStruct((devices,), jnp.int32),
            jax.ShapeDtypeStruct((mats,), jnp.int32),
        ],
        compiler_params=PACK_PARAMS,
        cost_estimate=pl.CostEstimate(
            flops=4 * mats * rows * cols, bytes_accessed=8 * mats * rows * cols, transcendentals=0
        ),
        name="pack",
    )(owner_table, gradients, momentum)


def momentum_kernel(chunk, owner_ref, other_ref, rank_ref, g_ref, m_ref, nm_ref, second_ref):
    step = pl.program_id(0)
    for j in range(chunk):
        i = step * chunk + j
        new, nesterov = nesterov_of(g_ref, m_ref, j)
        nm_ref[j] = new
        store_slot(1, (other_ref, rank_ref), i, owner_ref[i], lambda: nesterov, second_ref)


def update_momentum(gradients, momentum, owner_table, other, rank):
    mats, rows, cols = gradients.shape
    devices = other.shape[0]
    chunk = 8
    block = pl.BlockSpec((chunk, rows, cols), lambda i, *_: (i, 0, 0))
    return pl.pallas_call(
        functools.partial(momentum_kernel, chunk),
        grid_spec=pltpu.PrefetchScalarGridSpec(
            num_scalar_prefetch=3,
            grid=(mats // chunk,),
            in_specs=[block, block],
            out_specs=[block, whole((devices, rows, cols))],
        ),
        out_shape=[
            jax.ShapeDtypeStruct(momentum.shape, jnp.float32),
            jax.ShapeDtypeStruct((devices, rows, cols), jnp.bfloat16),
        ],
        compiler_params=PARAMS,
        cost_estimate=pl.CostEstimate(
            flops=4 * mats * rows * cols, bytes_accessed=12 * mats * rows * cols, transcendentals=0
        ),
        name="update_momentum",
    )(owner_table, other, rank, gradients, momentum)


def matmul(lhs, rhs, rhs_dim):
    return lax.dot_general(
        lhs, rhs, (((1,), (rhs_dim,)), ((), ())), preferred_element_type=jnp.float32
    )


def sum_rows(values):
    rows, cols = values.shape
    if rows % 8:
        return jnp.sum(values, axis=0, keepdims=True)
    return jnp.sum(values.reshape(rows // 8, 8, cols), axis=0)


def gather_blocks(x_ref, x_s, row_size, col_size):
    _, rows, cols = x_ref.shape
    height = rows * row_size
    total = 0.0
    for r in range(row_size):
        for c in range(col_size):
            block = x_ref[r * col_size + c]
            x_s[r * rows : (r + 1) * rows, c * cols : (c + 1) * cols] = block
            wide = block.astype(jnp.float32)
            total = total + sum_rows(wide * wide)
    x_s[height:, :] = jnp.zeros((x_s.shape[0] - height, x_s.shape[1]), x_s.dtype)
    return 1.0 / (jnp.sqrt(jnp.sum(total, keepdims=True)) + epsilon)


def newton_schulz(height, inverse, x_s, y_s, gram_s, write):
    padded, width = x_s.shape
    tile = height // TILES
    update_scale = 0.2 * math.sqrt(max(height, width))
    for ref in (y_s, gram_s):
        ref[height:, :] = jnp.zeros((padded - height, ref.shape[1]), ref.dtype)
    for iteration in range(ITERS):
        src = x_s if iteration == 0 else y_s
        for t in range(TILES):
            span = slice(t * tile, (t + 1) * tile)
            gram = matmul(src[span, :], src[...], 1)
            if iteration == 0:
                gram = gram * (inverse * inverse)
            gram_s[span, :] = gram.astype(jnp.bfloat16)
        for t in range(TILES):
            span = slice(t * tile, (t + 1) * tile)
            square = matmul(gram_s[span, :], gram_s[...], 0)
            mixing = coef_b * gram_s[span, :].astype(jnp.float32) + coef_c * square
            combined = coef_a * src[span, :].astype(jnp.float32) + matmul(
                mixing.astype(jnp.bfloat16), src[...], 0
            )
            if iteration == 0:
                combined = combined * inverse
            if iteration + 1 < ITERS:
                y_s[span, :] = combined.astype(jnp.bfloat16)
            else:
                write(t, (update_scale * combined).astype(jnp.bfloat16))


def stage_place(row_offset, col_offset, row_size, width):
    high = row_offset // LOW * width + col_offset
    return row_offset % LOW * (row_size // LOW * width) + high


def ortho_kernel(row_size, col_size, slot, other_ref, x_ref, *refs):
    _, rows, cols = x_ref.shape
    width = col_size // HALVES
    places = row_size * width
    height = rows * row_size
    tile = height // TILES
    if slot:
        owned_ref, back_ref, x_s, y_s, gram_s, out_s, sems = refs[1:]
    else:
        owned_ref, low_refs = refs[0], refs[1 : 1 + LOW]
        x_s, y_s, gram_s, out_s, sems, back_ref = refs[1 + LOW :]
    row, col = lax.axis_index("dp"), lax.axis_index("owner")
    me = row * col_size + col
    owns = other_ref[me] != me
    low = col < width
    inverse = gather_blocks(x_ref, x_s, row_size, col_size)

    def copy_out(t):
        span = pl.ds(t * tile, tile)
        return pltpu.make_async_copy(out_s.at[span], owned_ref.at[slot, span], sems.at[t])

    def write(t, result):
        out_s[t * tile : (t + 1) * tile, :] = jnp.where(owns, result, jnp.zeros_like(result))
        copy_out(t).start()
        for j in range(row_size // TILES):
            block = result[j * rows : (j + 1) * rows, :]
            r = t * (row_size // TILES) + j
            for c in range(width):
                if slot:
                    place = r * width + c
                else:
                    place = stage_place(r ^ row, c ^ (col % width), row_size, width)
                back_ref[place] = jnp.where(
                    low,
                    block[:, c * cols : (c + 1) * cols],
                    block[:, (c + width) * cols : (c + width + 1) * cols],
                )

    newton_schulz(height, inverse, x_s, y_s, gram_s, write)
    if not slot:
        for k in range(LOW):
            low_refs[k][...] = back_ref[k * places // LOW : (k + 1) * places // LOW]
    for t in range(TILES):
        copy_out(t).wait()


def orthogonalize(slot, other, arrived, row_size, col_size, owned=None):
    devices, rows, cols = arrived.shape
    height, width = rows * row_size, cols * col_size
    padded = round_up(height, 256)
    places = devices // HALVES
    anywhere = pl.BlockSpec(memory_space=pl.ANY)
    in_specs, operands = [SMEM, whole(arrived.shape)], [other, arrived]
    scratch_shapes = [
        pltpu.VMEM((padded, width), jnp.bfloat16),
        pltpu.VMEM((padded, width), jnp.bfloat16),
        pltpu.VMEM((padded, padded), jnp.bfloat16),
        pltpu.VMEM((height, width), jnp.bfloat16),
        pltpu.SemaphoreType.DMA((TILES,)),
    ]
    if slot:
        in_specs.append(anywhere)
        operands.append(owned)
        back = [(places, rows, cols)]
    else:
        back = [(places // LOW, rows, cols)] * LOW
        scratch_shapes.append(pltpu.VMEM((places, rows, cols), jnp.bfloat16))
    owned, *back = pl.pallas_call(
        functools.partial(ortho_kernel, row_size, col_size, slot),
        grid=(1,),
        in_specs=in_specs,
        out_specs=[anywhere] + [whole(shape) for shape in back],
        out_shape=[jax.ShapeDtypeStruct((CAP, height, width), jnp.bfloat16)]
        + [jax.ShapeDtypeStruct(shape, jnp.bfloat16) for shape in back],
        scratch_shapes=scratch_shapes,
        input_output_aliases={2: 0} if slot else {},
        compiler_params=PARAMS,
        cost_estimate=pl.CostEstimate(
            flops=2 * ITERS * padded * padded * (2 * width + padded),
            bytes_accessed=6 * padded * width,
            transcendentals=0,
        ),
        name="orthogonalize",
    )(*operands)
    return owned, back


def restage_kernel(*refs):
    low_refs, high_refs = refs[:LOW], refs[LOW:]
    for h, high_ref in enumerate(high_refs):
        for k, low_ref in enumerate(low_refs):
            high_ref[k] = low_ref[h]


def restage(blocks):
    highs, rows, cols = blocks[0].shape
    out = jax.ShapeDtypeStruct((LOW, rows, cols), blocks[0].dtype)
    return pl.pallas_call(
        restage_kernel,
        grid=(1,),
        in_specs=[whole(blocks[0].shape)] * LOW,
        out_specs=[whole(out.shape)] * highs,
        out_shape=[out] * highs,
        compiler_params=PARAMS,
        cost_estimate=pl.CostEstimate(
            flops=0, bytes_accessed=4 * LOW * highs * rows * cols, transcendentals=0
        ),
        name="restage",
    )(*blocks)


def unpack_kernel(chunk, col_size, owner_ref, other_ref, rank_ref, *refs):
    width = col_size // HALVES
    high_refs, second_ref, update_ref, first_s, update_s, sems = refs[:-5], *refs[-5:]
    row, col = lax.axis_index("dp"), lax.axis_index("owner")
    half = col // width
    for h, high_ref in enumerate(high_refs):
        first_s[h * LOW : (h + 1) * LOW] = high_ref[...]

    def copy_out(k):
        span = pl.ds(k * chunk, chunk)
        return pltpu.make_async_copy(update_s.at[span], update_ref.at[span], sems.at[k])

    chunks = update_s.shape[0] // chunk
    for i in range(chunks * chunk):
        owner = owner_ref[i]
        host = jnp.where((owner % col_size) // width == half, owner, other_ref[owner])
        host_row, host_col = host // col_size, host % width
        offset = host_row ^ row
        high = offset // LOW * width + (host_col ^ (col % width))

        @pl.when(rank_ref[i] == 0)
        def _():
            update_s[i] = first_s[high * LOW + offset % LOW]

        @pl.when(rank_ref[i] == 1)
        def _():
            update_s[i] = second_ref[host_row * width + host_col]

        if i % chunk == chunk - 1:
            copy_out(i // chunk).start()
    for k in range(chunks):
        copy_out(k).wait()


def unpack(owner_table, other, rank, first, second, col_size):
    _, rows, cols = second.shape
    mats = owner_table.shape[0]
    chunk = 8
    return pl.pallas_call(
        functools.partial(unpack_kernel, chunk, col_size),
        grid_spec=pltpu.PrefetchScalarGridSpec(
            num_scalar_prefetch=3,
            grid=(1,),
            in_specs=[whole(first[0].shape)] * len(first) + [whole(second.shape)],
            out_specs=pl.BlockSpec(memory_space=pl.ANY),
            scratch_shapes=[
                pltpu.VMEM(second.shape, jnp.bfloat16),
                pltpu.VMEM((mats, rows, cols), jnp.bfloat16),
                pltpu.SemaphoreType.DMA((mats // chunk,)),
            ],
        ),
        out_shape=jax.ShapeDtypeStruct((mats, rows, cols), jnp.bfloat16),
        compiler_params=PARAMS,
        cost_estimate=pl.CostEstimate(
            flops=0, bytes_accessed=4 * mats * rows * cols, transcendentals=0
        ),
        name="unpack",
    )(owner_table, other, rank, *first, second)


def exchange(blocks, groups=None):
    return lax.all_to_all(
        blocks, AXES, split_axis=0, concat_axis=0, tiled=True, axis_index_groups=groups
    )


def swap(block, offset, devices):
    return lax.ppermute(block, AXES, [(d, d ^ offset) for d in range(devices)])


def on_device(gradients, momentum, owner_table):
    row_size = lax.axis_size("dp")
    col_size = lax.axis_size("owner")
    devices = row_size * col_size
    width = col_size // HALVES
    halves = [
        [r * col_size + half * width + c for r in range(row_size) for c in range(width)]
        for half in range(HALVES)
    ]
    first, other, rank = pack(gradients, momentum, owner_table, devices, col_size)
    arrived_first = exchange(first)
    new_momentum, second = update_momentum(gradients, momentum, owner_table, other, rank)
    arrived_first, second = lax.optimization_barrier((arrived_first, second))
    arrived_second = exchange(second)
    owned, back_first = orthogonalize(0, other, arrived_first, row_size, col_size)
    low = [back_first[0]] + [
        swap(back_first[k], k * col_size, devices) for k in range(1, LOW)
    ]
    high = restage(low)
    _, arrived_second = lax.optimization_barrier((high, arrived_second))
    returned_first = [high[0]] + [
        swap(high[r * width + c], r * LOW * col_size + c, devices)
        for r in range(row_size // LOW)
        for c in range(width)
        if r or c
    ]
    owned, back_second = orthogonalize(1, other, arrived_second, row_size, col_size, owned)
    returned_first, back_second = lax.optimization_barrier((returned_first, back_second))
    returned_second = exchange(back_second[0], halves)
    update = unpack(owner_table, other, rank, returned_first, returned_second, col_size)
    return (new_momentum, update, owned)


def solution(mesh):
    return jax.shard_map(
        on_device,
        mesh=mesh,
        in_specs=(P(None, "dp", "owner"), P(None, "dp", "owner"), P()),
        out_specs=(P(None, "dp", "owner"), P(None, "dp", "owner"), P(("dp", "owner"), None, None)),
        check_vma=False,
    )
```

```python
import functools
import math

import jax
import jax.numpy as jnp
from jax import lax
from jax.experimental import pallas as pl
from jax.experimental.pallas import tpu as pltpu
from jax.sharding import PartitionSpec as P

ITERS = 2
CAP = 2
HALVES = 2
TILES = 2
LOW = 4

coef_a = 3.4445
coef_b = -4.775
coef_c = 2.0315
momentum_beta = 0.95
epsilon = 1e-07

AXES = ("dp", "owner")
FORWARD_AXES = ("owner", "dp")
MIB = 1024 * 1024
PARAMS = pltpu.CompilerParams(vmem_limit_bytes=24 * MIB)
PACK_PARAMS = pltpu.CompilerParams(vmem_limit_bytes=60 * MIB)
SMEM = pl.BlockSpec(memory_space=pltpu.SMEM)


def round_up(value, multiple):
    return -(-value // multiple) * multiple


def whole(shape):
    return pl.BlockSpec(shape, lambda *_: (0,) * len(shape))


def nesterov_of(grad_ref, momentum_ref, j):
    grad = grad_ref[j].astype(jnp.float32)
    new = momentum_beta * momentum_ref[j] + grad
    return new, (grad + momentum_beta * new).astype(jnp.bfloat16)


def store_slot(slot, plan, i, owner, nesterov, slot_ref, col_size):
    other_ref, rank_ref = plan
    row_size = slot_ref.shape[0] // col_size

    def place(d):
        return d % col_size * row_size + d // col_size

    @pl.when(rank_ref[i] == slot)
    def _():
        block = nesterov()
        slot_ref[place(owner)] = block
        slot_ref[place(other_ref[owner])] = block


def make_plan(col_size, owner_ref, other_ref, rank_ref, count_ref, list_ref):
    devices, mats = other_ref.shape[0], rank_ref.shape[0]

    def clear(d, _):
        count_ref[d] = 0
        return 0

    lax.fori_loop(0, devices, clear, 0, unroll=8)

    def rank_matrix(i, _):
        owner = owner_ref[i]
        rank = count_ref[owner]
        rank_ref[i] = rank
        count_ref[owner] = rank + 1
        return 0

    lax.fori_loop(0, mats, rank_matrix, 0, unroll=8)

    def list_device(d, found):
        owns = jnp.minimum(count_ref[d], 1)
        half = (d % col_size) // (col_size // HALVES)
        row = 2 * jnp.where(owns == 1, half, 1 - half) + owns
        place = found[0]
        for k in range(1, 2 * HALVES):
            place = jnp.where(row == k, found[k], place)
        list_ref[row * devices + place] = d
        return tuple(n + jnp.where(row == k, 1, 0) for k, n in enumerate(found))

    found = lax.fori_loop(0, devices, list_device, (0,) * (2 * HALVES), unroll=8)
    for half in range(HALVES):

        def pair(k, _):
            idle = list_ref[2 * half * devices + k]
            other_ref[list_ref[(2 * half + 1) * devices + k]] = idle
            other_ref[idle] = idle
            return 0

        lax.fori_loop(0, found[2 * half + 1], pair, 0)


def pack_kernel(
    chunk, col_size, owner_ref, g_ref, m_ref, first_ref, other_ref, rank_ref,
    count_ref, list_ref, g_s, m_s, sems,
):
    mats = rank_ref.shape[0]

    def loads(k):
        span = pl.ds(k * chunk, chunk)
        return (
            pltpu.make_async_copy(g_ref.at[span], g_s.at[span], sems.at[0, k]),
            pltpu.make_async_copy(m_ref.at[span], m_s.at[span], sems.at[1, k]),
        )

    for k in range(mats // chunk):
        for load in loads(k):
            load.start()
    make_plan(col_size, owner_ref, other_ref, rank_ref, count_ref, list_ref)
    for k in range(mats // chunk):
        for load in loads(k):
            load.wait()
        for i in range(k * chunk, (k + 1) * chunk):
            store_slot(
                0, (other_ref, rank_ref), i, owner_ref[i],
                lambda: nesterov_of(g_s, m_s, i)[1], first_ref, col_size,
            )


def pack(gradients, momentum, owner_table, devices, col_size):
    mats, rows, cols = gradients.shape
    chunk = 8
    anywhere = pl.BlockSpec(memory_space=pl.ANY)
    return pl.pallas_call(
        functools.partial(pack_kernel, chunk, col_size),
        grid_spec=pltpu.PrefetchScalarGridSpec(
            num_scalar_prefetch=1,
            grid=(1,),
            in_specs=[anywhere, anywhere],
            out_specs=[whole((devices, rows, cols)), SMEM, SMEM],
            scratch_shapes=[
                pltpu.SMEM((devices,), jnp.int32),
                pltpu.SMEM((2 * HALVES * devices,), jnp.int32),
                pltpu.VMEM(gradients.shape, gradients.dtype),
                pltpu.VMEM(momentum.shape, momentum.dtype),
                pltpu.SemaphoreType.DMA((2, mats // chunk)),
            ],
        ),
        out_shape=[
            jax.ShapeDtypeStruct((devices, rows, cols), jnp.bfloat16),
            jax.ShapeDtypeStruct((devices,), jnp.int32),
            jax.ShapeDtypeStruct((mats,), jnp.int32),
        ],
        compiler_params=PACK_PARAMS,
        cost_estimate=pl.CostEstimate(
            flops=4 * mats * rows * cols, bytes_accessed=8 * mats * rows * cols, transcendentals=0
        ),
        name="pack",
    )(owner_table, gradients, momentum)


def momentum_kernel(
    chunk, col_size, owner_ref, other_ref, rank_ref, g_ref, m_ref, nm_ref, second_ref, place_ref
):
    step = pl.program_id(0)
    width = col_size // HALVES
    row, col = lax.axis_index("dp"), lax.axis_index("owner")
    for j in range(chunk):
        i = step * chunk + j
        new, nesterov = nesterov_of(g_ref, m_ref, j)
        nm_ref[j] = new
        owner = owner_ref[i]
        plan = other_ref, rank_ref
        store_slot(1, plan, i, owner, lambda: nesterov, second_ref, col_size)

        near = (owner % col_size) // width == col // width
        host = jnp.where(near, owner, other_ref[owner])
        host_row, host_col = host // col_size, host % width
        offset = host_row ^ row
        high = offset // LOW * width + (host_col ^ (col % width))
        place_ref[i] = jnp.where(
            rank_ref[i] == 0,
            high * LOW + offset % LOW,
            second_ref.shape[0] // HALVES + host_row * width + host_col,
        )


def update_momentum(gradients, momentum, owner_table, other, rank, col_size):
    mats, rows, cols = gradients.shape
    devices = other.shape[0]
    chunk = 8
    block = pl.BlockSpec((chunk, rows, cols), lambda i, *_: (i, 0, 0))
    return pl.pallas_call(
        functools.partial(momentum_kernel, chunk, col_size),
        grid_spec=pltpu.PrefetchScalarGridSpec(
            num_scalar_prefetch=3,
            grid=(mats // chunk,),
            in_specs=[block, block],
            out_specs=[block, whole((devices, rows, cols)), SMEM],
        ),
        out_shape=[
            jax.ShapeDtypeStruct(momentum.shape, jnp.float32),
            jax.ShapeDtypeStruct((devices, rows, cols), jnp.bfloat16),
            jax.ShapeDtypeStruct((mats,), jnp.int32),
        ],
        compiler_params=PARAMS,
        cost_estimate=pl.CostEstimate(
            flops=4 * mats * rows * cols, bytes_accessed=12 * mats * rows * cols, transcendentals=0
        ),
        name="update_momentum",
    )(owner_table, other, rank, gradients, momentum)


def matmul(lhs, rhs, rhs_dim):
    return lax.dot_general(
        lhs, rhs, (((1,), (rhs_dim,)), ((), ())), preferred_element_type=jnp.float32
    )


def sum_rows(values):
    rows, cols = values.shape
    if rows % 8:
        return jnp.sum(values, axis=0, keepdims=True)
    return jnp.sum(values.reshape(rows // 8, 8, cols), axis=0)


def gather_blocks(x_ref, x_s, row_size, col_size):
    _, rows, cols = x_ref.shape
    height = rows * row_size
    total = 0.0
    for r in range(row_size):
        for c in range(col_size):
            block = x_ref[c * row_size + r]
            x_s[r * rows : (r + 1) * rows, c * cols : (c + 1) * cols] = block
            wide = block.astype(jnp.float32)
            total = total + sum_rows(wide * wide)
    x_s[height:, :] = jnp.zeros((x_s.shape[0] - height, x_s.shape[1]), x_s.dtype)
    return 1.0 / (jnp.sqrt(jnp.sum(total, keepdims=True)) + epsilon)


def newton_schulz(height, inverse, x_s, y_s, gram_s, write):
    padded, width = x_s.shape
    tile = height // TILES
    update_scale = 0.2 * math.sqrt(max(height, width))
    for ref in (y_s, gram_s):
        ref[height:, :] = jnp.zeros((padded - height, ref.shape[1]), ref.dtype)
    for iteration in range(ITERS):
        src = x_s if iteration == 0 else y_s
        for t in range(TILES):
            span = slice(t * tile, (t + 1) * tile)
            gram = matmul(src[span, :], src[...], 1)
            if iteration == 0:
                gram = gram * (inverse * inverse)
            gram_s[span, :] = gram.astype(jnp.bfloat16)
        for t in range(TILES):
            span = slice(t * tile, (t + 1) * tile)
            square = matmul(gram_s[span, :], gram_s[...], 0)
            mixing = coef_b * gram_s[span, :].astype(jnp.float32) + coef_c * square
            combined = coef_a * src[span, :].astype(jnp.float32) + matmul(
                mixing.astype(jnp.bfloat16), src[...], 0
            )
            if iteration == 0:
                combined = combined * inverse
            if iteration + 1 < ITERS:
                y_s[span, :] = combined.astype(jnp.bfloat16)
            else:
                write(t, (update_scale * combined).astype(jnp.bfloat16))


def stage_place(row_offset, col_offset, row_size, width):
    high = row_offset // LOW * width + col_offset
    return row_offset % LOW * (row_size // LOW * width) + high


def ortho_kernel(row_size, col_size, slot, other_ref, x_ref, *refs):
    _, rows, cols = x_ref.shape
    width = col_size // HALVES
    places = row_size * width
    height = rows * row_size
    tile = height // TILES
    if slot:
        owned_ref, back_ref, x_s, y_s, gram_s, out_s, sems = refs[1:]
    else:
        owned_ref, low_refs = refs[0], refs[1 : 1 + LOW]
        x_s, y_s, gram_s, out_s, sems, back_ref = refs[1 + LOW :]
    row, col = lax.axis_index("dp"), lax.axis_index("owner")
    me = row * col_size + col
    owns = other_ref[me] != me
    low = col < width
    inverse = gather_blocks(x_ref, x_s, row_size, col_size)

    def copy_out(t):
        span = pl.ds(t * tile, tile)
        return pltpu.make_async_copy(out_s.at[span], owned_ref.at[slot, span], sems.at[t])

    def write(t, result):
        out_s[t * tile : (t + 1) * tile, :] = jnp.where(owns, result, jnp.zeros_like(result))
        copy_out(t).start()
        for j in range(row_size // TILES):
            block = result[j * rows : (j + 1) * rows, :]
            r = t * (row_size // TILES) + j
            for c in range(width):
                if slot:
                    place = r * width + c
                else:
                    place = stage_place(r ^ row, c ^ (col % width), row_size, width)
                back_ref[place] = jnp.where(
                    low,
                    block[:, c * cols : (c + 1) * cols],
                    block[:, (c + width) * cols : (c + width + 1) * cols],
                )

    newton_schulz(height, inverse, x_s, y_s, gram_s, write)
    if not slot:
        for k in range(LOW):
            low_refs[k][...] = back_ref[k * places // LOW : (k + 1) * places // LOW]
    for t in range(TILES):
        copy_out(t).wait()


def orthogonalize(slot, other, arrived, row_size, col_size, owned=None):
    devices, rows, cols = arrived.shape
    height, width = rows * row_size, cols * col_size
    padded = round_up(height, 256)
    places = devices // HALVES
    anywhere = pl.BlockSpec(memory_space=pl.ANY)
    in_specs, operands = [SMEM, whole(arrived.shape)], [other, arrived]
    scratch_shapes = [
        pltpu.VMEM((padded, width), jnp.bfloat16),
        pltpu.VMEM((padded, width), jnp.bfloat16),
        pltpu.VMEM((padded, padded), jnp.bfloat16),
        pltpu.VMEM((height, width), jnp.bfloat16),
        pltpu.SemaphoreType.DMA((TILES,)),
    ]
    if slot:
        in_specs.append(anywhere)
        operands.append(owned)
        back = [(places, rows, cols)]
    else:
        back = [(places // LOW, rows, cols)] * LOW
        scratch_shapes.append(pltpu.VMEM((places, rows, cols), jnp.bfloat16))
    owned, *back = pl.pallas_call(
        functools.partial(ortho_kernel, row_size, col_size, slot),
        grid=(1,),
        in_specs=in_specs,
        out_specs=[anywhere] + [whole(shape) for shape in back],
        out_shape=[jax.ShapeDtypeStruct((CAP, height, width), jnp.bfloat16)]
        + [jax.ShapeDtypeStruct(shape, jnp.bfloat16) for shape in back],
        scratch_shapes=scratch_shapes,
        input_output_aliases={2: 0} if slot else {},
        compiler_params=PARAMS,
        cost_estimate=pl.CostEstimate(
            flops=2 * ITERS * padded * padded * (2 * width + padded),
            bytes_accessed=6 * padded * width,
            transcendentals=0,
        ),
        name="orthogonalize",
    )(*operands)
    return owned, back


def restage_kernel(*refs):
    low_refs, high_refs = refs[:LOW], refs[LOW:]
    for h, high_ref in enumerate(high_refs):
        for k, low_ref in enumerate(low_refs):
            high_ref[k] = low_ref[h]


def restage(blocks):
    highs, rows, cols = blocks[0].shape
    out = jax.ShapeDtypeStruct((LOW, rows, cols), blocks[0].dtype)
    return pl.pallas_call(
        restage_kernel,
        grid=(1,),
        in_specs=[whole(blocks[0].shape)] * LOW,
        out_specs=[whole(out.shape)] * highs,
        out_shape=[out] * highs,
        compiler_params=PARAMS,
        cost_estimate=pl.CostEstimate(
            flops=0, bytes_accessed=4 * LOW * highs * rows * cols, transcendentals=0
        ),
        name="restage",
    )(*blocks)


def unpack_kernel(chunk, place_ref, *refs):
    high_refs, second_ref, update_ref, back_s, update_s, sems = refs[:-5], *refs[-5:]
    for h, high_ref in enumerate(high_refs):
        back_s[h * LOW : (h + 1) * LOW] = high_ref[...]
    back_s[second_ref.shape[0] :] = second_ref[...]

    def copy_out(k):
        span = pl.ds(k * chunk, chunk)
        return pltpu.make_async_copy(update_s.at[span], update_ref.at[span], sems.at[k])

    chunks = update_s.shape[0] // chunk
    for k in range(chunks):
        for i in range(k * chunk, (k + 1) * chunk):
            update_s[i] = back_s[place_ref[i]]
        copy_out(k).start()
    for k in range(chunks):
        copy_out(k).wait()


def unpack(place, first, second):
    places, rows, cols = second.shape
    mats = place.shape[0]
    chunk = 8
    return pl.pallas_call(
        functools.partial(unpack_kernel, chunk),
        grid_spec=pltpu.PrefetchScalarGridSpec(
            num_scalar_prefetch=1,
            grid=(1,),
            in_specs=[whole(first[0].shape)] * len(first) + [whole(second.shape)],
            out_specs=pl.BlockSpec(memory_space=pl.ANY),
            scratch_shapes=[
                pltpu.VMEM((CAP * places, rows, cols), jnp.bfloat16),
                pltpu.VMEM((mats, rows, cols), jnp.bfloat16),
                pltpu.SemaphoreType.DMA((mats // chunk,)),
            ],
        ),
        out_shape=jax.ShapeDtypeStruct((mats, rows, cols), jnp.bfloat16),
        compiler_params=PARAMS,
        cost_estimate=pl.CostEstimate(
            flops=0, bytes_accessed=4 * mats * rows * cols, transcendentals=0
        ),
        name="unpack",
    )(place, *first, second)


def exchange(blocks, axes, groups=None):
    return lax.all_to_all(
        blocks, axes, split_axis=0, concat_axis=0, tiled=True, axis_index_groups=groups
    )


def swap(block, offset, devices):
    return lax.ppermute(block, AXES, [(d, d ^ offset) for d in range(devices)])


def on_device(gradients, momentum, owner_table):
    row_size = lax.axis_size("dp")
    col_size = lax.axis_size("owner")
    devices = row_size * col_size
    width = col_size // HALVES
    halves = [
        [r * col_size + half * width + c for r in range(row_size) for c in range(width)]
        for half in range(HALVES)
    ]
    first, other, rank = pack(gradients, momentum, owner_table, devices, col_size)
    arrived_first = exchange(first, FORWARD_AXES)
    new_momentum, second, place = update_momentum(
        gradients, momentum, owner_table, other, rank, col_size
    )
    arrived_first, second = lax.optimization_barrier((arrived_first, second))
    arrived_second = exchange(second, FORWARD_AXES)
    owned, back_first = orthogonalize(0, other, arrived_first, row_size, col_size)
    low = [back_first[0]] + [
        swap(back_first[k], k * col_size, devices) for k in range(1, LOW)
    ]
    high = restage(low)
    _, arrived_second = lax.optimization_barrier((high, arrived_second))
    returned_first = [high[0]] + [
        swap(high[r * width + c], r * LOW * col_size + c, devices)
        for r in range(row_size // LOW)
        for c in range(width)
        if r or c
    ]
    owned, back_second = orthogonalize(1, other, arrived_second, row_size, col_size, owned)
    returned_first, back_second = lax.optimization_barrier((returned_first, back_second))
    returned_second = exchange(back_second[0], AXES, halves)
    update = unpack(place, returned_first, returned_second)
    return (new_momentum, update, owned)


def solution(mesh):
    return jax.shard_map(
        on_device,
        mesh=mesh,
        in_specs=(P(None, "dp", "owner"), P(None, "dp", "owner"), P()),
        out_specs=(P(None, "dp", "owner"), P(None, "dp", "owner"), P(("dp", "owner"), None, None)),
        check_vma=False,
    )
```

```python
import functools
import math

import jax
import jax.numpy as jnp
from jax import lax
from jax.experimental import pallas as pl
from jax.experimental.pallas import tpu as pltpu
from jax.sharding import PartitionSpec as P

ITERS = 2
CAP = 2
HALVES = 2
TILES = 2
LOW = 4

coef_a = 3.4445
coef_b = -4.775
coef_c = 2.0315
momentum_beta = 0.95
epsilon = 1e-07

AXES = ("dp", "owner")
MIB = 1024 * 1024
PARAMS = pltpu.CompilerParams(vmem_limit_bytes=24 * MIB)
PACK_PARAMS = pltpu.CompilerParams(vmem_limit_bytes=60 * MIB)
SMEM = pl.BlockSpec(memory_space=pltpu.SMEM)
VMEM = pl.BlockSpec(memory_space=pltpu.VMEM)


def round_up(value, multiple):
    return -(-value // multiple) * multiple


def whole(shape):
    return pl.BlockSpec(shape, lambda *_: (0,) * len(shape))


def nesterov_of(grad_ref, momentum_ref, j):
    grad = grad_ref[j].astype(jnp.float32)
    new = momentum_beta * momentum_ref[j] + grad
    return new, (grad + momentum_beta * new).astype(jnp.bfloat16)


def store_slot(slot, plan, i, owner, nesterov, slot_ref):
    other_ref, rank_ref = plan

    @pl.when(rank_ref[i] == slot)
    def _():
        block = nesterov()
        slot_ref[owner] = block
        slot_ref[other_ref[owner]] = block


def make_plan(col_size, owner_ref, other_ref, rank_ref, count_ref, list_ref):
    devices, mats = other_ref.shape[0], rank_ref.shape[0]

    def clear(d, _):
        count_ref[d] = 0
        return 0

    lax.fori_loop(0, devices, clear, 0, unroll=8)

    def rank_matrix(i, _):
        owner = owner_ref[i]
        rank = count_ref[owner]
        rank_ref[i] = rank
        count_ref[owner] = rank + 1
        return 0

    lax.fori_loop(0, mats, rank_matrix, 0, unroll=8)

    def list_device(d, found):
        owns = jnp.minimum(count_ref[d], 1)
        half = (d % col_size) // (col_size // HALVES)
        row = 2 * jnp.where(owns == 1, half, 1 - half) + owns
        place = found[0]
        for k in range(1, 2 * HALVES):
            place = jnp.where(row == k, found[k], place)
        list_ref[row * devices + place] = d
        return tuple(n + jnp.where(row == k, 1, 0) for k, n in enumerate(found))

    found = lax.fori_loop(0, devices, list_device, (0,) * (2 * HALVES), unroll=8)
    for half in range(HALVES):

        def pair(k, _):
            idle = list_ref[2 * half * devices + k]
            other_ref[list_ref[(2 * half + 1) * devices + k]] = idle
            other_ref[idle] = idle
            return 0

        lax.fori_loop(0, found[2 * half + 1], pair, 0)


def pack_kernel(
    chunk, col_size, owner_ref, g_ref, m_ref, first_ref, other_ref, rank_ref,
    count_ref, list_ref, g_s, m_s, sems,
):
    mats = rank_ref.shape[0]

    def loads(k):
        span = pl.ds(k * chunk, chunk)
        return (
            pltpu.make_async_copy(g_ref.at[span], g_s.at[span], sems.at[0, k]),
            pltpu.make_async_copy(m_ref.at[span], m_s.at[span], sems.at[1, k]),
        )

    for k in range(mats // chunk):
        for load in loads(k):
            load.start()
    make_plan(col_size, owner_ref, other_ref, rank_ref, count_ref, list_ref)
    for k in range(mats // chunk):
        for load in loads(k):
            load.wait()
        for i in range(k * chunk, (k + 1) * chunk):
            store_slot(
                0, (other_ref, rank_ref), i, owner_ref[i],
                lambda: nesterov_of(g_s, m_s, i)[1], first_ref,
            )


def pack(gradients, momentum, owner_table, devices, col_size):
    mats, rows, cols = gradients.shape
    chunk = 8
    anywhere = pl.BlockSpec(memory_space=pl.ANY)
    return pl.pallas_call(
        functools.partial(pack_kernel, chunk, col_size),
        grid_spec=pltpu.PrefetchScalarGridSpec(
            num_scalar_prefetch=1,
            grid=(1,),
            in_specs=[anywhere, anywhere],
            out_specs=[whole((devices, rows, cols)), SMEM, SMEM],
            scratch_shapes=[
                pltpu.SMEM((devices,), jnp.int32),
                pltpu.SMEM((2 * HALVES * devices,), jnp.int32),
                pltpu.VMEM(gradients.shape, gradients.dtype),
                pltpu.VMEM(momentum.shape, momentum.dtype),
                pltpu.SemaphoreType.DMA((2, mats // chunk)),
            ],
        ),
        out_shape=[
            jax.ShapeDtypeStruct((devices, rows, cols), jnp.bfloat16),
            jax.ShapeDtypeStruct((devices,), jnp.int32),
            jax.ShapeDtypeStruct((mats,), jnp.int32),
        ],
        compiler_params=PACK_PARAMS,
        cost_estimate=pl.CostEstimate(
            flops=4 * mats * rows * cols, bytes_accessed=8 * mats * rows * cols, transcendentals=0
        ),
        name="pack",
    )(owner_table, gradients, momentum)


def momentum_kernel(
    chunk, col_size, owner_ref, other_ref, rank_ref, g_ref, m_ref, nm_ref, second_ref, place_ref
):
    step = pl.program_id(0)
    width = col_size // HALVES
    row, col = lax.axis_index("dp"), lax.axis_index("owner")
    for j in range(chunk):
        i = step * chunk + j
        new, nesterov = nesterov_of(g_ref, m_ref, j)
        nm_ref[j] = new
        owner = owner_ref[i]
        plan = other_ref, rank_ref
        store_slot(1, plan, i, owner, lambda: nesterov, second_ref)

        near = (owner % col_size) // width == col // width
        host = jnp.where(near, owner, other_ref[owner])
        host_row, host_col = host // col_size, host % width
        offset = host_row ^ row
        high = offset // LOW * width + (host_col ^ (col % width))
        place_ref[i] = jnp.where(
            rank_ref[i] == 0,
            high * LOW + offset % LOW,
            second_ref.shape[0] // HALVES + host_row * width + host_col,
        )


def update_momentum(gradients, momentum, owner_table, other, rank, col_size):
    mats, rows, cols = gradients.shape
    devices = other.shape[0]
    chunk = 8
    block = pl.BlockSpec((chunk, rows, cols), lambda i, *_: (i, 0, 0))
    return pl.pallas_call(
        functools.partial(momentum_kernel, chunk, col_size),
        grid_spec=pltpu.PrefetchScalarGridSpec(
            num_scalar_prefetch=3,
            grid=(mats // chunk,),
            in_specs=[block, block],
            out_specs=[block, whole((devices, rows, cols)), SMEM],
        ),
        out_shape=[
            jax.ShapeDtypeStruct(momentum.shape, jnp.float32),
            jax.ShapeDtypeStruct((devices, rows, cols), jnp.bfloat16),
            jax.ShapeDtypeStruct((mats,), jnp.int32),
        ],
        compiler_params=PARAMS,
        cost_estimate=pl.CostEstimate(
            flops=4 * mats * rows * cols, bytes_accessed=12 * mats * rows * cols, transcendentals=0
        ),
        name="update_momentum",
    )(owner_table, other, rank, gradients, momentum)


def matmul(lhs, rhs, rhs_dim):
    return lax.dot_general(
        lhs, rhs, (((1,), (rhs_dim,)), ((), ())), preferred_element_type=jnp.float32
    )


def sum_rows(values):
    rows, cols = values.shape
    if rows % 8:
        return jnp.sum(values, axis=0, keepdims=True)
    return jnp.sum(values.reshape(rows // 8, 8, cols), axis=0)


def gather_blocks(x_ref, x_s, row_size, col_size):
    _, rows, cols = x_ref.shape
    height = rows * row_size
    total = 0.0
    for r in range(row_size):
        for c in range(col_size):
            block = x_ref[r * col_size + c]
            x_s[r * rows : (r + 1) * rows, c * cols : (c + 1) * cols] = block
            wide = block.astype(jnp.float32)
            total = total + sum_rows(wide * wide)
    x_s[height:, :] = jnp.zeros((x_s.shape[0] - height, x_s.shape[1]), x_s.dtype)
    return 1.0 / (jnp.sqrt(jnp.sum(total, keepdims=True)) + epsilon)


def newton_schulz(height, inverse, x_s, y_s, gram_s, write):
    padded, width = x_s.shape
    tile = height // TILES
    update_scale = 0.2 * math.sqrt(max(height, width))
    for ref in (y_s, gram_s):
        ref[height:, :] = jnp.zeros((padded - height, ref.shape[1]), ref.dtype)
    for iteration in range(ITERS):
        src = x_s if iteration == 0 else y_s
        for t in range(TILES):
            span = slice(t * tile, (t + 1) * tile)
            gram = matmul(src[span, :], src[...], 1)
            if iteration == 0:
                gram = gram * (inverse * inverse)
            gram_s[span, :] = gram.astype(jnp.bfloat16)
        for t in range(TILES):
            span = slice(t * tile, (t + 1) * tile)
            square = matmul(gram_s[span, :], gram_s[...], 0)
            mixing = coef_b * gram_s[span, :].astype(jnp.float32) + coef_c * square
            combined = coef_a * src[span, :].astype(jnp.float32) + matmul(
                mixing.astype(jnp.bfloat16), src[...], 0
            )
            if iteration == 0:
                combined = combined * inverse
            if iteration + 1 < ITERS:
                y_s[span, :] = combined.astype(jnp.bfloat16)
            else:
                write(t, (update_scale * combined).astype(jnp.bfloat16))


def stage_place(row_offset, col_offset, row_size, width):
    high = row_offset // LOW * width + col_offset
    return row_offset % LOW * (row_size // LOW * width) + high


def ortho_kernel(row_size, col_size, slot, other_ref, x_ref, *refs):
    _, rows, cols = x_ref.shape
    width = col_size // HALVES
    places = row_size * width
    height = rows * row_size
    tile = height // TILES
    if slot:
        owned_ref, back_ref, x_s, y_s, gram_s, out_s, sems = refs[1:]
    else:
        owned_ref, low_refs = refs[0], refs[1 : 1 + LOW]
        x_s, y_s, gram_s, out_s, sems, back_ref = refs[1 + LOW :]
    row, col = lax.axis_index("dp"), lax.axis_index("owner")
    me = row * col_size + col
    owns = other_ref[me] != me
    low = col < width
    inverse = gather_blocks(x_ref, x_s, row_size, col_size)

    def copy_out(t):
        span = pl.ds(t * tile, tile)
        return pltpu.make_async_copy(out_s.at[span], owned_ref.at[slot, span], sems.at[t])

    def write(t, result):
        out_s[t * tile : (t + 1) * tile, :] = jnp.where(owns, result, jnp.zeros_like(result))
        copy_out(t).start()
        for j in range(row_size // TILES):
            block = result[j * rows : (j + 1) * rows, :]
            r = t * (row_size // TILES) + j
            for c in range(width):
                if slot:
                    place = r * width + c
                else:
                    place = stage_place(r ^ row, c ^ (col % width), row_size, width)
                back_ref[place] = jnp.where(
                    low,
                    block[:, c * cols : (c + 1) * cols],
                    block[:, (c + width) * cols : (c + width + 1) * cols],
                )

    newton_schulz(height, inverse, x_s, y_s, gram_s, write)
    if not slot:
        for k in range(LOW):
            low_refs[k][...] = back_ref[k * places // LOW : (k + 1) * places // LOW]
    for t in range(TILES):
        copy_out(t).wait()


def orthogonalize(slot, other, arrived, row_size, col_size, owned=None):
    devices, rows, cols = arrived.shape
    height, width = rows * row_size, cols * col_size
    padded = round_up(height, 256)
    places = devices // HALVES
    anywhere = pl.BlockSpec(memory_space=pl.ANY)
    in_specs, operands = [SMEM, VMEM], [other, arrived]
    scratch_shapes = [
        pltpu.VMEM((padded, width), jnp.bfloat16),
        pltpu.VMEM((padded, width), jnp.bfloat16),
        pltpu.VMEM((padded, padded), jnp.bfloat16),
        pltpu.VMEM((height, width), jnp.bfloat16),
        pltpu.SemaphoreType.DMA((TILES,)),
    ]
    if slot:
        in_specs.append(anywhere)
        operands.append(owned)
        back = [(places, rows, cols)]
    else:
        back = [(places // LOW, rows, cols)] * LOW
        scratch_shapes.append(pltpu.VMEM((places, rows, cols), jnp.bfloat16))
    owned, *back = pl.pallas_call(
        functools.partial(ortho_kernel, row_size, col_size, slot),
        in_specs=in_specs,
        out_specs=[anywhere] + [VMEM] * len(back),
        out_shape=[jax.ShapeDtypeStruct((CAP, height, width), jnp.bfloat16)]
        + [jax.ShapeDtypeStruct(shape, jnp.bfloat16) for shape in back],
        scratch_shapes=scratch_shapes,
        input_output_aliases={2: 0} if slot else {},
        compiler_params=PARAMS,
        cost_estimate=pl.CostEstimate(
            flops=2 * ITERS * padded * padded * (2 * width + padded),
            bytes_accessed=6 * padded * width,
            transcendentals=0,
        ),
        name="orthogonalize",
    )(*operands)
    return owned, back


def restage_kernel(*refs):
    low_refs, high_refs = refs[:LOW], refs[LOW:]
    for h, high_ref in enumerate(high_refs):
        for k, low_ref in enumerate(low_refs):
            high_ref[k] = low_ref[h]


def restage(blocks):
    highs, rows, cols = blocks[0].shape
    out = jax.ShapeDtypeStruct((LOW, rows, cols), blocks[0].dtype)
    return pl.pallas_call(
        restage_kernel,
        grid=(1,),
        in_specs=[whole(blocks[0].shape)] * LOW,
        out_specs=[whole(out.shape)] * highs,
        out_shape=[out] * highs,
        compiler_params=PARAMS,
        cost_estimate=pl.CostEstimate(
            flops=0, bytes_accessed=4 * LOW * highs * rows * cols, transcendentals=0
        ),
        name="restage",
    )(*blocks)


def unpack_kernel(chunk, place_ref, *refs):
    high_refs, second_ref, update_ref, back_s, update_s, sems = refs[:-5], *refs[-5:]
    for h, high_ref in enumerate(high_refs):
        back_s[h * LOW : (h + 1) * LOW] = high_ref[...]
    back_s[second_ref.shape[0] :] = second_ref[...]

    def copy_out(k):
        span = pl.ds(k * chunk, chunk)
        return pltpu.make_async_copy(update_s.at[span], update_ref.at[span], sems.at[k])

    chunks = update_s.shape[0] // chunk
    for k in range(chunks):
        for i in range(k * chunk, (k + 1) * chunk):
            update_s[i] = back_s[place_ref[i]]
        copy_out(k).start()
    for k in range(chunks):
        copy_out(k).wait()


def unpack(place, first, second):
    places, rows, cols = second.shape
    mats = place.shape[0]
    chunk = 8
    return pl.pallas_call(
        functools.partial(unpack_kernel, chunk),
        grid_spec=pltpu.PrefetchScalarGridSpec(
            num_scalar_prefetch=1,
            grid=(1,),
            in_specs=[whole(first[0].shape)] * len(first) + [whole(second.shape)],
            out_specs=pl.BlockSpec(memory_space=pl.ANY),
            scratch_shapes=[
                pltpu.VMEM((CAP * places, rows, cols), jnp.bfloat16),
                pltpu.VMEM((mats, rows, cols), jnp.bfloat16),
                pltpu.SemaphoreType.DMA((mats // chunk,)),
            ],
        ),
        out_shape=jax.ShapeDtypeStruct((mats, rows, cols), jnp.bfloat16),
        compiler_params=PARAMS,
        cost_estimate=pl.CostEstimate(
            flops=0, bytes_accessed=4 * mats * rows * cols, transcendentals=0
        ),
        name="unpack",
    )(place, *first, second)


def exchange(blocks, axes, groups=None):
    return lax.all_to_all(
        blocks, axes, split_axis=0, concat_axis=0, tiled=True, axis_index_groups=groups
    )


def swap(block, offset, devices):
    return lax.ppermute(block, AXES, [(d, d ^ offset) for d in range(devices)])


def on_device(gradients, momentum, owner_table):
    row_size = lax.axis_size("dp")
    col_size = lax.axis_size("owner")
    devices = row_size * col_size
    width = col_size // HALVES
    halves = [
        [r * col_size + half * width + c for r in range(row_size) for c in range(width)]
        for half in range(HALVES)
    ]
    first, other, rank = pack(gradients, momentum, owner_table, devices, col_size)
    arrived_first = exchange(first, AXES)
    new_momentum, second, place = update_momentum(
        gradients, momentum, owner_table, other, rank, col_size
    )
    arrived_first, second = lax.optimization_barrier((arrived_first, second))
    arrived_second = exchange(second, AXES)
    owned, back_first = orthogonalize(0, other, arrived_first, row_size, col_size)
    low = [back_first[0]] + [
        swap(back_first[k], k * col_size, devices) for k in range(1, LOW)
    ]
    high = restage(low)
    _, arrived_second = lax.optimization_barrier((high, arrived_second))
    returned_first = [high[0]] + [
        swap(high[r * width + c], r * LOW * col_size + c, devices)
        for r in range(row_size // LOW)
        for c in range(width)
        if r or c
    ]
    owned, back_second = orthogonalize(1, other, arrived_second, row_size, col_size, owned)
    returned_first, back_second = lax.optimization_barrier((returned_first, back_second))
    returned_second = exchange(back_second[0], AXES, halves)
    update = unpack(place, returned_first, returned_second)
    return (new_momentum, update, owned)


def solution(mesh):
    return jax.shard_map(
        on_device,
        mesh=mesh,
        in_specs=(P(None, "dp", "owner"), P(None, "dp", "owner"), P()),
        out_specs=(P(None, "dp", "owner"), P(None, "dp", "owner"), P(("dp", "owner"), None, None)),
        check_vma=False,
    )
```

```python
import functools
import math

import jax
import jax.numpy as jnp
from jax import lax
from jax.experimental import pallas as pl
from jax.experimental.pallas import tpu as pltpu
from jax.sharding import PartitionSpec as P

ITERS = 2
CAP = 2
HALVES = 2
ROW_TILES = (1, 2)
LOW = 4

coef_a = 3.4445
coef_b = -4.775
coef_c = 2.0315
momentum_beta = 0.95
epsilon = 1e-07

AXES = ("dp", "owner")
MIB = 1024 * 1024
PARAMS = pltpu.CompilerParams(vmem_limit_bytes=24 * MIB)
PACK_PARAMS = pltpu.CompilerParams(vmem_limit_bytes=60 * MIB)
SMEM = pl.BlockSpec(memory_space=pltpu.SMEM)
VMEM = pl.BlockSpec(memory_space=pltpu.VMEM)
ANYWHERE = pl.BlockSpec(memory_space=pl.ANY)


def round_up(value, multiple):
    return -(-value // multiple) * multiple


def whole(shape):
    return pl.BlockSpec(shape, lambda *_: (0,) * len(shape))


def nesterov_of(grad_ref, momentum_ref, j):
    grad = grad_ref[j].astype(jnp.float32)
    new = momentum_beta * momentum_ref[j] + grad
    return new, (grad + momentum_beta * new).astype(jnp.bfloat16)


def make_plan(col_size, owner_ref, other_ref, rank_ref, count_ref, list_ref):
    devices, mats = other_ref.shape[0], rank_ref.shape[0]

    def clear(d, _):
        count_ref[d] = 0
        return 0

    lax.fori_loop(0, devices, clear, 0, unroll=8)

    def rank_matrix(i, _):
        owner = owner_ref[i]
        rank = count_ref[owner]
        rank_ref[i] = rank
        count_ref[owner] = rank + 1
        return 0

    lax.fori_loop(0, mats, rank_matrix, 0, unroll=8)

    def list_device(d, found):
        owns = jnp.minimum(count_ref[d], 1)
        half = (d % col_size) // (col_size // HALVES)
        row = 2 * jnp.where(owns == 1, half, 1 - half) + owns
        place = found[0]
        for k in range(1, 2 * HALVES):
            place = jnp.where(row == k, found[k], place)
        list_ref[row * devices + place] = d
        return tuple(n + jnp.where(row == k, 1, 0) for k, n in enumerate(found))

    found = lax.fori_loop(0, devices, list_device, (0,) * (2 * HALVES), unroll=8)
    for half in range(HALVES):

        def pair(k, _):
            idle = list_ref[2 * half * devices + k]
            other_ref[list_ref[(2 * half + 1) * devices + k]] = idle
            other_ref[idle] = idle
            return 0

        lax.fori_loop(0, found[2 * half + 1], pair, 0)


def pack_kernel(
    chunk, col_size, owner_ref, g_ref, m_ref, first_ref, other_ref, rank_ref,
    count_ref, list_ref, g_s, m_s, block_s, load_sems, store_sems,
):
    mats = rank_ref.shape[0]

    def loads(k):
        span = pl.ds(k * chunk, chunk)
        return (
            pltpu.make_async_copy(g_ref.at[span], g_s.at[span], load_sems.at[0, k]),
            pltpu.make_async_copy(m_ref.at[span], m_s.at[span], load_sems.at[1, k]),
        )

    def stores(i):
        owner = owner_ref[i]
        return [
            pltpu.make_async_copy(block_s.at[i], first_ref.at[host], store_sems.at[n, i])
            for n, host in enumerate((owner, other_ref[owner]))
        ]

    for k in range(mats // chunk):
        for load in loads(k):
            load.start()
    make_plan(col_size, owner_ref, other_ref, rank_ref, count_ref, list_ref)
    for k in range(mats // chunk):
        for load in loads(k):
            load.wait()
        for i in range(k * chunk, (k + 1) * chunk):

            @pl.when(rank_ref[i] == 0)
            def _():
                block_s[i] = nesterov_of(g_s, m_s, i)[1]
                for store in stores(i):
                    store.start()

    for i in range(mats):

        @pl.when(rank_ref[i] == 0)
        def _():
            for store in stores(i):
                store.wait()


def pack(gradients, momentum, owner_table, devices, col_size):
    mats, rows, cols = gradients.shape
    chunk = 8
    return pl.pallas_call(
        functools.partial(pack_kernel, chunk, col_size),
        in_specs=[SMEM, ANYWHERE, ANYWHERE],
        out_specs=[ANYWHERE, SMEM, SMEM],
        out_shape=[
            jax.ShapeDtypeStruct((devices, rows, cols), jnp.bfloat16),
            jax.ShapeDtypeStruct((devices,), jnp.int32),
            jax.ShapeDtypeStruct((mats,), jnp.int32),
        ],
        scratch_shapes=[
            pltpu.SMEM((devices,), jnp.int32),
            pltpu.SMEM((2 * HALVES * devices,), jnp.int32),
            pltpu.VMEM(gradients.shape, gradients.dtype),
            pltpu.VMEM(momentum.shape, momentum.dtype),
            pltpu.VMEM(gradients.shape, jnp.bfloat16),
            pltpu.SemaphoreType.DMA((2, mats // chunk)),
            pltpu.SemaphoreType.DMA((2, mats)),
        ],
        compiler_params=PACK_PARAMS,
        cost_estimate=pl.CostEstimate(
            flops=4 * mats * rows * cols, bytes_accessed=8 * mats * rows * cols, transcendentals=0
        ),
        name="pack",
    )(owner_table, gradients, momentum)


def momentum_kernel(
    chunk, col_size, owner_ref, other_ref, rank_ref, g_ref, m_ref, nm_ref, second_ref, place_ref
):
    step = pl.program_id(0)
    width = col_size // HALVES
    row, col = lax.axis_index("dp"), lax.axis_index("owner")
    for j in range(chunk):
        i = step * chunk + j
        new, nesterov = nesterov_of(g_ref, m_ref, j)
        nm_ref[j] = new
        owner = owner_ref[i]

        @pl.when(rank_ref[i] == 1)
        def _():
            second_ref[owner] = nesterov
            second_ref[other_ref[owner]] = nesterov

        near = (owner % col_size) // width == col // width
        host = jnp.where(near, owner, other_ref[owner])
        host_row, host_col = host // col_size, host % width
        offset = host_row ^ row
        high = offset // LOW * width + (host_col ^ (col % width))
        place_ref[i] = jnp.where(
            rank_ref[i] == 0,
            high * LOW + offset % LOW,
            host_row * width + host_col,
        )


def update_momentum(gradients, momentum, owner_table, other, rank, col_size):
    mats, rows, cols = gradients.shape
    devices = other.shape[0]
    chunk = 8
    block = pl.BlockSpec((chunk, rows, cols), lambda i, *_: (i, 0, 0))
    return pl.pallas_call(
        functools.partial(momentum_kernel, chunk, col_size),
        grid_spec=pltpu.PrefetchScalarGridSpec(
            num_scalar_prefetch=3,
            grid=(mats // chunk,),
            in_specs=[block, block],
            out_specs=[block, whole((devices, rows, cols)), SMEM],
        ),
        out_shape=[
            jax.ShapeDtypeStruct(momentum.shape, jnp.float32),
            jax.ShapeDtypeStruct((devices, rows, cols), jnp.bfloat16),
            jax.ShapeDtypeStruct((mats,), jnp.int32),
        ],
        compiler_params=PARAMS,
        cost_estimate=pl.CostEstimate(
            flops=4 * mats * rows * cols, bytes_accessed=12 * mats * rows * cols, transcendentals=0
        ),
        name="update_momentum",
    )(owner_table, other, rank, gradients, momentum)


def matmul(lhs, rhs, rhs_dim):
    return lax.dot_general(
        lhs, rhs, (((1,), (rhs_dim,)), ((), ())), preferred_element_type=jnp.float32
    )


def sum_rows(values):
    rows, cols = values.shape
    if rows % 8:
        return jnp.sum(values, axis=0, keepdims=True)
    return jnp.sum(values.reshape(rows // 8, 8, cols), axis=0)


def gather_blocks(x_ref, x_s, row_size, col_size):
    _, rows, cols = x_ref.shape
    height = rows * row_size
    total = 0.0
    for r in range(row_size):
        for c in range(col_size):
            block = x_ref[r * col_size + c]
            x_s[r * rows : (r + 1) * rows, c * cols : (c + 1) * cols] = block
            wide = block.astype(jnp.float32)
            total = total + sum_rows(wide * wide)
    x_s[height:, :] = jnp.zeros((x_s.shape[0] - height, x_s.shape[1]), x_s.dtype)
    return 1.0 / (jnp.sqrt(jnp.sum(total, keepdims=True)) + epsilon)


def newton_schulz(height, tiles, inverse, x_s, y_s, gram_s, write):
    padded, width = x_s.shape
    tile = height // tiles
    update_scale = 0.2 * math.sqrt(max(height, width))
    for ref in (y_s, gram_s):
        ref[height:, :] = jnp.zeros((padded - height, ref.shape[1]), ref.dtype)
    for iteration in range(ITERS):
        src = x_s if iteration == 0 else y_s
        for t in range(tiles):
            span = slice(t * tile, (t + 1) * tile)
            gram = matmul(src[span, :], src[...], 1)
            if iteration == 0:
                gram = gram * (inverse * inverse)
            gram_s[span, :] = gram.astype(jnp.bfloat16)
        for t in range(tiles):
            span = slice(t * tile, (t + 1) * tile)
            square = matmul(gram_s[span, :], gram_s[...], 0)
            mixing = coef_b * gram_s[span, :].astype(jnp.float32) + coef_c * square
            combined = coef_a * src[span, :].astype(jnp.float32) + matmul(
                mixing.astype(jnp.bfloat16), src[...], 0
            )
            if iteration == 0:
                combined = combined * inverse
            if iteration + 1 < ITERS:
                y_s[span, :] = combined.astype(jnp.bfloat16)
            else:
                write(t, (update_scale * combined).astype(jnp.bfloat16))


def stage_place(row_offset, col_offset, row_size, width):
    high = row_offset // LOW * width + col_offset
    return row_offset % LOW * (row_size // LOW * width) + high


def ortho_kernel(row_size, col_size, slot, other_ref, x_ref, *refs):
    _, rows, cols = x_ref.shape
    width = col_size // HALVES
    places = row_size * width
    height = rows * row_size
    tiles = ROW_TILES[slot]
    tile = height // tiles
    if slot:
        whole_ref, back_ref, x_s, y_s, gram_s = refs
    else:
        owned_ref, low_refs = refs[0], refs[1 : 1 + LOW]
        x_s, y_s, gram_s, whole_ref, back_ref, sems = refs[1 + LOW :]
    row, col = lax.axis_index("dp"), lax.axis_index("owner")
    me = row * col_size + col
    owns = other_ref[me] != me
    low = col < width
    inverse = gather_blocks(x_ref, x_s, row_size, col_size)

    def copy_out(t):
        span = pl.ds(t * tile, tile)
        return pltpu.make_async_copy(whole_ref.at[span], owned_ref.at[slot, span], sems.at[t])

    def write(t, result):
        whole_ref[t * tile : (t + 1) * tile, :] = jnp.where(owns, result, jnp.zeros_like(result))
        if not slot:
            copy_out(t).start()
        for j in range(row_size // tiles):
            block = result[j * rows : (j + 1) * rows, :]
            r = t * (row_size // tiles) + j
            for c in range(width):
                if slot:
                    place = r * width + c
                else:
                    place = stage_place(r ^ row, c ^ (col % width), row_size, width)
                back_ref[place] = jnp.where(
                    low,
                    block[:, c * cols : (c + 1) * cols],
                    block[:, (c + width) * cols : (c + width + 1) * cols],
                )

    newton_schulz(height, tiles, inverse, x_s, y_s, gram_s, write)
    if not slot:
        for k in range(LOW):
            low_refs[k][...] = back_ref[k * places // LOW : (k + 1) * places // LOW]
        for t in range(tiles):
            copy_out(t).wait()


def orthogonalize(slot, other, arrived, row_size, col_size):
    devices, rows, cols = arrived.shape
    height, width = rows * row_size, cols * col_size
    padded = round_up(height, 256)
    places = devices // HALVES
    scratch_shapes = [
        pltpu.VMEM((padded, width), jnp.bfloat16),
        pltpu.VMEM((padded, width), jnp.bfloat16),
        pltpu.VMEM((padded, padded), jnp.bfloat16),
    ]
    if slot:
        out_specs = [VMEM, VMEM]
        out = [(height, width), (places, rows, cols)]
    else:
        out_specs = [ANYWHERE] + [VMEM] * LOW
        out = [(CAP, height, width)] + [(places // LOW, rows, cols)] * LOW
        scratch_shapes += [
            pltpu.VMEM((height, width), jnp.bfloat16),
            pltpu.VMEM((places, rows, cols), jnp.bfloat16),
            pltpu.SemaphoreType.DMA((ROW_TILES[slot],)),
        ]
    return pl.pallas_call(
        functools.partial(ortho_kernel, row_size, col_size, slot),
        in_specs=[SMEM, VMEM],
        out_specs=out_specs,
        out_shape=[jax.ShapeDtypeStruct(shape, jnp.bfloat16) for shape in out],
        scratch_shapes=scratch_shapes,
        compiler_params=PARAMS,
        cost_estimate=pl.CostEstimate(
            flops=2 * ITERS * padded * padded * (2 * width + padded),
            bytes_accessed=6 * padded * width,
            transcendentals=0,
        ),
        name="orthogonalize",
    )(other, arrived)


def restage_kernel(*refs):
    low_refs, high_refs = refs[:LOW], refs[LOW:]
    for h, high_ref in enumerate(high_refs):
        for k, low_ref in enumerate(low_refs):
            high_ref[k] = low_ref[h]


def restage(blocks):
    highs, rows, cols = blocks[0].shape
    out = jax.ShapeDtypeStruct((LOW, rows, cols), blocks[0].dtype)
    return pl.pallas_call(
        restage_kernel,
        grid=(1,),
        in_specs=[whole(blocks[0].shape)] * LOW,
        out_specs=[whole(out.shape)] * highs,
        out_shape=[out] * highs,
        compiler_params=PARAMS,
        cost_estimate=pl.CostEstimate(
            flops=0, bytes_accessed=4 * LOW * highs * rows * cols, transcendentals=0
        ),
        name="restage",
    )(*blocks)


def copy_blocks(slot, rank_ref, place_ref, back_ref, update_ref, sems, act):
    for i in range(update_ref.shape[0]):

        @pl.when(rank_ref[i] == slot)
        def _():
            copy = pltpu.make_async_copy(
                back_ref.at[place_ref[i]], update_ref.at[i], sems.at[i]
            )
            act(copy)


def start(copy):
    copy.start()


def wait(copy):
    copy.wait()


def early_kernel(rank_ref, place_ref, whole_ref, owned_in, *refs):
    high_refs, (owned_ref, update_ref, back_s, own_sem, sems) = refs[:-5], refs[-5:]
    own = pltpu.make_async_copy(whole_ref, owned_ref.at[CAP - 1], own_sem)
    own.start()
    for h, high_ref in enumerate(high_refs):
        back_s[h * LOW : (h + 1) * LOW] = high_ref[...]
    copy_blocks(0, rank_ref, place_ref, back_s, update_ref, sems, start)
    copy_blocks(0, rank_ref, place_ref, back_s, update_ref, sems, wait)
    own.wait()


def store_early(rank, place, matrix, owned, first):
    _, rows, cols = first[0].shape
    mats = rank.shape[0]
    return pl.pallas_call(
        early_kernel,
        in_specs=[SMEM, SMEM, VMEM, ANYWHERE] + [VMEM] * len(first),
        out_specs=[ANYWHERE, ANYWHERE],
        out_shape=[
            jax.ShapeDtypeStruct(owned.shape, jnp.bfloat16),
            jax.ShapeDtypeStruct((mats, rows, cols), jnp.bfloat16),
        ],
        scratch_shapes=[
            pltpu.VMEM((LOW * len(first), rows, cols), jnp.bfloat16),
            pltpu.SemaphoreType.DMA(()),
            pltpu.SemaphoreType.DMA((mats,)),
        ],
        input_output_aliases={3: 0},
        compiler_params=PARAMS,
        cost_estimate=pl.CostEstimate(
            flops=0, bytes_accessed=8 * mats * rows * cols, transcendentals=0
        ),
        name="store_early",
    )(rank, place, matrix, owned, *first)


def late_kernel(rank_ref, place_ref, back_ref, update_in, update_ref, sems):
    copy_blocks(1, rank_ref, place_ref, back_ref, update_ref, sems, start)
    copy_blocks(1, rank_ref, place_ref, back_ref, update_ref, sems, wait)


def store_late(rank, place, second, update):
    return pl.pallas_call(
        late_kernel,
        in_specs=[SMEM, SMEM, VMEM, ANYWHERE],
        out_specs=ANYWHERE,
        out_shape=jax.ShapeDtypeStruct(update.shape, jnp.bfloat16),
        scratch_shapes=[pltpu.SemaphoreType.DMA((rank.shape[0],))],
        input_output_aliases={3: 0},
        compiler_params=PARAMS,
        cost_estimate=pl.CostEstimate(flops=0, bytes_accessed=4 * second.size, transcendentals=0),
        name="store_late",
    )(rank, place, second, update)


def exchange(blocks, axes, groups=None):
    return lax.all_to_all(
        blocks, axes, split_axis=0, concat_axis=0, tiled=True, axis_index_groups=groups
    )


def swap(block, offset, devices):
    return lax.ppermute(block, AXES, [(d, d ^ offset) for d in range(devices)])


def on_device(gradients, momentum, owner_table):
    row_size = lax.axis_size("dp")
    col_size = lax.axis_size("owner")
    devices = row_size * col_size
    width = col_size // HALVES
    halves = [
        [r * col_size + half * width + c for r in range(row_size) for c in range(width)]
        for half in range(HALVES)
    ]
    first, other, rank = pack(gradients, momentum, owner_table, devices, col_size)
    arrived_first = exchange(first, AXES)
    new_momentum, second, place = update_momentum(
        gradients, momentum, owner_table, other, rank, col_size
    )
    arrived_first, second = lax.optimization_barrier((arrived_first, second))
    arrived_second = exchange(second, AXES)
    owned, *back_first = orthogonalize(0, other, arrived_first, row_size, col_size)
    low = [back_first[0]] + [
        swap(back_first[k], k * col_size, devices) for k in range(1, LOW)
    ]
    high = restage(low)
    _, arrived_second = lax.optimization_barrier((high, arrived_second))
    returned_first = [high[0]] + [
        swap(high[r * width + c], r * LOW * col_size + c, devices)
        for r in range(row_size // LOW)
        for c in range(width)
        if r or c
    ]
    matrix, back_second = orthogonalize(1, other, arrived_second, row_size, col_size)
    returned_first, back_second = lax.optimization_barrier((returned_first, back_second))
    returned_second = exchange(back_second, AXES, halves)
    owned, update = store_early(rank, place, matrix, owned, returned_first)
    update = store_late(rank, place, returned_second, update)
    return (new_momentum, update, owned)


def solution(mesh):
    return jax.shard_map(
        on_device,
        mesh=mesh,
        in_specs=(P(None, "dp", "owner"), P(None, "dp", "owner"), P()),
        out_specs=(P(None, "dp", "owner"), P(None, "dp", "owner"), P(("dp", "owner"), None, None)),
        check_vma=False,
    )
```

```python
import functools
import math

import jax
import jax.numpy as jnp
from jax import lax
from jax.experimental import pallas as pl
from jax.experimental.pallas import tpu as pltpu
from jax.sharding import PartitionSpec as P

ITERS = 2
CAP = 2
HALVES = 2
TILES = 2
LOW = 4

coef_a = 3.4445
coef_b = -4.775
coef_c = 2.0315
momentum_beta = 0.95
epsilon = 1e-07

AXES = ("dp", "owner")
MIB = 1024 * 1024
PARAMS = pltpu.CompilerParams(vmem_limit_bytes=24 * MIB)
PACK_PARAMS = pltpu.CompilerParams(vmem_limit_bytes=60 * MIB)
SMEM = pl.BlockSpec(memory_space=pltpu.SMEM)
VMEM = pl.BlockSpec(memory_space=pltpu.VMEM)
ANYWHERE = pl.BlockSpec(memory_space=pl.ANY)


def round_up(value, multiple):
    return -(-value // multiple) * multiple


def whole(shape):
    return pl.BlockSpec(shape, lambda *_: (0,) * len(shape))


def nesterov_of(grad_ref, momentum_ref, j):
    grad = grad_ref[j].astype(jnp.float32)
    new = momentum_beta * momentum_ref[j] + grad
    return new, (grad + momentum_beta * new).astype(jnp.bfloat16)


def make_plan(col_size, owner_ref, other_ref, rank_ref, count_ref, list_ref):
    devices, mats = other_ref.shape[0], rank_ref.shape[0]

    def clear(d, _):
        count_ref[d] = 0
        return 0

    lax.fori_loop(0, devices, clear, 0, unroll=8)

    def rank_matrix(i, _):
        owner = owner_ref[i]
        rank = count_ref[owner]
        rank_ref[i] = rank
        count_ref[owner] = rank + 1
        return 0

    lax.fori_loop(0, mats, rank_matrix, 0, unroll=8)

    def list_device(d, found):
        owns = jnp.minimum(count_ref[d], 1)
        half = (d % col_size) // (col_size // HALVES)
        row = 2 * jnp.where(owns == 1, half, 1 - half) + owns
        place = found[0]
        for k in range(1, 2 * HALVES):
            place = jnp.where(row == k, found[k], place)
        list_ref[row * devices + place] = d
        return tuple(n + jnp.where(row == k, 1, 0) for k, n in enumerate(found))

    found = lax.fori_loop(0, devices, list_device, (0,) * (2 * HALVES), unroll=8)
    for half in range(HALVES):

        def pair(k, _):
            idle = list_ref[2 * half * devices + k]
            other_ref[list_ref[(2 * half + 1) * devices + k]] = idle
            other_ref[idle] = idle
            return 0

        lax.fori_loop(0, found[2 * half + 1], pair, 0)


def pack_kernel(
    chunk, col_size, owner_ref, g_ref, m_ref, first_ref, other_ref, rank_ref,
    count_ref, list_ref, g_s, m_s, sems,
):
    mats = rank_ref.shape[0]

    def loads(k):
        span = pl.ds(k * chunk, chunk)
        return (
            pltpu.make_async_copy(g_ref.at[span], g_s.at[span], sems.at[0, k]),
            pltpu.make_async_copy(m_ref.at[span], m_s.at[span], sems.at[1, k]),
        )

    for k in range(mats // chunk):
        for load in loads(k):
            load.start()
    make_plan(col_size, owner_ref, other_ref, rank_ref, count_ref, list_ref)
    for k in range(mats // chunk):
        for load in loads(k):
            load.wait()
        for i in range(k * chunk, (k + 1) * chunk):

            @pl.when(rank_ref[i] == 0)
            def _():
                nesterov = nesterov_of(g_s, m_s, i)[1]
                first_ref[owner_ref[i]] = nesterov
                first_ref[other_ref[owner_ref[i]]] = nesterov


def pack(gradients, momentum, owner_table, devices, col_size):
    mats, rows, cols = gradients.shape
    chunk = 8
    return pl.pallas_call(
        functools.partial(pack_kernel, chunk, col_size),
        grid_spec=pltpu.PrefetchScalarGridSpec(
            num_scalar_prefetch=1,
            grid=(1,),
            in_specs=[ANYWHERE, ANYWHERE],
            out_specs=[whole((devices, rows, cols)), SMEM, SMEM],
            scratch_shapes=[
                pltpu.SMEM((devices,), jnp.int32),
                pltpu.SMEM((2 * HALVES * devices,), jnp.int32),
                pltpu.VMEM(gradients.shape, gradients.dtype),
                pltpu.VMEM(momentum.shape, momentum.dtype),
                pltpu.SemaphoreType.DMA((2, mats // chunk)),
            ],
        ),
        out_shape=[
            jax.ShapeDtypeStruct((devices, rows, cols), jnp.bfloat16),
            jax.ShapeDtypeStruct((devices,), jnp.int32),
            jax.ShapeDtypeStruct((mats,), jnp.int32),
        ],
        compiler_params=PACK_PARAMS,
        cost_estimate=pl.CostEstimate(
            flops=4 * mats * rows * cols, bytes_accessed=8 * mats * rows * cols, transcendentals=0
        ),
        name="pack",
    )(owner_table, gradients, momentum)


def momentum_kernel(
    chunk, col_size, owner_ref, other_ref, rank_ref, g_ref, m_ref, nm_ref, second_ref, list_ref,
    count_ref,
):
    step = pl.program_id(0)
    width = col_size // HALVES
    row, col = lax.axis_index("dp"), lax.axis_index("owner")
    listed = list_ref.shape[0] // CAP

    @pl.when(step == 0)
    def _():
        for slot in range(CAP):
            count_ref[slot] = 0

    for j in range(chunk):
        i = step * chunk + j
        new, nesterov = nesterov_of(g_ref, m_ref, j)
        nm_ref[j] = new
        owner = owner_ref[i]

        @pl.when(rank_ref[i] == 1)
        def _():
            second_ref[owner] = nesterov
            second_ref[other_ref[owner]] = nesterov

        near = (owner % col_size) // width == col // width
        host = jnp.where(near, owner, other_ref[owner])
        host_row, host_col = host // col_size, host % width
        offset = host_row ^ row
        high = offset // LOW * width + (host_col ^ (col % width))
        place = jnp.where(
            rank_ref[i] == 0, high * LOW + offset % LOW, host_row * width + host_col
        )
        rank = rank_ref[i]
        entry = count_ref[rank]
        count_ref[rank] = entry + 1
        list_ref[rank * listed + 2 * entry] = i
        list_ref[rank * listed + 2 * entry + 1] = place


def update_momentum(gradients, momentum, owner_table, other, rank, col_size):
    mats, rows, cols = gradients.shape
    devices = other.shape[0]
    chunk = 8
    block = pl.BlockSpec((chunk, rows, cols), lambda i, *_: (i, 0, 0))
    return pl.pallas_call(
        functools.partial(momentum_kernel, chunk, col_size),
        grid_spec=pltpu.PrefetchScalarGridSpec(
            num_scalar_prefetch=3,
            grid=(mats // chunk,),
            in_specs=[block, block],
            out_specs=[block, whole((devices, rows, cols)), SMEM],
            scratch_shapes=[pltpu.SMEM((CAP,), jnp.int32)],
        ),
        out_shape=[
            jax.ShapeDtypeStruct(momentum.shape, jnp.float32),
            jax.ShapeDtypeStruct((devices, rows, cols), jnp.bfloat16),
            jax.ShapeDtypeStruct((2 * mats,), jnp.int32),
        ],
        compiler_params=PARAMS,
        cost_estimate=pl.CostEstimate(
            flops=4 * mats * rows * cols, bytes_accessed=12 * mats * rows * cols, transcendentals=0
        ),
        name="update_momentum",
    )(owner_table, other, rank, gradients, momentum)


def matmul(lhs, rhs, rhs_dim):
    return lax.dot_general(
        lhs, rhs, (((1,), (rhs_dim,)), ((), ())), preferred_element_type=jnp.float32
    )


def sum_rows(values):
    rows, cols = values.shape
    if rows % 8:
        return jnp.sum(values, axis=0, keepdims=True)
    return jnp.sum(values.reshape(rows // 8, 8, cols), axis=0)


def gather_blocks(x_ref, x_s, row_size, col_size):
    _, rows, cols = x_ref.shape
    height = rows * row_size
    total = 0.0
    for r in range(row_size):
        for c in range(col_size):
            block = x_ref[r * col_size + c]
            x_s[r * rows : (r + 1) * rows, c * cols : (c + 1) * cols] = block
            wide = block.astype(jnp.float32)
            total = total + sum_rows(wide * wide)
    x_s[height:, :] = jnp.zeros((x_s.shape[0] - height, x_s.shape[1]), x_s.dtype)
    return 1.0 / (jnp.sqrt(jnp.sum(total, keepdims=True)) + epsilon)


def newton_schulz(height, tiles, inverse, x_s, y_s, gram_s, write):
    padded, width = x_s.shape
    tile = height // tiles
    update_scale = 0.2 * math.sqrt(max(height, width))
    for ref in (y_s, gram_s):
        ref[height:, :] = jnp.zeros((padded - height, ref.shape[1]), ref.dtype)
    for iteration in range(ITERS):
        src = x_s if iteration == 0 else y_s
        for t in range(tiles):
            span = slice(t * tile, (t + 1) * tile)
            gram = matmul(src[span, :], src[...], 1)
            if iteration == 0:
                gram = gram * (inverse * inverse)
            gram_s[span, :] = gram.astype(jnp.bfloat16)
        for t in range(tiles):
            span = slice(t * tile, (t + 1) * tile)
            square = matmul(gram_s[span, :], gram_s[...], 0)
            mixing = coef_b * gram_s[span, :].astype(jnp.float32) + coef_c * square
            combined = coef_a * src[span, :].astype(jnp.float32) + matmul(
                mixing.astype(jnp.bfloat16), src[...], 0
            )
            if iteration == 0:
                combined = combined * inverse
            if iteration + 1 < ITERS:
                y_s[span, :] = combined.astype(jnp.bfloat16)
            else:
                write(t, (update_scale * combined).astype(jnp.bfloat16))


def stage_place(row_offset, col_offset, row_size, width):
    high = row_offset // LOW * width + col_offset
    return row_offset % LOW * (row_size // LOW * width) + high


def ortho_kernel(row_size, col_size, slot, other_ref, x_ref, *refs):
    _, rows, cols = x_ref.shape
    width = col_size // HALVES
    places = row_size * width
    height = rows * row_size
    tiles = TILES
    tile = height // tiles
    if slot:
        whole_ref, out_ref, x_s, y_s, gram_s, back_ref, sems = refs
    else:
        owned_ref, low_refs = refs[0], refs[1 : 1 + LOW]
        x_s, y_s, gram_s, back_ref, sems, whole_ref = refs[1 + LOW :]
    row, col = lax.axis_index("dp"), lax.axis_index("owner")
    me = row * col_size + col
    owns = other_ref[me] != me
    low = col < width
    inverse = gather_blocks(x_ref, x_s, row_size, col_size)

    def copy_out(t):
        if slot:
            span = pl.ds(t * (places // tiles), places // tiles)
            return pltpu.make_async_copy(back_ref.at[span], out_ref.at[span], sems.at[t])
        span = pl.ds(t * tile, tile)
        return pltpu.make_async_copy(whole_ref.at[span], owned_ref.at[slot, span], sems.at[t])

    def write(t, result):
        whole_ref[t * tile : (t + 1) * tile, :] = jnp.where(owns, result, jnp.zeros_like(result))
        for j in range(row_size // tiles):
            block = result[j * rows : (j + 1) * rows, :]
            r = t * (row_size // tiles) + j
            for c in range(width):
                if slot:
                    place = r * width + c
                else:
                    place = stage_place(r ^ row, c ^ (col % width), row_size, width)
                back_ref[place] = jnp.where(
                    low,
                    block[:, c * cols : (c + 1) * cols],
                    block[:, (c + width) * cols : (c + width + 1) * cols],
                )
        copy_out(t).start()

    newton_schulz(height, tiles, inverse, x_s, y_s, gram_s, write)
    if not slot:
        for k in range(LOW):
            low_refs[k][...] = back_ref[k * places // LOW : (k + 1) * places // LOW]
    for t in range(tiles):
        copy_out(t).wait()


def orthogonalize(slot, other, arrived, row_size, col_size):
    devices, rows, cols = arrived.shape
    height, width = rows * row_size, cols * col_size
    padded = round_up(height, 256)
    places = devices // HALVES
    scratch_shapes = [
        pltpu.VMEM((padded, width), jnp.bfloat16),
        pltpu.VMEM((padded, width), jnp.bfloat16),
        pltpu.VMEM((padded, padded), jnp.bfloat16),
        pltpu.VMEM((places, rows, cols), jnp.bfloat16),
        pltpu.SemaphoreType.DMA((TILES,)),
    ]
    if slot:
        out_specs = [VMEM, ANYWHERE]
        out = [(height, width), (places, rows, cols)]
    else:
        out_specs = [ANYWHERE] + [VMEM] * LOW
        out = [(CAP, height, width)] + [(places // LOW, rows, cols)] * LOW
        scratch_shapes.append(pltpu.VMEM((height, width), jnp.bfloat16))
    return pl.pallas_call(
        functools.partial(ortho_kernel, row_size, col_size, slot),
        in_specs=[SMEM, VMEM],
        out_specs=out_specs,
        out_shape=[jax.ShapeDtypeStruct(shape, jnp.bfloat16) for shape in out],
        scratch_shapes=scratch_shapes,
        compiler_params=PARAMS,
        cost_estimate=pl.CostEstimate(
            flops=2 * ITERS * padded * padded * (2 * width + padded),
            bytes_accessed=6 * padded * width,
            transcendentals=0,
        ),
        name="orthogonalize",
    )(other, arrived)


def restage_kernel(*refs):
    low_refs, high_refs = refs[:LOW], refs[LOW:]
    for h, high_ref in enumerate(high_refs):
        for k, low_ref in enumerate(low_refs):
            high_ref[k] = low_ref[h]


def restage(blocks):
    highs, rows, cols = blocks[0].shape
    out = jax.ShapeDtypeStruct((LOW, rows, cols), blocks[0].dtype)
    return pl.pallas_call(
        restage_kernel,
        grid=(1,),
        in_specs=[whole(blocks[0].shape)] * LOW,
        out_specs=[whole(out.shape)] * highs,
        out_shape=[out] * highs,
        compiler_params=PARAMS,
        cost_estimate=pl.CostEstimate(
            flops=0, bytes_accessed=4 * LOW * highs * rows * cols, transcendentals=0
        ),
        name="restage",
    )(*blocks)


def start_blocks(slot, list_ref, back_ref, update_ref, sem):
    listed = list_ref.shape[0] // CAP
    for k in range(update_ref.shape[0] // CAP):
        matrix = list_ref[slot * listed + 2 * k]
        place = list_ref[slot * listed + 2 * k + 1]
        pltpu.make_async_copy(back_ref.at[place], update_ref.at[matrix], sem).start()


def wait_blocks(back_ref, update_ref, sem):
    span = pl.ds(0, update_ref.shape[0] // CAP)
    pltpu.make_async_copy(back_ref.at[span], update_ref.at[span], sem).wait()


def early_kernel(list_ref, whole_ref, owned_in, *refs):
    high_refs, (owned_ref, update_ref, back_s, own_sem, sem) = refs[:-5], refs[-5:]
    own = pltpu.make_async_copy(whole_ref, owned_ref.at[CAP - 1], own_sem)
    own.start()
    for h, high_ref in enumerate(high_refs):
        back_s[h * LOW : (h + 1) * LOW] = high_ref[...]
    start_blocks(0, list_ref, back_s, update_ref, sem)
    wait_blocks(back_s, update_ref, sem)
    own.wait()


def store_early(places, mats, matrix, owned, first):
    _, rows, cols = first[0].shape
    return pl.pallas_call(
        early_kernel,
        in_specs=[SMEM, VMEM, ANYWHERE] + [VMEM] * len(first),
        out_specs=[ANYWHERE, ANYWHERE],
        out_shape=[
            jax.ShapeDtypeStruct(owned.shape, jnp.bfloat16),
            jax.ShapeDtypeStruct((mats, rows, cols), jnp.bfloat16),
        ],
        scratch_shapes=[
            pltpu.VMEM((LOW * len(first), rows, cols), jnp.bfloat16),
            pltpu.SemaphoreType.DMA(()),
            pltpu.SemaphoreType.DMA(()),
        ],
        input_output_aliases={2: 0},
        compiler_params=PARAMS,
        cost_estimate=pl.CostEstimate(
            flops=0, bytes_accessed=8 * mats * rows * cols, transcendentals=0
        ),
        name="store_early",
    )(places, matrix, owned, *first)


def late_kernel(list_ref, back_ref, update_in, update_ref, sem):
    start_blocks(1, list_ref, back_ref, update_ref, sem)
    wait_blocks(back_ref, update_ref, sem)


def store_late(places, second, update):
    return pl.pallas_call(
        late_kernel,
        in_specs=[SMEM, VMEM, ANYWHERE],
        out_specs=ANYWHERE,
        out_shape=jax.ShapeDtypeStruct(update.shape, jnp.bfloat16),
        scratch_shapes=[pltpu.SemaphoreType.DMA(())],
        input_output_aliases={2: 0},
        compiler_params=PARAMS,
        cost_estimate=pl.CostEstimate(flops=0, bytes_accessed=4 * second.size, transcendentals=0),
        name="store_late",
    )(places, second, update)


def exchange(blocks, axes, groups=None):
    return lax.all_to_all(
        blocks, axes, split_axis=0, concat_axis=0, tiled=True, axis_index_groups=groups
    )


def swap(block, offset, devices):
    return lax.ppermute(block, AXES, [(d, d ^ offset) for d in range(devices)])


def on_device(gradients, momentum, owner_table):
    row_size = lax.axis_size("dp")
    col_size = lax.axis_size("owner")
    devices = row_size * col_size
    width = col_size // HALVES
    halves = [
        [r * col_size + half * width + c for r in range(row_size) for c in range(width)]
        for half in range(HALVES)
    ]
    first, other, rank = pack(gradients, momentum, owner_table, devices, col_size)
    arrived_first = exchange(first, AXES)
    new_momentum, second, places = update_momentum(
        gradients, momentum, owner_table, other, rank, col_size
    )
    arrived_first, second = lax.optimization_barrier((arrived_first, second))
    arrived_second = exchange(second, AXES)
    owned, *back_first = orthogonalize(0, other, arrived_first, row_size, col_size)
    low = [back_first[0]] + [
        swap(back_first[k], k * col_size, devices) for k in range(1, LOW)
    ]
    high = restage(low)
    _, arrived_second = lax.optimization_barrier((high, arrived_second))
    returned_first = [high[0]] + [
        swap(high[r * width + c], r * LOW * col_size + c, devices)
        for r in range(row_size // LOW)
        for c in range(width)
        if r or c
    ]
    matrix, back_second = orthogonalize(1, other, arrived_second, row_size, col_size)
    returned_first, back_second = lax.optimization_barrier((returned_first, back_second))
    returned_second = exchange(back_second, AXES, halves)
    owned, update = store_early(
        places, owner_table.shape[0], matrix, owned, returned_first
    )
    update = store_late(places, returned_second, update)
    return (new_momentum, update, owned)


def solution(mesh):
    return jax.shard_map(
        on_device,
        mesh=mesh,
        in_specs=(P(None, "dp", "owner"), P(None, "dp", "owner"), P()),
        out_specs=(P(None, "dp", "owner"), P(None, "dp", "owner"), P(("dp", "owner"), None, None)),
        check_vma=False,
    )
```

```python
import functools
import math

import jax
import jax.numpy as jnp
from jax import lax
from jax.experimental import pallas as pl
from jax.experimental.pallas import tpu as pltpu
from jax.sharding import PartitionSpec as P

ITERS = 2
CAP = 2
HALVES = 2
TILES = 2
LOW = 4

coef_a = 3.4445
coef_b = -4.775
coef_c = 2.0315
momentum_beta = 0.95
epsilon = 1e-07

AXES = ("dp", "owner")
MIB = 1024 * 1024
PARAMS = pltpu.CompilerParams(vmem_limit_bytes=24 * MIB)
PACK_PARAMS = pltpu.CompilerParams(vmem_limit_bytes=60 * MIB)
SMEM = pl.BlockSpec(memory_space=pltpu.SMEM)
VMEM = pl.BlockSpec(memory_space=pltpu.VMEM)
ANYWHERE = pl.BlockSpec(memory_space=pl.ANY)


def round_up(value, multiple):
    return -(-value // multiple) * multiple


def whole(shape):
    return pl.BlockSpec(shape, lambda *_: (0,) * len(shape))


def nesterov_of(grad_ref, momentum_ref, j):
    grad = grad_ref[j].astype(jnp.float32)
    new = momentum_beta * momentum_ref[j] + grad
    return new, (grad + momentum_beta * new).astype(jnp.bfloat16)


def make_plan(col_size, owner_ref, other_ref, rank_ref, count_ref, list_ref):
    devices, mats = other_ref.shape[0], rank_ref.shape[0]

    def clear(d, _):
        count_ref[d] = 0
        return 0

    lax.fori_loop(0, devices, clear, 0, unroll=8)

    def rank_matrix(i, _):
        owner = owner_ref[i]
        rank = count_ref[owner]
        rank_ref[i] = rank
        count_ref[owner] = rank + 1
        return 0

    lax.fori_loop(0, mats, rank_matrix, 0, unroll=8)

    def list_device(d, found):
        owns = jnp.minimum(count_ref[d], 1)
        half = (d % col_size) // (col_size // HALVES)
        row = 2 * jnp.where(owns == 1, half, 1 - half) + owns
        place = found[0]
        for k in range(1, 2 * HALVES):
            place = jnp.where(row == k, found[k], place)
        list_ref[row * devices + place] = d
        return tuple(n + jnp.where(row == k, 1, 0) for k, n in enumerate(found))

    found = lax.fori_loop(0, devices, list_device, (0,) * (2 * HALVES), unroll=8)
    for half in range(HALVES):

        def pair(k, _):
            idle = list_ref[2 * half * devices + k]
            other_ref[list_ref[(2 * half + 1) * devices + k]] = idle
            other_ref[idle] = idle
            return 0

        lax.fori_loop(0, found[2 * half + 1], pair, 0)


def pack_kernel(
    chunk, col_size, owner_ref, g_ref, m_ref, first_ref, other_ref, rank_ref,
    count_ref, list_ref, g_s, m_s, sems,
):
    mats = rank_ref.shape[0]

    def loads(k):
        span = pl.ds(k * chunk, chunk)
        return (
            pltpu.make_async_copy(g_ref.at[span], g_s.at[span], sems.at[0, k]),
            pltpu.make_async_copy(m_ref.at[span], m_s.at[span], sems.at[1, k]),
        )

    for k in range(mats // chunk):
        for load in loads(k):
            load.start()
    make_plan(col_size, owner_ref, other_ref, rank_ref, count_ref, list_ref)
    for k in range(mats // chunk):
        for load in loads(k):
            load.wait()
        for i in range(k * chunk, (k + 1) * chunk):

            @pl.when(rank_ref[i] == 0)
            def _():
                nesterov = nesterov_of(g_s, m_s, i)[1]
                first_ref[owner_ref[i]] = nesterov
                first_ref[other_ref[owner_ref[i]]] = nesterov


def pack(gradients, momentum, owner_table, devices, col_size):
    mats, rows, cols = gradients.shape
    chunk = 8
    return pl.pallas_call(
        functools.partial(pack_kernel, chunk, col_size),
        grid_spec=pltpu.PrefetchScalarGridSpec(
            num_scalar_prefetch=1,
            grid=(1,),
            in_specs=[ANYWHERE, ANYWHERE],
            out_specs=[whole((devices, rows, cols)), SMEM, SMEM],
            scratch_shapes=[
                pltpu.SMEM((devices,), jnp.int32),
                pltpu.SMEM((2 * HALVES * devices,), jnp.int32),
                pltpu.VMEM(gradients.shape, gradients.dtype),
                pltpu.VMEM(momentum.shape, momentum.dtype),
                pltpu.SemaphoreType.DMA((2, mats // chunk)),
            ],
        ),
        out_shape=[
            jax.ShapeDtypeStruct((devices, rows, cols), jnp.bfloat16),
            jax.ShapeDtypeStruct((devices,), jnp.int32),
            jax.ShapeDtypeStruct((mats,), jnp.int32),
        ],
        compiler_params=PACK_PARAMS,
        cost_estimate=pl.CostEstimate(
            flops=4 * mats * rows * cols, bytes_accessed=8 * mats * rows * cols, transcendentals=0
        ),
        name="pack",
    )(owner_table, gradients, momentum)


def momentum_kernel(
    chunk, col_size, owner_ref, other_ref, rank_ref, g_ref, m_ref, nm_ref, second_ref, list_ref,
    count_ref,
):
    step = pl.program_id(0)
    width = col_size // HALVES
    row, col = lax.axis_index("dp"), lax.axis_index("owner")
    listed = list_ref.shape[0] // CAP

    @pl.when(step == 0)
    def _():
        for slot in range(CAP):
            count_ref[slot] = 0

    for j in range(chunk):
        i = step * chunk + j
        new, nesterov = nesterov_of(g_ref, m_ref, j)
        nm_ref[j] = new
        owner = owner_ref[i]

        @pl.when(rank_ref[i] == 1)
        def _():
            second_ref[owner] = nesterov
            second_ref[other_ref[owner]] = nesterov

        near = (owner % col_size) // width == col // width
        host = jnp.where(near, owner, other_ref[owner])
        host_row, host_col = host // col_size, host % width
        offset = host_row ^ row
        high = offset // LOW * width + (host_col ^ (col % width))
        place = jnp.where(
            rank_ref[i] == 0, high * LOW + offset % LOW, host_row * width + host_col
        )
        rank = rank_ref[i]
        entry = count_ref[rank]
        count_ref[rank] = entry + 1
        list_ref[rank * listed + 2 * entry] = i
        list_ref[rank * listed + 2 * entry + 1] = place


def update_momentum(gradients, momentum, owner_table, other, rank, col_size):
    mats, rows, cols = gradients.shape
    devices = other.shape[0]
    chunk = 8
    block = pl.BlockSpec((chunk, rows, cols), lambda i, *_: (i, 0, 0))
    return pl.pallas_call(
        functools.partial(momentum_kernel, chunk, col_size),
        grid_spec=pltpu.PrefetchScalarGridSpec(
            num_scalar_prefetch=3,
            grid=(mats // chunk,),
            in_specs=[block, block],
            out_specs=[block, whole((devices, rows, cols)), SMEM],
            scratch_shapes=[pltpu.SMEM((CAP,), jnp.int32)],
        ),
        out_shape=[
            jax.ShapeDtypeStruct(momentum.shape, jnp.float32),
            jax.ShapeDtypeStruct((devices, rows, cols), jnp.bfloat16),
            jax.ShapeDtypeStruct((2 * mats,), jnp.int32),
        ],
        compiler_params=PARAMS,
        cost_estimate=pl.CostEstimate(
            flops=4 * mats * rows * cols, bytes_accessed=12 * mats * rows * cols, transcendentals=0
        ),
        name="update_momentum",
    )(owner_table, other, rank, gradients, momentum)


def matmul(lhs, rhs, rhs_dim):
    return lax.dot_general(
        lhs, rhs, (((1,), (rhs_dim,)), ((), ())), preferred_element_type=jnp.float32
    )


def sum_rows(values):
    rows, cols = values.shape
    if rows % 8:
        return jnp.sum(values, axis=0, keepdims=True)
    return jnp.sum(values.reshape(rows // 8, 8, cols), axis=0)


def gather_blocks(x_ref, x_s, row_size, col_size):
    _, rows, cols = x_ref.shape
    height = rows * row_size
    total = 0.0
    for r in range(row_size):
        for c in range(col_size):
            block = x_ref[r * col_size + c]
            x_s[r * rows : (r + 1) * rows, c * cols : (c + 1) * cols] = block
            wide = block.astype(jnp.float32)
            total = total + sum_rows(wide * wide)
    x_s[height:, :] = jnp.zeros((x_s.shape[0] - height, x_s.shape[1]), x_s.dtype)
    return 1.0 / (jnp.sqrt(jnp.sum(total, keepdims=True)) + epsilon)


def newton_schulz(height, tiles, inverse, x_s, y_s, gram_s, write):
    padded, width = x_s.shape
    tile = height // tiles
    update_scale = 0.2 * math.sqrt(max(height, width))
    for ref in (y_s, gram_s):
        ref[height:, :] = jnp.zeros((padded - height, ref.shape[1]), ref.dtype)
    for iteration in range(ITERS):
        src = x_s if iteration == 0 else y_s
        for t in range(tiles):
            span = slice(t * tile, (t + 1) * tile)
            gram = matmul(src[span, :], src[...], 1)
            if iteration == 0:
                gram = gram * (inverse * inverse)
            gram_s[span, :] = gram.astype(jnp.bfloat16)
        for t in range(tiles):
            span = slice(t * tile, (t + 1) * tile)
            square = matmul(gram_s[span, :], gram_s[...], 0)
            mixing = coef_b * gram_s[span, :].astype(jnp.float32) + coef_c * square
            combined = coef_a * src[span, :].astype(jnp.float32) + matmul(
                mixing.astype(jnp.bfloat16), src[...], 0
            )
            if iteration == 0:
                combined = combined * inverse
            if iteration + 1 < ITERS:
                y_s[span, :] = combined.astype(jnp.bfloat16)
            else:
                write(t, (update_scale * combined).astype(jnp.bfloat16))


def stage_place(row_offset, col_offset, row_size, width):
    high = row_offset // LOW * width + col_offset
    return row_offset % LOW * (row_size // LOW * width) + high


def ortho_kernel(row_size, col_size, slot, other_ref, x_ref, *refs):
    _, rows, cols = x_ref.shape
    width = col_size // HALVES
    places = row_size * width
    height = rows * row_size
    tiles = TILES
    tile = height // tiles
    if slot:
        whole_ref, out_ref, x_s, y_s, gram_s, back_ref, sems = refs
    else:
        owned_ref, low_refs = refs[0], refs[1 : 1 + LOW]
        x_s, y_s, gram_s, back_ref, sems, whole_ref = refs[1 + LOW :]
    row, col = lax.axis_index("dp"), lax.axis_index("owner")
    me = row * col_size + col
    owns = other_ref[me] != me
    low = col < width
    inverse = gather_blocks(x_ref, x_s, row_size, col_size)

    def copy_out(t):
        if slot:
            span = pl.ds(t * (places // tiles), places // tiles)
            return pltpu.make_async_copy(back_ref.at[span], out_ref.at[span], sems.at[t])
        span = pl.ds(t * tile, tile)
        return pltpu.make_async_copy(whole_ref.at[span], owned_ref.at[slot, span], sems.at[t])

    def write(t, result):
        whole_ref[t * tile : (t + 1) * tile, :] = jnp.where(owns, result, jnp.zeros_like(result))
        for j in range(row_size // tiles):
            block = result[j * rows : (j + 1) * rows, :]
            r = t * (row_size // tiles) + j
            for c in range(width):
                if slot:
                    place = r * width + c
                else:
                    place = stage_place(r ^ row, c ^ (col % width), row_size, width)
                back_ref[place] = jnp.where(
                    low,
                    block[:, c * cols : (c + 1) * cols],
                    block[:, (c + width) * cols : (c + width + 1) * cols],
                )
        copy_out(t).start()

    newton_schulz(height, tiles, inverse, x_s, y_s, gram_s, write)
    if not slot:
        for k in range(LOW):
            low_refs[k][...] = back_ref[k * places // LOW : (k + 1) * places // LOW]
    for t in range(tiles):
        copy_out(t).wait()


def orthogonalize(slot, other, arrived, row_size, col_size):
    devices, rows, cols = arrived.shape
    height, width = rows * row_size, cols * col_size
    padded = round_up(height, 256)
    places = devices // HALVES
    scratch_shapes = [
        pltpu.VMEM((padded, width), jnp.bfloat16),
        pltpu.VMEM((padded, width), jnp.bfloat16),
        pltpu.VMEM((padded, padded), jnp.bfloat16),
        pltpu.VMEM((places, rows, cols), jnp.bfloat16),
        pltpu.SemaphoreType.DMA((TILES,)),
    ]
    if slot:
        out_specs = [VMEM, ANYWHERE]
        out = [(height, width), (places, rows, cols)]
    else:
        out_specs = [ANYWHERE] + [VMEM] * LOW
        out = [(CAP, height, width)] + [(places // LOW, rows, cols)] * LOW
        scratch_shapes.append(pltpu.VMEM((height, width), jnp.bfloat16))
    return pl.pallas_call(
        functools.partial(ortho_kernel, row_size, col_size, slot),
        in_specs=[SMEM, VMEM],
        out_specs=out_specs,
        out_shape=[
            pltpu.HBM(shape, jnp.bfloat16)
            if spec is ANYWHERE
            else jax.ShapeDtypeStruct(shape, jnp.bfloat16)
            for spec, shape in zip(out_specs, out)
        ],
        scratch_shapes=scratch_shapes,
        compiler_params=PARAMS,
        cost_estimate=pl.CostEstimate(
            flops=2 * ITERS * padded * padded * (2 * width + padded),
            bytes_accessed=6 * padded * width,
            transcendentals=0,
        ),
        name="orthogonalize",
    )(other, arrived)


def restage_kernel(*refs):
    low_refs, high_refs = refs[:LOW], refs[LOW:]
    for h, high_ref in enumerate(high_refs):
        for k, low_ref in enumerate(low_refs):
            high_ref[k] = low_ref[h]


def restage(blocks):
    highs, rows, cols = blocks[0].shape
    out = jax.ShapeDtypeStruct((LOW, rows, cols), blocks[0].dtype)
    return pl.pallas_call(
        restage_kernel,
        grid=(1,),
        in_specs=[whole(blocks[0].shape)] * LOW,
        out_specs=[whole(out.shape)] * highs,
        out_shape=[out] * highs,
        compiler_params=PARAMS,
        cost_estimate=pl.CostEstimate(
            flops=0, bytes_accessed=4 * LOW * highs * rows * cols, transcendentals=0
        ),
        name="restage",
    )(*blocks)


def start_blocks(slot, list_ref, back_ref, update_ref, sem):
    listed = list_ref.shape[0] // CAP
    for k in range(update_ref.shape[0] // CAP):
        matrix = list_ref[slot * listed + 2 * k]
        place = list_ref[slot * listed + 2 * k + 1]
        pltpu.make_async_copy(back_ref.at[place], update_ref.at[matrix], sem).start()


def wait_blocks(back_ref, update_ref, sem):
    span = pl.ds(0, update_ref.shape[0] // CAP)
    pltpu.make_async_copy(back_ref.at[span], update_ref.at[span], sem).wait()


def early_kernel(list_ref, whole_ref, owned_in, *refs):
    high_refs, (owned_ref, update_ref, back_s, own_sem, sem) = refs[:-5], refs[-5:]
    own = pltpu.make_async_copy(whole_ref, owned_ref.at[CAP - 1], own_sem)
    own.start()
    for h, high_ref in enumerate(high_refs):
        back_s[h * LOW : (h + 1) * LOW] = high_ref[...]
    start_blocks(0, list_ref, back_s, update_ref, sem)
    wait_blocks(back_s, update_ref, sem)
    own.wait()


def store_early(places, mats, matrix, owned, first):
    _, rows, cols = first[0].shape
    return pl.pallas_call(
        early_kernel,
        in_specs=[SMEM, VMEM, ANYWHERE] + [VMEM] * len(first),
        out_specs=[ANYWHERE, ANYWHERE],
        out_shape=[
            jax.ShapeDtypeStruct(owned.shape, jnp.bfloat16),
            jax.ShapeDtypeStruct((mats, rows, cols), jnp.bfloat16),
        ],
        scratch_shapes=[
            pltpu.VMEM((LOW * len(first), rows, cols), jnp.bfloat16),
            pltpu.SemaphoreType.DMA(()),
            pltpu.SemaphoreType.DMA(()),
        ],
        input_output_aliases={2: 0},
        compiler_params=PARAMS,
        cost_estimate=pl.CostEstimate(
            flops=0, bytes_accessed=8 * mats * rows * cols, transcendentals=0
        ),
        name="store_early",
    )(places, matrix, owned, *first)


def late_kernel(list_ref, back_ref, update_in, update_ref, sem):
    start_blocks(1, list_ref, back_ref, update_ref, sem)
    wait_blocks(back_ref, update_ref, sem)


def store_late(places, second, update):
    return pl.pallas_call(
        late_kernel,
        in_specs=[SMEM, VMEM, ANYWHERE],
        out_specs=ANYWHERE,
        out_shape=jax.ShapeDtypeStruct(update.shape, jnp.bfloat16),
        scratch_shapes=[pltpu.SemaphoreType.DMA(())],
        input_output_aliases={2: 0},
        compiler_params=PARAMS,
        cost_estimate=pl.CostEstimate(flops=0, bytes_accessed=4 * second.size, transcendentals=0),
        name="store_late",
    )(places, second, update)


def exchange(blocks, axes, groups=None):
    return lax.all_to_all(
        blocks, axes, split_axis=0, concat_axis=0, tiled=True, axis_index_groups=groups
    )


def swap(block, offset, devices):
    return lax.ppermute(block, AXES, [(d, d ^ offset) for d in range(devices)])


def on_device(gradients, momentum, owner_table):
    row_size = lax.axis_size("dp")
    col_size = lax.axis_size("owner")
    devices = row_size * col_size
    width = col_size // HALVES
    halves = [
        [r * col_size + half * width + c for r in range(row_size) for c in range(width)]
        for half in range(HALVES)
    ]
    first, other, rank = pack(gradients, momentum, owner_table, devices, col_size)
    arrived_first = exchange(first, AXES)
    new_momentum, second, places = update_momentum(
        gradients, momentum, owner_table, other, rank, col_size
    )
    arrived_first, second = lax.optimization_barrier((arrived_first, second))
    arrived_second = exchange(second, AXES)
    owned, *back_first = orthogonalize(0, other, arrived_first, row_size, col_size)
    low = [back_first[0]] + [
        swap(back_first[k], k * col_size, devices) for k in range(1, LOW)
    ]
    high = restage(low)
    _, arrived_second = lax.optimization_barrier((high, arrived_second))
    returned_first = [high[0]] + [
        swap(high[r * width + c], r * LOW * col_size + c, devices)
        for r in range(row_size // LOW)
        for c in range(width)
        if r or c
    ]
    matrix, back_second = orthogonalize(1, other, arrived_second, row_size, col_size)
    returned_first, back_second = lax.optimization_barrier((returned_first, back_second))
    returned_second = exchange(back_second, AXES, halves)
    owned, update = store_early(
        places, owner_table.shape[0], matrix, owned, returned_first
    )
    update = store_late(places, returned_second, update)
    return (new_momentum, update, owned)


def solution(mesh):
    return jax.shard_map(
        on_device,
        mesh=mesh,
        in_specs=(P(None, "dp", "owner"), P(None, "dp", "owner"), P()),
        out_specs=(P(None, "dp", "owner"), P(None, "dp", "owner"), P(("dp", "owner"), None, None)),
        check_vma=False,
    )
```

```python
import functools
import math

import jax
import jax.numpy as jnp
from jax import lax
from jax.experimental import pallas as pl
from jax.experimental.pallas import tpu as pltpu
from jax.sharding import PartitionSpec as P

ITERS = 2
CAP = 2
HALVES = 2
TILES = 2
LOW = 4

coef_a = 3.4445
coef_b = -4.775
coef_c = 2.0315
momentum_beta = 0.95
epsilon = 1e-07

AXES = ("dp", "owner")
MIB = 1024 * 1024
PARAMS = pltpu.CompilerParams(vmem_limit_bytes=24 * MIB)
PACK_PARAMS = pltpu.CompilerParams(vmem_limit_bytes=60 * MIB)
SMEM = pl.BlockSpec(memory_space=pltpu.SMEM)
VMEM = pl.BlockSpec(memory_space=pltpu.VMEM)
ANYWHERE = pl.BlockSpec(memory_space=pl.ANY)


def round_up(value, multiple):
    return -(-value // multiple) * multiple


def whole(shape):
    return pl.BlockSpec(shape, lambda *_: (0,) * len(shape))


def nesterov_of(grad_ref, momentum_ref, j):
    grad = grad_ref[j].astype(jnp.float32)
    new = momentum_beta * momentum_ref[j] + grad
    return new, (grad + momentum_beta * new).astype(jnp.bfloat16)


def order_place(d, col_size):
    width = col_size // HALVES
    col = d % col_size
    return d - col + col % width * HALVES + col // width


def make_plan(col_size, owner_ref, other_ref, rank_ref, count_ref, list_ref, first_list):
    devices, mats = other_ref.shape[0], rank_ref.shape[0]

    def clear(d, _):
        count_ref[d] = 0
        return 0

    lax.fori_loop(0, devices, clear, 0, unroll=8)

    def rank_matrix(i, found):
        owner = owner_ref[i]
        rank = count_ref[owner]
        rank_ref[i] = rank
        count_ref[owner] = rank + 1
        first_list[found] = i
        return found + 1 - rank

    lax.fori_loop(0, mats, rank_matrix, 0, unroll=8)

    def list_device(d, found):
        owns = jnp.minimum(count_ref[d], 1)
        half = (d % col_size) // (col_size // HALVES)
        row = 2 * jnp.where(owns == 1, half, 1 - half) + owns
        place = found[0]
        for k in range(1, 2 * HALVES):
            place = jnp.where(row == k, found[k], place)
        list_ref[row * devices + place] = d
        return tuple(n + jnp.where(row == k, 1, 0) for k, n in enumerate(found))

    found = lax.fori_loop(0, devices, list_device, (0,) * (2 * HALVES), unroll=8)
    for half in range(HALVES):

        def pair(k, _):
            idle = list_ref[2 * half * devices + k]
            other_ref[list_ref[(2 * half + 1) * devices + k]] = idle
            other_ref[idle] = idle
            return 0

        lax.fori_loop(0, found[2 * half + 1], pair, 0)


def pack_kernel(
    chunk, col_size, owner_ref, g_ref, m_ref, first_ref, other_ref, rank_ref,
    count_ref, list_ref, first_list, g_s, m_s, block_s, load_sems, store_sem,
):
    mats = rank_ref.shape[0]
    loads = []
    for k in range(mats // chunk):
        span = pl.ds(k * chunk, chunk)
        loads += [
            pltpu.make_async_copy(g_ref.at[span], g_s.at[span], load_sems.at[0, k]),
            pltpu.make_async_copy(m_ref.at[span], m_s.at[span], load_sems.at[1, k]),
        ]
    for load in loads:
        load.start()
    make_plan(col_size, owner_ref, other_ref, rank_ref, count_ref, list_ref, first_list)
    for load in loads:
        load.wait()
    for k in range(mats // CAP):
        i = first_list[k]
        block_s[k] = nesterov_of(g_s, m_s, i)[1]
        owner = owner_ref[i]
        for host in (owner, other_ref[owner]):
            place = order_place(host, col_size)
            pltpu.make_async_copy(block_s.at[k], first_ref.at[place], store_sem).start()
    pltpu.make_async_copy(first_ref, first_ref, store_sem).wait()


def pack(gradients, momentum, owner_table, devices, col_size):
    mats, rows, cols = gradients.shape
    chunk = 8
    return pl.pallas_call(
        functools.partial(pack_kernel, chunk, col_size),
        in_specs=[SMEM, ANYWHERE, ANYWHERE],
        out_specs=[ANYWHERE, SMEM, SMEM],
        out_shape=[
            pltpu.HBM((devices, rows, cols), jnp.bfloat16),
            jax.ShapeDtypeStruct((devices,), jnp.int32),
            jax.ShapeDtypeStruct((mats,), jnp.int32),
        ],
        scratch_shapes=[
            pltpu.SMEM((devices,), jnp.int32),
            pltpu.SMEM((2 * HALVES * devices,), jnp.int32),
            pltpu.SMEM((mats,), jnp.int32),
            pltpu.VMEM(gradients.shape, gradients.dtype),
            pltpu.VMEM(momentum.shape, momentum.dtype),
            pltpu.VMEM((mats // CAP, rows, cols), jnp.bfloat16),
            pltpu.SemaphoreType.DMA((2, mats // chunk)),
            pltpu.SemaphoreType.DMA(()),
        ],
        compiler_params=PACK_PARAMS,
        cost_estimate=pl.CostEstimate(
            flops=4 * mats * rows * cols, bytes_accessed=8 * mats * rows * cols, transcendentals=0
        ),
        name="pack",
    )(owner_table, gradients, momentum)


def momentum_kernel(
    chunk, col_size, owner_ref, other_ref, rank_ref, g_ref, m_ref, nm_ref, second_ref, list_ref,
    count_ref,
):
    step = pl.program_id(0)
    width = col_size // HALVES
    row, col = lax.axis_index("dp"), lax.axis_index("owner")
    listed = list_ref.shape[0] // CAP

    @pl.when(step == 0)
    def _():
        for slot in range(CAP):
            count_ref[slot] = 0

    for j in range(chunk):
        i = step * chunk + j
        new, nesterov = nesterov_of(g_ref, m_ref, j)
        nm_ref[j] = new
        owner = owner_ref[i]

        @pl.when(rank_ref[i] == 1)
        def _():
            second_ref[order_place(owner, col_size)] = nesterov
            second_ref[order_place(other_ref[owner], col_size)] = nesterov

        near = (owner % col_size) // width == col // width
        host = jnp.where(near, owner, other_ref[owner])
        host_row, host_col = host // col_size, host % width
        offset = host_row ^ row
        high = offset // LOW * width + (host_col ^ (col % width))
        place = jnp.where(
            rank_ref[i] == 0, high * LOW + offset % LOW, host_row * width + host_col
        )
        rank = rank_ref[i]
        entry = count_ref[rank]
        count_ref[rank] = entry + 1
        list_ref[rank * listed + 2 * entry] = i
        list_ref[rank * listed + 2 * entry + 1] = place


def update_momentum(gradients, momentum, owner_table, other, rank, col_size):
    mats, rows, cols = gradients.shape
    devices = other.shape[0]
    chunk = 8
    block = pl.BlockSpec((chunk, rows, cols), lambda i, *_: (i, 0, 0))
    return pl.pallas_call(
        functools.partial(momentum_kernel, chunk, col_size),
        grid_spec=pltpu.PrefetchScalarGridSpec(
            num_scalar_prefetch=3,
            grid=(mats // chunk,),
            in_specs=[block, block],
            out_specs=[block, whole((devices, rows, cols)), SMEM],
            scratch_shapes=[pltpu.SMEM((CAP,), jnp.int32)],
        ),
        out_shape=[
            jax.ShapeDtypeStruct(momentum.shape, jnp.float32),
            jax.ShapeDtypeStruct((devices, rows, cols), jnp.bfloat16),
            jax.ShapeDtypeStruct((2 * mats,), jnp.int32),
        ],
        compiler_params=PARAMS,
        cost_estimate=pl.CostEstimate(
            flops=4 * mats * rows * cols, bytes_accessed=12 * mats * rows * cols, transcendentals=0
        ),
        name="update_momentum",
    )(owner_table, other, rank, gradients, momentum)


def matmul(lhs, rhs, rhs_dim):
    return lax.dot_general(
        lhs, rhs, (((1,), (rhs_dim,)), ((), ())), preferred_element_type=jnp.float32
    )


def sum_rows(values):
    rows, cols = values.shape
    if rows % 8:
        return jnp.sum(values, axis=0, keepdims=True)
    return jnp.sum(values.reshape(rows // 8, 8, cols), axis=0)


def gather_blocks(x_ref, x_s, row_size, col_size):
    _, rows, cols = x_ref.shape
    height = rows * row_size
    total = 0.0
    for r in range(row_size):
        for c in range(col_size):
            block = x_ref[order_place(r * col_size + c, col_size)]
            x_s[r * rows : (r + 1) * rows, c * cols : (c + 1) * cols] = block
            wide = block.astype(jnp.float32)
            total = total + sum_rows(wide * wide)
    x_s[height:, :] = jnp.zeros((x_s.shape[0] - height, x_s.shape[1]), x_s.dtype)
    return 1.0 / (jnp.sqrt(jnp.sum(total, keepdims=True)) + epsilon)


def newton_schulz(height, tiles, inverse, x_s, y_s, gram_s, write):
    padded, width = x_s.shape
    tile = height // tiles
    update_scale = 0.2 * math.sqrt(max(height, width))
    for ref in (y_s, gram_s):
        ref[height:, :] = jnp.zeros((padded - height, ref.shape[1]), ref.dtype)
    for iteration in range(ITERS):
        src = x_s if iteration == 0 else y_s
        for t in range(tiles):
            span = slice(t * tile, (t + 1) * tile)
            gram = matmul(src[span, :], src[...], 1)
            if iteration == 0:
                gram = gram * (inverse * inverse)
            gram_s[span, :] = gram.astype(jnp.bfloat16)
        for t in range(tiles):
            span = slice(t * tile, (t + 1) * tile)
            square = matmul(gram_s[span, :], gram_s[...], 0)
            mixing = coef_b * gram_s[span, :].astype(jnp.float32) + coef_c * square
            combined = coef_a * src[span, :].astype(jnp.float32) + matmul(
                mixing.astype(jnp.bfloat16), src[...], 0
            )
            if iteration == 0:
                combined = combined * inverse
            if iteration + 1 < ITERS:
                y_s[span, :] = combined.astype(jnp.bfloat16)
            else:
                write(t, (update_scale * combined).astype(jnp.bfloat16))


def stage_place(row_offset, col_offset, row_size, width):
    high = row_offset // LOW * width + col_offset
    return row_offset % LOW * (row_size // LOW * width) + high


def ortho_kernel(row_size, col_size, slot, other_ref, x_ref, *refs):
    _, rows, cols = x_ref.shape
    width = col_size // HALVES
    places = row_size * width
    height = rows * row_size
    tiles = TILES
    tile = height // tiles
    if slot:
        whole_ref, out_ref, x_s, y_s, gram_s, back_ref, sems = refs
    else:
        owned_ref, low_refs = refs[0], refs[1 : 1 + LOW]
        x_s, y_s, gram_s, back_ref, sems, whole_ref = refs[1 + LOW :]
    row, col = lax.axis_index("dp"), lax.axis_index("owner")
    me = row * col_size + col
    owns = other_ref[me] != me
    low = col < width
    inverse = gather_blocks(x_ref, x_s, row_size, col_size)

    def copy_out(t):
        if slot:
            span = pl.ds(t * (places // tiles), places // tiles)
            return pltpu.make_async_copy(back_ref.at[span], out_ref.at[span], sems.at[t])
        span = pl.ds(t * tile, tile)
        return pltpu.make_async_copy(whole_ref.at[span], owned_ref.at[slot, span], sems.at[t])

    def write(t, result):
        whole_ref[t * tile : (t + 1) * tile, :] = jnp.where(owns, result, jnp.zeros_like(result))
        for j in range(row_size // tiles):
            block = result[j * rows : (j + 1) * rows, :]
            r = t * (row_size // tiles) + j
            for c in range(width):
                if slot:
                    place = r * width + c
                else:
                    place = stage_place(r ^ row, c ^ (col % width), row_size, width)
                back_ref[place] = jnp.where(
                    low,
                    block[:, c * cols : (c + 1) * cols],
                    block[:, (c + width) * cols : (c + width + 1) * cols],
                )
        copy_out(t).start()

    newton_schulz(height, tiles, inverse, x_s, y_s, gram_s, write)
    if not slot:
        for k in range(LOW):
            low_refs[k][...] = back_ref[k * places // LOW : (k + 1) * places // LOW]
    for t in range(tiles):
        copy_out(t).wait()


def orthogonalize(slot, other, arrived, row_size, col_size):
    devices, rows, cols = arrived.shape
    height, width = rows * row_size, cols * col_size
    padded = round_up(height, 256)
    places = devices // HALVES
    scratch_shapes = [
        pltpu.VMEM((padded, width), jnp.bfloat16),
        pltpu.VMEM((padded, width), jnp.bfloat16),
        pltpu.VMEM((padded, padded), jnp.bfloat16),
        pltpu.VMEM((places, rows, cols), jnp.bfloat16),
        pltpu.SemaphoreType.DMA((TILES,)),
    ]
    if slot:
        out_specs = [VMEM, ANYWHERE]
        out = [(height, width), (places, rows, cols)]
    else:
        out_specs = [ANYWHERE] + [VMEM] * LOW
        out = [(CAP, height, width)] + [(places // LOW, rows, cols)] * LOW
        scratch_shapes.append(pltpu.VMEM((height, width), jnp.bfloat16))
    return pl.pallas_call(
        functools.partial(ortho_kernel, row_size, col_size, slot),
        in_specs=[SMEM, VMEM],
        out_specs=out_specs,
        out_shape=[
            pltpu.HBM(shape, jnp.bfloat16)
            if spec is ANYWHERE
            else jax.ShapeDtypeStruct(shape, jnp.bfloat16)
            for spec, shape in zip(out_specs, out)
        ],
        scratch_shapes=scratch_shapes,
        compiler_params=PARAMS,
        cost_estimate=pl.CostEstimate(
            flops=2 * ITERS * padded * padded * (2 * width + padded),
            bytes_accessed=6 * padded * width,
            transcendentals=0,
        ),
        name="orthogonalize",
    )(other, arrived)


def restage_kernel(*refs):
    low_refs, high_refs = refs[:LOW], refs[LOW:]
    for h, high_ref in enumerate(high_refs):
        for k, low_ref in enumerate(low_refs):
            high_ref[k] = low_ref[h]


def restage(blocks):
    highs, rows, cols = blocks[0].shape
    out = jax.ShapeDtypeStruct((LOW, rows, cols), blocks[0].dtype)
    return pl.pallas_call(
        restage_kernel,
        grid=(1,),
        in_specs=[whole(blocks[0].shape)] * LOW,
        out_specs=[whole(out.shape)] * highs,
        out_shape=[out] * highs,
        compiler_params=PARAMS,
        cost_estimate=pl.CostEstimate(
            flops=0, bytes_accessed=4 * LOW * highs * rows * cols, transcendentals=0
        ),
        name="restage",
    )(*blocks)


def start_blocks(slot, list_ref, back_ref, update_ref, sem):
    listed = list_ref.shape[0] // CAP
    for k in range(update_ref.shape[0] // CAP):
        matrix = list_ref[slot * listed + 2 * k]
        place = list_ref[slot * listed + 2 * k + 1]
        pltpu.make_async_copy(back_ref.at[place], update_ref.at[matrix], sem).start()


def wait_blocks(back_ref, update_ref, sem):
    span = pl.ds(0, update_ref.shape[0] // CAP)
    pltpu.make_async_copy(back_ref.at[span], update_ref.at[span], sem).wait()


def early_kernel(list_ref, whole_ref, owned_in, *refs):
    high_refs, (owned_ref, update_ref, back_s, own_sem, sem) = refs[:-5], refs[-5:]
    own = pltpu.make_async_copy(whole_ref, owned_ref.at[CAP - 1], own_sem)
    own.start()
    for h, high_ref in enumerate(high_refs):
        back_s[h * LOW : (h + 1) * LOW] = high_ref[...]
    start_blocks(0, list_ref, back_s, update_ref, sem)
    wait_blocks(back_s, update_ref, sem)
    own.wait()


def store_early(places, mats, matrix, owned, first):
    _, rows, cols = first[0].shape
    return pl.pallas_call(
        early_kernel,
        in_specs=[SMEM, VMEM, ANYWHERE] + [VMEM] * len(first),
        out_specs=[ANYWHERE, ANYWHERE],
        out_shape=[
            jax.ShapeDtypeStruct(owned.shape, jnp.bfloat16),
            jax.ShapeDtypeStruct((mats, rows, cols), jnp.bfloat16),
        ],
        scratch_shapes=[
            pltpu.VMEM((LOW * len(first), rows, cols), jnp.bfloat16),
            pltpu.SemaphoreType.DMA(()),
            pltpu.SemaphoreType.DMA(()),
        ],
        input_output_aliases={2: 0},
        compiler_params=PARAMS,
        cost_estimate=pl.CostEstimate(
            flops=0, bytes_accessed=8 * mats * rows * cols, transcendentals=0
        ),
        name="store_early",
    )(places, matrix, owned, *first)


def late_kernel(list_ref, back_ref, update_in, update_ref, sem):
    start_blocks(1, list_ref, back_ref, update_ref, sem)
    wait_blocks(back_ref, update_ref, sem)


def store_late(places, second, update):
    return pl.pallas_call(
        late_kernel,
        in_specs=[SMEM, VMEM, ANYWHERE],
        out_specs=ANYWHERE,
        out_shape=jax.ShapeDtypeStruct(update.shape, jnp.bfloat16),
        scratch_shapes=[pltpu.SemaphoreType.DMA(())],
        input_output_aliases={2: 0},
        compiler_params=PARAMS,
        cost_estimate=pl.CostEstimate(flops=0, bytes_accessed=4 * second.size, transcendentals=0),
        name="store_late",
    )(places, second, update)


def exchange(blocks, axes, groups=None):
    return lax.all_to_all(
        blocks, axes, split_axis=0, concat_axis=0, tiled=True, axis_index_groups=groups
    )


def swap(block, offset, devices):
    return lax.ppermute(block, AXES, [(d, d ^ offset) for d in range(devices)])


def on_device(gradients, momentum, owner_table):
    row_size = lax.axis_size("dp")
    col_size = lax.axis_size("owner")
    devices = row_size * col_size
    width = col_size // HALVES
    halves = [
        [r * col_size + half * width + c for r in range(row_size) for c in range(width)]
        for half in range(HALVES)
    ]
    first, other, rank = pack(gradients, momentum, owner_table, devices, col_size)
    order = sorted(range(devices), key=lambda d: order_place(d, col_size))
    arrived_first = exchange(first, AXES, [order])
    new_momentum, second, places = update_momentum(
        gradients, momentum, owner_table, other, rank, col_size
    )
    arrived_first, second = lax.optimization_barrier((arrived_first, second))
    arrived_second = exchange(second, AXES, [order])
    owned, *back_first = orthogonalize(0, other, arrived_first, row_size, col_size)
    low = [back_first[0]] + [
        swap(back_first[k], k * col_size, devices) for k in range(1, LOW)
    ]
    high = restage(low)
    _, arrived_second = lax.optimization_barrier((high, arrived_second))
    returned_first = [high[0]] + [
        swap(high[r * width + c], r * LOW * col_size + c, devices)
        for r in range(row_size // LOW)
        for c in range(width)
        if r or c
    ]
    matrix, back_second = orthogonalize(1, other, arrived_second, row_size, col_size)
    returned_first, back_second = lax.optimization_barrier((returned_first, back_second))
    returned_second = exchange(back_second, AXES, halves)
    owned, update = store_early(
        places, owner_table.shape[0], matrix, owned, returned_first
    )
    update = store_late(places, returned_second, update)
    return (new_momentum, update, owned)


def solution(mesh):
    return jax.shard_map(
        on_device,
        mesh=mesh,
        in_specs=(P(None, "dp", "owner"), P(None, "dp", "owner"), P()),
        out_specs=(P(None, "dp", "owner"), P(None, "dp", "owner"), P(("dp", "owner"), None, None)),
        check_vma=False,
    )
```

```python
import functools
import math

import jax
import jax.numpy as jnp
from jax import lax
from jax.experimental import pallas as pl
from jax.experimental.pallas import tpu as pltpu
from jax.sharding import PartitionSpec as P

ITERS = 2
CAP = 2
HALVES = 2
TILES = 2
LOW = 4

coef_a = 3.4445
coef_b = -4.775
coef_c = 2.0315
momentum_beta = 0.95
epsilon = 1e-07

AXES = ("dp", "owner")
MIB = 1024 * 1024
PARAMS = pltpu.CompilerParams(vmem_limit_bytes=24 * MIB)
PACK_PARAMS = pltpu.CompilerParams(vmem_limit_bytes=60 * MIB)
SMEM = pl.BlockSpec(memory_space=pltpu.SMEM)
VMEM = pl.BlockSpec(memory_space=pltpu.VMEM)
ANYWHERE = pl.BlockSpec(memory_space=pl.ANY)


def round_up(value, multiple):
    return -(-value // multiple) * multiple


def whole(shape):
    return pl.BlockSpec(shape, lambda *_: (0,) * len(shape))


def nesterov_of(grad_ref, momentum_ref, j):
    grad = grad_ref[j].astype(jnp.float32)
    new = momentum_beta * momentum_ref[j] + grad
    return new, (grad + momentum_beta * new).astype(jnp.bfloat16)


def make_plan(col_size, owner_ref, other_ref, rank_ref, count_ref, list_ref, first_list):
    devices, mats = other_ref.shape[0], rank_ref.shape[0]

    def clear(d, _):
        count_ref[d] = 0
        return 0

    lax.fori_loop(0, devices, clear, 0, unroll=8)

    def rank_matrix(i, found):
        owner = owner_ref[i]
        rank = count_ref[owner]
        rank_ref[i] = rank
        count_ref[owner] = rank + 1
        first_list[found] = i
        return found + 1 - rank

    lax.fori_loop(0, mats, rank_matrix, 0, unroll=8)

    def list_device(d, found):
        owns = jnp.minimum(count_ref[d], 1)
        half = (d % col_size) // (col_size // HALVES)
        row = 2 * jnp.where(owns == 1, half, 1 - half) + owns
        place = found[0]
        for k in range(1, 2 * HALVES):
            place = jnp.where(row == k, found[k], place)
        list_ref[row * devices + place] = d
        return tuple(n + jnp.where(row == k, 1, 0) for k, n in enumerate(found))

    found = lax.fori_loop(0, devices, list_device, (0,) * (2 * HALVES), unroll=8)
    for half in range(HALVES):

        def pair(k, _):
            idle = list_ref[2 * half * devices + k]
            other_ref[list_ref[(2 * half + 1) * devices + k]] = idle
            other_ref[idle] = idle
            return 0

        lax.fori_loop(0, found[2 * half + 1], pair, 0)


def pack_kernel(
    chunk, col_size, owner_ref, g_ref, m_ref, first_ref, other_ref, rank_ref,
    count_ref, list_ref, first_list, g_s, m_s, sems,
):
    mats = rank_ref.shape[0]

    loads = []
    for k in range(mats // chunk):
        span = pl.ds(k * chunk, chunk)
        loads += [
            pltpu.make_async_copy(g_ref.at[span], g_s.at[span], sems.at[0, k]),
            pltpu.make_async_copy(m_ref.at[span], m_s.at[span], sems.at[1, k]),
        ]
    for load in loads:
        load.start()
    make_plan(col_size, owner_ref, other_ref, rank_ref, count_ref, list_ref, first_list)
    for load in loads:
        load.wait()
    for k in range(mats // CAP):
        i = first_list[k]
        _, nesterov = nesterov_of(g_s, m_s, i)
        first_ref[owner_ref[i]] = nesterov
        first_ref[other_ref[owner_ref[i]]] = nesterov


def pack(gradients, momentum, owner_table, devices, col_size):
    mats, rows, cols = gradients.shape
    chunk = 8
    return pl.pallas_call(
        functools.partial(pack_kernel, chunk, col_size),
        grid_spec=pltpu.PrefetchScalarGridSpec(
            num_scalar_prefetch=1,
            grid=(1,),
            in_specs=[ANYWHERE, ANYWHERE],
            out_specs=[whole((devices, rows, cols)), SMEM, SMEM],
            scratch_shapes=[
                pltpu.SMEM((devices,), jnp.int32),
                pltpu.SMEM((2 * HALVES * devices,), jnp.int32),
                pltpu.SMEM((mats,), jnp.int32),
                pltpu.VMEM(gradients.shape, gradients.dtype),
                pltpu.VMEM(momentum.shape, momentum.dtype),
                pltpu.SemaphoreType.DMA((2, mats // chunk)),
            ],
        ),
        out_shape=[
            jax.ShapeDtypeStruct((devices, rows, cols), jnp.bfloat16),
            jax.ShapeDtypeStruct((devices,), jnp.int32),
            jax.ShapeDtypeStruct((mats,), jnp.int32),
        ],
        compiler_params=PACK_PARAMS,
        cost_estimate=pl.CostEstimate(
            flops=4 * mats * rows * cols, bytes_accessed=8 * mats * rows * cols, transcendentals=0
        ),
        name="pack",
    )(owner_table, gradients, momentum)


def momentum_kernel(
    chunk, col_size, owner_ref, other_ref, rank_ref, g_ref, m_ref, nm_ref, second_ref, list_ref,
    count_ref,
):
    step = pl.program_id(0)
    width = col_size // HALVES
    row, col = lax.axis_index("dp"), lax.axis_index("owner")
    listed = list_ref.shape[0] // CAP

    @pl.when(step == 0)
    def _():
        for slot in range(CAP):
            count_ref[slot] = 0

    for j in range(chunk):
        i = step * chunk + j
        new, nesterov = nesterov_of(g_ref, m_ref, j)
        nm_ref[j] = new
        owner = owner_ref[i]

        @pl.when(rank_ref[i] == 1)
        def _():
            second_ref[owner] = nesterov
            second_ref[other_ref[owner]] = nesterov

        near = (owner % col_size) // width == col // width
        host = jnp.where(near, owner, other_ref[owner])
        host_row, host_col = host // col_size, host % width
        offset = host_row ^ row
        high = offset // LOW * width + (host_col ^ (col % width))
        place = jnp.where(
            rank_ref[i] == 0, high * LOW + offset % LOW, host_row * width + host_col
        )
        rank = rank_ref[i]
        entry = count_ref[rank]
        count_ref[rank] = entry + 1
        list_ref[rank * listed + 2 * entry] = i
        list_ref[rank * listed + 2 * entry + 1] = place


def update_momentum(gradients, momentum, owner_table, other, rank, col_size):
    mats, rows, cols = gradients.shape
    devices = other.shape[0]
    chunk = 8
    block = pl.BlockSpec((chunk, rows, cols), lambda i, *_: (i, 0, 0))
    return pl.pallas_call(
        functools.partial(momentum_kernel, chunk, col_size),
        grid_spec=pltpu.PrefetchScalarGridSpec(
            num_scalar_prefetch=3,
            grid=(mats // chunk,),
            in_specs=[block, block],
            out_specs=[block, whole((devices, rows, cols)), SMEM],
            scratch_shapes=[pltpu.SMEM((CAP,), jnp.int32)],
        ),
        out_shape=[
            jax.ShapeDtypeStruct(momentum.shape, jnp.float32),
            jax.ShapeDtypeStruct((devices, rows, cols), jnp.bfloat16),
            jax.ShapeDtypeStruct((2 * mats,), jnp.int32),
        ],
        compiler_params=PARAMS,
        cost_estimate=pl.CostEstimate(
            flops=4 * mats * rows * cols, bytes_accessed=12 * mats * rows * cols, transcendentals=0
        ),
        name="update_momentum",
    )(owner_table, other, rank, gradients, momentum)


def matmul(lhs, rhs, rhs_dim):
    return lax.dot_general(
        lhs, rhs, (((1,), (rhs_dim,)), ((), ())), preferred_element_type=jnp.float32
    )


def sum_rows(values):
    rows, cols = values.shape
    if rows % 8:
        return jnp.sum(values, axis=0, keepdims=True)
    return jnp.sum(values.reshape(rows // 8, 8, cols), axis=0)


def gather_blocks(x_ref, x_s, row_size, col_size):
    _, rows, cols = x_ref.shape
    height = rows * row_size
    total = 0.0
    for r in range(row_size):
        for c in range(col_size):
            block = x_ref[r * col_size + c]
            x_s[r * rows : (r + 1) * rows, c * cols : (c + 1) * cols] = block
            wide = block.astype(jnp.float32)
            total = total + sum_rows(wide * wide)
    x_s[height:, :] = jnp.zeros((x_s.shape[0] - height, x_s.shape[1]), x_s.dtype)
    return 1.0 / (jnp.sqrt(jnp.sum(total, keepdims=True)) + epsilon)


def update_scale(height, width):
    return 0.2 * math.sqrt(max(height, width))


def newton_schulz(height, inverse, x_s, y_s, gram_s, finish):
    padded = x_s.shape[0]
    tile = height // TILES
    for ref in (y_s, gram_s):
        ref[height:, :] = jnp.zeros((padded - height, ref.shape[1]), ref.dtype)
    for iteration in range(ITERS):
        src = x_s if iteration == 0 else y_s
        for t in range(TILES):
            span = slice(t * tile, (t + 1) * tile)
            gram = matmul(src[span, :], src[...], 1)
            if iteration == 0:
                gram = gram * (inverse * inverse)
            gram_s[span, :] = gram.astype(jnp.bfloat16)
        for t in range(TILES):
            span = slice(t * tile, (t + 1) * tile)
            square = matmul(gram_s[span, :], gram_s[...], 0)
            mixing = coef_b * gram_s[span, :].astype(jnp.float32) + coef_c * square
            mixing = mixing.astype(jnp.bfloat16)
            if iteration + 1 < ITERS:
                combined = combine(src, span, slice(None), mixing)
                if iteration == 0:
                    combined = combined * inverse
                y_s[span, :] = combined.astype(jnp.bfloat16)
            else:
                finish(t, span, mixing)


def combine(src, span, columns, mixing):
    return coef_a * src[span, columns].astype(jnp.float32) + matmul(mixing, src[:, columns], 0)


def stage_place(row_offset, col_offset, row_size, width):
    high = row_offset // LOW * width + col_offset
    return row_offset % LOW * (row_size // LOW * width) + high


def ortho_kernel(row_size, col_size, slot, other_ref, x_ref, *refs):
    _, rows, cols = x_ref.shape
    width = col_size // HALVES
    places = row_size * width
    height = rows * row_size
    tile = height // TILES
    if slot:
        y_s, mix_ref, out_ref, x_s, gram_s, back_ref, sems = refs
    else:
        owned_ref, low_refs = refs[0], refs[1 : 1 + LOW]
        x_s, gram_s, back_ref, sems, y_s, whole_ref = refs[1 + LOW :]
    row, col = lax.axis_index("dp"), lax.axis_index("owner")
    me = row * col_size + col
    inverse = gather_blocks(x_ref, x_s, row_size, col_size)
    scale = update_scale(height, cols * col_size)

    def copy_out(t):
        if slot:
            span = pl.ds(t * (places // TILES), places // TILES)
            return pltpu.make_async_copy(back_ref.at[span], out_ref.at[span], sems.at[t])
        span = pl.ds(t * tile, tile)
        return pltpu.make_async_copy(whole_ref.at[span], owned_ref.at[slot, span], sems.at[t])

    def finish(t, span, mixing):
        if slot:
            mix_ref[span, :] = mixing
            near = pl.ds(pl.multiple_of(col // width * (width * cols), width * cols), width * cols)
            result = (scale * combine(y_s, span, near, mixing)).astype(jnp.bfloat16)
        else:
            result = (scale * combine(y_s, span, slice(None), mixing)).astype(jnp.bfloat16)
            owns = other_ref[me] != me
            whole_ref[span, :] = jnp.where(owns, result, jnp.zeros_like(result))
            half = width * cols
            result = jnp.where(col < width, result[:, :half], result[:, half:])
        for j in range(row_size // TILES):
            r = t * (row_size // TILES) + j
            for c in range(width):
                if slot:
                    place = r * width + c
                else:
                    place = stage_place(r ^ row, c ^ (col % width), row_size, width)
                back_ref[place] = result[
                    j * rows : (j + 1) * rows, c * cols : (c + 1) * cols
                ]
        copy_out(t).start()

    newton_schulz(height, inverse, x_s, y_s, gram_s, finish)
    if not slot:
        for k in range(LOW):
            low_refs[k][...] = back_ref[k * places // LOW : (k + 1) * places // LOW]
    for t in range(TILES):
        copy_out(t).wait()


def orthogonalize(slot, other, arrived, row_size, col_size):
    devices, rows, cols = arrived.shape
    height, width = rows * row_size, cols * col_size
    padded = round_up(height, 256)
    places = devices // HALVES
    scratch_shapes = [
        pltpu.VMEM((padded, width), jnp.bfloat16),
        pltpu.VMEM((padded, padded), jnp.bfloat16),
        pltpu.VMEM((places, rows, cols), jnp.bfloat16),
        pltpu.SemaphoreType.DMA((TILES,)),
    ]
    if slot:
        out_specs = [VMEM, VMEM, ANYWHERE]
        out = [(padded, width), (height, padded), (places, rows, cols)]
    else:
        out_specs = [ANYWHERE] + [VMEM] * LOW
        out = [(CAP, height, width)] + [(places // LOW, rows, cols)] * LOW
        scratch_shapes += [
            pltpu.VMEM((padded, width), jnp.bfloat16),
            pltpu.VMEM((height, width), jnp.bfloat16),
        ]
    return pl.pallas_call(
        functools.partial(ortho_kernel, row_size, col_size, slot),
        in_specs=[SMEM, VMEM],
        out_specs=out_specs,
        out_shape=[
            pltpu.HBM(shape, jnp.bfloat16)
            if spec is ANYWHERE
            else jax.ShapeDtypeStruct(shape, jnp.bfloat16)
            for spec, shape in zip(out_specs, out)
        ],
        scratch_shapes=scratch_shapes,
        compiler_params=PARAMS,
        cost_estimate=pl.CostEstimate(
            flops=2 * ITERS * padded * padded * (2 * width + padded),
            bytes_accessed=6 * padded * width,
            transcendentals=0,
        ),
        name="orthogonalize",
    )(other, arrived)


def restage_kernel(*refs):
    low_refs, high_refs = refs[:LOW], refs[LOW:]
    for h, high_ref in enumerate(high_refs):
        for k, low_ref in enumerate(low_refs):
            high_ref[k] = low_ref[h]


def restage(blocks):
    highs, rows, cols = blocks[0].shape
    out = jax.ShapeDtypeStruct((LOW, rows, cols), blocks[0].dtype)
    return pl.pallas_call(
        restage_kernel,
        grid=(1,),
        in_specs=[whole(blocks[0].shape)] * LOW,
        out_specs=[whole(out.shape)] * highs,
        out_shape=[out] * highs,
        compiler_params=PARAMS,
        cost_estimate=pl.CostEstimate(
            flops=0, bytes_accessed=4 * LOW * highs * rows * cols, transcendentals=0
        ),
        name="restage",
    )(*blocks)


def start_blocks(slot, list_ref, back_ref, update_ref, sem):
    listed = list_ref.shape[0] // CAP
    for k in range(update_ref.shape[0] // CAP):
        matrix = list_ref[slot * listed + 2 * k]
        place = list_ref[slot * listed + 2 * k + 1]
        pltpu.make_async_copy(back_ref.at[place], update_ref.at[matrix], sem).start()


def wait_blocks(back_ref, update_ref, sem):
    span = pl.ds(0, update_ref.shape[0] // CAP)
    pltpu.make_async_copy(back_ref.at[span], update_ref.at[span], sem).wait()


def early_kernel(col_size, list_ref, other_ref, y_ref, mix_ref, owned_in, *refs):
    high_refs, (owned_ref, update_ref, back_s, whole_s, own_sems, sem) = refs[:-6], refs[-6:]
    for h, high_ref in enumerate(high_refs):
        back_s[h * LOW : (h + 1) * LOW] = high_ref[...]
    start_blocks(0, list_ref, back_s, update_ref, sem)
    me = lax.axis_index("dp") * col_size + lax.axis_index("owner")
    owns = other_ref[me] != me
    height, width = whole_s.shape
    tile = height // TILES
    copies = []
    for t in range(TILES):
        span = slice(t * tile, (t + 1) * tile)
        result = combine(y_ref, span, slice(None), mix_ref[span, :])
        result = (update_scale(height, width) * result).astype(jnp.bfloat16)
        whole_s[span, :] = jnp.where(owns, result, jnp.zeros_like(result))
        rows = pl.ds(t * tile, tile)
        copies.append(
            pltpu.make_async_copy(whole_s.at[rows], owned_ref.at[CAP - 1, rows], own_sems.at[t])
        )
        copies[-1].start()
    for copy in copies:
        copy.wait()
    wait_blocks(back_s, update_ref, sem)


def store_early(places, other, current, mixing, owned, first, mats, col_size):
    _, rows, cols = first[0].shape
    _, height, width = owned.shape
    return pl.pallas_call(
        functools.partial(early_kernel, col_size),
        in_specs=[SMEM, SMEM, VMEM, VMEM, ANYWHERE] + [VMEM] * len(first),
        out_specs=[ANYWHERE, ANYWHERE],
        out_shape=[
            jax.ShapeDtypeStruct(owned.shape, jnp.bfloat16),
            jax.ShapeDtypeStruct((mats, rows, cols), jnp.bfloat16),
        ],
        scratch_shapes=[
            pltpu.VMEM((LOW * len(first), rows, cols), jnp.bfloat16),
            pltpu.VMEM((height, width), jnp.bfloat16),
            pltpu.SemaphoreType.DMA((TILES,)),
            pltpu.SemaphoreType.DMA(()),
        ],
        input_output_aliases={4: 0},
        compiler_params=PARAMS,
        cost_estimate=pl.CostEstimate(
            flops=2 * height * height * width,
            bytes_accessed=8 * mats * rows * cols,
            transcendentals=0,
        ),
        name="store_early",
    )(places, other, current, mixing, owned, *first)


def late_kernel(list_ref, back_ref, update_in, update_ref, sem):
    start_blocks(1, list_ref, back_ref, update_ref, sem)
    wait_blocks(back_ref, update_ref, sem)


def store_late(places, second, update):
    return pl.pallas_call(
        late_kernel,
        in_specs=[SMEM, VMEM, ANYWHERE],
        out_specs=ANYWHERE,
        out_shape=jax.ShapeDtypeStruct(update.shape, jnp.bfloat16),
        scratch_shapes=[pltpu.SemaphoreType.DMA(())],
        input_output_aliases={2: 0},
        compiler_params=PARAMS,
        cost_estimate=pl.CostEstimate(flops=0, bytes_accessed=4 * second.size, transcendentals=0),
        name="store_late",
    )(places, second, update)


def exchange(blocks, axes, groups=None):
    return lax.all_to_all(
        blocks, axes, split_axis=0, concat_axis=0, tiled=True, axis_index_groups=groups
    )


def swap(block, offset, devices):
    return lax.ppermute(block, AXES, [(d, d ^ offset) for d in range(devices)])


def on_device(gradients, momentum, owner_table):
    row_size = lax.axis_size("dp")
    col_size = lax.axis_size("owner")
    devices = row_size * col_size
    width = col_size // HALVES
    halves = [
        [r * col_size + half * width + c for r in range(row_size) for c in range(width)]
        for half in range(HALVES)
    ]
    first, other, rank = pack(gradients, momentum, owner_table, devices, col_size)
    arrived_first = exchange(first, AXES)
    new_momentum, second, places = update_momentum(
        gradients, momentum, owner_table, other, rank, col_size
    )
    arrived_first, second = lax.optimization_barrier((arrived_first, second))
    arrived_second = exchange(second, AXES)
    owned, *back_first = orthogonalize(0, other, arrived_first, row_size, col_size)
    low = [back_first[0]] + [
        swap(back_first[k], k * col_size, devices) for k in range(1, LOW)
    ]
    high = restage(low)
    _, arrived_second = lax.optimization_barrier((high, arrived_second))
    returned_first = [high[0]] + [
        swap(high[r * width + c], r * LOW * col_size + c, devices)
        for r in range(row_size // LOW)
        for c in range(width)
        if r or c
    ]
    current, mixing, back_second = orthogonalize(1, other, arrived_second, row_size, col_size)
    returned_first, back_second = lax.optimization_barrier((returned_first, back_second))
    returned_second = exchange(back_second, AXES, halves)
    owned, update = store_early(
        places, other, current, mixing, owned, returned_first, owner_table.shape[0], col_size
    )
    update = store_late(places, returned_second, update)
    return (new_momentum, update, owned)


def solution(mesh):
    return jax.shard_map(
        on_device,
        mesh=mesh,
        in_specs=(P(None, "dp", "owner"), P(None, "dp", "owner"), P()),
        out_specs=(P(None, "dp", "owner"), P(None, "dp", "owner"), P(("dp", "owner"), None, None)),
        check_vma=False,
    )
```

```python
import functools
import math

import jax
import jax.numpy as jnp
from jax import lax
from jax.experimental import pallas as pl
from jax.experimental.pallas import tpu as pltpu
from jax.sharding import PartitionSpec as P

ITERS = 2
CAP = 2
HALVES = 2
TILES = 2
LOW = 4

coef_a = 3.4445
coef_b = -4.775
coef_c = 2.0315
momentum_beta = 0.95
epsilon = 1e-07

AXES = ("dp", "owner")
MIB = 1024 * 1024
PARAMS = pltpu.CompilerParams(vmem_limit_bytes=24 * MIB)
PACK_PARAMS = pltpu.CompilerParams(vmem_limit_bytes=60 * MIB)
SMEM = pl.BlockSpec(memory_space=pltpu.SMEM)
VMEM = pl.BlockSpec(memory_space=pltpu.VMEM)
ANYWHERE = pl.BlockSpec(memory_space=pl.ANY)


def round_up(value, multiple):
    return -(-value // multiple) * multiple


def whole(shape):
    return pl.BlockSpec(shape, lambda *_: (0,) * len(shape))


def nesterov_of(grad_ref, momentum_ref, j):
    grad = grad_ref[j].astype(jnp.float32)
    new = momentum_beta * momentum_ref[j] + grad
    return new, (grad + momentum_beta * new).astype(jnp.bfloat16)


def make_plan(col_size, owner_ref, other_ref, rank_ref, count_ref, list_ref):
    devices, mats = other_ref.shape[0], rank_ref.shape[0]

    def clear(d, _):
        count_ref[d] = 0
        return 0

    lax.fori_loop(0, devices, clear, 0, unroll=8)

    def rank_matrix(i, _):
        owner = owner_ref[i]
        rank = count_ref[owner]
        rank_ref[i] = rank
        count_ref[owner] = rank + 1
        return 0

    lax.fori_loop(0, mats, rank_matrix, 0, unroll=8)

    def list_device(d, found):
        owns = jnp.minimum(count_ref[d], 1)
        half = (d % col_size) // (col_size // HALVES)
        row = 2 * jnp.where(owns == 1, half, 1 - half) + owns
        place = found[0]
        for k in range(1, 2 * HALVES):
            place = jnp.where(row == k, found[k], place)
        list_ref[row * devices + place] = d
        return tuple(n + jnp.where(row == k, 1, 0) for k, n in enumerate(found))

    found = lax.fori_loop(0, devices, list_device, (0,) * (2 * HALVES), unroll=8)
    for half in range(HALVES):

        def pair(k, _):
            idle = list_ref[2 * half * devices + k]
            other_ref[list_ref[(2 * half + 1) * devices + k]] = idle
            other_ref[idle] = idle
            return 0

        lax.fori_loop(0, found[2 * half + 1], pair, 0)


def pack_kernel(
    chunk, col_size, owner_ref, g_ref, m_ref, first_ref, other_ref, rank_ref,
    count_ref, list_ref, g_s, m_s, sems,
):
    mats = rank_ref.shape[0]

    def loads(k):
        span = pl.ds(k * chunk, chunk)
        return (
            pltpu.make_async_copy(g_ref.at[span], g_s.at[span], sems.at[0, k]),
            pltpu.make_async_copy(m_ref.at[span], m_s.at[span], sems.at[1, k]),
        )

    for k in range(mats // chunk):
        for load in loads(k):
            load.start()
    make_plan(col_size, owner_ref, other_ref, rank_ref, count_ref, list_ref)
    for k in range(mats // chunk):
        for load in loads(k):
            load.wait()
        for i in range(k * chunk, (k + 1) * chunk):

            @pl.when(rank_ref[i] == 0)
            def _():
                nesterov = nesterov_of(g_s, m_s, i)[1]
                first_ref[owner_ref[i]] = nesterov
                first_ref[other_ref[owner_ref[i]]] = nesterov


def pack(gradients, momentum, owner_table, devices, col_size):
    mats, rows, cols = gradients.shape
    chunk = 8
    return pl.pallas_call(
        functools.partial(pack_kernel, chunk, col_size),
        grid_spec=pltpu.PrefetchScalarGridSpec(
            num_scalar_prefetch=1,
            grid=(1,),
            in_specs=[ANYWHERE, ANYWHERE],
            out_specs=[whole((devices, rows, cols)), SMEM, SMEM],
            scratch_shapes=[
                pltpu.SMEM((devices,), jnp.int32),
                pltpu.SMEM((2 * HALVES * devices,), jnp.int32),
                pltpu.VMEM(gradients.shape, gradients.dtype),
                pltpu.VMEM(momentum.shape, momentum.dtype),
                pltpu.SemaphoreType.DMA((2, mats // chunk)),
            ],
        ),
        out_shape=[
            jax.ShapeDtypeStruct((devices, rows, cols), jnp.bfloat16),
            jax.ShapeDtypeStruct((devices,), jnp.int32),
            jax.ShapeDtypeStruct((mats,), jnp.int32),
        ],
        compiler_params=PACK_PARAMS,
        cost_estimate=pl.CostEstimate(
            flops=4 * mats * rows * cols, bytes_accessed=8 * mats * rows * cols, transcendentals=0
        ),
        name="pack",
    )(owner_table, gradients, momentum)


def momentum_kernel(
    chunk, col_size, owner_ref, other_ref, rank_ref, g_ref, m_ref, nm_ref, second_ref, list_ref,
    count_ref,
):
    step = pl.program_id(0)
    width = col_size // HALVES
    row, col = lax.axis_index("dp"), lax.axis_index("owner")
    listed = list_ref.shape[0] // CAP

    @pl.when(step == 0)
    def _():
        for slot in range(CAP):
            count_ref[slot] = 0

    for j in range(chunk):
        i = step * chunk + j
        new, nesterov = nesterov_of(g_ref, m_ref, j)
        nm_ref[j] = new
        owner = owner_ref[i]

        @pl.when(rank_ref[i] == 1)
        def _():
            second_ref[owner] = nesterov
            second_ref[other_ref[owner]] = nesterov

        near = (owner % col_size) // width == col // width
        host = jnp.where(near, owner, other_ref[owner])
        host_row, host_col = host // col_size, host % width
        offset = host_row ^ row
        high = offset // LOW * width + (host_col ^ (col % width))
        place = jnp.where(
            rank_ref[i] == 0, high * LOW + offset % LOW, host_row * width + host_col
        )
        rank = rank_ref[i]
        entry = count_ref[rank]
        count_ref[rank] = entry + 1
        list_ref[rank * listed + 2 * entry] = i
        list_ref[rank * listed + 2 * entry + 1] = place


def update_momentum(gradients, momentum, owner_table, other, rank, col_size):
    mats, rows, cols = gradients.shape
    devices = other.shape[0]
    chunk = 8
    block = pl.BlockSpec((chunk, rows, cols), lambda i, *_: (i, 0, 0))
    return pl.pallas_call(
        functools.partial(momentum_kernel, chunk, col_size),
        grid_spec=pltpu.PrefetchScalarGridSpec(
            num_scalar_prefetch=3,
            grid=(mats // chunk,),
            in_specs=[block, block],
            out_specs=[block, whole((devices, rows, cols)), SMEM],
            scratch_shapes=[pltpu.SMEM((CAP,), jnp.int32)],
        ),
        out_shape=[
            jax.ShapeDtypeStruct(momentum.shape, jnp.float32),
            jax.ShapeDtypeStruct((devices, rows, cols), jnp.bfloat16),
            jax.ShapeDtypeStruct((2 * mats,), jnp.int32),
        ],
        compiler_params=PARAMS,
        cost_estimate=pl.CostEstimate(
            flops=4 * mats * rows * cols, bytes_accessed=12 * mats * rows * cols, transcendentals=0
        ),
        name="update_momentum",
    )(owner_table, other, rank, gradients, momentum)


def matmul(lhs, rhs, rhs_dim):
    return lax.dot_general(
        lhs, rhs, (((1,), (rhs_dim,)), ((), ())), preferred_element_type=jnp.float32
    )


def sum_rows(values):
    rows, cols = values.shape
    if rows % 8:
        return jnp.sum(values, axis=0, keepdims=True)
    return jnp.sum(values.reshape(rows // 8, 8, cols), axis=0)


def gather_blocks(x_ref, x_s, row_size, col_size):
    _, rows, cols = x_ref.shape
    height = rows * row_size
    total = 0.0
    for r in range(row_size):
        for c in range(col_size):
            block = x_ref[r * col_size + c]
            x_s[r * rows : (r + 1) * rows, c * cols : (c + 1) * cols] = block
            wide = block.astype(jnp.float32)
            total = total + sum_rows(wide * wide)
    x_s[height:, :] = jnp.zeros((x_s.shape[0] - height, x_s.shape[1]), x_s.dtype)
    return 1.0 / (jnp.sqrt(jnp.sum(total, keepdims=True)) + epsilon)


def update_scale(height, width):
    return 0.2 * math.sqrt(max(height, width))


def newton_schulz(height, inverse, x_s, y_s, gram_s, finish):
    padded = x_s.shape[0]
    tile = height // TILES
    for ref in (y_s, gram_s):
        ref[height:, :] = jnp.zeros((padded - height, ref.shape[1]), ref.dtype)
    for iteration in range(ITERS):
        src = x_s if iteration == 0 else y_s
        for t in range(TILES):
            span = slice(t * tile, (t + 1) * tile)
            gram = matmul(src[span, :], src[...], 1)
            if iteration == 0:
                gram = gram * (inverse * inverse)
            gram_s[span, :] = gram.astype(jnp.bfloat16)
        for t in range(TILES):
            span = slice(t * tile, (t + 1) * tile)
            square = matmul(gram_s[span, :], gram_s[...], 0)
            mixing = coef_b * gram_s[span, :].astype(jnp.float32) + coef_c * square
            mixing = mixing.astype(jnp.bfloat16)
            if iteration + 1 < ITERS:
                combined = combine(src, span, slice(None), mixing)
                if iteration == 0:
                    combined = combined * inverse
                y_s[span, :] = combined.astype(jnp.bfloat16)
            else:
                finish(t, span, mixing)


def combine(src, span, columns, mixing):
    return coef_a * src[span, columns].astype(jnp.float32) + matmul(mixing, src[:, columns], 0)


def stage_place(row_offset, col_offset, row_size, width):
    high = row_offset // LOW * width + col_offset
    return row_offset % LOW * (row_size // LOW * width) + high


def ortho_kernel(row_size, col_size, slot, other_ref, x_ref, *refs):
    _, rows, cols = x_ref.shape
    width = col_size // HALVES
    places = row_size * width
    height = rows * row_size
    tile = height // TILES
    if slot:
        y_s, mix_ref, out_ref, x_s, gram_s, back_ref, sems = refs
    else:
        owned_ref, low_refs = refs[0], refs[1 : 1 + LOW]
        x_s, gram_s, back_ref, sems, y_s, whole_ref = refs[1 + LOW :]
    row, col = lax.axis_index("dp"), lax.axis_index("owner")
    me = row * col_size + col
    inverse = gather_blocks(x_ref, x_s, row_size, col_size)
    scale = update_scale(height, cols * col_size)

    def copy_out(t):
        if slot:
            span = pl.ds(t * (places // TILES), places // TILES)
            return pltpu.make_async_copy(back_ref.at[span], out_ref.at[span], sems.at[t])
        span = pl.ds(t * tile, tile)
        return pltpu.make_async_copy(whole_ref.at[span], owned_ref.at[slot, span], sems.at[t])

    def finish(t, span, mixing):
        if slot:
            mix_ref[span, :] = mixing
            near = pl.ds(pl.multiple_of(col // width * (width * cols), width * cols), width * cols)
            result = (scale * combine(y_s, span, near, mixing)).astype(jnp.bfloat16)
        else:
            result = (scale * combine(y_s, span, slice(None), mixing)).astype(jnp.bfloat16)
            owns = other_ref[me] != me
            whole_ref[span, :] = jnp.where(owns, result, jnp.zeros_like(result))
            half = width * cols
            result = jnp.where(col < width, result[:, :half], result[:, half:])
        for j in range(row_size // TILES):
            r = t * (row_size // TILES) + j
            for c in range(width):
                if slot:
                    place = r * width + c
                else:
                    place = stage_place(r ^ row, c ^ (col % width), row_size, width)
                back_ref[place] = result[
                    j * rows : (j + 1) * rows, c * cols : (c + 1) * cols
                ]
        copy_out(t).start()

    newton_schulz(height, inverse, x_s, y_s, gram_s, finish)
    if not slot:
        for k in range(LOW):
            low_refs[k][...] = back_ref[k * places // LOW : (k + 1) * places // LOW]
    for t in range(TILES):
        copy_out(t).wait()


def orthogonalize(slot, other, arrived, row_size, col_size):
    devices, rows, cols = arrived.shape
    height, width = rows * row_size, cols * col_size
    padded = round_up(height, 256)
    places = devices // HALVES
    scratch_shapes = [
        pltpu.VMEM((padded, width), jnp.bfloat16),
        pltpu.VMEM((padded, padded), jnp.bfloat16),
        pltpu.VMEM((places, rows, cols), jnp.bfloat16),
        pltpu.SemaphoreType.DMA((TILES,)),
    ]
    if slot:
        out_specs = [VMEM, VMEM, ANYWHERE]
        out = [(padded, width), (height, padded), (places, rows, cols)]
    else:
        out_specs = [ANYWHERE] + [VMEM] * LOW
        out = [(CAP, height, width)] + [(places // LOW, rows, cols)] * LOW
        scratch_shapes += [
            pltpu.VMEM((padded, width), jnp.bfloat16),
            pltpu.VMEM((height, width), jnp.bfloat16),
        ]
    return pl.pallas_call(
        functools.partial(ortho_kernel, row_size, col_size, slot),
        in_specs=[SMEM, VMEM],
        out_specs=out_specs,
        out_shape=[
            (pltpu.HBM if spec is ANYWHERE else pltpu.VMEM)(shape, jnp.bfloat16)
            for spec, shape in zip(out_specs, out)
        ],
        scratch_shapes=scratch_shapes,
        compiler_params=PARAMS,
        cost_estimate=pl.CostEstimate(
            flops=2 * ITERS * padded * padded * (2 * width + padded),
            bytes_accessed=6 * padded * width,
            transcendentals=0,
        ),
        name="orthogonalize",
    )(other, arrived)


def restage_kernel(*refs):
    low_refs, high_refs = refs[:LOW], refs[LOW:]
    for h, high_ref in enumerate(high_refs):
        for k, low_ref in enumerate(low_refs):
            high_ref[k] = low_ref[h]


def restage(blocks):
    highs, rows, cols = blocks[0].shape
    out = jax.ShapeDtypeStruct((LOW, rows, cols), blocks[0].dtype)
    return pl.pallas_call(
        restage_kernel,
        grid=(1,),
        in_specs=[whole(blocks[0].shape)] * LOW,
        out_specs=[whole(out.shape)] * highs,
        out_shape=[out] * highs,
        compiler_params=PARAMS,
        cost_estimate=pl.CostEstimate(
            flops=0, bytes_accessed=4 * LOW * highs * rows * cols, transcendentals=0
        ),
        name="restage",
    )(*blocks)


def start_blocks(slot, list_ref, back_ref, update_ref, sem):
    listed = list_ref.shape[0] // CAP
    for k in range(update_ref.shape[0] // CAP):
        matrix = list_ref[slot * listed + 2 * k]
        place = list_ref[slot * listed + 2 * k + 1]
        pltpu.make_async_copy(back_ref.at[place], update_ref.at[matrix], sem).start()


def wait_blocks(back_ref, update_ref, sem):
    span = pl.ds(0, update_ref.shape[0] // CAP)
    pltpu.make_async_copy(back_ref.at[span], update_ref.at[span], sem).wait()


def early_kernel(col_size, list_ref, other_ref, y_ref, mix_ref, owned_in, *refs):
    high_refs, (owned_ref, update_ref, back_s, whole_s, own_sems, sem) = refs[:-6], refs[-6:]
    for h, high_ref in enumerate(high_refs):
        back_s[h * LOW : (h + 1) * LOW] = high_ref[...]
    start_blocks(0, list_ref, back_s, update_ref, sem)
    me = lax.axis_index("dp") * col_size + lax.axis_index("owner")
    owns = other_ref[me] != me
    height, width = whole_s.shape
    tile = height // TILES
    copies = []
    for t in range(TILES):
        span = slice(t * tile, (t + 1) * tile)
        result = combine(y_ref, span, slice(None), mix_ref[span, :])
        result = (update_scale(height, width) * result).astype(jnp.bfloat16)
        whole_s[span, :] = jnp.where(owns, result, jnp.zeros_like(result))
        rows = pl.ds(t * tile, tile)
        copies.append(
            pltpu.make_async_copy(whole_s.at[rows], owned_ref.at[CAP - 1, rows], own_sems.at[t])
        )
        copies[-1].start()
    for copy in copies:
        copy.wait()
    wait_blocks(back_s, update_ref, sem)


def store_early(places, other, current, mixing, owned, first, mats, col_size):
    _, rows, cols = first[0].shape
    _, height, width = owned.shape
    return pl.pallas_call(
        functools.partial(early_kernel, col_size),
        in_specs=[SMEM, SMEM, VMEM, VMEM, ANYWHERE] + [VMEM] * len(first),
        out_specs=[ANYWHERE, ANYWHERE],
        out_shape=[
            jax.ShapeDtypeStruct(owned.shape, jnp.bfloat16),
            jax.ShapeDtypeStruct((mats, rows, cols), jnp.bfloat16),
        ],
        scratch_shapes=[
            pltpu.VMEM((LOW * len(first), rows, cols), jnp.bfloat16),
            pltpu.VMEM((height, width), jnp.bfloat16),
            pltpu.SemaphoreType.DMA((TILES,)),
            pltpu.SemaphoreType.DMA(()),
        ],
        input_output_aliases={4: 0},
        compiler_params=PARAMS,
        cost_estimate=pl.CostEstimate(
            flops=2 * height * height * width,
            bytes_accessed=8 * mats * rows * cols,
            transcendentals=0,
        ),
        name="store_early",
    )(places, other, current, mixing, owned, *first)


def late_kernel(list_ref, back_ref, update_in, update_ref, sem):
    start_blocks(1, list_ref, back_ref, update_ref, sem)
    wait_blocks(back_ref, update_ref, sem)


def store_late(places, second, update):
    return pl.pallas_call(
        late_kernel,
        in_specs=[SMEM, VMEM, ANYWHERE],
        out_specs=ANYWHERE,
        out_shape=jax.ShapeDtypeStruct(update.shape, jnp.bfloat16),
        scratch_shapes=[pltpu.SemaphoreType.DMA(())],
        input_output_aliases={2: 0},
        compiler_params=PARAMS,
        cost_estimate=pl.CostEstimate(flops=0, bytes_accessed=4 * second.size, transcendentals=0),
        name="store_late",
    )(places, second, update)


def exchange(blocks, axes, groups=None):
    return lax.all_to_all(
        blocks, axes, split_axis=0, concat_axis=0, tiled=True, axis_index_groups=groups
    )


def swap(block, offset, devices):
    return lax.ppermute(block, AXES, [(d, d ^ offset) for d in range(devices)])


def on_device(gradients, momentum, owner_table):
    row_size = lax.axis_size("dp")
    col_size = lax.axis_size("owner")
    devices = row_size * col_size
    width = col_size // HALVES
    halves = [
        [r * col_size + half * width + c for r in range(row_size) for c in range(width)]
        for half in range(HALVES)
    ]
    first, other, rank = pack(gradients, momentum, owner_table, devices, col_size)
    arrived_first = exchange(first, AXES)
    new_momentum, second, places = update_momentum(
        gradients, momentum, owner_table, other, rank, col_size
    )
    arrived_first, second = lax.optimization_barrier((arrived_first, second))
    arrived_second = exchange(second, AXES)
    owned, *back_first = orthogonalize(0, other, arrived_first, row_size, col_size)
    low = [back_first[0]] + [
        swap(back_first[k], k * col_size, devices) for k in range(1, LOW)
    ]
    high = restage(low)
    _, arrived_second = lax.optimization_barrier((high, arrived_second))
    returned_first = [high[0]] + [
        swap(high[r * width + c], r * LOW * col_size + c, devices)
        for r in range(row_size // LOW)
        for c in range(width)
        if r or c
    ]
    current, mixing, back_second = orthogonalize(1, other, arrived_second, row_size, col_size)
    returned_first, back_second = lax.optimization_barrier((returned_first, back_second))
    returned_second = exchange(back_second, AXES, halves)
    owned, update = store_early(
        places, other, current, mixing, owned, returned_first, owner_table.shape[0], col_size
    )
    update = store_late(places, returned_second, update)
    return (new_momentum, update, owned)


def solution(mesh):
    return jax.shard_map(
        on_device,
        mesh=mesh,
        in_specs=(P(None, "dp", "owner"), P(None, "dp", "owner"), P()),
        out_specs=(P(None, "dp", "owner"), P(None, "dp", "owner"), P(("dp", "owner"), None, None)),
        check_vma=False,
    )
```

```python
import functools
import math

import jax
import jax.numpy as jnp
from jax import lax
from jax.experimental import pallas as pl
from jax.experimental.pallas import tpu as pltpu
from jax.sharding import PartitionSpec as P

ITERS = 2
CAP = 2
HALVES = 2
TILES = 2
LOW = 4

coef_a = 3.4445
coef_b = -4.775
coef_c = 2.0315
momentum_beta = 0.95
epsilon = 1e-07

AXES = ("dp", "owner")
MIB = 1024 * 1024
PARAMS = pltpu.CompilerParams(vmem_limit_bytes=24 * MIB)
PACK_PARAMS = pltpu.CompilerParams(vmem_limit_bytes=60 * MIB)
SMEM = pl.BlockSpec(memory_space=pltpu.SMEM)
VMEM = pl.BlockSpec(memory_space=pltpu.VMEM)
ANYWHERE = pl.BlockSpec(memory_space=pl.ANY)


def round_up(value, multiple):
    return -(-value // multiple) * multiple


def whole(shape):
    return pl.BlockSpec(shape, lambda *_: (0,) * len(shape))


def nesterov_of(grad_ref, momentum_ref, j):
    grad = grad_ref[j].astype(jnp.float32)
    new = momentum_beta * momentum_ref[j] + grad
    return new, (grad + momentum_beta * new).astype(jnp.bfloat16)


def make_plan(col_size, owner_ref, other_ref, rank_ref, count_ref, list_ref):
    devices, mats = other_ref.shape[0], rank_ref.shape[0]

    def clear(d, _):
        count_ref[d] = 0
        return 0

    lax.fori_loop(0, devices, clear, 0, unroll=8)

    def rank_matrix(i, _):
        owner = owner_ref[i]
        rank = count_ref[owner]
        rank_ref[i] = rank
        count_ref[owner] = rank + 1
        return 0

    lax.fori_loop(0, mats, rank_matrix, 0, unroll=8)

    def list_device(d, found):
        owns = jnp.minimum(count_ref[d], 1)
        half = (d % col_size) // (col_size // HALVES)
        row = 2 * jnp.where(owns == 1, half, 1 - half) + owns
        place = found[0]
        for k in range(1, 2 * HALVES):
            place = jnp.where(row == k, found[k], place)
        list_ref[row * devices + place] = d
        return tuple(n + jnp.where(row == k, 1, 0) for k, n in enumerate(found))

    found = lax.fori_loop(0, devices, list_device, (0,) * (2 * HALVES), unroll=8)
    for half in range(HALVES):

        def pair(k, _):
            idle = list_ref[2 * half * devices + k]
            other_ref[list_ref[(2 * half + 1) * devices + k]] = idle
            other_ref[idle] = idle
            return 0

        lax.fori_loop(0, found[2 * half + 1], pair, 0)


def pack_kernel(
    chunk, col_size, owner_ref, g_ref, m_ref, first_ref, other_ref, rank_ref,
    count_ref, list_ref, g_s, m_s, sems,
):
    mats = rank_ref.shape[0]

    def loads(k):
        span = pl.ds(k * chunk, chunk)
        return (
            pltpu.make_async_copy(g_ref.at[span], g_s.at[span], sems.at[0, k]),
            pltpu.make_async_copy(m_ref.at[span], m_s.at[span], sems.at[1, k]),
        )

    for k in range(mats // chunk):
        for load in loads(k):
            load.start()
    make_plan(col_size, owner_ref, other_ref, rank_ref, count_ref, list_ref)
    for k in range(mats // chunk):
        for load in loads(k):
            load.wait()
        for i in range(k * chunk, (k + 1) * chunk):

            @pl.when(rank_ref[i] == 0)
            def _():
                nesterov = nesterov_of(g_s, m_s, i)[1]
                first_ref[owner_ref[i]] = nesterov
                first_ref[other_ref[owner_ref[i]]] = nesterov


def pack(gradients, momentum, owner_table, devices, col_size):
    mats, rows, cols = gradients.shape
    chunk = 8
    return pl.pallas_call(
        functools.partial(pack_kernel, chunk, col_size),
        grid_spec=pltpu.PrefetchScalarGridSpec(
            num_scalar_prefetch=1,
            grid=(1,),
            in_specs=[ANYWHERE, ANYWHERE],
            out_specs=[whole((devices, rows, cols)), SMEM, SMEM],
            scratch_shapes=[
                pltpu.SMEM((devices,), jnp.int32),
                pltpu.SMEM((2 * HALVES * devices,), jnp.int32),
                pltpu.VMEM(gradients.shape, gradients.dtype),
                pltpu.VMEM(momentum.shape, momentum.dtype),
                pltpu.SemaphoreType.DMA((2, mats // chunk)),
            ],
        ),
        out_shape=[
            jax.ShapeDtypeStruct((devices, rows, cols), jnp.bfloat16),
            jax.ShapeDtypeStruct((devices,), jnp.int32),
            jax.ShapeDtypeStruct((mats,), jnp.int32),
        ],
        compiler_params=PACK_PARAMS,
        cost_estimate=pl.CostEstimate(
            flops=4 * mats * rows * cols, bytes_accessed=8 * mats * rows * cols, transcendentals=0
        ),
        name="pack",
    )(owner_table, gradients, momentum)


def momentum_kernel(
    chunk, col_size, owner_ref, other_ref, rank_ref, g_ref, m_ref, nm_ref, second_ref, list_ref,
    count_ref,
):
    step = pl.program_id(0)
    width = col_size // HALVES
    row, col = lax.axis_index("dp"), lax.axis_index("owner")
    listed = list_ref.shape[0] // CAP

    @pl.when(step == 0)
    def _():
        for slot in range(CAP):
            count_ref[slot] = 0

    for j in range(chunk):
        i = step * chunk + j
        new, nesterov = nesterov_of(g_ref, m_ref, j)
        nm_ref[j] = new
        owner = owner_ref[i]

        @pl.when(rank_ref[i] == 1)
        def _():
            second_ref[owner] = nesterov
            second_ref[other_ref[owner]] = nesterov

        near = (owner % col_size) // width == col // width
        host = jnp.where(near, owner, other_ref[owner])
        host_row, host_col = host // col_size, host % width
        offset = host_row ^ row
        high = offset // LOW * width + (host_col ^ (col % width))
        place = jnp.where(
            rank_ref[i] == 0, high * LOW + offset % LOW, host_row * width + host_col
        )
        rank = rank_ref[i]
        entry = count_ref[rank]
        count_ref[rank] = entry + 1
        list_ref[rank * listed + 2 * entry] = i
        list_ref[rank * listed + 2 * entry + 1] = place


def update_momentum(gradients, momentum, owner_table, other, rank, col_size):
    mats, rows, cols = gradients.shape
    devices = other.shape[0]
    chunk = 8
    block = pl.BlockSpec((chunk, rows, cols), lambda i, *_: (i, 0, 0))
    return pl.pallas_call(
        functools.partial(momentum_kernel, chunk, col_size),
        grid_spec=pltpu.PrefetchScalarGridSpec(
            num_scalar_prefetch=3,
            grid=(mats // chunk,),
            in_specs=[block, block],
            out_specs=[block, whole((devices, rows, cols)), SMEM],
            scratch_shapes=[pltpu.SMEM((CAP,), jnp.int32)],
        ),
        out_shape=[
            jax.ShapeDtypeStruct(momentum.shape, jnp.float32),
            jax.ShapeDtypeStruct((devices, rows, cols), jnp.bfloat16),
            jax.ShapeDtypeStruct((2 * mats,), jnp.int32),
        ],
        compiler_params=PARAMS,
        cost_estimate=pl.CostEstimate(
            flops=4 * mats * rows * cols, bytes_accessed=12 * mats * rows * cols, transcendentals=0
        ),
        name="update_momentum",
    )(owner_table, other, rank, gradients, momentum)


def matmul(lhs, rhs, rhs_dim):
    return lax.dot_general(
        lhs, rhs, (((1,), (rhs_dim,)), ((), ())), preferred_element_type=jnp.float32
    )


def sum_rows(values):
    rows, cols = values.shape
    if rows % 8:
        return jnp.sum(values, axis=0, keepdims=True)
    return jnp.sum(values.reshape(rows // 8, 8, cols), axis=0)


def gather_blocks(x_ref, x_s, row_size, col_size):
    _, rows, cols = x_ref.shape
    height = rows * row_size
    total = 0.0
    for r in range(row_size):
        for c in range(col_size):
            block = x_ref[r * col_size + c]
            x_s[r * rows : (r + 1) * rows, c * cols : (c + 1) * cols] = block
            wide = block.astype(jnp.float32)
            total = total + sum_rows(wide * wide)
    x_s[height:, :] = jnp.zeros((x_s.shape[0] - height, x_s.shape[1]), x_s.dtype)
    return 1.0 / (jnp.sqrt(jnp.sum(total, keepdims=True)) + epsilon)


def update_scale(height, width):
    return 0.2 * math.sqrt(max(height, width))


def newton_schulz(height, inverse, x_s, y_s, gram_s, finish):
    padded = x_s.shape[0]
    tile = height // TILES
    for ref in (y_s, gram_s):
        ref[height:, :] = jnp.zeros((padded - height, ref.shape[1]), ref.dtype)
    for iteration in range(ITERS):
        src = x_s if iteration == 0 else y_s
        for t in range(TILES):
            span = slice(t * tile, (t + 1) * tile)
            gram = matmul(src[span, :], src[...], 1)
            if iteration == 0:
                gram = gram * (inverse * inverse)
            gram_s[span, :] = gram.astype(jnp.bfloat16)
        for t in range(TILES):
            span = slice(t * tile, (t + 1) * tile)
            square = matmul(gram_s[span, :], gram_s[...], 0)
            mixing = coef_b * gram_s[span, :].astype(jnp.float32) + coef_c * square
            mixing = mixing.astype(jnp.bfloat16)
            if iteration + 1 < ITERS:
                combined = combine(src, span, slice(None), mixing)
                if iteration == 0:
                    combined = combined * inverse
                y_s[span, :] = combined.astype(jnp.bfloat16)
            else:
                finish(t, span, mixing)


def combine(src, span, columns, mixing):
    return coef_a * src[span, columns].astype(jnp.float32) + matmul(mixing, src[:, columns], 0)


def stage_place(row_offset, col_offset, row_size, width):
    high = row_offset // LOW * width + col_offset
    return row_offset % LOW * (row_size // LOW * width) + high


def ortho_kernel(row_size, col_size, slot, other_ref, x_ref, *refs):
    _, rows, cols = x_ref.shape
    width = col_size // HALVES
    half = width * cols
    places = row_size * width
    height = rows * row_size
    tile = height // TILES
    if slot:
        whole_ref, out_ref, x_s, y_s, gram_s, back_ref, sems, mix_s = refs
    else:
        owned_ref, low_refs = refs[0], refs[1 : 1 + LOW]
        x_s, y_s, gram_s, back_ref, sems, whole_ref = refs[1 + LOW :]
    row, col = lax.axis_index("dp"), lax.axis_index("owner")
    me = row * col_size + col
    owns = other_ref[me] != me
    inverse = gather_blocks(x_ref, x_s, row_size, col_size)

    def copy_out(t):
        if slot:
            span = pl.ds(t * (places // TILES), places // TILES)
            return pltpu.make_async_copy(back_ref.at[span], out_ref.at[span], sems.at[t])
        span = pl.ds(t * tile, tile)
        return pltpu.make_async_copy(whole_ref.at[span], owned_ref.at[slot, span], sems.at[t])

    def product(span, columns, mixing):
        result = update_scale(height, cols * col_size) * combine(y_s, span, columns, mixing)
        result = result.astype(jnp.bfloat16)
        whole_ref[span, columns] = jnp.where(owns, result, jnp.zeros_like(result))
        return result

    def columns_of(number):
        return pl.ds(pl.multiple_of(number * half, half), half)

    def finish(t, span, mixing):
        if slot:
            mix_s[span, :] = mixing
            result = product(span, columns_of(col // width), mixing)
        else:
            result = product(span, slice(None), mixing)
            result = jnp.where(col < width, result[:, :half], result[:, half:])
        for j in range(row_size // TILES):
            r = t * (row_size // TILES) + j
            for c in range(width):
                if slot:
                    place = r * width + c
                else:
                    place = stage_place(r ^ row, c ^ (col % width), row_size, width)
                back_ref[place] = result[
                    j * rows : (j + 1) * rows, c * cols : (c + 1) * cols
                ]
        copy_out(t).start()

    newton_schulz(height, inverse, x_s, y_s, gram_s, finish)
    if slot:
        for t in range(TILES):
            span = slice(t * tile, (t + 1) * tile)
            product(span, columns_of(1 - col // width), mix_s[span, :])
    else:
        for k in range(LOW):
            low_refs[k][...] = back_ref[k * places // LOW : (k + 1) * places // LOW]
    for t in range(TILES):
        copy_out(t).wait()


def orthogonalize(slot, other, arrived, row_size, col_size):
    devices, rows, cols = arrived.shape
    height, width = rows * row_size, cols * col_size
    padded = round_up(height, 256)
    places = devices // HALVES
    scratch_shapes = [
        pltpu.VMEM((padded, width), jnp.bfloat16),
        pltpu.VMEM((padded, width), jnp.bfloat16),
        pltpu.VMEM((padded, padded), jnp.bfloat16),
        pltpu.VMEM((places, rows, cols), jnp.bfloat16),
        pltpu.SemaphoreType.DMA((TILES,)),
    ]
    if slot:
        scratch_shapes.append(pltpu.VMEM((height, padded), jnp.bfloat16))
        out_specs = [VMEM, ANYWHERE]
        out = [(height, width), (places, rows, cols)]
    else:
        out_specs = [ANYWHERE] + [VMEM] * LOW
        out = [(CAP, height, width)] + [(places // LOW, rows, cols)] * LOW
        scratch_shapes.append(pltpu.VMEM((height, width), jnp.bfloat16))
    return pl.pallas_call(
        functools.partial(ortho_kernel, row_size, col_size, slot),
        in_specs=[SMEM, VMEM],
        out_specs=out_specs,
        out_shape=[
            pltpu.HBM(shape, jnp.bfloat16)
            if spec is ANYWHERE
            else jax.ShapeDtypeStruct(shape, jnp.bfloat16)
            for spec, shape in zip(out_specs, out)
        ],
        scratch_shapes=scratch_shapes,
        compiler_params=PARAMS,
        cost_estimate=pl.CostEstimate(
            flops=2 * ITERS * padded * padded * (2 * width + padded),
            bytes_accessed=6 * padded * width,
            transcendentals=0,
        ),
        name="orthogonalize",
    )(other, arrived)


def restage_kernel(*refs):
    low_refs, high_refs = refs[:LOW], refs[LOW:]
    for h, high_ref in enumerate(high_refs):
        for k, low_ref in enumerate(low_refs):
            high_ref[k] = low_ref[h]


def restage(blocks):
    highs, rows, cols = blocks[0].shape
    out = jax.ShapeDtypeStruct((LOW, rows, cols), blocks[0].dtype)
    return pl.pallas_call(
        restage_kernel,
        grid=(1,),
        in_specs=[whole(blocks[0].shape)] * LOW,
        out_specs=[whole(out.shape)] * highs,
        out_shape=[out] * highs,
        compiler_params=PARAMS,
        cost_estimate=pl.CostEstimate(
            flops=0, bytes_accessed=4 * LOW * highs * rows * cols, transcendentals=0
        ),
        name="restage",
    )(*blocks)


def start_blocks(slot, list_ref, back_ref, update_ref, sem):
    listed = list_ref.shape[0] // CAP
    for k in range(update_ref.shape[0] // CAP):
        matrix = list_ref[slot * listed + 2 * k]
        place = list_ref[slot * listed + 2 * k + 1]
        pltpu.make_async_copy(back_ref.at[place], update_ref.at[matrix], sem).start()


def wait_blocks(back_ref, update_ref, sem):
    span = pl.ds(0, update_ref.shape[0] // CAP)
    pltpu.make_async_copy(back_ref.at[span], update_ref.at[span], sem).wait()


def early_kernel(list_ref, whole_ref, owned_in, *refs):
    high_refs, (owned_ref, update_ref, back_s, own_sem, sem) = refs[:-5], refs[-5:]
    own = pltpu.make_async_copy(whole_ref, owned_ref.at[CAP - 1], own_sem)
    own.start()
    for h, high_ref in enumerate(high_refs):
        back_s[h * LOW : (h + 1) * LOW] = high_ref[...]
    start_blocks(0, list_ref, back_s, update_ref, sem)
    wait_blocks(back_s, update_ref, sem)
    own.wait()


def store_early(places, mats, matrix, owned, first):
    _, rows, cols = first[0].shape
    return pl.pallas_call(
        early_kernel,
        in_specs=[SMEM, VMEM, ANYWHERE] + [VMEM] * len(first),
        out_specs=[ANYWHERE, ANYWHERE],
        out_shape=[
            jax.ShapeDtypeStruct(owned.shape, jnp.bfloat16),
            jax.ShapeDtypeStruct((mats, rows, cols), jnp.bfloat16),
        ],
        scratch_shapes=[
            pltpu.VMEM((LOW * len(first), rows, cols), jnp.bfloat16),
            pltpu.SemaphoreType.DMA(()),
            pltpu.SemaphoreType.DMA(()),
        ],
        input_output_aliases={2: 0},
        compiler_params=PARAMS,
        cost_estimate=pl.CostEstimate(
            flops=0, bytes_accessed=8 * mats * rows * cols, transcendentals=0
        ),
        name="store_early",
    )(places, matrix, owned, *first)


def late_kernel(list_ref, back_ref, update_in, update_ref, sem):
    start_blocks(1, list_ref, back_ref, update_ref, sem)
    wait_blocks(back_ref, update_ref, sem)


def store_late(places, second, update):
    return pl.pallas_call(
        late_kernel,
        in_specs=[SMEM, VMEM, ANYWHERE],
        out_specs=ANYWHERE,
        out_shape=jax.ShapeDtypeStruct(update.shape, jnp.bfloat16),
        scratch_shapes=[pltpu.SemaphoreType.DMA(())],
        input_output_aliases={2: 0},
        compiler_params=PARAMS,
        cost_estimate=pl.CostEstimate(flops=0, bytes_accessed=4 * second.size, transcendentals=0),
        name="store_late",
    )(places, second, update)


def exchange(blocks, axes, groups=None):
    return lax.all_to_all(
        blocks, axes, split_axis=0, concat_axis=0, tiled=True, axis_index_groups=groups
    )


def swap(block, offset, devices):
    return lax.ppermute(block, AXES, [(d, d ^ offset) for d in range(devices)])


def on_device(gradients, momentum, owner_table):
    row_size = lax.axis_size("dp")
    col_size = lax.axis_size("owner")
    devices = row_size * col_size
    width = col_size // HALVES
    halves = [
        [r * col_size + half * width + c for r in range(row_size) for c in range(width)]
        for half in range(HALVES)
    ]
    first, other, rank = pack(gradients, momentum, owner_table, devices, col_size)
    arrived_first = exchange(first, AXES)
    new_momentum, second, places = update_momentum(
        gradients, momentum, owner_table, other, rank, col_size
    )
    arrived_first, second = lax.optimization_barrier((arrived_first, second))
    arrived_second = exchange(second, AXES)
    owned, *back_first = orthogonalize(0, other, arrived_first, row_size, col_size)
    low = [back_first[0]] + [
        swap(back_first[k], k * col_size, devices) for k in range(1, LOW)
    ]
    high = restage(low)
    _, arrived_second = lax.optimization_barrier((high, arrived_second))
    returned_first = [high[0]] + [
        swap(high[r * width + c], r * LOW * col_size + c, devices)
        for r in range(row_size // LOW)
        for c in range(width)
        if r or c
    ]
    matrix, back_second = orthogonalize(1, other, arrived_second, row_size, col_size)
    returned_first, back_second = lax.optimization_barrier((returned_first, back_second))
    returned_second = exchange(back_second, AXES, halves)
    owned, update = store_early(
        places, owner_table.shape[0], matrix, owned, returned_first
    )
    update = store_late(places, returned_second, update)
    return (new_momentum, update, owned)


def solution(mesh):
    return jax.shard_map(
        on_device,
        mesh=mesh,
        in_specs=(P(None, "dp", "owner"), P(None, "dp", "owner"), P()),
        out_specs=(P(None, "dp", "owner"), P(None, "dp", "owner"), P(("dp", "owner"), None, None)),
        check_vma=False,
    )
```

```python
import functools
import math

import jax
import jax.numpy as jnp
from jax import lax
from jax.experimental import pallas as pl
from jax.experimental.pallas import tpu as pltpu
from jax.sharding import PartitionSpec as P

ITERS = 2
CAP = 2
HALVES = 2
TILES = 2
LOW = 4

coef_a = 3.4445
coef_b = -4.775
coef_c = 2.0315
momentum_beta = 0.95
epsilon = 1e-07

AXES = ("dp", "owner")
MIB = 1024 * 1024
PARAMS = pltpu.CompilerParams(vmem_limit_bytes=24 * MIB)
PACK_PARAMS = pltpu.CompilerParams(vmem_limit_bytes=60 * MIB)
SMEM = pl.BlockSpec(memory_space=pltpu.SMEM)
VMEM = pl.BlockSpec(memory_space=pltpu.VMEM)
ANYWHERE = pl.BlockSpec(memory_space=pl.ANY)


def round_up(value, multiple):
    return -(-value // multiple) * multiple


def whole(shape):
    return pl.BlockSpec(shape, lambda *_: (0,) * len(shape))


def nesterov_of(grad_ref, momentum_ref, j):
    grad = grad_ref[j].astype(jnp.float32)
    new = momentum_beta * momentum_ref[j] + grad
    return new, (grad + momentum_beta * new).astype(jnp.bfloat16)


def order_place(d, col_size):
    row, col = d // col_size, d % col_size
    return row // 2 * (2 * col_size) + col * 2 + row % 2


def make_plan(col_size, owner_ref, other_ref, rank_ref, count_ref, list_ref):
    devices, mats = other_ref.shape[0], rank_ref.shape[0]

    def clear(d, _):
        count_ref[d] = 0
        return 0

    lax.fori_loop(0, devices, clear, 0, unroll=8)

    def rank_matrix(i, _):
        owner = owner_ref[i]
        rank = count_ref[owner]
        rank_ref[i] = rank
        count_ref[owner] = rank + 1
        return 0

    lax.fori_loop(0, mats, rank_matrix, 0, unroll=8)

    def list_device(d, found):
        owns = jnp.minimum(count_ref[d], 1)
        half = (d % col_size) // (col_size // HALVES)
        row = 2 * jnp.where(owns == 1, half, 1 - half) + owns
        place = found[0]
        for k in range(1, 2 * HALVES):
            place = jnp.where(row == k, found[k], place)
        list_ref[row * devices + place] = d
        return tuple(n + jnp.where(row == k, 1, 0) for k, n in enumerate(found))

    found = lax.fori_loop(0, devices, list_device, (0,) * (2 * HALVES), unroll=8)
    for half in range(HALVES):

        def pair(k, _):
            idle = list_ref[2 * half * devices + k]
            other_ref[list_ref[(2 * half + 1) * devices + k]] = idle
            other_ref[idle] = idle
            return 0

        lax.fori_loop(0, found[2 * half + 1], pair, 0)


def pack_kernel(
    chunk, col_size, owner_ref, g_ref, m_ref, first_ref, other_ref, rank_ref,
    count_ref, list_ref, g_s, m_s, sems,
):
    mats = rank_ref.shape[0]

    def loads(k):
        span = pl.ds(k * chunk, chunk)
        return (
            pltpu.make_async_copy(g_ref.at[span], g_s.at[span], sems.at[0, k]),
            pltpu.make_async_copy(m_ref.at[span], m_s.at[span], sems.at[1, k]),
        )

    for k in range(mats // chunk):
        for load in loads(k):
            load.start()
    make_plan(col_size, owner_ref, other_ref, rank_ref, count_ref, list_ref)
    for k in range(mats // chunk):
        for load in loads(k):
            load.wait()
        for i in range(k * chunk, (k + 1) * chunk):

            @pl.when(rank_ref[i] == 0)
            def _():
                nesterov = nesterov_of(g_s, m_s, i)[1]
                first_ref[order_place(owner_ref[i], col_size)] = nesterov
                first_ref[order_place(other_ref[owner_ref[i]], col_size)] = nesterov


def pack(gradients, momentum, owner_table, devices, col_size):
    mats, rows, cols = gradients.shape
    chunk = 8
    return pl.pallas_call(
        functools.partial(pack_kernel, chunk, col_size),
        grid_spec=pltpu.PrefetchScalarGridSpec(
            num_scalar_prefetch=1,
            grid=(1,),
            in_specs=[ANYWHERE, ANYWHERE],
            out_specs=[whole((devices, rows, cols)), SMEM, SMEM],
            scratch_shapes=[
                pltpu.SMEM((devices,), jnp.int32),
                pltpu.SMEM((2 * HALVES * devices,), jnp.int32),
                pltpu.VMEM(gradients.shape, gradients.dtype),
                pltpu.VMEM(momentum.shape, momentum.dtype),
                pltpu.SemaphoreType.DMA((2, mats // chunk)),
            ],
        ),
        out_shape=[
            jax.ShapeDtypeStruct((devices, rows, cols), jnp.bfloat16),
            jax.ShapeDtypeStruct((devices,), jnp.int32),
            jax.ShapeDtypeStruct((mats,), jnp.int32),
        ],
        compiler_params=PACK_PARAMS,
        cost_estimate=pl.CostEstimate(
            flops=4 * mats * rows * cols, bytes_accessed=8 * mats * rows * cols, transcendentals=0
        ),
        name="pack",
    )(owner_table, gradients, momentum)


def momentum_kernel(
    chunk, col_size, owner_ref, other_ref, rank_ref, g_ref, m_ref, nm_ref, second_ref, list_ref,
    count_ref,
):
    step = pl.program_id(0)
    width = col_size // HALVES
    row, col = lax.axis_index("dp"), lax.axis_index("owner")
    listed = list_ref.shape[0] // CAP

    @pl.when(step == 0)
    def _():
        for slot in range(CAP):
            count_ref[slot] = 0

    for j in range(chunk):
        i = step * chunk + j
        new, nesterov = nesterov_of(g_ref, m_ref, j)
        nm_ref[j] = new
        owner = owner_ref[i]

        @pl.when(rank_ref[i] == 1)
        def _():
            second_ref[order_place(owner, col_size)] = nesterov
            second_ref[order_place(other_ref[owner], col_size)] = nesterov

        near = (owner % col_size) // width == col // width
        host = jnp.where(near, owner, other_ref[owner])
        host_row, host_col = host // col_size, host % width
        offset = host_row ^ row
        high = offset // LOW * width + (host_col ^ (col % width))
        place = jnp.where(
            rank_ref[i] == 0, high * LOW + offset % LOW, host_row * width + host_col
        )
        rank = rank_ref[i]
        entry = count_ref[rank]
        count_ref[rank] = entry + 1
        list_ref[rank * listed + 2 * entry] = i
        list_ref[rank * listed + 2 * entry + 1] = place


def update_momentum(gradients, momentum, owner_table, other, rank, col_size):
    mats, rows, cols = gradients.shape
    devices = other.shape[0]
    chunk = 8
    block = pl.BlockSpec((chunk, rows, cols), lambda i, *_: (i, 0, 0))
    return pl.pallas_call(
        functools.partial(momentum_kernel, chunk, col_size),
        grid_spec=pltpu.PrefetchScalarGridSpec(
            num_scalar_prefetch=3,
            grid=(mats // chunk,),
            in_specs=[block, block],
            out_specs=[block, whole((devices, rows, cols)), SMEM],
            scratch_shapes=[pltpu.SMEM((CAP,), jnp.int32)],
        ),
        out_shape=[
            jax.ShapeDtypeStruct(momentum.shape, jnp.float32),
            jax.ShapeDtypeStruct((devices, rows, cols), jnp.bfloat16),
            jax.ShapeDtypeStruct((2 * mats,), jnp.int32),
        ],
        compiler_params=PARAMS,
        cost_estimate=pl.CostEstimate(
            flops=4 * mats * rows * cols, bytes_accessed=12 * mats * rows * cols, transcendentals=0
        ),
        name="update_momentum",
    )(owner_table, other, rank, gradients, momentum)


def matmul(lhs, rhs, rhs_dim):
    return lax.dot_general(
        lhs, rhs, (((1,), (rhs_dim,)), ((), ())), preferred_element_type=jnp.float32
    )


def sum_rows(values):
    rows, cols = values.shape
    if rows % 8:
        return jnp.sum(values, axis=0, keepdims=True)
    return jnp.sum(values.reshape(rows // 8, 8, cols), axis=0)


def gather_blocks(x_ref, x_s, row_size, col_size):
    _, rows, cols = x_ref.shape
    height = rows * row_size
    total = 0.0
    for r in range(row_size):
        for c in range(col_size):
            block = x_ref[order_place(r * col_size + c, col_size)]
            x_s[r * rows : (r + 1) * rows, c * cols : (c + 1) * cols] = block
            wide = block.astype(jnp.float32)
            total = total + sum_rows(wide * wide)
    x_s[height:, :] = jnp.zeros((x_s.shape[0] - height, x_s.shape[1]), x_s.dtype)
    return 1.0 / (jnp.sqrt(jnp.sum(total, keepdims=True)) + epsilon)


def update_scale(height, width):
    return 0.2 * math.sqrt(max(height, width))


def newton_schulz(height, inverse, x_s, y_s, gram_s, finish):
    padded = x_s.shape[0]
    tile = height // TILES
    for ref in (y_s, gram_s):
        ref[height:, :] = jnp.zeros((padded - height, ref.shape[1]), ref.dtype)
    for iteration in range(ITERS):
        src = x_s if iteration == 0 else y_s
        for t in range(TILES):
            span = slice(t * tile, (t + 1) * tile)
            gram = matmul(src[span, :], src[...], 1)
            if iteration == 0:
                gram = gram * (inverse * inverse)
            gram_s[span, :] = gram.astype(jnp.bfloat16)
        for t in range(TILES):
            span = slice(t * tile, (t + 1) * tile)
            square = matmul(gram_s[span, :], gram_s[...], 0)
            mixing = coef_b * gram_s[span, :].astype(jnp.float32) + coef_c * square
            mixing = mixing.astype(jnp.bfloat16)
            if iteration + 1 < ITERS:
                combined = combine(src, span, slice(None), mixing)
                if iteration == 0:
                    combined = combined * inverse
                y_s[span, :] = combined.astype(jnp.bfloat16)
            else:
                finish(t, span, mixing)


def combine(src, span, columns, mixing):
    return coef_a * src[span, columns].astype(jnp.float32) + matmul(mixing, src[:, columns], 0)


def stage_place(row_offset, col_offset, row_size, width):
    high = row_offset // LOW * width + col_offset
    return row_offset % LOW * (row_size // LOW * width) + high


def ortho_kernel(row_size, col_size, slot, other_ref, x_ref, *refs):
    _, rows, cols = x_ref.shape
    width = col_size // HALVES
    half = width * cols
    places = row_size * width
    height = rows * row_size
    tile = height // TILES
    if slot:
        whole_ref, out_ref, x_s, y_s, gram_s, back_ref, sems, mix_s = refs
    else:
        owned_ref, low_refs = refs[0], refs[1 : 1 + LOW]
        x_s, y_s, gram_s, back_ref, sems, whole_ref = refs[1 + LOW :]
    row, col = lax.axis_index("dp"), lax.axis_index("owner")
    me = row * col_size + col
    owns = other_ref[me] != me
    inverse = gather_blocks(x_ref, x_s, row_size, col_size)

    def copy_out(t):
        if slot:
            span = pl.ds(t * (places // TILES), places // TILES)
            return pltpu.make_async_copy(back_ref.at[span], out_ref.at[span], sems.at[t])
        span = pl.ds(t * tile, tile)
        return pltpu.make_async_copy(whole_ref.at[span], owned_ref.at[slot, span], sems.at[t])

    def product(span, columns, mixing):
        result = update_scale(height, cols * col_size) * combine(y_s, span, columns, mixing)
        result = result.astype(jnp.bfloat16)
        whole_ref[span, columns] = jnp.where(owns, result, jnp.zeros_like(result))
        return result

    def columns_of(number):
        return pl.ds(pl.multiple_of(number * half, half), half)

    def finish(t, span, mixing):
        if slot:
            mix_s[span, :] = mixing
            result = product(span, columns_of(col // width), mixing)
        else:
            result = product(span, slice(None), mixing)
            result = jnp.where(col < width, result[:, :half], result[:, half:])
        for j in range(row_size // TILES):
            r = t * (row_size // TILES) + j
            for c in range(width):
                if slot:
                    place = r * width + c
                else:
                    place = stage_place(r ^ row, c ^ (col % width), row_size, width)
                back_ref[place] = result[
                    j * rows : (j + 1) * rows, c * cols : (c + 1) * cols
                ]
        copy_out(t).start()

    newton_schulz(height, inverse, x_s, y_s, gram_s, finish)
    if slot:
        for t in range(TILES):
            span = slice(t * tile, (t + 1) * tile)
            product(span, columns_of(1 - col // width), mix_s[span, :])
    else:
        for k in range(LOW):
            low_refs[k][...] = back_ref[k * places // LOW : (k + 1) * places // LOW]
    for t in range(TILES):
        copy_out(t).wait()


def orthogonalize(slot, other, arrived, row_size, col_size):
    devices, rows, cols = arrived.shape
    height, width = rows * row_size, cols * col_size
    padded = round_up(height, 256)
    places = devices // HALVES
    scratch_shapes = [
        pltpu.VMEM((padded, width), jnp.bfloat16),
        pltpu.VMEM((padded, width), jnp.bfloat16),
        pltpu.VMEM((padded, padded), jnp.bfloat16),
        pltpu.VMEM((places, rows, cols), jnp.bfloat16),
        pltpu.SemaphoreType.DMA((TILES,)),
    ]
    if slot:
        scratch_shapes.append(pltpu.VMEM((height, padded), jnp.bfloat16))
        out_specs = [VMEM, ANYWHERE]
        out = [(height, width), (places, rows, cols)]
    else:
        out_specs = [ANYWHERE] + [VMEM] * LOW
        out = [(CAP, height, width)] + [(places // LOW, rows, cols)] * LOW
        scratch_shapes.append(pltpu.VMEM((height, width), jnp.bfloat16))
    return pl.pallas_call(
        functools.partial(ortho_kernel, row_size, col_size, slot),
        in_specs=[SMEM, VMEM],
        out_specs=out_specs,
        out_shape=[
            pltpu.HBM(shape, jnp.bfloat16)
            if spec is ANYWHERE
            else jax.ShapeDtypeStruct(shape, jnp.bfloat16)
            for spec, shape in zip(out_specs, out)
        ],
        scratch_shapes=scratch_shapes,
        compiler_params=PARAMS,
        cost_estimate=pl.CostEstimate(
            flops=2 * ITERS * padded * padded * (2 * width + padded),
            bytes_accessed=6 * padded * width,
            transcendentals=0,
        ),
        name="orthogonalize",
    )(other, arrived)


def restage_kernel(*refs):
    low_refs, high_refs = refs[:LOW], refs[LOW:]
    for h, high_ref in enumerate(high_refs):
        for k, low_ref in enumerate(low_refs):
            high_ref[k] = low_ref[h]


def restage(blocks):
    highs, rows, cols = blocks[0].shape
    out = jax.ShapeDtypeStruct((LOW, rows, cols), blocks[0].dtype)
    return pl.pallas_call(
        restage_kernel,
        grid=(1,),
        in_specs=[whole(blocks[0].shape)] * LOW,
        out_specs=[whole(out.shape)] * highs,
        out_shape=[out] * highs,
        compiler_params=PARAMS,
        cost_estimate=pl.CostEstimate(
            flops=0, bytes_accessed=4 * LOW * highs * rows * cols, transcendentals=0
        ),
        name="restage",
    )(*blocks)


def start_blocks(slot, list_ref, back_ref, update_ref, sem):
    listed = list_ref.shape[0] // CAP
    for k in range(update_ref.shape[0] // CAP):
        matrix = list_ref[slot * listed + 2 * k]
        place = list_ref[slot * listed + 2 * k + 1]
        pltpu.make_async_copy(back_ref.at[place], update_ref.at[matrix], sem).start()


def wait_blocks(back_ref, update_ref, sem):
    span = pl.ds(0, update_ref.shape[0] // CAP)
    pltpu.make_async_copy(back_ref.at[span], update_ref.at[span], sem).wait()


def early_kernel(list_ref, whole_ref, owned_in, *refs):
    high_refs, (owned_ref, update_ref, back_s, own_sem, sem) = refs[:-5], refs[-5:]
    own = pltpu.make_async_copy(whole_ref, owned_ref.at[CAP - 1], own_sem)
    own.start()
    for h, high_ref in enumerate(high_refs):
        back_s[h * LOW : (h + 1) * LOW] = high_ref[...]
    start_blocks(0, list_ref, back_s, update_ref, sem)
    wait_blocks(back_s, update_ref, sem)
    own.wait()


def store_early(places, mats, matrix, owned, first):
    _, rows, cols = first[0].shape
    return pl.pallas_call(
        early_kernel,
        in_specs=[SMEM, VMEM, ANYWHERE] + [VMEM] * len(first),
        out_specs=[ANYWHERE, ANYWHERE],
        out_shape=[
            jax.ShapeDtypeStruct(owned.shape, jnp.bfloat16),
            jax.ShapeDtypeStruct((mats, rows, cols), jnp.bfloat16),
        ],
        scratch_shapes=[
            pltpu.VMEM((LOW * len(first), rows, cols), jnp.bfloat16),
            pltpu.SemaphoreType.DMA(()),
            pltpu.SemaphoreType.DMA(()),
        ],
        input_output_aliases={2: 0},
        compiler_params=PARAMS,
        cost_estimate=pl.CostEstimate(
            flops=0, bytes_accessed=8 * mats * rows * cols, transcendentals=0
        ),
        name="store_early",
    )(places, matrix, owned, *first)


def late_kernel(list_ref, back_ref, update_in, update_ref, sem):
    start_blocks(1, list_ref, back_ref, update_ref, sem)
    wait_blocks(back_ref, update_ref, sem)


def store_late(places, second, update):
    return pl.pallas_call(
        late_kernel,
        in_specs=[SMEM, VMEM, ANYWHERE],
        out_specs=ANYWHERE,
        out_shape=jax.ShapeDtypeStruct(update.shape, jnp.bfloat16),
        scratch_shapes=[pltpu.SemaphoreType.DMA(())],
        input_output_aliases={2: 0},
        compiler_params=PARAMS,
        cost_estimate=pl.CostEstimate(flops=0, bytes_accessed=4 * second.size, transcendentals=0),
        name="store_late",
    )(places, second, update)


def exchange(blocks, axes, groups=None):
    return lax.all_to_all(
        blocks, axes, split_axis=0, concat_axis=0, tiled=True, axis_index_groups=groups
    )


def swap(block, offset, devices):
    return lax.ppermute(block, AXES, [(d, d ^ offset) for d in range(devices)])


def on_device(gradients, momentum, owner_table):
    row_size = lax.axis_size("dp")
    col_size = lax.axis_size("owner")
    devices = row_size * col_size
    width = col_size // HALVES
    halves = [
        [r * col_size + half * width + c for r in range(row_size) for c in range(width)]
        for half in range(HALVES)
    ]
    first, other, rank = pack(gradients, momentum, owner_table, devices, col_size)
    order = sorted(range(devices), key=lambda d: order_place(d, col_size))
    arrived_first = exchange(first, AXES, [order])
    new_momentum, second, places = update_momentum(
        gradients, momentum, owner_table, other, rank, col_size
    )
    arrived_first, second = lax.optimization_barrier((arrived_first, second))
    arrived_second = exchange(second, AXES, [order])
    owned, *back_first = orthogonalize(0, other, arrived_first, row_size, col_size)
    low = [back_first[0]] + [
        swap(back_first[k], k * col_size, devices) for k in range(1, LOW)
    ]
    high = restage(low)
    _, arrived_second = lax.optimization_barrier((high, arrived_second))
    returned_first = [high[0]] + [
        swap(high[r * width + c], r * LOW * col_size + c, devices)
        for r in range(row_size // LOW)
        for c in range(width)
        if r or c
    ]
    matrix, back_second = orthogonalize(1, other, arrived_second, row_size, col_size)
    returned_first, back_second = lax.optimization_barrier((returned_first, back_second))
    returned_second = exchange(back_second, AXES, halves)
    owned, update = store_early(
        places, owner_table.shape[0], matrix, owned, returned_first
    )
    update = store_late(places, returned_second, update)
    return (new_momentum, update, owned)


def solution(mesh):
    return jax.shard_map(
        on_device,
        mesh=mesh,
        in_specs=(P(None, "dp", "owner"), P(None, "dp", "owner"), P()),
        out_specs=(P(None, "dp", "owner"), P(None, "dp", "owner"), P(("dp", "owner"), None, None)),
        check_vma=False,
    )
```

```python
import functools
import math

import jax
import jax.numpy as jnp
from jax import lax
from jax.experimental import pallas as pl
from jax.experimental.pallas import tpu as pltpu
from jax.sharding import PartitionSpec as P

ITERS = 2
CAP = 2
HALVES = 2
TILES = 4
LOW = 4

coef_a = 3.4445
coef_b = -4.775
coef_c = 2.0315
momentum_beta = 0.95
epsilon = 1e-07

AXES = ("dp", "owner")
MIB = 1024 * 1024
PARAMS = pltpu.CompilerParams(vmem_limit_bytes=24 * MIB)
PACK_PARAMS = pltpu.CompilerParams(vmem_limit_bytes=60 * MIB)
SMEM = pl.BlockSpec(memory_space=pltpu.SMEM)
VMEM = pl.BlockSpec(memory_space=pltpu.VMEM)
ANYWHERE = pl.BlockSpec(memory_space=pl.ANY)


def round_up(value, multiple):
    return -(-value // multiple) * multiple


def whole(shape):
    return pl.BlockSpec(shape, lambda *_: (0,) * len(shape))


def nesterov_of(grad_ref, momentum_ref, j):
    grad = grad_ref[j].astype(jnp.float32)
    new = momentum_beta * momentum_ref[j] + grad
    return new, (grad + momentum_beta * new).astype(jnp.bfloat16)


def make_plan(col_size, owner_ref, other_ref, rank_ref, count_ref, list_ref):
    devices, mats = other_ref.shape[0], rank_ref.shape[0]

    def clear(d, _):
        count_ref[d] = 0
        return 0

    lax.fori_loop(0, devices, clear, 0, unroll=8)

    def rank_matrix(i, _):
        owner = owner_ref[i]
        rank = count_ref[owner]
        rank_ref[i] = rank
        count_ref[owner] = rank + 1
        return 0

    lax.fori_loop(0, mats, rank_matrix, 0, unroll=8)

    def list_device(d, found):
        owns = jnp.minimum(count_ref[d], 1)
        half = (d % col_size) // (col_size // HALVES)
        row = 2 * jnp.where(owns == 1, half, 1 - half) + owns
        place = found[0]
        for k in range(1, 2 * HALVES):
            place = jnp.where(row == k, found[k], place)
        list_ref[row * devices + place] = d
        return tuple(n + jnp.where(row == k, 1, 0) for k, n in enumerate(found))

    found = lax.fori_loop(0, devices, list_device, (0,) * (2 * HALVES), unroll=8)
    for half in range(HALVES):

        def pair(k, _):
            idle = list_ref[2 * half * devices + k]
            other_ref[list_ref[(2 * half + 1) * devices + k]] = idle
            other_ref[idle] = idle
            return 0

        lax.fori_loop(0, found[2 * half + 1], pair, 0)


def pack_kernel(
    chunk, col_size, owner_ref, g_ref, m_ref, first_ref, other_ref, rank_ref,
    count_ref, list_ref, g_s, m_s, sems,
):
    mats = rank_ref.shape[0]

    def loads(k):
        span = pl.ds(k * chunk, chunk)
        return (
            pltpu.make_async_copy(g_ref.at[span], g_s.at[span], sems.at[0, k]),
            pltpu.make_async_copy(m_ref.at[span], m_s.at[span], sems.at[1, k]),
        )

    for k in range(mats // chunk):
        for load in loads(k):
            load.start()
    make_plan(col_size, owner_ref, other_ref, rank_ref, count_ref, list_ref)
    for k in range(mats // chunk):
        for load in loads(k):
            load.wait()
        for i in range(k * chunk, (k + 1) * chunk):

            @pl.when(rank_ref[i] == 0)
            def _():
                nesterov = nesterov_of(g_s, m_s, i)[1]
                first_ref[owner_ref[i]] = nesterov
                first_ref[other_ref[owner_ref[i]]] = nesterov


def pack(gradients, momentum, owner_table, devices, col_size):
    mats, rows, cols = gradients.shape
    chunk = 8
    return pl.pallas_call(
        functools.partial(pack_kernel, chunk, col_size),
        grid_spec=pltpu.PrefetchScalarGridSpec(
            num_scalar_prefetch=1,
            grid=(1,),
            in_specs=[ANYWHERE, ANYWHERE],
            out_specs=[whole((devices, rows, cols)), SMEM, SMEM],
            scratch_shapes=[
                pltpu.SMEM((devices,), jnp.int32),
                pltpu.SMEM((2 * HALVES * devices,), jnp.int32),
                pltpu.VMEM(gradients.shape, gradients.dtype),
                pltpu.VMEM(momentum.shape, momentum.dtype),
                pltpu.SemaphoreType.DMA((2, mats // chunk)),
            ],
        ),
        out_shape=[
            jax.ShapeDtypeStruct((devices, rows, cols), jnp.bfloat16),
            jax.ShapeDtypeStruct((devices,), jnp.int32),
            jax.ShapeDtypeStruct((mats,), jnp.int32),
        ],
        compiler_params=PACK_PARAMS,
        cost_estimate=pl.CostEstimate(
            flops=4 * mats * rows * cols, bytes_accessed=8 * mats * rows * cols, transcendentals=0
        ),
        name="pack",
    )(owner_table, gradients, momentum)


def momentum_kernel(
    chunk, col_size, owner_ref, other_ref, rank_ref, g_ref, m_ref, nm_ref, second_ref, list_ref,
    count_ref,
):
    step = pl.program_id(0)
    width = col_size // HALVES
    row, col = lax.axis_index("dp"), lax.axis_index("owner")
    listed = list_ref.shape[0] // CAP

    @pl.when(step == 0)
    def _():
        for slot in range(CAP):
            count_ref[slot] = 0

    for j in range(chunk):
        i = step * chunk + j
        new, nesterov = nesterov_of(g_ref, m_ref, j)
        nm_ref[j] = new
        owner = owner_ref[i]

        @pl.when(rank_ref[i] == 1)
        def _():
            second_ref[owner] = nesterov
            second_ref[other_ref[owner]] = nesterov

        near = (owner % col_size) // width == col // width
        host = jnp.where(near, owner, other_ref[owner])
        host_row, host_col = host // col_size, host % width
        offset = host_row ^ row
        high = offset // LOW * width + (host_col ^ (col % width))
        place = jnp.where(
            rank_ref[i] == 0, high * LOW + offset % LOW, host_row * width + host_col
        )
        rank = rank_ref[i]
        entry = count_ref[rank]
        count_ref[rank] = entry + 1
        list_ref[rank * listed + 2 * entry] = i
        list_ref[rank * listed + 2 * entry + 1] = place


def update_momentum(gradients, momentum, owner_table, other, rank, col_size):
    mats, rows, cols = gradients.shape
    devices = other.shape[0]
    chunk = 8
    block = pl.BlockSpec((chunk, rows, cols), lambda i, *_: (i, 0, 0))
    return pl.pallas_call(
        functools.partial(momentum_kernel, chunk, col_size),
        grid_spec=pltpu.PrefetchScalarGridSpec(
            num_scalar_prefetch=3,
            grid=(mats // chunk,),
            in_specs=[block, block],
            out_specs=[block, whole((devices, rows, cols)), SMEM],
            scratch_shapes=[pltpu.SMEM((CAP,), jnp.int32)],
        ),
        out_shape=[
            jax.ShapeDtypeStruct(momentum.shape, jnp.float32),
            jax.ShapeDtypeStruct((devices, rows, cols), jnp.bfloat16),
            jax.ShapeDtypeStruct((2 * mats,), jnp.int32),
        ],
        compiler_params=PARAMS,
        cost_estimate=pl.CostEstimate(
            flops=4 * mats * rows * cols, bytes_accessed=12 * mats * rows * cols, transcendentals=0
        ),
        name="update_momentum",
    )(owner_table, other, rank, gradients, momentum)


def matmul(lhs, rhs, rhs_dim):
    return lax.dot_general(
        lhs, rhs, (((1,), (rhs_dim,)), ((), ())), preferred_element_type=jnp.float32
    )


def sum_rows(values):
    rows, cols = values.shape
    if rows % 8:
        return jnp.sum(values, axis=0, keepdims=True)
    return jnp.sum(values.reshape(rows // 8, 8, cols), axis=0)


def gather_blocks(x_ref, x_s, row_size, col_size):
    _, rows, cols = x_ref.shape
    height = rows * row_size
    total = 0.0
    for r in range(row_size):
        for c in range(col_size):
            block = x_ref[r * col_size + c]
            x_s[r * rows : (r + 1) * rows, c * cols : (c + 1) * cols] = block
            wide = block.astype(jnp.float32)
            total = total + sum_rows(wide * wide)
    x_s[height:, :] = jnp.zeros((x_s.shape[0] - height, x_s.shape[1]), x_s.dtype)
    return 1.0 / (jnp.sqrt(jnp.sum(total, keepdims=True)) + epsilon)


def update_scale(height, width):
    return 0.2 * math.sqrt(max(height, width))


def newton_schulz(height, inverse, x_s, y_s, gram_s, finish):
    padded = x_s.shape[0]
    tile = height // TILES
    for ref in (y_s, gram_s):
        ref[height:, :] = jnp.zeros((padded - height, ref.shape[1]), ref.dtype)
    for iteration in range(ITERS):
        src = x_s if iteration == 0 else y_s
        for t in range(TILES):
            span = slice(t * tile, (t + 1) * tile)
            gram = matmul(src[span, :], src[...], 1)
            if iteration == 0:
                gram = gram * (inverse * inverse)
            gram_s[span, :] = gram.astype(jnp.bfloat16)
        for t in range(TILES):
            span = slice(t * tile, (t + 1) * tile)
            square = matmul(gram_s[span, :], gram_s[...], 0)
            mixing = coef_b * gram_s[span, :].astype(jnp.float32) + coef_c * square
            mixing = mixing.astype(jnp.bfloat16)
            if iteration + 1 < ITERS:
                combined = combine(src, span, slice(None), mixing)
                if iteration == 0:
                    combined = combined * inverse
                y_s[span, :] = combined.astype(jnp.bfloat16)
            else:
                finish(t, span, mixing)


def combine(src, span, columns, mixing):
    return coef_a * src[span, columns].astype(jnp.float32) + matmul(mixing, src[:, columns], 0)


def stage_place(row_offset, col_offset, row_size, width):
    high = row_offset // LOW * width + col_offset
    return row_offset % LOW * (row_size // LOW * width) + high


def ortho_kernel(row_size, col_size, slot, other_ref, x_ref, *refs):
    _, rows, cols = x_ref.shape
    width = col_size // HALVES
    half = width * cols
    places = row_size * width
    height = rows * row_size
    tile = height // TILES
    if slot:
        whole_ref, out_ref, x_s, y_s, gram_s, back_ref, sems, mix_s = refs
    else:
        owned_ref, low_refs = refs[0], refs[1 : 1 + LOW]
        x_s, y_s, gram_s, back_ref, sems, whole_ref = refs[1 + LOW :]
    row, col = lax.axis_index("dp"), lax.axis_index("owner")
    me = row * col_size + col
    owns = other_ref[me] != me
    inverse = gather_blocks(x_ref, x_s, row_size, col_size)

    def copy_out(t):
        if slot:
            span = pl.ds(t * (places // TILES), places // TILES)
            return pltpu.make_async_copy(back_ref.at[span], out_ref.at[span], sems.at[t])
        span = pl.ds(t * tile, tile)
        return pltpu.make_async_copy(whole_ref.at[span], owned_ref.at[slot, span], sems.at[t])

    def product(span, columns, mixing):
        result = update_scale(height, cols * col_size) * combine(y_s, span, columns, mixing)
        result = result.astype(jnp.bfloat16)
        whole_ref[span, columns] = jnp.where(owns, result, jnp.zeros_like(result))
        return result

    def columns_of(number):
        return pl.ds(pl.multiple_of(number * half, half), half)

    def finish(t, span, mixing):
        if slot:
            mix_s[span, :] = mixing
            result = product(span, columns_of(col // width), mixing)
        else:
            result = product(span, slice(None), mixing)
            result = jnp.where(col < width, result[:, :half], result[:, half:])
        for j in range(row_size // TILES):
            r = t * (row_size // TILES) + j
            for c in range(width):
                if slot:
                    place = r * width + c
                else:
                    place = stage_place(r ^ row, c ^ (col % width), row_size, width)
                back_ref[place] = result[
                    j * rows : (j + 1) * rows, c * cols : (c + 1) * cols
                ]
        copy_out(t).start()

    newton_schulz(height, inverse, x_s, y_s, gram_s, finish)
    if slot:
        for t in range(TILES):
            span = slice(t * tile, (t + 1) * tile)
            product(span, columns_of(1 - col // width), mix_s[span, :])
    else:
        for k in range(LOW):
            low_refs[k][...] = back_ref[k * places // LOW : (k + 1) * places // LOW]
    for t in range(TILES):
        copy_out(t).wait()


def orthogonalize(slot, other, arrived, row_size, col_size):
    devices, rows, cols = arrived.shape
    height, width = rows * row_size, cols * col_size
    padded = round_up(height, 256)
    places = devices // HALVES
    scratch_shapes = [
        pltpu.VMEM((padded, width), jnp.bfloat16),
        pltpu.VMEM((padded, width), jnp.bfloat16),
        pltpu.VMEM((padded, padded), jnp.bfloat16),
        pltpu.VMEM((places, rows, cols), jnp.bfloat16),
        pltpu.SemaphoreType.DMA((TILES,)),
    ]
    if slot:
        scratch_shapes.append(pltpu.VMEM((height, padded), jnp.bfloat16))
        out_specs = [VMEM, ANYWHERE]
        out = [(height, width), (places, rows, cols)]
    else:
        out_specs = [ANYWHERE] + [VMEM] * LOW
        out = [(CAP, height, width)] + [(places // LOW, rows, cols)] * LOW
        scratch_shapes.append(pltpu.VMEM((height, width), jnp.bfloat16))
    return pl.pallas_call(
        functools.partial(ortho_kernel, row_size, col_size, slot),
        in_specs=[SMEM, VMEM],
        out_specs=out_specs,
        out_shape=[
            pltpu.HBM(shape, jnp.bfloat16)
            if spec is ANYWHERE
            else jax.ShapeDtypeStruct(shape, jnp.bfloat16)
            for spec, shape in zip(out_specs, out)
        ],
        scratch_shapes=scratch_shapes,
        compiler_params=PARAMS,
        cost_estimate=pl.CostEstimate(
            flops=2 * ITERS * padded * padded * (2 * width + padded),
            bytes_accessed=6 * padded * width,
            transcendentals=0,
        ),
        name="orthogonalize",
    )(other, arrived)


def restage_kernel(*refs):
    low_refs, high_refs = refs[:LOW], refs[LOW:]
    for h, high_ref in enumerate(high_refs):
        for k, low_ref in enumerate(low_refs):
            high_ref[k] = low_ref[h]


def restage(blocks):
    highs, rows, cols = blocks[0].shape
    out = jax.ShapeDtypeStruct((LOW, rows, cols), blocks[0].dtype)
    return pl.pallas_call(
        restage_kernel,
        grid=(1,),
        in_specs=[whole(blocks[0].shape)] * LOW,
        out_specs=[whole(out.shape)] * highs,
        out_shape=[out] * highs,
        compiler_params=PARAMS,
        cost_estimate=pl.CostEstimate(
            flops=0, bytes_accessed=4 * LOW * highs * rows * cols, transcendentals=0
        ),
        name="restage",
    )(*blocks)


def start_blocks(slot, list_ref, back_ref, update_ref, sem):
    listed = list_ref.shape[0] // CAP
    for k in range(update_ref.shape[0] // CAP):
        matrix = list_ref[slot * listed + 2 * k]
        place = list_ref[slot * listed + 2 * k + 1]
        pltpu.make_async_copy(back_ref.at[place], update_ref.at[matrix], sem).start()


def wait_blocks(back_ref, update_ref, sem):
    span = pl.ds(0, update_ref.shape[0] // CAP)
    pltpu.make_async_copy(back_ref.at[span], update_ref.at[span], sem).wait()


def early_kernel(list_ref, whole_ref, owned_in, *refs):
    high_refs, (owned_ref, update_ref, back_s, own_sem, sem) = refs[:-5], refs[-5:]
    own = pltpu.make_async_copy(whole_ref, owned_ref.at[CAP - 1], own_sem)
    own.start()
    for h, high_ref in enumerate(high_refs):
        back_s[h * LOW : (h + 1) * LOW] = high_ref[...]
    start_blocks(0, list_ref, back_s, update_ref, sem)
    wait_blocks(back_s, update_ref, sem)
    own.wait()


def store_early(places, mats, matrix, owned, first):
    _, rows, cols = first[0].shape
    return pl.pallas_call(
        early_kernel,
        in_specs=[SMEM, VMEM, ANYWHERE] + [VMEM] * len(first),
        out_specs=[ANYWHERE, ANYWHERE],
        out_shape=[
            jax.ShapeDtypeStruct(owned.shape, jnp.bfloat16),
            jax.ShapeDtypeStruct((mats, rows, cols), jnp.bfloat16),
        ],
        scratch_shapes=[
            pltpu.VMEM((LOW * len(first), rows, cols), jnp.bfloat16),
            pltpu.SemaphoreType.DMA(()),
            pltpu.SemaphoreType.DMA(()),
        ],
        input_output_aliases={2: 0},
        compiler_params=PARAMS,
        cost_estimate=pl.CostEstimate(
            flops=0, bytes_accessed=8 * mats * rows * cols, transcendentals=0
        ),
        name="store_early",
    )(places, matrix, owned, *first)


def late_kernel(list_ref, back_ref, update_in, update_ref, sem):
    start_blocks(1, list_ref, back_ref, update_ref, sem)
    wait_blocks(back_ref, update_ref, sem)


def store_late(places, second, update):
    return pl.pallas_call(
        late_kernel,
        in_specs=[SMEM, VMEM, ANYWHERE],
        out_specs=ANYWHERE,
        out_shape=jax.ShapeDtypeStruct(update.shape, jnp.bfloat16),
        scratch_shapes=[pltpu.SemaphoreType.DMA(())],
        input_output_aliases={2: 0},
        compiler_params=PARAMS,
        cost_estimate=pl.CostEstimate(flops=0, bytes_accessed=4 * second.size, transcendentals=0),
        name="store_late",
    )(places, second, update)


def exchange(blocks, axes, groups=None):
    return lax.all_to_all(
        blocks, axes, split_axis=0, concat_axis=0, tiled=True, axis_index_groups=groups
    )


def swap(block, offset, devices):
    return lax.ppermute(block, AXES, [(d, d ^ offset) for d in range(devices)])


def on_device(gradients, momentum, owner_table):
    row_size = lax.axis_size("dp")
    col_size = lax.axis_size("owner")
    devices = row_size * col_size
    width = col_size // HALVES
    halves = [
        [r * col_size + half * width + c for r in range(row_size) for c in range(width)]
        for half in range(HALVES)
    ]
    first, other, rank = pack(gradients, momentum, owner_table, devices, col_size)
    arrived_first = exchange(first, AXES)
    new_momentum, second, places = update_momentum(
        gradients, momentum, owner_table, other, rank, col_size
    )
    arrived_first, second = lax.optimization_barrier((arrived_first, second))
    arrived_second = exchange(second, AXES)
    owned, *back_first = orthogonalize(0, other, arrived_first, row_size, col_size)
    low = [back_first[0]] + [
        swap(back_first[k], k * col_size, devices) for k in range(1, LOW)
    ]
    high = restage(low)
    _, arrived_second = lax.optimization_barrier((high, arrived_second))
    returned_first = [high[0]] + [
        swap(high[r * width + c], r * LOW * col_size + c, devices)
        for r in range(row_size // LOW)
        for c in range(width)
        if r or c
    ]
    matrix, back_second = orthogonalize(1, other, arrived_second, row_size, col_size)
    returned_first, back_second = lax.optimization_barrier((returned_first, back_second))
    returned_second = exchange(back_second, AXES, halves)
    owned, update = store_early(
        places, owner_table.shape[0], matrix, owned, returned_first
    )
    update = store_late(places, returned_second, update)
    return (new_momentum, update, owned)


def solution(mesh):
    return jax.shard_map(
        on_device,
        mesh=mesh,
        in_specs=(P(None, "dp", "owner"), P(None, "dp", "owner"), P()),
        out_specs=(P(None, "dp", "owner"), P(None, "dp", "owner"), P(("dp", "owner"), None, None)),
        check_vma=False,
    )
```

```python
import functools
import math

import jax
import jax.numpy as jnp
from jax import lax
from jax.experimental import pallas as pl
from jax.experimental.pallas import tpu as pltpu
from jax.sharding import PartitionSpec as P

ITERS = 2
CAP = 2
HALVES = 2
TILES = 2
LOW = 4

coef_a = 3.4445
coef_b = -4.775
coef_c = 2.0315
momentum_beta = 0.95
epsilon = 1e-07

AXES = ("dp", "owner")
MIB = 1024 * 1024
PARAMS = pltpu.CompilerParams(vmem_limit_bytes=24 * MIB)
PACK_PARAMS = pltpu.CompilerParams(vmem_limit_bytes=60 * MIB)
SMEM = pl.BlockSpec(memory_space=pltpu.SMEM)
VMEM = pl.BlockSpec(memory_space=pltpu.VMEM)
ANYWHERE = pl.BlockSpec(memory_space=pl.ANY)


def round_up(value, multiple):
    return -(-value // multiple) * multiple


def whole(shape):
    return pl.BlockSpec(shape, lambda *_: (0,) * len(shape))


def nesterov_of(grad_ref, momentum_ref, j):
    grad = grad_ref[j].astype(jnp.float32)
    new = momentum_beta * momentum_ref[j] + grad
    return new, (grad + momentum_beta * new).astype(jnp.bfloat16)


def make_plan(col_size, owner_ref, other_ref, rank_ref, count_ref, list_ref):
    devices, mats = other_ref.shape[0], rank_ref.shape[0]

    def clear(d, _):
        count_ref[d] = 0
        return 0

    lax.fori_loop(0, devices, clear, 0, unroll=8)

    def rank_matrix(i, _):
        owner = owner_ref[i]
        rank = count_ref[owner]
        rank_ref[i] = rank
        count_ref[owner] = rank + 1
        return 0

    lax.fori_loop(0, mats, rank_matrix, 0, unroll=8)

    def list_device(d, found):
        owns = jnp.minimum(count_ref[d], 1)
        half = (d % col_size) // (col_size // HALVES)
        row = 2 * jnp.where(owns == 1, half, 1 - half) + owns
        place = found[0]
        for k in range(1, 2 * HALVES):
            place = jnp.where(row == k, found[k], place)
        list_ref[row * devices + place] = d
        return tuple(n + jnp.where(row == k, 1, 0) for k, n in enumerate(found))

    found = lax.fori_loop(0, devices, list_device, (0,) * (2 * HALVES), unroll=8)
    for half in range(HALVES):

        def pair(k, _):
            idle = list_ref[2 * half * devices + k]
            other_ref[list_ref[(2 * half + 1) * devices + k]] = idle
            other_ref[idle] = idle
            return 0

        lax.fori_loop(0, found[2 * half + 1], pair, 0)


def pack_kernel(
    chunk, col_size, owner_ref, g_ref, m_ref, first_ref, other_ref, rank_ref,
    count_ref, list_ref, g_s, m_s, sems,
):
    mats = rank_ref.shape[0]

    def loads(k):
        span = pl.ds(k * chunk, chunk)
        return (
            pltpu.make_async_copy(g_ref.at[span], g_s.at[span], sems.at[0, k]),
            pltpu.make_async_copy(m_ref.at[span], m_s.at[span], sems.at[1, k]),
        )

    for k in range(mats // chunk):
        for load in loads(k):
            load.start()
    make_plan(col_size, owner_ref, other_ref, rank_ref, count_ref, list_ref)
    for k in range(mats // chunk):
        for load in loads(k):
            load.wait()
        for i in range(k * chunk, (k + 1) * chunk):

            @pl.when(rank_ref[i] == 0)
            def _():
                nesterov = nesterov_of(g_s, m_s, i)[1]
                first_ref[owner_ref[i]] = nesterov
                first_ref[other_ref[owner_ref[i]]] = nesterov


def pack(gradients, momentum, owner_table, devices, col_size):
    mats, rows, cols = gradients.shape
    chunk = 8
    return pl.pallas_call(
        functools.partial(pack_kernel, chunk, col_size),
        grid_spec=pltpu.PrefetchScalarGridSpec(
            num_scalar_prefetch=1,
            grid=(1,),
            in_specs=[ANYWHERE, ANYWHERE],
            out_specs=[whole((devices, rows, cols)), SMEM, SMEM],
            scratch_shapes=[
                pltpu.SMEM((devices,), jnp.int32),
                pltpu.SMEM((2 * HALVES * devices,), jnp.int32),
                pltpu.VMEM(gradients.shape, gradients.dtype),
                pltpu.VMEM(momentum.shape, momentum.dtype),
                pltpu.SemaphoreType.DMA((2, mats // chunk)),
            ],
        ),
        out_shape=[
            jax.ShapeDtypeStruct((devices, rows, cols), jnp.bfloat16),
            jax.ShapeDtypeStruct((devices,), jnp.int32),
            jax.ShapeDtypeStruct((mats,), jnp.int32),
        ],
        compiler_params=PACK_PARAMS,
        cost_estimate=pl.CostEstimate(
            flops=4 * mats * rows * cols, bytes_accessed=8 * mats * rows * cols, transcendentals=0
        ),
        name="pack",
    )(owner_table, gradients, momentum)


def momentum_kernel(
    chunk, col_size, owner_ref, other_ref, rank_ref, g_ref, m_ref, nm_ref, second_ref, list_ref,
    count_ref,
):
    step = pl.program_id(0)
    width = col_size // HALVES
    row, col = lax.axis_index("dp"), lax.axis_index("owner")
    listed = list_ref.shape[0] // CAP

    @pl.when(step == 0)
    def _():
        for slot in range(CAP):
            count_ref[slot] = 0

    for j in range(chunk):
        i = step * chunk + j
        new, nesterov = nesterov_of(g_ref, m_ref, j)
        nm_ref[j] = new
        owner = owner_ref[i]

        @pl.when(rank_ref[i] == 1)
        def _():
            second_ref[owner] = nesterov
            second_ref[other_ref[owner]] = nesterov

        near = (owner % col_size) // width == col // width
        host = jnp.where(near, owner, other_ref[owner])
        host_row, host_col = host // col_size, host % width
        offset = host_row ^ row
        high = offset // LOW * width + (host_col ^ (col % width))
        place = jnp.where(
            rank_ref[i] == 0, high * LOW + offset % LOW, host_row * width + host_col
        )
        rank = rank_ref[i]
        entry = count_ref[rank]
        count_ref[rank] = entry + 1
        list_ref[rank * listed + 2 * entry] = i
        list_ref[rank * listed + 2 * entry + 1] = place


def update_momentum(gradients, momentum, owner_table, other, rank, col_size):
    mats, rows, cols = gradients.shape
    devices = other.shape[0]
    chunk = 8
    block = pl.BlockSpec((chunk, rows, cols), lambda i, *_: (i, 0, 0))
    return pl.pallas_call(
        functools.partial(momentum_kernel, chunk, col_size),
        grid_spec=pltpu.PrefetchScalarGridSpec(
            num_scalar_prefetch=3,
            grid=(mats // chunk,),
            in_specs=[block, block],
            out_specs=[block, whole((devices, rows, cols)), SMEM],
            scratch_shapes=[pltpu.SMEM((CAP,), jnp.int32)],
        ),
        out_shape=[
            jax.ShapeDtypeStruct(momentum.shape, jnp.float32),
            jax.ShapeDtypeStruct((devices, rows, cols), jnp.bfloat16),
            jax.ShapeDtypeStruct((2 * mats,), jnp.int32),
        ],
        compiler_params=PARAMS,
        cost_estimate=pl.CostEstimate(
            flops=4 * mats * rows * cols, bytes_accessed=12 * mats * rows * cols, transcendentals=0
        ),
        name="update_momentum",
    )(owner_table, other, rank, gradients, momentum)


def matmul(lhs, rhs, rhs_dim):
    return lax.dot_general(
        lhs, rhs, (((1,), (rhs_dim,)), ((), ())), preferred_element_type=jnp.float32
    )


def sum_rows(values):
    rows, cols = values.shape
    if rows % 8:
        return jnp.sum(values, axis=0, keepdims=True)
    return jnp.sum(values.reshape(rows // 8, 8, cols), axis=0)


def gather_blocks(x_ref, x_s, row_size, col_size):
    _, rows, cols = x_ref.shape
    height = rows * row_size
    total = 0.0
    for r in range(row_size):
        for c in range(col_size):
            block = x_ref[r * col_size + c]
            x_s[r * rows : (r + 1) * rows, c * cols : (c + 1) * cols] = block
            wide = block.astype(jnp.float32)
            total = total + sum_rows(wide * wide)
    x_s[height:, :] = jnp.zeros((x_s.shape[0] - height, x_s.shape[1]), x_s.dtype)
    return 1.0 / (jnp.sqrt(jnp.sum(total, keepdims=True)) + epsilon)


def update_scale(height, width):
    return 0.2 * math.sqrt(max(height, width))


def newton_schulz(height, inverse, x_s, y_s, gram_s, finish):
    padded = x_s.shape[0]
    tile = height // TILES
    for ref in (y_s, gram_s):
        ref[height:, :] = jnp.zeros((padded - height, ref.shape[1]), ref.dtype)
    for iteration in range(ITERS):
        src = x_s if iteration == 0 else y_s
        gram = matmul(src[:height, :], src[...], 1)
        if iteration == 0:
            gram = gram * (inverse * inverse)
        gram_s[:height, :] = gram.astype(jnp.bfloat16)
        for t in range(TILES):
            span = slice(t * tile, (t + 1) * tile)
            square = matmul(gram_s[span, :], gram_s[...], 0)
            mixing = coef_b * gram_s[span, :].astype(jnp.float32) + coef_c * square
            mixing = mixing.astype(jnp.bfloat16)
            if iteration + 1 < ITERS:
                combined = combine(src, span, slice(None), mixing)
                if iteration == 0:
                    combined = combined * inverse
                y_s[span, :] = combined.astype(jnp.bfloat16)
            else:
                finish(t, span, mixing)


def combine(src, span, columns, mixing):
    return coef_a * src[span, columns].astype(jnp.float32) + matmul(mixing, src[:, columns], 0)


def stage_place(row_offset, col_offset, row_size, width):
    high = row_offset // LOW * width + col_offset
    return row_offset % LOW * (row_size // LOW * width) + high


def ortho_kernel(row_size, col_size, slot, other_ref, x_ref, *refs):
    _, rows, cols = x_ref.shape
    width = col_size // HALVES
    half = width * cols
    places = row_size * width
    height = rows * row_size
    tile = height // TILES
    if slot:
        whole_ref, out_ref, x_s, y_s, gram_s, back_ref, sems, mix_s = refs
    else:
        owned_ref, low_refs = refs[0], refs[1 : 1 + LOW]
        x_s, y_s, gram_s, back_ref, sems, whole_ref = refs[1 + LOW :]
    row, col = lax.axis_index("dp"), lax.axis_index("owner")
    me = row * col_size + col
    owns = other_ref[me] != me
    inverse = gather_blocks(x_ref, x_s, row_size, col_size)

    def copy_out(t):
        if slot:
            span = pl.ds(t * (places // TILES), places // TILES)
            return pltpu.make_async_copy(back_ref.at[span], out_ref.at[span], sems.at[t])
        span = pl.ds(t * tile, tile)
        return pltpu.make_async_copy(whole_ref.at[span], owned_ref.at[slot, span], sems.at[t])

    def product(span, columns, mixing):
        result = update_scale(height, cols * col_size) * combine(y_s, span, columns, mixing)
        result = result.astype(jnp.bfloat16)
        whole_ref[span, columns] = jnp.where(owns, result, jnp.zeros_like(result))
        return result

    def columns_of(number):
        return pl.ds(pl.multiple_of(number * half, half), half)

    def finish(t, span, mixing):
        if slot:
            mix_s[span, :] = mixing
            result = product(span, columns_of(col // width), mixing)
        else:
            result = product(span, slice(None), mixing)
            result = jnp.where(col < width, result[:, :half], result[:, half:])
        for j in range(row_size // TILES):
            r = t * (row_size // TILES) + j
            for c in range(width):
                if slot:
                    place = r * width + c
                else:
                    place = stage_place(r ^ row, c ^ (col % width), row_size, width)
                back_ref[place] = result[
                    j * rows : (j + 1) * rows, c * cols : (c + 1) * cols
                ]
        copy_out(t).start()

    newton_schulz(height, inverse, x_s, y_s, gram_s, finish)
    if slot:
        for t in range(TILES):
            span = slice(t * tile, (t + 1) * tile)
            product(span, columns_of(1 - col // width), mix_s[span, :])
    else:
        for k in range(LOW):
            low_refs[k][...] = back_ref[k * places // LOW : (k + 1) * places // LOW]
    for t in range(TILES):
        copy_out(t).wait()


def orthogonalize(slot, other, arrived, row_size, col_size):
    devices, rows, cols = arrived.shape
    height, width = rows * row_size, cols * col_size
    padded = round_up(height, 256)
    places = devices // HALVES
    scratch_shapes = [
        pltpu.VMEM((padded, width), jnp.bfloat16),
        pltpu.VMEM((padded, width), jnp.bfloat16),
        pltpu.VMEM((padded, padded), jnp.bfloat16),
        pltpu.VMEM((places, rows, cols), jnp.bfloat16),
        pltpu.SemaphoreType.DMA((TILES,)),
    ]
    if slot:
        scratch_shapes.append(pltpu.VMEM((height, padded), jnp.bfloat16))
        out_specs = [VMEM, ANYWHERE]
        out = [(height, width), (places, rows, cols)]
    else:
        out_specs = [ANYWHERE] + [VMEM] * LOW
        out = [(CAP, height, width)] + [(places // LOW, rows, cols)] * LOW
        scratch_shapes.append(pltpu.VMEM((height, width), jnp.bfloat16))
    return pl.pallas_call(
        functools.partial(ortho_kernel, row_size, col_size, slot),
        in_specs=[SMEM, VMEM],
        out_specs=out_specs,
        out_shape=[
            pltpu.HBM(shape, jnp.bfloat16)
            if spec is ANYWHERE
            else jax.ShapeDtypeStruct(shape, jnp.bfloat16)
            for spec, shape in zip(out_specs, out)
        ],
        scratch_shapes=scratch_shapes,
        compiler_params=PARAMS,
        cost_estimate=pl.CostEstimate(
            flops=2 * ITERS * padded * padded * (2 * width + padded),
            bytes_accessed=6 * padded * width,
            transcendentals=0,
        ),
        name="orthogonalize",
    )(other, arrived)


def restage_kernel(*refs):
    low_refs, high_refs = refs[:LOW], refs[LOW:]
    for h, high_ref in enumerate(high_refs):
        for k, low_ref in enumerate(low_refs):
            high_ref[k] = low_ref[h]


def restage(blocks):
    highs, rows, cols = blocks[0].shape
    out = jax.ShapeDtypeStruct((LOW, rows, cols), blocks[0].dtype)
    return pl.pallas_call(
        restage_kernel,
        grid=(1,),
        in_specs=[whole(blocks[0].shape)] * LOW,
        out_specs=[whole(out.shape)] * highs,
        out_shape=[out] * highs,
        compiler_params=PARAMS,
        cost_estimate=pl.CostEstimate(
            flops=0, bytes_accessed=4 * LOW * highs * rows * cols, transcendentals=0
        ),
        name="restage",
    )(*blocks)


def start_blocks(slot, list_ref, back_ref, update_ref, sem):
    listed = list_ref.shape[0] // CAP
    for k in range(update_ref.shape[0] // CAP):
        matrix = list_ref[slot * listed + 2 * k]
        place = list_ref[slot * listed + 2 * k + 1]
        pltpu.make_async_copy(back_ref.at[place], update_ref.at[matrix], sem).start()


def wait_blocks(back_ref, update_ref, sem):
    span = pl.ds(0, update_ref.shape[0] // CAP)
    pltpu.make_async_copy(back_ref.at[span], update_ref.at[span], sem).wait()


def early_kernel(list_ref, whole_ref, owned_in, *refs):
    high_refs, (owned_ref, update_ref, back_s, own_sem, sem) = refs[:-5], refs[-5:]
    own = pltpu.make_async_copy(whole_ref, owned_ref.at[CAP - 1], own_sem)
    own.start()
    for h, high_ref in enumerate(high_refs):
        back_s[h * LOW : (h + 1) * LOW] = high_ref[...]
    start_blocks(0, list_ref, back_s, update_ref, sem)
    wait_blocks(back_s, update_ref, sem)
    own.wait()


def store_early(places, mats, matrix, owned, first):
    _, rows, cols = first[0].shape
    return pl.pallas_call(
        early_kernel,
        in_specs=[SMEM, VMEM, ANYWHERE] + [VMEM] * len(first),
        out_specs=[ANYWHERE, ANYWHERE],
        out_shape=[
            jax.ShapeDtypeStruct(owned.shape, jnp.bfloat16),
            jax.ShapeDtypeStruct((mats, rows, cols), jnp.bfloat16),
        ],
        scratch_shapes=[
            pltpu.VMEM((LOW * len(first), rows, cols), jnp.bfloat16),
            pltpu.SemaphoreType.DMA(()),
            pltpu.SemaphoreType.DMA(()),
        ],
        input_output_aliases={2: 0},
        compiler_params=PARAMS,
        cost_estimate=pl.CostEstimate(
            flops=0, bytes_accessed=8 * mats * rows * cols, transcendentals=0
        ),
        name="store_early",
    )(places, matrix, owned, *first)


def late_kernel(list_ref, back_ref, update_in, update_ref, sem):
    start_blocks(1, list_ref, back_ref, update_ref, sem)
    wait_blocks(back_ref, update_ref, sem)


def store_late(places, second, update):
    return pl.pallas_call(
        late_kernel,
        in_specs=[SMEM, VMEM, ANYWHERE],
        out_specs=ANYWHERE,
        out_shape=jax.ShapeDtypeStruct(update.shape, jnp.bfloat16),
        scratch_shapes=[pltpu.SemaphoreType.DMA(())],
        input_output_aliases={2: 0},
        compiler_params=PARAMS,
        cost_estimate=pl.CostEstimate(flops=0, bytes_accessed=4 * second.size, transcendentals=0),
        name="store_late",
    )(places, second, update)


def exchange(blocks, axes, groups=None):
    return lax.all_to_all(
        blocks, axes, split_axis=0, concat_axis=0, tiled=True, axis_index_groups=groups
    )


def swap(block, offset, devices):
    return lax.ppermute(block, AXES, [(d, d ^ offset) for d in range(devices)])


def on_device(gradients, momentum, owner_table):
    row_size = lax.axis_size("dp")
    col_size = lax.axis_size("owner")
    devices = row_size * col_size
    width = col_size // HALVES
    halves = [
        [r * col_size + half * width + c for r in range(row_size) for c in range(width)]
        for half in range(HALVES)
    ]
    first, other, rank = pack(gradients, momentum, owner_table, devices, col_size)
    arrived_first = exchange(first, AXES)
    new_momentum, second, places = update_momentum(
        gradients, momentum, owner_table, other, rank, col_size
    )
    arrived_first, second = lax.optimization_barrier((arrived_first, second))
    arrived_second = exchange(second, AXES)
    owned, *back_first = orthogonalize(0, other, arrived_first, row_size, col_size)
    low = [back_first[0]] + [
        swap(back_first[k], k * col_size, devices) for k in range(1, LOW)
    ]
    high = restage(low)
    _, arrived_second = lax.optimization_barrier((high, arrived_second))
    returned_first = [high[0]] + [
        swap(high[r * width + c], r * LOW * col_size + c, devices)
        for r in range(row_size // LOW)
        for c in range(width)
        if r or c
    ]
    matrix, back_second = orthogonalize(1, other, arrived_second, row_size, col_size)
    returned_first, back_second = lax.optimization_barrier((returned_first, back_second))
    returned_second = exchange(back_second, AXES, halves)
    owned, update = store_early(
        places, owner_table.shape[0], matrix, owned, returned_first
    )
    update = store_late(places, returned_second, update)
    return (new_momentum, update, owned)


def solution(mesh):
    return jax.shard_map(
        on_device,
        mesh=mesh,
        in_specs=(P(None, "dp", "owner"), P(None, "dp", "owner"), P()),
        out_specs=(P(None, "dp", "owner"), P(None, "dp", "owner"), P(("dp", "owner"), None, None)),
        check_vma=False,
    )
```

```python
import functools
import math

import jax
import jax.numpy as jnp
from jax import lax
from jax.experimental import pallas as pl
from jax.experimental.pallas import tpu as pltpu
from jax.sharding import PartitionSpec as P

ITERS = 2
CAP = 2
HALVES = 2
TILES = 2
COLUMNS = 256
LOW = 4

coef_a = 3.4445
coef_b = -4.775
coef_c = 2.0315
momentum_beta = 0.95
epsilon = 1e-07

AXES = ("dp", "owner")
MIB = 1024 * 1024
PARAMS = pltpu.CompilerParams(vmem_limit_bytes=24 * MIB)
PACK_PARAMS = pltpu.CompilerParams(vmem_limit_bytes=60 * MIB)
SMEM = pl.BlockSpec(memory_space=pltpu.SMEM)
VMEM = pl.BlockSpec(memory_space=pltpu.VMEM)
ANYWHERE = pl.BlockSpec(memory_space=pl.ANY)


def round_up(value, multiple):
    return -(-value // multiple) * multiple


def whole(shape):
    return pl.BlockSpec(shape, lambda *_: (0,) * len(shape))


def nesterov_of(grad_ref, momentum_ref, j):
    grad = grad_ref[j].astype(jnp.float32)
    new = momentum_beta * momentum_ref[j] + grad
    return new, (grad + momentum_beta * new).astype(jnp.bfloat16)


def make_plan(col_size, owner_ref, other_ref, rank_ref, count_ref, list_ref):
    devices, mats = other_ref.shape[0], rank_ref.shape[0]

    def clear(d, _):
        count_ref[d] = 0
        return 0

    lax.fori_loop(0, devices, clear, 0, unroll=8)

    def rank_matrix(i, _):
        owner = owner_ref[i]
        rank = count_ref[owner]
        rank_ref[i] = rank
        count_ref[owner] = rank + 1
        return 0

    lax.fori_loop(0, mats, rank_matrix, 0, unroll=8)

    def list_device(d, found):
        owns = jnp.minimum(count_ref[d], 1)
        half = (d % col_size) // (col_size // HALVES)
        row = 2 * jnp.where(owns == 1, half, 1 - half) + owns
        place = found[0]
        for k in range(1, 2 * HALVES):
            place = jnp.where(row == k, found[k], place)
        list_ref[row * devices + place] = d
        return tuple(n + jnp.where(row == k, 1, 0) for k, n in enumerate(found))

    found = lax.fori_loop(0, devices, list_device, (0,) * (2 * HALVES), unroll=8)
    for half in range(HALVES):

        def pair(k, _):
            idle = list_ref[2 * half * devices + k]
            other_ref[list_ref[(2 * half + 1) * devices + k]] = idle
            other_ref[idle] = idle
            return 0

        lax.fori_loop(0, found[2 * half + 1], pair, 0)


def pack_kernel(
    chunk, col_size, owner_ref, g_ref, m_ref, first_ref, other_ref, rank_ref,
    count_ref, list_ref, g_s, m_s, sems,
):
    mats = rank_ref.shape[0]

    def loads(k):
        span = pl.ds(k * chunk, chunk)
        return (
            pltpu.make_async_copy(g_ref.at[span], g_s.at[span], sems.at[0, k]),
            pltpu.make_async_copy(m_ref.at[span], m_s.at[span], sems.at[1, k]),
        )

    for k in range(mats // chunk):
        for load in loads(k):
            load.start()
    make_plan(col_size, owner_ref, other_ref, rank_ref, count_ref, list_ref)
    for k in range(mats // chunk):
        for load in loads(k):
            load.wait()
        for i in range(k * chunk, (k + 1) * chunk):

            @pl.when(rank_ref[i] == 0)
            def _():
                nesterov = nesterov_of(g_s, m_s, i)[1]
                first_ref[owner_ref[i]] = nesterov
                first_ref[other_ref[owner_ref[i]]] = nesterov


def pack(gradients, momentum, owner_table, devices, col_size):
    mats, rows, cols = gradients.shape
    chunk = 8
    return pl.pallas_call(
        functools.partial(pack_kernel, chunk, col_size),
        grid_spec=pltpu.PrefetchScalarGridSpec(
            num_scalar_prefetch=1,
            grid=(1,),
            in_specs=[ANYWHERE, ANYWHERE],
            out_specs=[whole((devices, rows, cols)), SMEM, SMEM],
            scratch_shapes=[
                pltpu.SMEM((devices,), jnp.int32),
                pltpu.SMEM((2 * HALVES * devices,), jnp.int32),
                pltpu.VMEM(gradients.shape, gradients.dtype),
                pltpu.VMEM(momentum.shape, momentum.dtype),
                pltpu.SemaphoreType.DMA((2, mats // chunk)),
            ],
        ),
        out_shape=[
            jax.ShapeDtypeStruct((devices, rows, cols), jnp.bfloat16),
            jax.ShapeDtypeStruct((devices,), jnp.int32),
            jax.ShapeDtypeStruct((mats,), jnp.int32),
        ],
        compiler_params=PACK_PARAMS,
        cost_estimate=pl.CostEstimate(
            flops=4 * mats * rows * cols, bytes_accessed=8 * mats * rows * cols, transcendentals=0
        ),
        name="pack",
    )(owner_table, gradients, momentum)


def momentum_kernel(
    chunk, col_size, owner_ref, other_ref, rank_ref, g_ref, m_ref, nm_ref, second_ref, list_ref,
    count_ref,
):
    step = pl.program_id(0)
    width = col_size // HALVES
    row, col = lax.axis_index("dp"), lax.axis_index("owner")
    listed = list_ref.shape[0] // CAP

    @pl.when(step == 0)
    def _():
        for slot in range(CAP):
            count_ref[slot] = 0

    for j in range(chunk):
        i = step * chunk + j
        new, nesterov = nesterov_of(g_ref, m_ref, j)
        nm_ref[j] = new
        owner = owner_ref[i]

        @pl.when(rank_ref[i] == 1)
        def _():
            second_ref[owner] = nesterov
            second_ref[other_ref[owner]] = nesterov

        near = (owner % col_size) // width == col // width
        host = jnp.where(near, owner, other_ref[owner])
        host_row, host_col = host // col_size, host % width
        offset = host_row ^ row
        high = offset // LOW * width + (host_col ^ (col % width))
        place = jnp.where(
            rank_ref[i] == 0, high * LOW + offset % LOW, host_row * width + host_col
        )
        rank = rank_ref[i]
        entry = count_ref[rank]
        count_ref[rank] = entry + 1
        list_ref[rank * listed + 2 * entry] = i
        list_ref[rank * listed + 2 * entry + 1] = place


def update_momentum(gradients, momentum, owner_table, other, rank, col_size):
    mats, rows, cols = gradients.shape
    devices = other.shape[0]
    chunk = 8
    block = pl.BlockSpec((chunk, rows, cols), lambda i, *_: (i, 0, 0))
    return pl.pallas_call(
        functools.partial(momentum_kernel, chunk, col_size),
        grid_spec=pltpu.PrefetchScalarGridSpec(
            num_scalar_prefetch=3,
            grid=(mats // chunk,),
            in_specs=[block, block],
            out_specs=[block, whole((devices, rows, cols)), SMEM],
            scratch_shapes=[pltpu.SMEM((CAP,), jnp.int32)],
        ),
        out_shape=[
            jax.ShapeDtypeStruct(momentum.shape, jnp.float32),
            jax.ShapeDtypeStruct((devices, rows, cols), jnp.bfloat16),
            jax.ShapeDtypeStruct((2 * mats,), jnp.int32),
        ],
        compiler_params=PARAMS,
        cost_estimate=pl.CostEstimate(
            flops=4 * mats * rows * cols, bytes_accessed=12 * mats * rows * cols, transcendentals=0
        ),
        name="update_momentum",
    )(owner_table, other, rank, gradients, momentum)


def matmul(lhs, rhs, rhs_dim):
    return lax.dot_general(
        lhs, rhs, (((1,), (rhs_dim,)), ((), ())), preferred_element_type=jnp.float32
    )


def sum_rows(values):
    rows, cols = values.shape
    if rows % 8:
        return jnp.sum(values, axis=0, keepdims=True)
    return jnp.sum(values.reshape(rows // 8, 8, cols), axis=0)


def gather_blocks(x_ref, x_s, row_size, col_size):
    _, rows, cols = x_ref.shape
    height = rows * row_size
    total = 0.0
    for r in range(row_size):
        for c in range(col_size):
            block = x_ref[r * col_size + c]
            x_s[r * rows : (r + 1) * rows, c * cols : (c + 1) * cols] = block
            wide = block.astype(jnp.float32)
            total = total + sum_rows(wide * wide)
    x_s[height:, :] = jnp.zeros((x_s.shape[0] - height, x_s.shape[1]), x_s.dtype)
    return 1.0 / (jnp.sqrt(jnp.sum(total, keepdims=True)) + epsilon)


def update_scale(height, width):
    return 0.2 * math.sqrt(max(height, width))


def newton_schulz(height, inverse, x_s, y_s, gram_s, mix_s, finish):
    padded = x_s.shape[0]
    tile = height // TILES
    for ref in (y_s, gram_s):
        ref[height:, :] = jnp.zeros((padded - height, ref.shape[1]), ref.dtype)
    for iteration in range(ITERS):
        src = x_s if iteration == 0 else y_s
        for c in range(0, padded, COLUMNS):
            columns = slice(c, c + COLUMNS)
            gram = matmul(src[:height, :], src[columns, :], 1)
            if iteration == 0:
                gram = gram * (inverse * inverse)
            gram_s[:height, columns] = gram.astype(jnp.bfloat16)
        for c in range(0, padded, COLUMNS):
            columns = slice(c, c + COLUMNS)
            square = matmul(gram_s[:height, :], gram_s[:, columns], 0)
            mixing = coef_b * gram_s[:height, columns].astype(jnp.float32) + coef_c * square
            mix_s[:, columns] = mixing.astype(jnp.bfloat16)
        for t in range(TILES):
            span = slice(t * tile, (t + 1) * tile)
            if iteration + 1 < ITERS:
                combined = combine(src, span, slice(None), mix_s[span, :])
                if iteration == 0:
                    combined = combined * inverse
                y_s[span, :] = combined.astype(jnp.bfloat16)
            else:
                finish(t, span, mix_s[span, :])


def combine(src, span, columns, mixing):
    return coef_a * src[span, columns].astype(jnp.float32) + matmul(mixing, src[:, columns], 0)


def stage_place(row_offset, col_offset, row_size, width):
    high = row_offset // LOW * width + col_offset
    return row_offset % LOW * (row_size // LOW * width) + high


def ortho_kernel(row_size, col_size, slot, other_ref, x_ref, *refs):
    _, rows, cols = x_ref.shape
    width = col_size // HALVES
    half = width * cols
    places = row_size * width
    height = rows * row_size
    tile = height // TILES
    if slot:
        whole_ref, out_ref, x_s, y_s, gram_s, back_ref, sems, mix_s = refs
    else:
        owned_ref, low_refs = refs[0], refs[1 : 1 + LOW]
        x_s, y_s, gram_s, back_ref, sems, mix_s, whole_ref = refs[1 + LOW :]
    row, col = lax.axis_index("dp"), lax.axis_index("owner")
    me = row * col_size + col
    owns = other_ref[me] != me
    inverse = gather_blocks(x_ref, x_s, row_size, col_size)

    def copy_out(t):
        if slot:
            span = pl.ds(t * (places // TILES), places // TILES)
            return pltpu.make_async_copy(back_ref.at[span], out_ref.at[span], sems.at[t])
        span = pl.ds(t * tile, tile)
        return pltpu.make_async_copy(whole_ref.at[span], owned_ref.at[slot, span], sems.at[t])

    def product(span, columns, mixing):
        result = update_scale(height, cols * col_size) * combine(y_s, span, columns, mixing)
        result = result.astype(jnp.bfloat16)
        whole_ref[span, columns] = jnp.where(owns, result, jnp.zeros_like(result))
        return result

    def columns_of(number):
        return pl.ds(pl.multiple_of(number * half, half), half)

    def finish(t, span, mixing):
        if slot:
            result = product(span, columns_of(col // width), mixing)
        else:
            result = product(span, slice(None), mixing)
            result = jnp.where(col < width, result[:, :half], result[:, half:])
        for j in range(row_size // TILES):
            r = t * (row_size // TILES) + j
            for c in range(width):
                if slot:
                    place = r * width + c
                else:
                    place = stage_place(r ^ row, c ^ (col % width), row_size, width)
                back_ref[place] = result[
                    j * rows : (j + 1) * rows, c * cols : (c + 1) * cols
                ]
        copy_out(t).start()

    newton_schulz(height, inverse, x_s, y_s, gram_s, mix_s, finish)
    if slot:
        for t in range(TILES):
            span = slice(t * tile, (t + 1) * tile)
            product(span, columns_of(1 - col // width), mix_s[span, :])
    else:
        for k in range(LOW):
            low_refs[k][...] = back_ref[k * places // LOW : (k + 1) * places // LOW]
    for t in range(TILES):
        copy_out(t).wait()


def orthogonalize(slot, other, arrived, row_size, col_size):
    devices, rows, cols = arrived.shape
    height, width = rows * row_size, cols * col_size
    padded = round_up(height, 256)
    places = devices // HALVES
    scratch_shapes = [
        pltpu.VMEM((padded, width), jnp.bfloat16),
        pltpu.VMEM((padded, width), jnp.bfloat16),
        pltpu.VMEM((padded, padded), jnp.bfloat16),
        pltpu.VMEM((places, rows, cols), jnp.bfloat16),
        pltpu.SemaphoreType.DMA((TILES,)),
        pltpu.VMEM((height, padded), jnp.bfloat16),
    ]
    if slot:
        out_specs = [VMEM, ANYWHERE]
        out = [(height, width), (places, rows, cols)]
    else:
        out_specs = [ANYWHERE] + [VMEM] * LOW
        out = [(CAP, height, width)] + [(places // LOW, rows, cols)] * LOW
        scratch_shapes.append(pltpu.VMEM((height, width), jnp.bfloat16))
    return pl.pallas_call(
        functools.partial(ortho_kernel, row_size, col_size, slot),
        in_specs=[SMEM, VMEM],
        out_specs=out_specs,
        out_shape=[
            pltpu.HBM(shape, jnp.bfloat16)
            if spec is ANYWHERE
            else jax.ShapeDtypeStruct(shape, jnp.bfloat16)
            for spec, shape in zip(out_specs, out)
        ],
        scratch_shapes=scratch_shapes,
        compiler_params=PARAMS,
        cost_estimate=pl.CostEstimate(
            flops=2 * ITERS * padded * padded * (2 * width + padded),
            bytes_accessed=6 * padded * width,
            transcendentals=0,
        ),
        name="orthogonalize",
    )(other, arrived)


def restage_kernel(*refs):
    low_refs, high_refs = refs[:LOW], refs[LOW:]
    for h, high_ref in enumerate(high_refs):
        for k, low_ref in enumerate(low_refs):
            high_ref[k] = low_ref[h]


def restage(blocks):
    highs, rows, cols = blocks[0].shape
    out = jax.ShapeDtypeStruct((LOW, rows, cols), blocks[0].dtype)
    return pl.pallas_call(
        restage_kernel,
        grid=(1,),
        in_specs=[whole(blocks[0].shape)] * LOW,
        out_specs=[whole(out.shape)] * highs,
        out_shape=[out] * highs,
        compiler_params=PARAMS,
        cost_estimate=pl.CostEstimate(
            flops=0, bytes_accessed=4 * LOW * highs * rows * cols, transcendentals=0
        ),
        name="restage",
    )(*blocks)


def start_blocks(slot, list_ref, back_ref, update_ref, sem):
    listed = list_ref.shape[0] // CAP
    for k in range(update_ref.shape[0] // CAP):
        matrix = list_ref[slot * listed + 2 * k]
        place = list_ref[slot * listed + 2 * k + 1]
        pltpu.make_async_copy(back_ref.at[place], update_ref.at[matrix], sem).start()


def wait_blocks(back_ref, update_ref, sem):
    span = pl.ds(0, update_ref.shape[0] // CAP)
    pltpu.make_async_copy(back_ref.at[span], update_ref.at[span], sem).wait()


def early_kernel(list_ref, whole_ref, owned_in, *refs):
    high_refs, (owned_ref, update_ref, back_s, own_sem, sem) = refs[:-5], refs[-5:]
    own = pltpu.make_async_copy(whole_ref, owned_ref.at[CAP - 1], own_sem)
    own.start()
    for h, high_ref in enumerate(high_refs):
        back_s[h * LOW : (h + 1) * LOW] = high_ref[...]
    start_blocks(0, list_ref, back_s, update_ref, sem)
    wait_blocks(back_s, update_ref, sem)
    own.wait()


def store_early(places, mats, matrix, owned, first):
    _, rows, cols = first[0].shape
    return pl.pallas_call(
        early_kernel,
        in_specs=[SMEM, VMEM, ANYWHERE] + [VMEM] * len(first),
        out_specs=[ANYWHERE, ANYWHERE],
        out_shape=[
            jax.ShapeDtypeStruct(owned.shape, jnp.bfloat16),
            jax.ShapeDtypeStruct((mats, rows, cols), jnp.bfloat16),
        ],
        scratch_shapes=[
            pltpu.VMEM((LOW * len(first), rows, cols), jnp.bfloat16),
            pltpu.SemaphoreType.DMA(()),
            pltpu.SemaphoreType.DMA(()),
        ],
        input_output_aliases={2: 0},
        compiler_params=PARAMS,
        cost_estimate=pl.CostEstimate(
            flops=0, bytes_accessed=8 * mats * rows * cols, transcendentals=0
        ),
        name="store_early",
    )(places, matrix, owned, *first)


def late_kernel(list_ref, back_ref, update_in, update_ref, sem):
    start_blocks(1, list_ref, back_ref, update_ref, sem)
    wait_blocks(back_ref, update_ref, sem)


def store_late(places, second, update):
    return pl.pallas_call(
        late_kernel,
        in_specs=[SMEM, VMEM, ANYWHERE],
        out_specs=ANYWHERE,
        out_shape=jax.ShapeDtypeStruct(update.shape, jnp.bfloat16),
        scratch_shapes=[pltpu.SemaphoreType.DMA(())],
        input_output_aliases={2: 0},
        compiler_params=PARAMS,
        cost_estimate=pl.CostEstimate(flops=0, bytes_accessed=4 * second.size, transcendentals=0),
        name="store_late",
    )(places, second, update)


def exchange(blocks, axes, groups=None):
    return lax.all_to_all(
        blocks, axes, split_axis=0, concat_axis=0, tiled=True, axis_index_groups=groups
    )


def swap(block, offset, devices):
    return lax.ppermute(block, AXES, [(d, d ^ offset) for d in range(devices)])


def on_device(gradients, momentum, owner_table):
    row_size = lax.axis_size("dp")
    col_size = lax.axis_size("owner")
    devices = row_size * col_size
    width = col_size // HALVES
    halves = [
        [r * col_size + half * width + c for r in range(row_size) for c in range(width)]
        for half in range(HALVES)
    ]
    first, other, rank = pack(gradients, momentum, owner_table, devices, col_size)
    arrived_first = exchange(first, AXES)
    new_momentum, second, places = update_momentum(
        gradients, momentum, owner_table, other, rank, col_size
    )
    arrived_first, second = lax.optimization_barrier((arrived_first, second))
    arrived_second = exchange(second, AXES)
    owned, *back_first = orthogonalize(0, other, arrived_first, row_size, col_size)
    low = [back_first[0]] + [
        swap(back_first[k], k * col_size, devices) for k in range(1, LOW)
    ]
    high = restage(low)
    _, arrived_second = lax.optimization_barrier((high, arrived_second))
    returned_first = [high[0]] + [
        swap(high[r * width + c], r * LOW * col_size + c, devices)
        for r in range(row_size // LOW)
        for c in range(width)
        if r or c
    ]
    matrix, back_second = orthogonalize(1, other, arrived_second, row_size, col_size)
    returned_first, back_second = lax.optimization_barrier((returned_first, back_second))
    returned_second = exchange(back_second, AXES, halves)
    owned, update = store_early(
        places, owner_table.shape[0], matrix, owned, returned_first
    )
    update = store_late(places, returned_second, update)
    return (new_momentum, update, owned)


def solution(mesh):
    return jax.shard_map(
        on_device,
        mesh=mesh,
        in_specs=(P(None, "dp", "owner"), P(None, "dp", "owner"), P()),
        out_specs=(P(None, "dp", "owner"), P(None, "dp", "owner"), P(("dp", "owner"), None, None)),
        check_vma=False,
    )
```

```python
import functools
import math

import jax
import jax.numpy as jnp
from jax import lax
from jax.experimental import pallas as pl
from jax.experimental.pallas import tpu as pltpu
from jax.sharding import PartitionSpec as P

ITERS = 2
CAP = 2
HALVES = 2
TILES = 2
LOW = 4

coef_a = 3.4445
coef_b = -4.775
coef_c = 2.0315
momentum_beta = 0.95
epsilon = 1e-07

AXES = ("dp", "owner")
MIB = 1024 * 1024
PARAMS = pltpu.CompilerParams(vmem_limit_bytes=24 * MIB)
PACK_PARAMS = pltpu.CompilerParams(vmem_limit_bytes=60 * MIB)
SMEM = pl.BlockSpec(memory_space=pltpu.SMEM)
VMEM = pl.BlockSpec(memory_space=pltpu.VMEM)
ANYWHERE = pl.BlockSpec(memory_space=pl.ANY)


def round_up(value, multiple):
    return -(-value // multiple) * multiple


def whole(shape):
    return pl.BlockSpec(shape, lambda *_: (0,) * len(shape))


def nesterov_of(grad_ref, momentum_ref, j):
    grad = grad_ref[j].astype(jnp.float32)
    new = momentum_beta * momentum_ref[j] + grad
    return new, (grad + momentum_beta * new).astype(jnp.bfloat16)


def make_plan(col_size, owner_ref, other_ref, rank_ref, count_ref, list_ref):
    devices, mats = other_ref.shape[0], rank_ref.shape[0]

    def clear(d, _):
        count_ref[d] = 0
        return 0

    lax.fori_loop(0, devices, clear, 0, unroll=8)

    def rank_matrix(i, _):
        owner = owner_ref[i]
        rank = count_ref[owner]
        rank_ref[i] = rank
        count_ref[owner] = rank + 1
        return 0

    lax.fori_loop(0, mats, rank_matrix, 0, unroll=8)

    def list_device(d, found):
        owns = jnp.minimum(count_ref[d], 1)
        half = (d % col_size) // (col_size // HALVES)
        row = 2 * jnp.where(owns == 1, half, 1 - half) + owns
        place = found[0]
        for k in range(1, 2 * HALVES):
            place = jnp.where(row == k, found[k], place)
        list_ref[row * devices + place] = d
        return tuple(n + jnp.where(row == k, 1, 0) for k, n in enumerate(found))

    found = lax.fori_loop(0, devices, list_device, (0,) * (2 * HALVES), unroll=8)
    for half in range(HALVES):

        def pair(k, _):
            idle = list_ref[2 * half * devices + k]
            other_ref[list_ref[(2 * half + 1) * devices + k]] = idle
            other_ref[idle] = idle
            return 0

        lax.fori_loop(0, found[2 * half + 1], pair, 0)


def pack_kernel(
    chunk, col_size, owner_ref, g_ref, m_ref, out_ref, other_ref, rank_ref,
    count_ref, list_ref, g_s, m_s, sems, first_ref, out_sems,
):
    mats = rank_ref.shape[0]

    def loads(k):
        span = pl.ds(k * chunk, chunk)
        return (
            pltpu.make_async_copy(g_ref.at[span], g_s.at[span], sems.at[0, k]),
            pltpu.make_async_copy(m_ref.at[span], m_s.at[span], sems.at[1, k]),
        )

    for k in range(mats // chunk):
        for load in loads(k):
            load.start()
    make_plan(col_size, owner_ref, other_ref, rank_ref, count_ref, list_ref)
    for k in range(mats // chunk):
        for load in loads(k):
            load.wait()
        for i in range(k * chunk, (k + 1) * chunk):

            @pl.when(rank_ref[i] == 0)
            def _():
                nesterov = nesterov_of(g_s, m_s, i)[1]
                first_ref[owner_ref[i]] = nesterov
                first_ref[other_ref[owner_ref[i]]] = nesterov

    stores = []
    parts = out_sems.shape[0]
    part = first_ref.shape[0] // parts
    for k in range(parts):
        span = pl.ds(k * part, part)
        stores.append(
            pltpu.make_async_copy(first_ref.at[span], out_ref.at[span], out_sems.at[k])
        )
    for store in stores:
        store.start()
    for store in stores:
        store.wait()


def pack(gradients, momentum, owner_table, devices, col_size):
    mats, rows, cols = gradients.shape
    chunk = 8
    return pl.pallas_call(
        functools.partial(pack_kernel, chunk, col_size),
        grid_spec=pltpu.PrefetchScalarGridSpec(
            num_scalar_prefetch=1,
            grid=(1,),
            in_specs=[ANYWHERE, ANYWHERE],
            out_specs=[ANYWHERE, SMEM, SMEM],
            scratch_shapes=[
                pltpu.SMEM((devices,), jnp.int32),
                pltpu.SMEM((2 * HALVES * devices,), jnp.int32),
                pltpu.VMEM(gradients.shape, gradients.dtype),
                pltpu.VMEM(momentum.shape, momentum.dtype),
                pltpu.SemaphoreType.DMA((2, mats // chunk)),
                pltpu.VMEM((devices, rows, cols), jnp.bfloat16),
                pltpu.SemaphoreType.DMA((8,)),
            ],
        ),
        out_shape=[
            pltpu.HBM((devices, rows, cols), jnp.bfloat16),
            jax.ShapeDtypeStruct((devices,), jnp.int32),
            jax.ShapeDtypeStruct((mats,), jnp.int32),
        ],
        compiler_params=PACK_PARAMS,
        cost_estimate=pl.CostEstimate(
            flops=4 * mats * rows * cols, bytes_accessed=8 * mats * rows * cols, transcendentals=0
        ),
        name="pack",
    )(owner_table, gradients, momentum)


def momentum_kernel(
    chunk, col_size, owner_ref, other_ref, rank_ref, g_ref, m_ref, nm_ref, second_ref, list_ref,
    count_ref,
):
    step = pl.program_id(0)
    width = col_size // HALVES
    row, col = lax.axis_index("dp"), lax.axis_index("owner")
    listed = list_ref.shape[0] // CAP

    @pl.when(step == 0)
    def _():
        for slot in range(CAP):
            count_ref[slot] = 0

    for j in range(chunk):
        i = step * chunk + j
        new, nesterov = nesterov_of(g_ref, m_ref, j)
        nm_ref[j] = new
        owner = owner_ref[i]

        @pl.when(rank_ref[i] == 1)
        def _():
            second_ref[owner] = nesterov
            second_ref[other_ref[owner]] = nesterov

        near = (owner % col_size) // width == col // width
        host = jnp.where(near, owner, other_ref[owner])
        host_row, host_col = host // col_size, host % width
        offset = host_row ^ row
        high = offset // LOW * width + (host_col ^ (col % width))
        place = jnp.where(
            rank_ref[i] == 0, high * LOW + offset % LOW, host_row * width + host_col
        )
        rank = rank_ref[i]
        entry = count_ref[rank]
        count_ref[rank] = entry + 1
        list_ref[rank * listed + 2 * entry] = i
        list_ref[rank * listed + 2 * entry + 1] = place


def update_momentum(gradients, momentum, owner_table, other, rank, col_size):
    mats, rows, cols = gradients.shape
    devices = other.shape[0]
    chunk = 8
    block = pl.BlockSpec((chunk, rows, cols), lambda i, *_: (i, 0, 0))
    return pl.pallas_call(
        functools.partial(momentum_kernel, chunk, col_size),
        grid_spec=pltpu.PrefetchScalarGridSpec(
            num_scalar_prefetch=3,
            grid=(mats // chunk,),
            in_specs=[block, block],
            out_specs=[block, whole((devices, rows, cols)), SMEM],
            scratch_shapes=[pltpu.SMEM((CAP,), jnp.int32)],
        ),
        out_shape=[
            jax.ShapeDtypeStruct(momentum.shape, jnp.float32),
            jax.ShapeDtypeStruct((devices, rows, cols), jnp.bfloat16),
            jax.ShapeDtypeStruct((2 * mats,), jnp.int32),
        ],
        compiler_params=PARAMS,
        cost_estimate=pl.CostEstimate(
            flops=4 * mats * rows * cols, bytes_accessed=12 * mats * rows * cols, transcendentals=0
        ),
        name="update_momentum",
    )(owner_table, other, rank, gradients, momentum)


def matmul(lhs, rhs, rhs_dim):
    return lax.dot_general(
        lhs, rhs, (((1,), (rhs_dim,)), ((), ())), preferred_element_type=jnp.float32
    )


def sum_rows(values):
    rows, cols = values.shape
    if rows % 8:
        return jnp.sum(values, axis=0, keepdims=True)
    return jnp.sum(values.reshape(rows // 8, 8, cols), axis=0)


def gather_blocks(x_ref, x_s, row_size, col_size):
    _, rows, cols = x_ref.shape
    height = rows * row_size
    total = 0.0
    for r in range(row_size):
        for c in range(col_size):
            block = x_ref[r * col_size + c]
            x_s[r * rows : (r + 1) * rows, c * cols : (c + 1) * cols] = block
            wide = block.astype(jnp.float32)
            total = total + sum_rows(wide * wide)
    x_s[height:, :] = jnp.zeros((x_s.shape[0] - height, x_s.shape[1]), x_s.dtype)
    return 1.0 / (jnp.sqrt(jnp.sum(total, keepdims=True)) + epsilon)


def update_scale(height, width):
    return 0.2 * math.sqrt(max(height, width))


def newton_schulz(height, inverse, x_s, y_s, gram_s, finish):
    padded = x_s.shape[0]
    tile = height // TILES
    for ref in (y_s, gram_s):
        ref[height:, :] = jnp.zeros((padded - height, ref.shape[1]), ref.dtype)
    for iteration in range(ITERS):
        src = x_s if iteration == 0 else y_s
        for t in range(TILES):
            span = slice(t * tile, (t + 1) * tile)
            gram = matmul(src[span, :], src[...], 1)
            if iteration == 0:
                gram = gram * (inverse * inverse)
            gram_s[span, :] = gram.astype(jnp.bfloat16)
        for t in range(TILES):
            span = slice(t * tile, (t + 1) * tile)
            square = matmul(gram_s[span, :], gram_s[...], 0)
            mixing = coef_b * gram_s[span, :].astype(jnp.float32) + coef_c * square
            mixing = mixing.astype(jnp.bfloat16)
            if iteration + 1 < ITERS:
                combined = combine(src, span, slice(None), mixing)
                if iteration == 0:
                    combined = combined * inverse
                y_s[span, :] = combined.astype(jnp.bfloat16)
            else:
                finish(t, span, mixing)


def combine(src, span, columns, mixing):
    return coef_a * src[span, columns].astype(jnp.float32) + matmul(mixing, src[:, columns], 0)


def stage_place(row_offset, col_offset, row_size, width):
    high = row_offset // LOW * width + col_offset
    return row_offset % LOW * (row_size // LOW * width) + high


def ortho_kernel(row_size, col_size, slot, other_ref, x_ref, *refs):
    _, rows, cols = x_ref.shape
    width = col_size // HALVES
    half = width * cols
    places = row_size * width
    height = rows * row_size
    tile = height // TILES
    if slot:
        whole_ref, out_ref, x_s, y_s, gram_s, back_ref, sems, mix_s = refs
    else:
        owned_ref, low_refs = refs[0], refs[1 : 1 + LOW]
        x_s, y_s, gram_s, back_ref, sems, whole_ref = refs[1 + LOW :]
    row, col = lax.axis_index("dp"), lax.axis_index("owner")
    me = row * col_size + col
    owns = other_ref[me] != me
    inverse = gather_blocks(x_ref, x_s, row_size, col_size)

    def copy_out(t):
        if slot:
            span = pl.ds(t * (places // TILES), places // TILES)
            return pltpu.make_async_copy(back_ref.at[span], out_ref.at[span], sems.at[t])
        span = pl.ds(t * tile, tile)
        return pltpu.make_async_copy(whole_ref.at[span], owned_ref.at[slot, span], sems.at[t])

    def product(span, columns, mixing):
        result = update_scale(height, cols * col_size) * combine(y_s, span, columns, mixing)
        result = result.astype(jnp.bfloat16)
        whole_ref[span, columns] = jnp.where(owns, result, jnp.zeros_like(result))
        return result

    def columns_of(number):
        return pl.ds(pl.multiple_of(number * half, half), half)

    def finish(t, span, mixing):
        if slot:
            mix_s[span, :] = mixing
            result = product(span, columns_of(col // width), mixing)
        else:
            result = product(span, slice(None), mixing)
            result = jnp.where(col < width, result[:, :half], result[:, half:])
        for j in range(row_size // TILES):
            r = t * (row_size // TILES) + j
            for c in range(width):
                if slot:
                    place = r * width + c
                else:
                    place = stage_place(r ^ row, c ^ (col % width), row_size, width)
                back_ref[place] = result[
                    j * rows : (j + 1) * rows, c * cols : (c + 1) * cols
                ]
        copy_out(t).start()

    newton_schulz(height, inverse, x_s, y_s, gram_s, finish)
    if slot:
        for t in range(TILES):
            span = slice(t * tile, (t + 1) * tile)
            product(span, columns_of(1 - col // width), mix_s[span, :])
    else:
        for k in range(LOW):
            low_refs[k][...] = back_ref[k * places // LOW : (k + 1) * places // LOW]
    for t in range(TILES):
        copy_out(t).wait()


def orthogonalize(slot, other, arrived, row_size, col_size):
    devices, rows, cols = arrived.shape
    height, width = rows * row_size, cols * col_size
    padded = round_up(height, 256)
    places = devices // HALVES
    scratch_shapes = [
        pltpu.VMEM((padded, width), jnp.bfloat16),
        pltpu.VMEM((padded, width), jnp.bfloat16),
        pltpu.VMEM((padded, padded), jnp.bfloat16),
        pltpu.VMEM((places, rows, cols), jnp.bfloat16),
        pltpu.SemaphoreType.DMA((TILES,)),
    ]
    if slot:
        scratch_shapes.append(pltpu.VMEM((height, padded), jnp.bfloat16))
        out_specs = [VMEM, ANYWHERE]
        out = [(height, width), (places, rows, cols)]
    else:
        out_specs = [ANYWHERE] + [VMEM] * LOW
        out = [(CAP, height, width)] + [(places // LOW, rows, cols)] * LOW
        scratch_shapes.append(pltpu.VMEM((height, width), jnp.bfloat16))
    return pl.pallas_call(
        functools.partial(ortho_kernel, row_size, col_size, slot),
        in_specs=[SMEM, VMEM],
        out_specs=out_specs,
        out_shape=[
            pltpu.HBM(shape, jnp.bfloat16)
            if spec is ANYWHERE
            else jax.ShapeDtypeStruct(shape, jnp.bfloat16)
            for spec, shape in zip(out_specs, out)
        ],
        scratch_shapes=scratch_shapes,
        compiler_params=PARAMS,
        cost_estimate=pl.CostEstimate(
            flops=2 * ITERS * padded * padded * (2 * width + padded),
            bytes_accessed=6 * padded * width,
            transcendentals=0,
        ),
        name="orthogonalize",
    )(other, arrived)


def restage_kernel(*refs):
    low_refs, high_refs = refs[:LOW], refs[LOW:]
    for h, high_ref in enumerate(high_refs):
        for k, low_ref in enumerate(low_refs):
            high_ref[k] = low_ref[h]


def restage(blocks):
    highs, rows, cols = blocks[0].shape
    out = jax.ShapeDtypeStruct((LOW, rows, cols), blocks[0].dtype)
    return pl.pallas_call(
        restage_kernel,
        grid=(1,),
        in_specs=[whole(blocks[0].shape)] * LOW,
        out_specs=[whole(out.shape)] * highs,
        out_shape=[out] * highs,
        compiler_params=PARAMS,
        cost_estimate=pl.CostEstimate(
            flops=0, bytes_accessed=4 * LOW * highs * rows * cols, transcendentals=0
        ),
        name="restage",
    )(*blocks)


def start_blocks(slot, list_ref, back_ref, update_ref, sem):
    listed = list_ref.shape[0] // CAP
    for k in range(update_ref.shape[0] // CAP):
        matrix = list_ref[slot * listed + 2 * k]
        place = list_ref[slot * listed + 2 * k + 1]
        pltpu.make_async_copy(back_ref.at[place], update_ref.at[matrix], sem).start()


def wait_blocks(back_ref, update_ref, sem):
    span = pl.ds(0, update_ref.shape[0] // CAP)
    pltpu.make_async_copy(back_ref.at[span], update_ref.at[span], sem).wait()


def early_kernel(list_ref, whole_ref, owned_in, *refs):
    high_refs, (owned_ref, update_ref, back_s, own_sem, sem) = refs[:-5], refs[-5:]
    own = pltpu.make_async_copy(whole_ref, owned_ref.at[CAP - 1], own_sem)
    own.start()
    for h, high_ref in enumerate(high_refs):
        back_s[h * LOW : (h + 1) * LOW] = high_ref[...]
    start_blocks(0, list_ref, back_s, update_ref, sem)
    wait_blocks(back_s, update_ref, sem)
    own.wait()


def store_early(places, mats, matrix, owned, first):
    _, rows, cols = first[0].shape
    return pl.pallas_call(
        early_kernel,
        in_specs=[SMEM, VMEM, ANYWHERE] + [VMEM] * len(first),
        out_specs=[ANYWHERE, ANYWHERE],
        out_shape=[
            jax.ShapeDtypeStruct(owned.shape, jnp.bfloat16),
            jax.ShapeDtypeStruct((mats, rows, cols), jnp.bfloat16),
        ],
        scratch_shapes=[
            pltpu.VMEM((LOW * len(first), rows, cols), jnp.bfloat16),
            pltpu.SemaphoreType.DMA(()),
            pltpu.SemaphoreType.DMA(()),
        ],
        input_output_aliases={2: 0},
        compiler_params=PARAMS,
        cost_estimate=pl.CostEstimate(
            flops=0, bytes_accessed=8 * mats * rows * cols, transcendentals=0
        ),
        name="store_early",
    )(places, matrix, owned, *first)


def late_kernel(list_ref, back_ref, update_in, update_ref, sem):
    start_blocks(1, list_ref, back_ref, update_ref, sem)
    wait_blocks(back_ref, update_ref, sem)


def store_late(places, second, update):
    return pl.pallas_call(
        late_kernel,
        in_specs=[SMEM, VMEM, ANYWHERE],
        out_specs=ANYWHERE,
        out_shape=jax.ShapeDtypeStruct(update.shape, jnp.bfloat16),
        scratch_shapes=[pltpu.SemaphoreType.DMA(())],
        input_output_aliases={2: 0},
        compiler_params=PARAMS,
        cost_estimate=pl.CostEstimate(flops=0, bytes_accessed=4 * second.size, transcendentals=0),
        name="store_late",
    )(places, second, update)


def exchange(blocks, axes, groups=None):
    return lax.all_to_all(
        blocks, axes, split_axis=0, concat_axis=0, tiled=True, axis_index_groups=groups
    )


def swap(block, offset, devices):
    return lax.ppermute(block, AXES, [(d, d ^ offset) for d in range(devices)])


def on_device(gradients, momentum, owner_table):
    row_size = lax.axis_size("dp")
    col_size = lax.axis_size("owner")
    devices = row_size * col_size
    width = col_size // HALVES
    halves = [
        [r * col_size + half * width + c for r in range(row_size) for c in range(width)]
        for half in range(HALVES)
    ]
    first, other, rank = pack(gradients, momentum, owner_table, devices, col_size)
    arrived_first = exchange(first, AXES)
    new_momentum, second, places = update_momentum(
        gradients, momentum, owner_table, other, rank, col_size
    )
    arrived_first, second = lax.optimization_barrier((arrived_first, second))
    arrived_second = exchange(second, AXES)
    owned, *back_first = orthogonalize(0, other, arrived_first, row_size, col_size)
    low = [back_first[0]] + [
        swap(back_first[k], k * col_size, devices) for k in range(1, LOW)
    ]
    high = restage(low)
    _, arrived_second = lax.optimization_barrier((high, arrived_second))
    returned_first = [high[0]] + [
        swap(high[r * width + c], r * LOW * col_size + c, devices)
        for r in range(row_size // LOW)
        for c in range(width)
        if r or c
    ]
    matrix, back_second = orthogonalize(1, other, arrived_second, row_size, col_size)
    returned_first, back_second = lax.optimization_barrier((returned_first, back_second))
    returned_second = exchange(back_second, AXES, halves)
    owned, update = store_early(
        places, owner_table.shape[0], matrix, owned, returned_first
    )
    update = store_late(places, returned_second, update)
    return (new_momentum, update, owned)


def solution(mesh):
    return jax.shard_map(
        on_device,
        mesh=mesh,
        in_specs=(P(None, "dp", "owner"), P(None, "dp", "owner"), P()),
        out_specs=(P(None, "dp", "owner"), P(None, "dp", "owner"), P(("dp", "owner"), None, None)),
        check_vma=False,
    )
```

```python
import functools
import math

import jax
import jax.numpy as jnp
from jax import lax
from jax.experimental import pallas as pl
from jax.experimental.pallas import tpu as pltpu
from jax.sharding import PartitionSpec as P

ITERS = 2
CAP = 2
HALVES = 2
TILES = 2
LOW = 4

coef_a = 3.4445
coef_b = -4.775
coef_c = 2.0315
momentum_beta = 0.95
epsilon = 1e-07

AXES = ("dp", "owner")
MIB = 1024 * 1024
PARAMS = pltpu.CompilerParams(vmem_limit_bytes=24 * MIB)
PACK_PARAMS = pltpu.CompilerParams(vmem_limit_bytes=60 * MIB)
SMEM = pl.BlockSpec(memory_space=pltpu.SMEM)
VMEM = pl.BlockSpec(memory_space=pltpu.VMEM)
ANYWHERE = pl.BlockSpec(memory_space=pl.ANY)


def round_up(value, multiple):
    return -(-value // multiple) * multiple


def whole(shape):
    return pl.BlockSpec(shape, lambda *_: (0,) * len(shape))


def nesterov_of(grad_ref, momentum_ref, j):
    grad = grad_ref[j].astype(jnp.float32)
    new = momentum_beta * momentum_ref[j] + grad
    return new, (grad + momentum_beta * new).astype(jnp.bfloat16)


def make_plan(col_size, owner_ref, other_ref, rank_ref, count_ref, list_ref):
    devices, mats = other_ref.shape[0], rank_ref.shape[0]

    def clear(d, _):
        count_ref[d] = 0
        return 0

    lax.fori_loop(0, devices, clear, 0, unroll=8)

    def rank_matrix(i, _):
        owner = owner_ref[i]
        rank = count_ref[owner]
        rank_ref[i] = rank
        count_ref[owner] = rank + 1
        return 0

    lax.fori_loop(0, mats, rank_matrix, 0, unroll=8)

    def list_device(d, found):
        owns = jnp.minimum(count_ref[d], 1)
        half = (d % col_size) // (col_size // HALVES)
        row = 2 * jnp.where(owns == 1, half, 1 - half) + owns
        place = found[0]
        for k in range(1, 2 * HALVES):
            place = jnp.where(row == k, found[k], place)
        list_ref[row * devices + place] = d
        return tuple(n + jnp.where(row == k, 1, 0) for k, n in enumerate(found))

    found = lax.fori_loop(0, devices, list_device, (0,) * (2 * HALVES), unroll=8)
    for half in range(HALVES):

        def pair(k, _):
            idle = list_ref[2 * half * devices + k]
            other_ref[list_ref[(2 * half + 1) * devices + k]] = idle
            other_ref[idle] = idle
            return 0

        lax.fori_loop(0, found[2 * half + 1], pair, 0)


def pack_kernel(
    chunk, col_size, owner_ref, g_ref, m_ref, first_ref, other_ref, rank_ref,
    count_ref, list_ref, g_s, m_s, sems,
):
    mats = rank_ref.shape[0]

    def loads(k):
        span = pl.ds(k * chunk, chunk)
        return (
            pltpu.make_async_copy(g_ref.at[span], g_s.at[span], sems.at[0, k]),
            pltpu.make_async_copy(m_ref.at[span], m_s.at[span], sems.at[1, k]),
        )

    for k in range(mats // chunk):
        for load in loads(k):
            load.start()
    make_plan(col_size, owner_ref, other_ref, rank_ref, count_ref, list_ref)
    for k in range(mats // chunk):
        for load in loads(k):
            load.wait()
        for i in range(k * chunk, (k + 1) * chunk):

            @pl.when(rank_ref[i] == 0)
            def _():
                nesterov = nesterov_of(g_s, m_s, i)[1]
                first_ref[owner_ref[i]] = nesterov
                first_ref[other_ref[owner_ref[i]]] = nesterov


def pack(gradients, momentum, owner_table, devices, col_size):
    mats, rows, cols = gradients.shape
    chunk = 16
    return pl.pallas_call(
        functools.partial(pack_kernel, chunk, col_size),
        grid_spec=pltpu.PrefetchScalarGridSpec(
            num_scalar_prefetch=1,
            grid=(1,),
            in_specs=[ANYWHERE, ANYWHERE],
            out_specs=[whole((devices, rows, cols)), SMEM, SMEM],
            scratch_shapes=[
                pltpu.SMEM((devices,), jnp.int32),
                pltpu.SMEM((2 * HALVES * devices,), jnp.int32),
                pltpu.VMEM(gradients.shape, gradients.dtype),
                pltpu.VMEM(momentum.shape, momentum.dtype),
                pltpu.SemaphoreType.DMA((2, mats // chunk)),
            ],
        ),
        out_shape=[
            jax.ShapeDtypeStruct((devices, rows, cols), jnp.bfloat16),
            jax.ShapeDtypeStruct((devices,), jnp.int32),
            jax.ShapeDtypeStruct((mats,), jnp.int32),
        ],
        compiler_params=PACK_PARAMS,
        cost_estimate=pl.CostEstimate(
            flops=4 * mats * rows * cols, bytes_accessed=8 * mats * rows * cols, transcendentals=0
        ),
        name="pack",
    )(owner_table, gradients, momentum)


def momentum_kernel(
    chunk, col_size, owner_ref, other_ref, rank_ref, g_ref, m_ref, nm_ref, second_ref, list_ref,
    count_ref,
):
    step = pl.program_id(0)
    width = col_size // HALVES
    row, col = lax.axis_index("dp"), lax.axis_index("owner")
    listed = list_ref.shape[0] // CAP

    @pl.when(step == 0)
    def _():
        for slot in range(CAP):
            count_ref[slot] = 0

    for j in range(chunk):
        i = step * chunk + j
        new, nesterov = nesterov_of(g_ref, m_ref, j)
        nm_ref[j] = new
        owner = owner_ref[i]

        @pl.when(rank_ref[i] == 1)
        def _():
            second_ref[owner] = nesterov
            second_ref[other_ref[owner]] = nesterov

        near = (owner % col_size) // width == col // width
        host = jnp.where(near, owner, other_ref[owner])
        host_row, host_col = host // col_size, host % width
        offset = host_row ^ row
        high = offset // LOW * width + (host_col ^ (col % width))
        place = jnp.where(
            rank_ref[i] == 0, high * LOW + offset % LOW, host_row * width + host_col
        )
        rank = rank_ref[i]
        entry = count_ref[rank]
        count_ref[rank] = entry + 1
        list_ref[rank * listed + 2 * entry] = i
        list_ref[rank * listed + 2 * entry + 1] = place


def update_momentum(gradients, momentum, owner_table, other, rank, col_size):
    mats, rows, cols = gradients.shape
    devices = other.shape[0]
    chunk = 8
    block = pl.BlockSpec((chunk, rows, cols), lambda i, *_: (i, 0, 0))
    return pl.pallas_call(
        functools.partial(momentum_kernel, chunk, col_size),
        grid_spec=pltpu.PrefetchScalarGridSpec(
            num_scalar_prefetch=3,
            grid=(mats // chunk,),
            in_specs=[block, block],
            out_specs=[block, whole((devices, rows, cols)), SMEM],
            scratch_shapes=[pltpu.SMEM((CAP,), jnp.int32)],
        ),
        out_shape=[
            jax.ShapeDtypeStruct(momentum.shape, jnp.float32),
            jax.ShapeDtypeStruct((devices, rows, cols), jnp.bfloat16),
            jax.ShapeDtypeStruct((2 * mats,), jnp.int32),
        ],
        compiler_params=PARAMS,
        cost_estimate=pl.CostEstimate(
            flops=4 * mats * rows * cols, bytes_accessed=12 * mats * rows * cols, transcendentals=0
        ),
        name="update_momentum",
    )(owner_table, other, rank, gradients, momentum)


def matmul(lhs, rhs, rhs_dim):
    return lax.dot_general(
        lhs, rhs, (((1,), (rhs_dim,)), ((), ())), preferred_element_type=jnp.float32
    )


def sum_rows(values):
    rows, cols = values.shape
    if rows % 8:
        return jnp.sum(values, axis=0, keepdims=True)
    return jnp.sum(values.reshape(rows // 8, 8, cols), axis=0)


def gather_blocks(x_ref, x_s, row_size, col_size):
    _, rows, cols = x_ref.shape
    height = rows * row_size
    total = 0.0
    for r in range(row_size):
        for c in range(col_size):
            block = x_ref[r * col_size + c]
            x_s[r * rows : (r + 1) * rows, c * cols : (c + 1) * cols] = block
            wide = block.astype(jnp.float32)
            total = total + sum_rows(wide * wide)
    x_s[height:, :] = jnp.zeros((x_s.shape[0] - height, x_s.shape[1]), x_s.dtype)
    return 1.0 / (jnp.sqrt(jnp.sum(total, keepdims=True)) + epsilon)


def update_scale(height, width):
    return 0.2 * math.sqrt(max(height, width))


def newton_schulz(height, inverse, x_s, y_s, gram_s, finish):
    padded = x_s.shape[0]
    tile = height // TILES
    for ref in (y_s, gram_s):
        ref[height:, :] = jnp.zeros((padded - height, ref.shape[1]), ref.dtype)
    for iteration in range(ITERS):
        src = x_s if iteration == 0 else y_s
        for t in range(TILES):
            span = slice(t * tile, (t + 1) * tile)
            gram = matmul(src[span, :], src[...], 1)
            if iteration == 0:
                gram = gram * (inverse * inverse)
            gram_s[span, :] = gram.astype(jnp.bfloat16)
        for t in range(TILES):
            span = slice(t * tile, (t + 1) * tile)
            square = matmul(gram_s[span, :], gram_s[...], 0)
            mixing = coef_b * gram_s[span, :].astype(jnp.float32) + coef_c * square
            mixing = mixing.astype(jnp.bfloat16)
            if iteration + 1 < ITERS:
                combined = combine(src, span, slice(None), mixing)
                if iteration == 0:
                    combined = combined * inverse
                y_s[span, :] = combined.astype(jnp.bfloat16)
            else:
                finish(t, span, mixing)


def combine(src, span, columns, mixing):
    return coef_a * src[span, columns].astype(jnp.float32) + matmul(mixing, src[:, columns], 0)


def stage_place(row_offset, col_offset, row_size, width):
    high = row_offset // LOW * width + col_offset
    return row_offset % LOW * (row_size // LOW * width) + high


def ortho_kernel(row_size, col_size, slot, other_ref, x_ref, *refs):
    _, rows, cols = x_ref.shape
    width = col_size // HALVES
    half = width * cols
    places = row_size * width
    height = rows * row_size
    tile = height // TILES
    if slot:
        whole_ref, out_ref, x_s, y_s, gram_s, back_ref, sems, mix_s = refs
    else:
        owned_ref, low_refs = refs[0], refs[1 : 1 + LOW]
        x_s, y_s, gram_s, back_ref, sems, whole_ref = refs[1 + LOW :]
    row, col = lax.axis_index("dp"), lax.axis_index("owner")
    me = row * col_size + col
    owns = other_ref[me] != me
    inverse = gather_blocks(x_ref, x_s, row_size, col_size)

    def copy_out(t):
        if slot:
            span = pl.ds(t * (places // TILES), places // TILES)
            return pltpu.make_async_copy(back_ref.at[span], out_ref.at[span], sems.at[t])
        span = pl.ds(t * tile, tile)
        return pltpu.make_async_copy(whole_ref.at[span], owned_ref.at[slot, span], sems.at[t])

    def product(span, columns, mixing):
        result = update_scale(height, cols * col_size) * combine(y_s, span, columns, mixing)
        result = result.astype(jnp.bfloat16)
        whole_ref[span, columns] = jnp.where(owns, result, jnp.zeros_like(result))
        return result

    def columns_of(number):
        return pl.ds(pl.multiple_of(number * half, half), half)

    def finish(t, span, mixing):
        if slot:
            mix_s[span, :] = mixing
            result = product(span, columns_of(col // width), mixing)
        else:
            result = product(span, slice(None), mixing)
            result = jnp.where(col < width, result[:, :half], result[:, half:])
        for j in range(row_size // TILES):
            r = t * (row_size // TILES) + j
            for c in range(width):
                if slot:
                    place = r * width + c
                else:
                    place = stage_place(r ^ row, c ^ (col % width), row_size, width)
                back_ref[place] = result[
                    j * rows : (j + 1) * rows, c * cols : (c + 1) * cols
                ]
        copy_out(t).start()

    newton_schulz(height, inverse, x_s, y_s, gram_s, finish)
    if slot:
        for t in range(TILES):
            span = slice(t * tile, (t + 1) * tile)
            product(span, columns_of(1 - col // width), mix_s[span, :])
    else:
        for k in range(LOW):
            low_refs[k][...] = back_ref[k * places // LOW : (k + 1) * places // LOW]
    for t in range(TILES):
        copy_out(t).wait()


def orthogonalize(slot, other, arrived, row_size, col_size):
    devices, rows, cols = arrived.shape
    height, width = rows * row_size, cols * col_size
    padded = round_up(height, 256)
    places = devices // HALVES
    scratch_shapes = [
        pltpu.VMEM((padded, width), jnp.bfloat16),
        pltpu.VMEM((padded, width), jnp.bfloat16),
        pltpu.VMEM((padded, padded), jnp.bfloat16),
        pltpu.VMEM((places, rows, cols), jnp.bfloat16),
        pltpu.SemaphoreType.DMA((TILES,)),
    ]
    if slot:
        scratch_shapes.append(pltpu.VMEM((height, padded), jnp.bfloat16))
        out_specs = [VMEM, ANYWHERE]
        out = [(height, width), (places, rows, cols)]
    else:
        out_specs = [ANYWHERE] + [VMEM] * LOW
        out = [(CAP, height, width)] + [(places // LOW, rows, cols)] * LOW
        scratch_shapes.append(pltpu.VMEM((height, width), jnp.bfloat16))
    return pl.pallas_call(
        functools.partial(ortho_kernel, row_size, col_size, slot),
        in_specs=[SMEM, VMEM],
        out_specs=out_specs,
        out_shape=[
            pltpu.HBM(shape, jnp.bfloat16)
            if spec is ANYWHERE
            else jax.ShapeDtypeStruct(shape, jnp.bfloat16)
            for spec, shape in zip(out_specs, out)
        ],
        scratch_shapes=scratch_shapes,
        compiler_params=PARAMS,
        cost_estimate=pl.CostEstimate(
            flops=2 * ITERS * padded * padded * (2 * width + padded),
            bytes_accessed=6 * padded * width,
            transcendentals=0,
        ),
        name="orthogonalize",
    )(other, arrived)


def restage_kernel(*refs):
    low_refs, high_refs = refs[:LOW], refs[LOW:]
    for h, high_ref in enumerate(high_refs):
        for k, low_ref in enumerate(low_refs):
            high_ref[k] = low_ref[h]


def restage(blocks):
    highs, rows, cols = blocks[0].shape
    out = jax.ShapeDtypeStruct((LOW, rows, cols), blocks[0].dtype)
    return pl.pallas_call(
        restage_kernel,
        grid=(1,),
        in_specs=[whole(blocks[0].shape)] * LOW,
        out_specs=[whole(out.shape)] * highs,
        out_shape=[out] * highs,
        compiler_params=PARAMS,
        cost_estimate=pl.CostEstimate(
            flops=0, bytes_accessed=4 * LOW * highs * rows * cols, transcendentals=0
        ),
        name="restage",
    )(*blocks)


def start_blocks(slot, list_ref, back_ref, update_ref, sem):
    listed = list_ref.shape[0] // CAP
    for k in range(update_ref.shape[0] // CAP):
        matrix = list_ref[slot * listed + 2 * k]
        place = list_ref[slot * listed + 2 * k + 1]
        pltpu.make_async_copy(back_ref.at[place], update_ref.at[matrix], sem).start()


def wait_blocks(back_ref, update_ref, sem):
    span = pl.ds(0, update_ref.shape[0] // CAP)
    pltpu.make_async_copy(back_ref.at[span], update_ref.at[span], sem).wait()


def early_kernel(list_ref, whole_ref, owned_in, *refs):
    high_refs, (owned_ref, update_ref, back_s, own_sem, sem) = refs[:-5], refs[-5:]
    own = pltpu.make_async_copy(whole_ref, owned_ref.at[CAP - 1], own_sem)
    own.start()
    for h, high_ref in enumerate(high_refs):
        back_s[h * LOW : (h + 1) * LOW] = high_ref[...]
    start_blocks(0, list_ref, back_s, update_ref, sem)
    wait_blocks(back_s, update_ref, sem)
    own.wait()


def store_early(places, mats, matrix, owned, first):
    _, rows, cols = first[0].shape
    return pl.pallas_call(
        early_kernel,
        in_specs=[SMEM, VMEM, ANYWHERE] + [VMEM] * len(first),
        out_specs=[ANYWHERE, ANYWHERE],
        out_shape=[
            jax.ShapeDtypeStruct(owned.shape, jnp.bfloat16),
            jax.ShapeDtypeStruct((mats, rows, cols), jnp.bfloat16),
        ],
        scratch_shapes=[
            pltpu.VMEM((LOW * len(first), rows, cols), jnp.bfloat16),
            pltpu.SemaphoreType.DMA(()),
            pltpu.SemaphoreType.DMA(()),
        ],
        input_output_aliases={2: 0},
        compiler_params=PARAMS,
        cost_estimate=pl.CostEstimate(
            flops=0, bytes_accessed=8 * mats * rows * cols, transcendentals=0
        ),
        name="store_early",
    )(places, matrix, owned, *first)


def late_kernel(list_ref, back_ref, update_in, update_ref, sem):
    start_blocks(1, list_ref, back_ref, update_ref, sem)
    wait_blocks(back_ref, update_ref, sem)


def store_late(places, second, update):
    return pl.pallas_call(
        late_kernel,
        in_specs=[SMEM, VMEM, ANYWHERE],
        out_specs=ANYWHERE,
        out_shape=jax.ShapeDtypeStruct(update.shape, jnp.bfloat16),
        scratch_shapes=[pltpu.SemaphoreType.DMA(())],
        input_output_aliases={2: 0},
        compiler_params=PARAMS,
        cost_estimate=pl.CostEstimate(flops=0, bytes_accessed=4 * second.size, transcendentals=0),
        name="store_late",
    )(places, second, update)


def exchange(blocks, axes, groups=None):
    return lax.all_to_all(
        blocks, axes, split_axis=0, concat_axis=0, tiled=True, axis_index_groups=groups
    )


def swap(block, offset, devices):
    return lax.ppermute(block, AXES, [(d, d ^ offset) for d in range(devices)])


def on_device(gradients, momentum, owner_table):
    row_size = lax.axis_size("dp")
    col_size = lax.axis_size("owner")
    devices = row_size * col_size
    width = col_size // HALVES
    halves = [
        [r * col_size + half * width + c for r in range(row_size) for c in range(width)]
        for half in range(HALVES)
    ]
    first, other, rank = pack(gradients, momentum, owner_table, devices, col_size)
    arrived_first = exchange(first, AXES)
    new_momentum, second, places = update_momentum(
        gradients, momentum, owner_table, other, rank, col_size
    )
    arrived_first, second = lax.optimization_barrier((arrived_first, second))
    arrived_second = exchange(second, AXES)
    owned, *back_first = orthogonalize(0, other, arrived_first, row_size, col_size)
    low = [back_first[0]] + [
        swap(back_first[k], k * col_size, devices) for k in range(1, LOW)
    ]
    high = restage(low)
    _, arrived_second = lax.optimization_barrier((high, arrived_second))
    returned_first = [high[0]] + [
        swap(high[r * width + c], r * LOW * col_size + c, devices)
        for r in range(row_size // LOW)
        for c in range(width)
        if r or c
    ]
    matrix, back_second = orthogonalize(1, other, arrived_second, row_size, col_size)
    returned_first, back_second = lax.optimization_barrier((returned_first, back_second))
    returned_second = exchange(back_second, AXES, halves)
    owned, update = store_early(
        places, owner_table.shape[0], matrix, owned, returned_first
    )
    update = store_late(places, returned_second, update)
    return (new_momentum, update, owned)


def solution(mesh):
    return jax.shard_map(
        on_device,
        mesh=mesh,
        in_specs=(P(None, "dp", "owner"), P(None, "dp", "owner"), P()),
        out_specs=(P(None, "dp", "owner"), P(None, "dp", "owner"), P(("dp", "owner"), None, None)),
        check_vma=False,
    )
```

```python
import functools
import math

import jax
import jax.numpy as jnp
from jax import lax
from jax.experimental import pallas as pl
from jax.experimental.pallas import tpu as pltpu
from jax.sharding import PartitionSpec as P

ITERS = 2
CAP = 2
HALVES = 2
TILES = 2
LOW = 4

coef_a = 3.4445
coef_b = -4.775
coef_c = 2.0315
momentum_beta = 0.95
epsilon = 1e-07

AXES = ("dp", "owner")
MIB = 1024 * 1024
PARAMS = pltpu.CompilerParams(vmem_limit_bytes=24 * MIB)
PACK_PARAMS = pltpu.CompilerParams(vmem_limit_bytes=60 * MIB)
SMEM = pl.BlockSpec(memory_space=pltpu.SMEM)
VMEM = pl.BlockSpec(memory_space=pltpu.VMEM)
ANYWHERE = pl.BlockSpec(memory_space=pl.ANY)


def round_up(value, multiple):
    return -(-value // multiple) * multiple


def whole(shape):
    return pl.BlockSpec(shape, lambda *_: (0,) * len(shape))


def nesterov_of(grad_ref, momentum_ref, j):
    grad = grad_ref[j].astype(jnp.float32)
    new = momentum_beta * momentum_ref[j] + grad
    return new, (grad + momentum_beta * new).astype(jnp.bfloat16)


def make_plan(col_size, owner_ref, other_ref, rank_ref, count_ref, list_ref):
    devices, mats = other_ref.shape[0], rank_ref.shape[0]

    def clear(d, _):
        count_ref[d] = 0
        return 0

    lax.fori_loop(0, devices, clear, 0, unroll=32)

    def rank_matrix(i, _):
        owner = owner_ref[i]
        rank = count_ref[owner]
        rank_ref[i] = rank
        count_ref[owner] = rank + 1
        return 0

    lax.fori_loop(0, mats, rank_matrix, 0, unroll=32)

    def list_device(d, found):
        owns = jnp.minimum(count_ref[d], 1)
        half = (d % col_size) // (col_size // HALVES)
        row = 2 * jnp.where(owns == 1, half, 1 - half) + owns
        place = found[0]
        for k in range(1, 2 * HALVES):
            place = jnp.where(row == k, found[k], place)
        list_ref[row * devices + place] = d
        return tuple(n + jnp.where(row == k, 1, 0) for k, n in enumerate(found))

    found = lax.fori_loop(0, devices, list_device, (0,) * (2 * HALVES), unroll=32)
    for half in range(HALVES):

        def pair(k, _):
            idle = list_ref[2 * half * devices + k]
            other_ref[list_ref[(2 * half + 1) * devices + k]] = idle
            other_ref[idle] = idle
            return 0

        lax.fori_loop(0, found[2 * half + 1], pair, 0)


def pack_kernel(
    chunk, col_size, owner_ref, g_ref, m_ref, first_ref, other_ref, rank_ref,
    count_ref, list_ref, g_s, m_s, sems,
):
    mats = rank_ref.shape[0]

    def loads(k):
        span = pl.ds(k * chunk, chunk)
        return (
            pltpu.make_async_copy(g_ref.at[span], g_s.at[span], sems.at[0, k]),
            pltpu.make_async_copy(m_ref.at[span], m_s.at[span], sems.at[1, k]),
        )

    for k in range(mats // chunk):
        for load in loads(k):
            load.start()
    make_plan(col_size, owner_ref, other_ref, rank_ref, count_ref, list_ref)
    for k in range(mats // chunk):
        for load in loads(k):
            load.wait()
        for i in range(k * chunk, (k + 1) * chunk):

            @pl.when(rank_ref[i] == 0)
            def _():
                nesterov = nesterov_of(g_s, m_s, i)[1]
                first_ref[owner_ref[i]] = nesterov
                first_ref[other_ref[owner_ref[i]]] = nesterov


def pack(gradients, momentum, owner_table, devices, col_size):
    mats, rows, cols = gradients.shape
    chunk = 16
    return pl.pallas_call(
        functools.partial(pack_kernel, chunk, col_size),
        grid_spec=pltpu.PrefetchScalarGridSpec(
            num_scalar_prefetch=1,
            grid=(1,),
            in_specs=[ANYWHERE, ANYWHERE],
            out_specs=[whole((devices, rows, cols)), SMEM, SMEM],
            scratch_shapes=[
                pltpu.SMEM((devices,), jnp.int32),
                pltpu.SMEM((2 * HALVES * devices,), jnp.int32),
                pltpu.VMEM(gradients.shape, gradients.dtype),
                pltpu.VMEM(momentum.shape, momentum.dtype),
                pltpu.SemaphoreType.DMA((2, mats // chunk)),
            ],
        ),
        out_shape=[
            jax.ShapeDtypeStruct((devices, rows, cols), jnp.bfloat16),
            jax.ShapeDtypeStruct((devices,), jnp.int32),
            jax.ShapeDtypeStruct((mats,), jnp.int32),
        ],
        compiler_params=PACK_PARAMS,
        cost_estimate=pl.CostEstimate(
            flops=4 * mats * rows * cols, bytes_accessed=8 * mats * rows * cols, transcendentals=0
        ),
        name="pack",
    )(owner_table, gradients, momentum)


def momentum_kernel(
    chunk, col_size, owner_ref, other_ref, rank_ref, g_ref, m_ref, nm_ref, second_ref, list_ref,
    count_ref,
):
    step = pl.program_id(0)
    width = col_size // HALVES
    row, col = lax.axis_index("dp"), lax.axis_index("owner")
    listed = list_ref.shape[0] // CAP

    @pl.when(step == 0)
    def _():
        for slot in range(CAP):
            count_ref[slot] = 0

    for j in range(chunk):
        i = step * chunk + j
        new, nesterov = nesterov_of(g_ref, m_ref, j)
        nm_ref[j] = new
        owner = owner_ref[i]

        @pl.when(rank_ref[i] == 1)
        def _():
            second_ref[owner] = nesterov
            second_ref[other_ref[owner]] = nesterov

        near = (owner % col_size) // width == col // width
        host = jnp.where(near, owner, other_ref[owner])
        host_row, host_col = host // col_size, host % width
        offset = host_row ^ row
        high = offset // LOW * width + (host_col ^ (col % width))
        place = jnp.where(
            rank_ref[i] == 0, high * LOW + offset % LOW, host_row * width + host_col
        )
        rank = rank_ref[i]
        entry = count_ref[rank]
        count_ref[rank] = entry + 1
        list_ref[rank * listed + 2 * entry] = i
        list_ref[rank * listed + 2 * entry + 1] = place


def update_momentum(gradients, momentum, owner_table, other, rank, col_size):
    mats, rows, cols = gradients.shape
    devices = other.shape[0]
    chunk = 8
    block = pl.BlockSpec((chunk, rows, cols), lambda i, *_: (i, 0, 0))
    return pl.pallas_call(
        functools.partial(momentum_kernel, chunk, col_size),
        grid_spec=pltpu.PrefetchScalarGridSpec(
            num_scalar_prefetch=3,
            grid=(mats // chunk,),
            in_specs=[block, block],
            out_specs=[block, whole((devices, rows, cols)), SMEM],
            scratch_shapes=[pltpu.SMEM((CAP,), jnp.int32)],
        ),
        out_shape=[
            jax.ShapeDtypeStruct(momentum.shape, jnp.float32),
            jax.ShapeDtypeStruct((devices, rows, cols), jnp.bfloat16),
            jax.ShapeDtypeStruct((2 * mats,), jnp.int32),
        ],
        compiler_params=PARAMS,
        cost_estimate=pl.CostEstimate(
            flops=4 * mats * rows * cols, bytes_accessed=12 * mats * rows * cols, transcendentals=0
        ),
        name="update_momentum",
    )(owner_table, other, rank, gradients, momentum)


def matmul(lhs, rhs, rhs_dim):
    return lax.dot_general(
        lhs, rhs, (((1,), (rhs_dim,)), ((), ())), preferred_element_type=jnp.float32
    )


def sum_rows(values):
    rows, cols = values.shape
    if rows % 8:
        return jnp.sum(values, axis=0, keepdims=True)
    return jnp.sum(values.reshape(rows // 8, 8, cols), axis=0)


def gather_blocks(x_ref, x_s, row_size, col_size):
    _, rows, cols = x_ref.shape
    height = rows * row_size
    total = 0.0
    for r in range(row_size):
        for c in range(col_size):
            block = x_ref[r * col_size + c]
            x_s[r * rows : (r + 1) * rows, c * cols : (c + 1) * cols] = block
            wide = block.astype(jnp.float32)
            total = total + sum_rows(wide * wide)
    x_s[height:, :] = jnp.zeros((x_s.shape[0] - height, x_s.shape[1]), x_s.dtype)
    return 1.0 / (jnp.sqrt(jnp.sum(total, keepdims=True)) + epsilon)


def update_scale(height, width):
    return 0.2 * math.sqrt(max(height, width))


def newton_schulz(height, inverse, x_s, y_s, gram_s, finish):
    padded = x_s.shape[0]
    tile = height // TILES
    for ref in (y_s, gram_s):
        ref[height:, :] = jnp.zeros((padded - height, ref.shape[1]), ref.dtype)
    for iteration in range(ITERS):
        src = x_s if iteration == 0 else y_s
        for t in range(TILES):
            span = slice(t * tile, (t + 1) * tile)
            gram = matmul(src[span, :], src[...], 1)
            if iteration == 0:
                gram = gram * (inverse * inverse)
            gram_s[span, :] = gram.astype(jnp.bfloat16)
        for t in range(TILES):
            span = slice(t * tile, (t + 1) * tile)
            square = matmul(gram_s[span, :], gram_s[...], 0)
            mixing = coef_b * gram_s[span, :].astype(jnp.float32) + coef_c * square
            mixing = mixing.astype(jnp.bfloat16)
            if iteration + 1 < ITERS:
                combined = combine(src, span, slice(None), mixing)
                if iteration == 0:
                    combined = combined * inverse
                y_s[span, :] = combined.astype(jnp.bfloat16)
            else:
                finish(t, span, mixing)


def combine(src, span, columns, mixing):
    return coef_a * src[span, columns].astype(jnp.float32) + matmul(mixing, src[:, columns], 0)


def stage_place(row_offset, col_offset, row_size, width):
    high = row_offset // LOW * width + col_offset
    return row_offset % LOW * (row_size // LOW * width) + high


def ortho_kernel(row_size, col_size, slot, other_ref, x_ref, *refs):
    _, rows, cols = x_ref.shape
    width = col_size // HALVES
    half = width * cols
    places = row_size * width
    height = rows * row_size
    tile = height // TILES
    if slot:
        whole_ref, out_ref, x_s, y_s, gram_s, back_ref, sems, mix_s = refs
    else:
        owned_ref, low_refs = refs[0], refs[1 : 1 + LOW]
        x_s, y_s, gram_s, back_ref, sems, whole_ref = refs[1 + LOW :]
    row, col = lax.axis_index("dp"), lax.axis_index("owner")
    me = row * col_size + col
    owns = other_ref[me] != me
    inverse = gather_blocks(x_ref, x_s, row_size, col_size)

    def copy_out(t):
        if slot:
            span = pl.ds(t * (places // TILES), places // TILES)
            return pltpu.make_async_copy(back_ref.at[span], out_ref.at[span], sems.at[t])
        span = pl.ds(t * tile, tile)
        return pltpu.make_async_copy(whole_ref.at[span], owned_ref.at[slot, span], sems.at[t])

    def product(span, columns, mixing):
        result = update_scale(height, cols * col_size) * combine(y_s, span, columns, mixing)
        result = result.astype(jnp.bfloat16)
        whole_ref[span, columns] = jnp.where(owns, result, jnp.zeros_like(result))
        return result

    def columns_of(number):
        return pl.ds(pl.multiple_of(number * half, half), half)

    def finish(t, span, mixing):
        if slot:
            mix_s[span, :] = mixing
            result = product(span, columns_of(col // width), mixing)
        else:
            result = product(span, slice(None), mixing)
            result = jnp.where(col < width, result[:, :half], result[:, half:])
        for j in range(row_size // TILES):
            r = t * (row_size // TILES) + j
            for c in range(width):
                if slot:
                    place = r * width + c
                else:
                    place = stage_place(r ^ row, c ^ (col % width), row_size, width)
                back_ref[place] = result[
                    j * rows : (j + 1) * rows, c * cols : (c + 1) * cols
                ]
        copy_out(t).start()

    newton_schulz(height, inverse, x_s, y_s, gram_s, finish)
    if slot:
        for t in range(TILES):
            span = slice(t * tile, (t + 1) * tile)
            product(span, columns_of(1 - col // width), mix_s[span, :])
    else:
        for k in range(LOW):
            low_refs[k][...] = back_ref[k * places // LOW : (k + 1) * places // LOW]
    for t in range(TILES):
        copy_out(t).wait()


def orthogonalize(slot, other, arrived, row_size, col_size):
    devices, rows, cols = arrived.shape
    height, width = rows * row_size, cols * col_size
    padded = round_up(height, 256)
    places = devices // HALVES
    scratch_shapes = [
        pltpu.VMEM((padded, width), jnp.bfloat16),
        pltpu.VMEM((padded, width), jnp.bfloat16),
        pltpu.VMEM((padded, padded), jnp.bfloat16),
        pltpu.VMEM((places, rows, cols), jnp.bfloat16),
        pltpu.SemaphoreType.DMA((TILES,)),
    ]
    if slot:
        scratch_shapes.append(pltpu.VMEM((height, padded), jnp.bfloat16))
        out_specs = [VMEM, ANYWHERE]
        out = [(height, width), (places, rows, cols)]
    else:
        out_specs = [ANYWHERE] + [VMEM] * LOW
        out = [(CAP, height, width)] + [(places // LOW, rows, cols)] * LOW
        scratch_shapes.append(pltpu.VMEM((height, width), jnp.bfloat16))
    return pl.pallas_call(
        functools.partial(ortho_kernel, row_size, col_size, slot),
        in_specs=[SMEM, VMEM],
        out_specs=out_specs,
        out_shape=[
            pltpu.HBM(shape, jnp.bfloat16)
            if spec is ANYWHERE
            else jax.ShapeDtypeStruct(shape, jnp.bfloat16)
            for spec, shape in zip(out_specs, out)
        ],
        scratch_shapes=scratch_shapes,
        compiler_params=PARAMS,
        cost_estimate=pl.CostEstimate(
            flops=2 * ITERS * padded * padded * (2 * width + padded),
            bytes_accessed=6 * padded * width,
            transcendentals=0,
        ),
        name="orthogonalize",
    )(other, arrived)


def restage_kernel(*refs):
    low_refs, high_refs = refs[:LOW], refs[LOW:]
    for h, high_ref in enumerate(high_refs):
        for k, low_ref in enumerate(low_refs):
            high_ref[k] = low_ref[h]


def restage(blocks):
    highs, rows, cols = blocks[0].shape
    out = jax.ShapeDtypeStruct((LOW, rows, cols), blocks[0].dtype)
    return pl.pallas_call(
        restage_kernel,
        grid=(1,),
        in_specs=[whole(blocks[0].shape)] * LOW,
        out_specs=[whole(out.shape)] * highs,
        out_shape=[out] * highs,
        compiler_params=PARAMS,
        cost_estimate=pl.CostEstimate(
            flops=0, bytes_accessed=4 * LOW * highs * rows * cols, transcendentals=0
        ),
        name="restage",
    )(*blocks)


def start_blocks(slot, list_ref, back_ref, update_ref, sem):
    listed = list_ref.shape[0] // CAP
    for k in range(update_ref.shape[0] // CAP):
        matrix = list_ref[slot * listed + 2 * k]
        place = list_ref[slot * listed + 2 * k + 1]
        pltpu.make_async_copy(back_ref.at[place], update_ref.at[matrix], sem).start()


def wait_blocks(back_ref, update_ref, sem):
    span = pl.ds(0, update_ref.shape[0] // CAP)
    pltpu.make_async_copy(back_ref.at[span], update_ref.at[span], sem).wait()


def early_kernel(list_ref, whole_ref, owned_in, *refs):
    high_refs, (owned_ref, update_ref, back_s, own_sem, sem) = refs[:-5], refs[-5:]
    own = pltpu.make_async_copy(whole_ref, owned_ref.at[CAP - 1], own_sem)
    own.start()
    for h, high_ref in enumerate(high_refs):
        back_s[h * LOW : (h + 1) * LOW] = high_ref[...]
    start_blocks(0, list_ref, back_s, update_ref, sem)
    wait_blocks(back_s, update_ref, sem)
    own.wait()


def store_early(places, mats, matrix, owned, first):
    _, rows, cols = first[0].shape
    return pl.pallas_call(
        early_kernel,
        in_specs=[SMEM, VMEM, ANYWHERE] + [VMEM] * len(first),
        out_specs=[ANYWHERE, ANYWHERE],
        out_shape=[
            jax.ShapeDtypeStruct(owned.shape, jnp.bfloat16),
            jax.ShapeDtypeStruct((mats, rows, cols), jnp.bfloat16),
        ],
        scratch_shapes=[
            pltpu.VMEM((LOW * len(first), rows, cols), jnp.bfloat16),
            pltpu.SemaphoreType.DMA(()),
            pltpu.SemaphoreType.DMA(()),
        ],
        input_output_aliases={2: 0},
        compiler_params=PARAMS,
        cost_estimate=pl.CostEstimate(
            flops=0, bytes_accessed=8 * mats * rows * cols, transcendentals=0
        ),
        name="store_early",
    )(places, matrix, owned, *first)


def late_kernel(list_ref, back_ref, update_in, update_ref, sem):
    start_blocks(1, list_ref, back_ref, update_ref, sem)
    wait_blocks(back_ref, update_ref, sem)


def store_late(places, second, update):
    return pl.pallas_call(
        late_kernel,
        in_specs=[SMEM, VMEM, ANYWHERE],
        out_specs=ANYWHERE,
        out_shape=jax.ShapeDtypeStruct(update.shape, jnp.bfloat16),
        scratch_shapes=[pltpu.SemaphoreType.DMA(())],
        input_output_aliases={2: 0},
        compiler_params=PARAMS,
        cost_estimate=pl.CostEstimate(flops=0, bytes_accessed=4 * second.size, transcendentals=0),
        name="store_late",
    )(places, second, update)


def exchange(blocks, axes, groups=None):
    return lax.all_to_all(
        blocks, axes, split_axis=0, concat_axis=0, tiled=True, axis_index_groups=groups
    )


def swap(block, offset, devices):
    return lax.ppermute(block, AXES, [(d, d ^ offset) for d in range(devices)])


def on_device(gradients, momentum, owner_table):
    row_size = lax.axis_size("dp")
    col_size = lax.axis_size("owner")
    devices = row_size * col_size
    width = col_size // HALVES
    halves = [
        [r * col_size + half * width + c for r in range(row_size) for c in range(width)]
        for half in range(HALVES)
    ]
    first, other, rank = pack(gradients, momentum, owner_table, devices, col_size)
    arrived_first = exchange(first, AXES)
    new_momentum, second, places = update_momentum(
        gradients, momentum, owner_table, other, rank, col_size
    )
    arrived_first, second = lax.optimization_barrier((arrived_first, second))
    arrived_second = exchange(second, AXES)
    owned, *back_first = orthogonalize(0, other, arrived_first, row_size, col_size)
    low = [back_first[0]] + [
        swap(back_first[k], k * col_size, devices) for k in range(1, LOW)
    ]
    high = restage(low)
    _, arrived_second = lax.optimization_barrier((high, arrived_second))
    returned_first = [high[0]] + [
        swap(high[r * width + c], r * LOW * col_size + c, devices)
        for r in range(row_size // LOW)
        for c in range(width)
        if r or c
    ]
    matrix, back_second = orthogonalize(1, other, arrived_second, row_size, col_size)
    returned_first, back_second = lax.optimization_barrier((returned_first, back_second))
    returned_second = exchange(back_second, AXES, halves)
    owned, update = store_early(
        places, owner_table.shape[0], matrix, owned, returned_first
    )
    update = store_late(places, returned_second, update)
    return (new_momentum, update, owned)


def solution(mesh):
    return jax.shard_map(
        on_device,
        mesh=mesh,
        in_specs=(P(None, "dp", "owner"), P(None, "dp", "owner"), P()),
        out_specs=(P(None, "dp", "owner"), P(None, "dp", "owner"), P(("dp", "owner"), None, None)),
        check_vma=False,
    )
```
